32 devices in a mesh: fsdp: 4 (over y, x), ctx: 8 (over z, core).
Axes of the slice: x: 2, y: 2, z: 4, core: 2. Of those that a mesh axis runs over, the one named last changes fastest.
Arguments:
- tokens: bfloat16 [2, 4, 1024, 1536], P(None, 'fsdp', 'ctx'), may hold values from -6 to 6
- doc_starts: int32 [2, 4, 4], P(None, 'fsdp'), may hold values from 0 to 1023, as said below
- routes: int32 [2, 4, 1024, 4], P(None, 'fsdp', 'ctx'), may hold values from 0 to 7, all different within a row; in each aligned block of 128 rows (0 to 127, 128 to 255, ..., all dimensions but the last counted through in order) at most 80 rows name the same one
- gates: float32 [2, 4, 1024, 4], P(None, 'fsdp', 'ctx'), may hold values from 0.3 to 1.2
- attn_gain: bfloat16 [1536], P('fsdp'), may hold values from 0.25 to 1.75
- w_q: bfloat16 [1536, 1536], P('fsdp'), may hold values from -0.625 to 0.625
- key_value_weight: bfloat16 [1536, 1024], P('fsdp'), may hold values from -0.625 to 0.625
- w_o: bfloat16 [1536, 1536], P('fsdp'), may hold values from -0.15625 to 0.15625
- moe_gain: bfloat16 [1536], P('fsdp'), may hold values from 0.25 to 1.75
- expert_in: bfloat16 [8, 1536, 1024], P('fsdp'), may hold values from -0.15625 to 0.15625
- expert_out: bfloat16 [8, 512, 1536], P('fsdp'), may hold values from -0.25 to 0.25
- cotangent: bfloat16 [2, 4, 1024, 1536], P(None, 'fsdp', 'ctx'), may hold values from -6 to 6
Outputs:
- block_output: bfloat16 [2, 4, 1024, 1536], P(None, 'fsdp', 'ctx')
- input_grad: float32 [2, 4, 1024, 1536], P(None, 'fsdp', 'ctx')
- attn_gain_grad: float32 [1536], P('fsdp')
- w_q_grad: float32 [1536, 1536], P('fsdp')
- w_kv_grad: float32 [1536, 1024], P('fsdp')
- w_o_grad: float32 [1536, 1536], P('fsdp')
- moe_gain_grad: float32 [1536], P('fsdp')
- expert_in_grad: float32 [8, 1536, 1024], P('fsdp')
- expert_out_grad: float32 [8, 512, 1536], P('fsdp')
The draws below stay inside these ranges and needn't reach their ends.
Inputs may be any that keep to these rules, and one draw needn't show every extreme that they name: `doc_starts`: each sequence's 4 starts rise strictly from 0. `routes`: each row names 4 different experts; among the 128 rows of one device (aligned blocks) no expert is named more than 80 times, and in some block one is named exactly 80 times.
All inputs are finite; a program needn't handle non-finite values.
Results may differ from the reference program's by a relative error of at most 0.019.
Values may be sent and summed in bfloat16 or wider, within the bound.
A program may use at most 320 MiB of HBM per device.

```python
import math
import jax
import jax.numpy as jnp
import numpy as np
from jax import lax

MODEL_WIDTH = 1536
QUERY_HEADS = 24
KEY_VALUE_HEADS = 8
HEAD_SIZE = 64
F = 512
E = 8
TOP = 4
MB = 2
NDOC = 4
SEQUENCE_TOKENS = 1024
DEV_TOKENS = 128
NS = 4
CAP = 80


def draw_doc_starts(key, part):
    key = jax.random.fold_in(key, 11)
    pick_key, early_key, late_key, spread_key = jax.random.split(key, 4)
    number = MB * NS
    chosen = jax.random.randint(pick_key, (1, NS), 0, MB)
    spanning = (jnp.arange(MB, dtype=jnp.int32)[:, None] == chosen).reshape(number, 1)
    zeros_col = jnp.zeros((number, 1), jnp.int32)
    early = jax.random.randint(early_key, (number, 1), 1, DEV_TOKENS)
    late = jax.vmap(lambda subkey: jax.random.permutation(subkey, DEV_TOKENS)[:NDOC - 2])(jax.random.split(late_key, number))
    late = jnp.sort(late, axis=1) + (SEQUENCE_TOKENS - DEV_TOKENS)
    long_starts = jnp.concatenate([zeros_col, early, late], axis=1)
    spread = jax.vmap(lambda subkey: jax.random.permutation(subkey, SEQUENCE_TOKENS - 1)[:NDOC - 1])(jax.random.split(spread_key, number))
    spread = jnp.sort(spread, axis=1) + 1
    spread_starts = jnp.concatenate([zeros_col, spread], axis=1)
    starts = jnp.where(spanning, long_starts, spread_starts)
    return starts.reshape(MB, NS, NDOC).astype(jnp.int32)


def block_levels(stream_key, shape, cuts, low, top_value):
    def one(position, shards_of):
        draws = jax.random.uniform(jax.random.fold_in(jax.random.fold_in(stream_key, 6), position), (shards_of,), jnp.float32, low / len(cuts), top_value / len(cuts))
        return jnp.repeat(jnp.exp(draws), shape[position] // shards_of).reshape((-1,) + (1,) * (len(shape) - position - 1))

    loudness = one(*cuts[0])
    for cut in cuts[1:]:
        loudness = loudness * one(*cut)
    return loudness


def shared_out(key, own, number, rows, count, top, bound, skew):
    order = jax.random.permutation(key, count)
    packed, common = load_shares(count, rows * top, bound, skew, True), load_shares(count, rows * top, bound, skew, False)
    places = jnp.arange(count)

    def named(lengths, rotation):
        used = int((lengths > 0).sum())
        fixed = max(1, used // 4)
        shifted = fixed + (places - fixed + rotation * (used - fixed)) % max(1, count - fixed)
        return jnp.zeros((count,), jnp.int32).at[order[jnp.where(places < fixed, places, shifted)]].set(jnp.asarray(lengths, jnp.int32))

    lengths = jnp.where(number % 4 == 0, named(packed, number // 4), named(common, number - number // 4 - 1))
    mixed = jax.random.permutation(jax.random.fold_in(own, 3), count)
    source_of, sink = mixed[0:count // 2 * 2:2], mixed[1:count // 2 * 2:2]
    room = jnp.minimum(lengths[source_of] - 1, bound - lengths[sink]) // 2
    room = jnp.where((source_of == order[0]) | (sink == order[0]) | (lengths[sink] == 0), 0, jnp.maximum(room, 0))
    shifted = jax.random.randint(jax.random.fold_in(own, 4), (count // 2,), 0, 1 << 20) % (room + 1)
    lengths = lengths.at[source_of].add(-shifted).at[sink].add(shifted)
    labels = jnp.searchsorted(jnp.cumsum(lengths), jnp.arange(rows * top), side="right").astype(jnp.int32)
    table = labels.reshape(top, rows).T
    table = table[jax.random.permutation(jax.random.fold_in(own, 1), rows)]
    rotation = jax.random.randint(jax.random.fold_in(own, 2), (rows, 1), 0, top)
    return jnp.take_along_axis(table, (jnp.arange(top)[None, :] + rotation) % top, axis=1)


def load_shares(amount, total, reach, slope, full):
    weights = [(1 << 20) // math.isqrt(grade ** slope) + 1 for grade in range(1, amount + 1)]
    largest = reach if full else min(reach, max(-(-total // amount), total * weights[0] // sum(weights)))
    least = 1 if total - largest >= amount - 1 else 0
    holding, surplus = [largest] + [least] * (amount - 1), total - largest - least * (amount - 1)
    while surplus > 0:
        free = [i for i in range(1, amount) if holding[i] < largest] or [i for i in range(1, amount) if holding[i] < reach]
        mass, remaining = sum([weights[i] for i in free]), surplus
        for i in free:
            more = min(reach - holding[i], max(1, remaining * weights[i] // mass), surplus)
            holding[i] = holding[i] + more
            surplus = surplus - more
    return np.array(holding)


def normal_values(rng, dims, scale, most, cuts=(), kind=jnp.bfloat16):
    array = jax.random.normal(rng, dims, jnp.float32) * scale
    if len(cuts) > 0:
        array = block_levels(rng, dims, cuts, -0.22, 0.18) * array
    return jnp.clip(array, min=-most, max=most).astype(kind)


def setup_inputs(seed: int = 0) -> dict:
    seeds = jax.random.split(jax.random.key(seed), 13)
    tokens = normal_values(seeds[0], (MB, NS, SEQUENCE_TOKENS, MODEL_WIDTH), 1.0, 6.0, ((1, 4), (2, 8)))
    doc_starts = draw_doc_starts(jax.random.fold_in(seeds[12], 71), 0)
    routes_keys = jax.random.split(jax.random.fold_in(seeds[2], 1), MB * NS * SEQUENCE_TOKENS // DEV_TOKENS)
    routes_turns = jax.random.permutation(jax.random.fold_in(seeds[2], 3), MB * NS * SEQUENCE_TOKENS // DEV_TOKENS)
    routes = jax.vmap(lambda own, number: shared_out(jax.random.fold_in(seeds[2], 2), own, number, DEV_TOKENS, E, TOP, CAP, 1))(routes_keys, routes_turns).reshape((MB, NS, SEQUENCE_TOKENS, TOP))
    gates = jnp.clip(jnp.exp(math.log(1.2) - 1.3862944 * jax.random.uniform(seeds[3], (MB, NS, SEQUENCE_TOKENS, TOP), jnp.float32) ** block_levels(seeds[3], (MB, NS, SEQUENCE_TOKENS, TOP), ((1, 4), (2, 8)), -0.2, 0.2)), 0.3, 1.2)
    attn_gain = jnp.clip(1.0 + 0.15 * jax.random.normal(seeds[4], (MODEL_WIDTH,), jnp.float32), 0.25, 1.75).astype(jnp.bfloat16)
    w_q = normal_values(seeds[5], (MODEL_WIDTH, QUERY_HEADS * HEAD_SIZE), (MODEL_WIDTH // 16) ** -0.5, 0.625, ((0, 4),))
    key_value_weight = normal_values(seeds[6], (MODEL_WIDTH, 2 * KEY_VALUE_HEADS * HEAD_SIZE), (MODEL_WIDTH // 16) ** -0.5, 0.625, ((0, 4),))
    w_o = normal_values(seeds[7], (QUERY_HEADS * HEAD_SIZE, MODEL_WIDTH), (QUERY_HEADS * HEAD_SIZE) ** -0.5, 0.15625, ((0, 4),))
    moe_gain = jnp.clip(1.0 + 0.15 * jax.random.normal(seeds[8], (MODEL_WIDTH,), jnp.float32), 0.25, 1.75).astype(jnp.bfloat16)
    expert_in = normal_values(seeds[9], (E, MODEL_WIDTH, 2 * F), MODEL_WIDTH ** -0.5, 0.15625, ((0, 4),))
    expert_out = normal_values(seeds[10], (E, F, MODEL_WIDTH), F ** -0.5, 0.25, ((0, 4),))
    cotangent = normal_values(seeds[11], (MB, NS, SEQUENCE_TOKENS, MODEL_WIDTH), 1.0, 6.0, ((1, 4), (2, 8)))
    return {"tokens": tokens, "doc_starts": doc_starts, "routes": routes, "gates": gates, "attn_gain": attn_gain, "w_q": w_q, "key_value_weight": key_value_weight, "w_o": w_o, "moe_gain": moe_gain, "expert_in": expert_in, "expert_out": expert_out, "cotangent": cotangent}


eps = 1e-05
theta = 10000.0
highest = lax.Precision.HIGHEST

@jax.custom_vjp
def low(v):
    return lax.optimization_barrier(v.astype(jnp.bfloat16)).astype(jnp.float32)

@jax.custom_vjp
def low_back(v):
    return v

def low_keep(v):
    return (low(v), None)

def low_pass(kept, grad):
    return (grad,)

def back_keep(v):
    return (v, None)

def back_low(kept, grad):
    return (low(grad),)
low.defvjp(low_keep, low_pass)
low_back.defvjp(back_keep, back_low)

def rms_scale(weight_matrix, gain_vector):
    inverse = lax.rsqrt(lax.optimization_barrier(jnp.mean(weight_matrix * weight_matrix, axis=-1, keepdims=True)) + eps)
    return weight_matrix * inverse * gain_vector

def turn_angles(positions):
    frequency = theta ** (-jnp.arange(0, HEAD_SIZE, 2, dtype=jnp.float32) / HEAD_SIZE)
    angles = positions.astype(jnp.float32)[:, None] * frequency[None, :]
    doubled = jnp.concatenate([angles, angles], axis=1)
    return (jnp.cos(doubled)[:, None, :], jnp.sin(doubled)[:, None, :])

def apply_rotary(value_rows, cosine_table, sine_table):
    half_width = HEAD_SIZE // 2
    turned = jnp.concatenate([-value_rows[..., half_width:], value_rows[..., :half_width]], axis=-1)
    return value_rows * cosine_table + turned * sine_table

def document_index(doc_begin, positions):
    return lax.optimization_barrier(jnp.sum((doc_begin[None, :] <= positions[:, None]).astype(jnp.int32), axis=1))

def sequence_block(sequence, params, doc_begin, route, gate):
    gain_one, query_weight, pair_weight, output_weight, gain_two, expand, reduce_weight = params
    normed = low(rms_scale(sequence, gain_one))
    query_pre = jnp.dot(normed, query_weight, precision=highest)
    paired_preactivation = jnp.dot(normed, pair_weight, precision=highest)
    key_feature_width = KEY_VALUE_HEADS * HEAD_SIZE
    positions = jnp.arange(SEQUENCE_TOKENS, dtype=jnp.int32)
    cosine_table, sine_table = turn_angles(positions)
    query = low(apply_rotary(low_back(query_pre).reshape(SEQUENCE_TOKENS, QUERY_HEADS, HEAD_SIZE), cosine_table, sine_table))
    key_rows = low(apply_rotary(low_back(paired_preactivation[:, :key_feature_width]).reshape(SEQUENCE_TOKENS, KEY_VALUE_HEADS, HEAD_SIZE), cosine_table, sine_table))
    value_rows = low(low_back(paired_preactivation[:, key_feature_width:])).reshape(SEQUENCE_TOKENS, KEY_VALUE_HEADS, HEAD_SIZE)
    query_group_size = QUERY_HEADS // KEY_VALUE_HEADS
    keys_all = jnp.repeat(key_rows, query_group_size, axis=1)
    values_all = jnp.repeat(value_rows, query_group_size, axis=1)
    docs = document_index(doc_begin, positions)
    query_size = min(512, SEQUENCE_TOKENS)

    def query_block(first):
        query_part = lax.dynamic_slice_in_dim(query, first, query_size, 0)
        query_place = first + jnp.arange(query_size, dtype=jnp.int32)
        query_docs = lax.dynamic_slice_in_dim(docs, first, query_size, 0)
        score = low_back(jnp.einsum('qhd,khd->hqk', query_part, keys_all, precision=highest) / HEAD_SIZE)
        visible = (positions[None, :] <= query_place[:, None]) & (docs[None, :] == query_docs[:, None])
        attn_prob = jax.nn.softmax(jnp.where(visible[None], score, -1e+30), axis=-1)
        return jnp.einsum('hqk,khd->qhd', low(attn_prob), values_all, precision=highest)
    firsts = jnp.arange(SEQUENCE_TOKENS // query_size, dtype=jnp.int32) * query_size
    attended = lax.map(jax.checkpoint(query_block), firsts).reshape(SEQUENCE_TOKENS, QUERY_HEADS * HEAD_SIZE)
    attn = low(low_back(attended))
    middle = sequence + low_back(jnp.dot(attn, output_weight, precision=highest))
    moe_in = low(rms_scale(middle, gain_two))
    chosen = (route[:, :, None] == jnp.arange(E, dtype=jnp.int32)[None, None, :]).astype(jnp.float32)
    combine = lax.optimization_barrier(jnp.sum(gate[:, :, None] * chosen, axis=1))

    def add_expert(total, expert):
        up_gate = low_back(jnp.dot(moe_in, expand[expert], precision=highest))
        active = low(jax.nn.silu(up_gate[:, :F]) * up_gate[:, F:])
        result = low_back(jnp.dot(active, reduce_weight[expert], precision=highest))
        return (total + lax.dynamic_slice_in_dim(combine, expert, 1, 1) * result, None)
    mixed, _ = lax.scan(add_expert, jnp.zeros_like(middle), jnp.arange(E, dtype=jnp.int32))
    return middle + mixed

def reference(tokens, doc_starts, routes, gates, attn_gain, w_q, key_value_weight, w_o, moe_gain, expert_in, expert_out, cotangent):
    params = tuple((weight.astype(jnp.float32) for weight in (attn_gain, w_q, key_value_weight, w_o, moe_gain, expert_in, expert_out)))
    number = MB * NS
    inputs = (tokens.astype(jnp.float32).reshape(number, SEQUENCE_TOKENS, MODEL_WIDTH), doc_starts.reshape(number, NDOC), routes.reshape(number, SEQUENCE_TOKENS, TOP), gates.reshape(number, SEQUENCE_TOKENS, TOP), cotangent.astype(jnp.float32).reshape(number, SEQUENCE_TOKENS, MODEL_WIDTH))

    def step(totals, element):
        sequence, doc_begin, route, gate, out_grad = element
        value, pull_back = jax.vjp(lambda first, second: sequence_block(first, second, doc_begin, route, gate), sequence, params)
        sequence_grad, param_grads = pull_back(out_grad)
        totals = jax.tree.map(lambda left, right: left + right, totals, param_grads)
        return (totals, (value.astype(jnp.bfloat16), sequence_grad))
    start_totals = jax.tree.map(jnp.zeros_like, params)
    totals, (outputs, input_grads) = lax.scan(step, start_totals, inputs)
    return (outputs.reshape(MB, NS, SEQUENCE_TOKENS, MODEL_WIDTH), input_grads.reshape(MB, NS, SEQUENCE_TOKENS, MODEL_WIDTH), totals[0], totals[1], totals[2], totals[3], totals[4], totals[5], totals[6])
```

```python
import functools

import jax
import jax.numpy as jnp
from jax import lax
from jax.experimental import pallas as pl
from jax.experimental.pallas import tpu as pltpu
from jax.sharding import PartitionSpec as P

MODEL_WIDTH = 1536
QUERY_HEADS = 24
KEY_VALUE_HEADS = 8
HEAD_SIZE = 64
GROUP = QUERY_HEADS // KEY_VALUE_HEADS
KEY_WIDTH = KEY_VALUE_HEADS * HEAD_SIZE
F = 512
E = 8
TOP = 4
MB = 2
LANES = 128
PAIRS = KEY_WIDTH // LANES
PAIR_QUERY = 2 * GROUP * HEAD_SIZE
F_BLOCK = 256
VMEM_LIMIT = 60 * 1024 * 1024

eps = 1e-05
theta = 10000.0

NT = (((1,), (1,)), ((), ()))
TN = (((0,), (0,)), ((), ()))
bf16 = jnp.bfloat16
f32 = jnp.float32


def dot(left, right, dims=(((1,), (0,)), ((), ()))):
    return lax.dot_general(left, right, dims, preferred_element_type=f32)


def rotation_tables(positions):
    frequency = theta ** (-jnp.arange(0, HEAD_SIZE, 2, dtype=f32) / HEAD_SIZE)
    angles = positions.astype(f32)[:, None] * frequency[None, :]
    cosine, sine = jnp.cos(angles), jnp.sin(angles)
    repeat = LANES // HEAD_SIZE
    cosine = jnp.concatenate([cosine, cosine] * repeat, axis=1)
    sine = jnp.concatenate([-sine, sine] * repeat, axis=1)
    return cosine, sine


def lane_index(shape):
    return lax.broadcasted_iota(jnp.int32, shape, 1)


def rotate(tile, cosine, sine):
    half = HEAD_SIZE // 2
    ahead = pltpu.roll(tile, LANES - half, 1)
    behind = pltpu.roll(tile, half, 1)
    first = lane_index(tile.shape) % HEAD_SIZE < half
    return tile * cosine + jnp.where(first, ahead, behind) * sine


def rotate_pairs_kernel(pair_ref, cosine_ref, sine_ref, out_ref):
    cosine, sine = cosine_ref[...], sine_ref[...]
    for i in range(2 * KEY_WIDTH // LANES):
        cols = slice(i * LANES, (i + 1) * LANES)
        tile = pair_ref[:, cols]
        if i < KEY_WIDTH // LANES:
            tile = rotate(tile, cosine, sine)
        out_ref[:, cols] = tile.astype(bf16)


def rotate_pairs(pair_pre, cosine, sine):
    return pl.pallas_call(
        rotate_pairs_kernel,
        out_shape=jax.ShapeDtypeStruct(pair_pre.shape, bf16),
        compiler_params=pltpu.CompilerParams(vmem_limit_bytes=VMEM_LIMIT),
        name="rotate_pairs",
    )(pair_pre, cosine, sine)


def pair_gradient_kernel(count, cosine_ref, sine_ref, *refs):
    out_ref = refs[-1]
    cosine, sine = cosine_ref[...], sine_ref[...]
    for i in range(2 * KEY_WIDTH // LANES):
        cols = slice(i * LANES, (i + 1) * LANES)
        total = refs[0][:, cols].astype(f32)
        for ref in refs[1:count]:
            total = total + ref[:, cols].astype(f32)
        if i < KEY_WIDTH // LANES:
            total = rotate(total, cosine, -sine)
        out_ref[:, cols] = total.astype(bf16)


def pair_gradient(parts, cosine, sine):
    return pl.pallas_call(
        functools.partial(pair_gradient_kernel, len(parts)),
        out_shape=jax.ShapeDtypeStruct(parts[0].shape, bf16),
        compiler_params=pltpu.CompilerParams(vmem_limit_bytes=VMEM_LIMIT),
        name="pair_gradient",
    )(cosine, sine, *parts)


def grouped(tiles, half):
    mine = lane_index(tiles[0].shape) // HEAD_SIZE == half
    rows = []
    for j in range(GROUP * half, GROUP * half + GROUP):
        tile = tiles[j // 2]
        if j % 2 != half:
            tile = pltpu.roll(tile, HEAD_SIZE, 1)
        rows.append(jnp.where(mine, tile, 0.0))
    return jnp.concatenate(rows, axis=0).astype(bf16)


def ungrouped(per_half, rows):
    heads = []
    for j in range(2 * GROUP):
        half, place = j // GROUP, j % GROUP
        tile = per_half[half][place * rows : (place + 1) * rows]
        if j % 2 != half:
            tile = pltpu.roll(tile, HEAD_SIZE, 1)
        heads.append(tile)
    low = lane_index(heads[0].shape) < HEAD_SIZE
    return [jnp.where(low, heads[2 * i], heads[2 * i + 1]) for i in range(GROUP)]


def query_tiles(query_ref, cosine, sine):
    tiles = []
    for i in range(GROUP):
        tile = rotate(query_ref[:, i * LANES : (i + 1) * LANES], cosine, sine)
        tiles.append(tile.astype(bf16).astype(f32) * (1.0 / HEAD_SIZE))
    return tiles


def attention_forward_kernel(query_ref, cosine_ref, sine_ref, key_ref, value_ref, bias_ref, out_ref):
    rows = query_ref.shape[0]
    tiles = query_tiles(query_ref, cosine_ref[...], sine_ref[...])
    key, value = key_ref[...], value_ref[...]
    bias = bias_ref[...]
    results = []
    for half in range(2):
        scores = dot(grouped(tiles, half), key, NT)
        scores = jnp.concatenate(
            [scores[g * rows : (g + 1) * rows] + bias for g in range(GROUP)], axis=0
        )
        peak = jnp.max(scores, axis=1, keepdims=True)
        weights = jnp.exp(scores - peak)
        total = jnp.sum(weights, axis=1, keepdims=True)
        results.append(dot(weights.astype(bf16), value) / total)
    for i, tile in enumerate(ungrouped(results, rows)):
        out_ref[:, i * LANES : (i + 1) * LANES] = tile.astype(bf16)


def attention_forward(query_pre, cosine, sine, pairs, bias):
    rows, length = bias.shape
    whole = lambda shape: pl.BlockSpec(shape, lambda p: (0, 0))
    return pl.pallas_call(
        attention_forward_kernel,
        grid=(PAIRS,),
        in_specs=[
            pl.BlockSpec((rows, PAIR_QUERY), lambda p: (0, p)),
            whole((rows, LANES)),
            whole((rows, LANES)),
            pl.BlockSpec((length, LANES), lambda p: (0, p)),
            pl.BlockSpec((length, LANES), lambda p: (0, p + PAIRS)),
            whole((rows, length)),
        ],
        out_specs=pl.BlockSpec((rows, PAIR_QUERY), lambda p: (0, p)),
        out_shape=jax.ShapeDtypeStruct((rows, MODEL_WIDTH), bf16),
        compiler_params=pltpu.CompilerParams(vmem_limit_bytes=VMEM_LIMIT),
        cost_estimate=pl.CostEstimate(
            flops=16 * rows * length * MODEL_WIDTH,
            bytes_accessed=4 * length * MODEL_WIDTH,
            transcendentals=rows * length * QUERY_HEADS,
        ),
        name="attention_forward",
    )(query_pre, cosine, sine, pairs, pairs, bias)


def attention_backward_kernel(
    query_ref, cosine_ref, sine_ref, key_ref, value_ref, bias_ref, grad_ref, query_out, pair_out
):
    rows = query_ref.shape[0]
    cosine, sine = cosine_ref[...], sine_ref[...]
    tiles = query_tiles(query_ref, cosine, sine)
    grads = [grad_ref[:, i * LANES : (i + 1) * LANES].astype(f32) for i in range(GROUP)]
    key, value = key_ref[...], value_ref[...]
    key_grad, value_grad = None, None
    query_grads = []
    for half in range(2):
        query = grouped(tiles, half)
        grad = grouped(grads, half)
        scores = dot(key, query, NT) + bias_ref[...]
        weights = jnp.exp(scores - jnp.max(scores, axis=0, keepdims=True))
        prob = weights * (1.0 / jnp.sum(weights, axis=0, keepdims=True))
        prob_grad = dot(value, grad, NT)
        delta = jnp.sum(prob * prob_grad, axis=0, keepdims=True)
        score_grad = (prob * (prob_grad - delta)).astype(bf16)
        value_part = dot(prob.astype(bf16), grad)
        key_part = dot(score_grad, query)
        value_grad = value_part if half == 0 else value_grad + value_part
        key_grad = key_part if half == 0 else key_grad + key_part
        query_grads.append(dot(score_grad, key, TN))
    for i, tile in enumerate(ungrouped(query_grads, rows)):
        tile = rotate(tile * (1.0 / HEAD_SIZE), cosine, -sine)
        query_out[:, i * LANES : (i + 1) * LANES] = tile.astype(bf16)
    first = pl.multiple_of(pl.program_id(0) * LANES, LANES)
    pair_out[:, pl.ds(first, LANES)] = key_grad.astype(bf16)
    pair_out[:, pl.ds(first + KEY_WIDTH, LANES)] = value_grad.astype(bf16)


def attention_backward(query_pre, cosine, sine, pairs, bias, grad):
    rows = query_pre.shape[0]
    length = pairs.shape[0]
    whole = lambda shape: pl.BlockSpec(shape, lambda p: (0, 0))
    return pl.pallas_call(
        attention_backward_kernel,
        grid=(PAIRS,),
        in_specs=[
            pl.BlockSpec((rows, PAIR_QUERY), lambda p: (0, p)),
            whole((rows, LANES)),
            whole((rows, LANES)),
            pl.BlockSpec((length, LANES), lambda p: (0, p)),
            pl.BlockSpec((length, LANES), lambda p: (0, p + PAIRS)),
            whole(bias.shape),
            pl.BlockSpec((rows, PAIR_QUERY), lambda p: (0, p)),
        ],
        out_specs=[
            pl.BlockSpec((rows, PAIR_QUERY), lambda p: (0, p)),
            whole((length, 2 * KEY_WIDTH)),
        ],
        out_shape=[
            jax.ShapeDtypeStruct((rows, MODEL_WIDTH), bf16),
            jax.ShapeDtypeStruct((length, 2 * KEY_WIDTH), bf16),
        ],
        compiler_params=pltpu.CompilerParams(vmem_limit_bytes=VMEM_LIMIT),
        cost_estimate=pl.CostEstimate(
            flops=40 * rows * length * MODEL_WIDTH,
            bytes_accessed=8 * length * MODEL_WIDTH,
            transcendentals=rows * length * QUERY_HEADS,
        ),
        name="attention_backward",
    )(query_pre, cosine, sine, pairs, pairs, bias, grad)


def experts_kernel(parts, rows, steps, combine_ref, gate_ref, up_ref, down_ref, *refs):
    rows_in, grads_in = refs[:parts], refs[parts : 2 * parts]
    refs = refs[2 * parts :]
    results, row_grads = refs[:parts], refs[parts : 2 * parts]
    active_out, gate_out, up_out, rows_all, grads_all, result_sum, grad_sum = refs[2 * parts :]
    step = pl.program_id(0) * pl.num_programs(1) + pl.program_id(1)

    @pl.when(step == 0)
    def _():
        for k in range(parts):
            place = slice(k * rows, (k + 1) * rows)
            rows_all[place] = rows_in[k][...]
            grads_all[place] = grads_in[k][...]
        result_sum[...] = jnp.zeros_like(result_sum)
        grad_sum[...] = jnp.zeros_like(grad_sum)

    inputs, out_grad, combine = rows_all[...], grads_all[...], combine_ref[0]
    gate_weight, up_weight, down_weight = gate_ref[0], up_ref[0], down_ref[0]
    gate = dot(inputs, gate_weight)
    up = dot(inputs, up_weight)
    sigmoid = jax.nn.sigmoid(gate)
    silu = gate * sigmoid
    active = (silu * up * combine).astype(bf16)
    active_grad = dot(out_grad, down_weight, NT) * combine
    gate_grad = (active_grad * up * sigmoid * (1.0 + gate * (1.0 - sigmoid))).astype(bf16)
    up_grad = (active_grad * silu).astype(bf16)
    active_out[...] = active
    gate_out[...] = gate_grad
    up_out[...] = up_grad
    result_sum[...] += dot(active, down_weight)
    grad_sum[...] += dot(gate_grad, gate_weight, NT) + dot(up_grad, up_weight, NT)

    @pl.when(step == steps - 1)
    def _():
        for k in range(parts):
            place = slice(k * rows, (k + 1) * rows)
            results[k][...] = result_sum[place].astype(bf16)
            row_grads[k][...] = grad_sum[place].astype(bf16)


def experts(row_parts, grad_parts, combine, expert_in, expert_out):
    parts = len(row_parts)
    rows = row_parts[0].shape[0]
    held = expert_in.shape[0]
    tokens = parts * rows
    blocks = F // F_BLOCK
    whole = pl.BlockSpec((rows, MODEL_WIDTH), lambda e, b: (0, 0))
    piece = pl.BlockSpec((tokens, F_BLOCK), lambda e, b: (0, e * blocks + b))
    row_shape = jax.ShapeDtypeStruct((rows, MODEL_WIDTH), bf16)
    piece_shape = jax.ShapeDtypeStruct((tokens, held * F), bf16)
    out = pl.pallas_call(
        functools.partial(experts_kernel, parts, rows, held * blocks),
        grid=(held, blocks),
        in_specs=[
            pl.BlockSpec((1, tokens, 1), lambda e, b: (e, 0, 0)),
            pl.BlockSpec((1, MODEL_WIDTH, F_BLOCK), lambda e, b: (e, 0, b)),
            pl.BlockSpec((1, MODEL_WIDTH, F_BLOCK), lambda e, b: (e, 0, b + blocks)),
            pl.BlockSpec((1, F_BLOCK, MODEL_WIDTH), lambda e, b: (e, b, 0)),
        ]
        + [whole] * (2 * parts),
        out_specs=[whole] * (2 * parts) + [piece] * 3,
        out_shape=[row_shape] * (2 * parts) + [piece_shape] * 3,
        scratch_shapes=[
            pltpu.VMEM((tokens, MODEL_WIDTH), bf16),
            pltpu.VMEM((tokens, MODEL_WIDTH), bf16),
            pltpu.VMEM((tokens, MODEL_WIDTH), f32),
            pltpu.VMEM((tokens, MODEL_WIDTH), f32),
        ],
        compiler_params=pltpu.CompilerParams(vmem_limit_bytes=VMEM_LIMIT),
        cost_estimate=pl.CostEstimate(
            flops=12 * tokens * held * MODEL_WIDTH * F,
            bytes_accessed=6 * held * MODEL_WIDTH * F + 20 * tokens * MODEL_WIDTH,
            transcendentals=tokens * held * F,
        ),
        name="experts",
    )(combine, expert_in, expert_in, expert_out, *row_parts, *grad_parts)
    return out[:parts], out[parts : 2 * parts], out[2 * parts :]


def expert_weights_kernel(parts, rows, *refs):
    row_refs, grad_refs = refs[: MB * parts], refs[MB * parts : 2 * MB * parts]
    refs = refs[2 * MB * parts :]
    active_refs, gate_refs, up_refs = refs[:MB], refs[MB : 2 * MB], refs[2 * MB : 3 * MB]
    gate_out, up_out, down_out, turned, grads_all = refs[3 * MB :]
    step = pl.program_id(0) * pl.num_programs(1) + pl.program_id(1)

    @pl.when(step == 0)
    def _():
        for k in range(MB * parts):
            place = slice(k * rows, (k + 1) * rows)
            turned[:, place] = row_refs[k][...].T
            grads_all[place] = grad_refs[k][...]

    join = lambda items: jnp.concatenate([item[...] for item in items], axis=0)
    gate_out[0] = dot(turned[...], join(gate_refs)).astype(bf16)
    up_out[0] = dot(turned[...], join(up_refs)).astype(bf16)
    down_out[0] = dot(join(active_refs), grads_all[...], TN).astype(bf16)


def expert_weights(row_parts, grad_parts, pieces, held):
    rows = row_parts[0].shape[0]
    parts = len(row_parts) // MB
    tokens = parts * rows
    blocks = F // F_BLOCK
    whole = pl.BlockSpec((rows, MODEL_WIDTH), lambda e, b: (0, 0))
    piece = pl.BlockSpec((tokens, F_BLOCK), lambda e, b: (0, e * blocks + b))
    wide = pl.BlockSpec((1, MODEL_WIDTH, F_BLOCK), lambda e, b: (e, 0, b))
    return pl.pallas_call(
        functools.partial(expert_weights_kernel, parts, rows),
        grid=(held, blocks),
        in_specs=[whole] * (2 * MB * parts) + [piece] * (3 * MB),
        out_specs=[wide, wide, pl.BlockSpec((1, F_BLOCK, MODEL_WIDTH), lambda e, b: (e, b, 0))],
        out_shape=[
            jax.ShapeDtypeStruct((held, MODEL_WIDTH, F), bf16),
            jax.ShapeDtypeStruct((held, MODEL_WIDTH, F), bf16),
            jax.ShapeDtypeStruct((held, F, MODEL_WIDTH), bf16),
        ],
        scratch_shapes=[
            pltpu.VMEM((MODEL_WIDTH, MB * tokens), bf16),
            pltpu.VMEM((MB * tokens, MODEL_WIDTH), bf16),
        ],
        compiler_params=pltpu.CompilerParams(vmem_limit_bytes=VMEM_LIMIT),
        cost_estimate=pl.CostEstimate(
            flops=6 * MB * tokens * held * MODEL_WIDTH * F,
            bytes_accessed=6 * held * MODEL_WIDTH * F + 8 * MB * tokens * MODEL_WIDTH,
            transcendentals=0,
        ),
        name="expert_weights",
    )(*row_parts, *grad_parts, *[pieces[m][i] for i in range(3) for m in range(MB)])


class Links:
    def __init__(self):
        self.shards = lax.axis_size("fsdp")
        self.contexts = lax.axis_size("ctx")
        self.chips = self.contexts // 2
        self.shard = lax.axis_index("fsdp")
        self.context = lax.axis_index("ctx")
        self.chip = self.context // 2
        self.core = self.context % 2

    def across(self, array, k):
        return lax.ppermute(array, "fsdp", [(i, i ^ k) for i in range(self.shards)])

    def other_core(self, array):
        return lax.ppermute(array, "ctx", [(i, i ^ 1) for i in range(self.contexts)])

    def shift(self, array, s):
        n = self.contexts
        return lax.ppermute(array, "ctx", [(i, (i + 2 * s) % n) for i in range(n)])

    def step(self, array, first, last, direction):
        pairs = [
            (2 * i + core, 2 * (i + direction) + core) for i in range(first, last + 1) for core in range(2)
        ]
        return lax.ppermute(array, "ctx", pairs)

    def to_relative(self, array):
        width = array.shape[-1] // (2 * self.shards)
        pieces = [[array[..., (2 * b + h) * width : (2 * b + h + 1) * width] for b in range(self.shards)] for h in range(2)]
        return jnp.concatenate(sum(self._swapped(pieces), []), axis=-1)

    def to_absolute(self, array):
        width = array.shape[-1] // (2 * self.shards)
        pieces = [
            [array[..., (h * self.shards + b) * width : (h * self.shards + b + 1) * width] for b in range(self.shards)]
            for h in range(2)
        ]
        pieces = self._swapped(pieces)
        return jnp.concatenate([pieces[h][b] for b in range(self.shards) for h in range(2)], axis=-1)

    def _swapped(self, pieces):
        bit = 1
        while bit < self.shards:
            flag = (self.shard & bit) != 0
            pieces = [[jnp.where(flag, row[b ^ bit], row[b]) for b in range(self.shards)] for row in pieces]
            bit *= 2
        flag = self.core == 1
        return [
            [jnp.where(flag, pieces[1 - h][b], pieces[h][b]) for b in range(self.shards)] for h in range(2)
        ]

    def gather_rows(self, weight):
        half = weight.shape[0] // 2
        mine = lax.dynamic_slice_in_dim(weight, self.core * half, half, 0)
        rest = lax.dynamic_slice_in_dim(weight, (1 - self.core) * half, half, 0)
        arrived = [self.across(mine, k) for k in range(1, self.shards)]
        passed = [self.other_core(part) for part in arrived]
        return jnp.concatenate([mine] + arrived + [rest] + passed, axis=0)

    def scatter_rows(self, grad):
        half = grad.shape[0] // 2
        mine = grad[:half].astype(f32) + self.other_core(grad[half:]).astype(f32)
        mine = mine.astype(bf16)
        size = half // self.shards
        total = mine[:size].astype(f32)
        for k in range(1, self.shards):
            total = total + self.across(mine[k * size : (k + 1) * size], k).astype(f32)
        return total.astype(bf16)

    def core_halves(self, grad):
        half = grad.shape[0] // 2
        mine = lax.dynamic_slice_in_dim(grad, self.core * half, half, 0)
        rest = lax.dynamic_slice_in_dim(grad, (1 - self.core) * half, half, 0)
        return (mine.astype(f32) + self.other_core(rest).astype(f32)).astype(bf16)

    def sum_over_chips(self, half):
        n = self.chips
        size = half.shape[0] // n
        block = lambda j: lax.dynamic_slice_in_dim(half, jnp.clip(j, 0, n - 1) * size, size, 0).astype(f32)
        from_left, from_right = None, None
        for t in range(1, n):
            right, left = block(n - t + self.chip), block(t - n + self.chip)
            if t > 1:
                right = right + from_left.astype(f32)
                left = left + from_right.astype(f32)
            from_left = self.step(right.astype(bf16), 0, t - 1, 1)
            from_right = self.step(left.astype(bf16), n - t, n - 1, -1)
        total = block(self.chip) + from_left.astype(f32) + from_right.astype(f32)
        total = total.astype(bf16)
        going_right, going_left = [total], [total]
        for t in range(1, n):
            going_right.append(self.step(going_right[-1], t - 1, n - 2, 1))
            going_left.append(self.step(going_left[-1], 1, n - t, -1))
        return [total] + [going_right[t] + going_left[n - t] for t in range(1, n)]

    def place_rows(self, blocks, out, column):
        size = blocks[0].shape[0]
        others = [self.other_core(block) for block in blocks]
        for core, items in ((self.core, blocks), (1 - self.core, others)):
            for t, item in enumerate(items):
                row = (core * self.chips + (self.chip - t + self.chips) % self.chips) * size
                out = lax.dynamic_update_slice(out, item.astype(f32), (row, column))
        return out


def shards(
    tokens,
    doc_starts,
    routes,
    gates,
    attn_gain,
    w_q,
    key_value_weight,
    w_o,
    moe_gain,
    expert_in,
    expert_out,
    cotangent,
):
    links = Links()
    rows = tokens.shape[2]
    length = rows * links.contexts
    held = expert_in.shape[0]
    positions = links.context * rows + jnp.arange(rows, dtype=jnp.int32)
    cosine, sine = rotation_tables(positions)
    chips_back = (links.chip - jnp.arange(links.chips, dtype=jnp.int32) + links.chips) % links.chips
    chunk_ids = jnp.concatenate([2 * chips_back + links.core, 2 * chips_back + 1 - links.core])
    key_places = (chunk_ids[:, None] * rows + jnp.arange(rows, dtype=jnp.int32)[None, :]).reshape(length)

    gains = lax.all_gather(jnp.stack([attn_gain, moe_gain]), "fsdp", axis=1, tiled=True).astype(f32)
    gain_one, gain_two = links.to_relative(gains[0]), gains[1]

    pair_weight = links.gather_rows(key_value_weight)
    query_weight = links.gather_rows(w_q)
    output_weight = links.gather_rows(w_o)

    flat_tokens = tokens.reshape(MB * rows, MODEL_WIDTH)
    relative = links.to_relative(flat_tokens).astype(f32)
    scale_one = lax.rsqrt(jnp.mean(relative * relative, axis=-1, keepdims=True) + eps)
    unit_one = relative * scale_one
    normed = (unit_one * gain_one).astype(bf16)
    pairs = rotate_pairs(
        dot(normed, pair_weight), jnp.concatenate([cosine] * MB), jnp.concatenate([sine] * MB)
    )
    query_pre = dot(normed, query_weight)

    expert_ids = jnp.arange(E, dtype=jnp.int32)
    chosen = (routes.reshape(MB, rows, TOP)[..., None] == expert_ids).astype(f32)
    combine = jnp.sum(gates.reshape(MB, rows, TOP)[..., None] * chosen, axis=2)
    combine = jnp.concatenate([combine] + [links.across(combine, k) for k in range(1, links.shards)], axis=1)
    combine = lax.dynamic_slice_in_dim(combine, links.shard * held, held, 2)
    combine = combine.transpose(0, 2, 1)[..., None]

    all_pairs, biases, biases_turned = [], [], []
    for m in range(MB):
        own = pairs[m * rows : (m + 1) * rows]
        near = jnp.concatenate([own] + [links.shift(own, s) for s in range(1, links.chips)], axis=0)
        all_pairs.append(jnp.concatenate([near, links.other_core(near)], axis=0))
        starts = doc_starts[m, 0]
        begin = jnp.max(jnp.where(starts[None, :] <= positions[:, None], starts[None, :], 0), axis=1)
        seen = (key_places[None, :] <= positions[:, None]) & (key_places[None, :] >= begin[:, None])
        biases.append(jnp.where(seen, 0.0, -1e30).astype(f32))
        places, begins = jnp.tile(positions, GROUP), jnp.tile(begin, GROUP)
        seen = (key_places[:, None] <= places[None, :]) & (key_places[:, None] >= begins[None, :])
        biases_turned.append(jnp.where(seen, 0.0, -1e30).astype(f32))

    kept = []
    outputs = []
    for m in range(MB):
        own = slice(m * rows, (m + 1) * rows)
        attn = attention_forward(query_pre[own], cosine, sine, all_pairs[m], biases[m])
        attn = links.to_relative(attn)
        middle = flat_tokens[own].astype(f32) + dot(attn, output_weight)
        scale_two = lax.rsqrt(jnp.mean(middle * middle, axis=-1, keepdims=True) + eps)
        unit_two = middle * scale_two
        moe_in = (unit_two * gain_two).astype(bf16)
        out_grad = cotangent[m, 0]
        row_parts = [moe_in] + [links.across(moe_in, k) for k in range(1, links.shards)]
        grad_parts = [out_grad] + [links.across(out_grad, k) for k in range(1, links.shards)]
        results, row_grads, pieces = experts(row_parts, grad_parts, combine[m], expert_in, expert_out)
        final = middle + results[0].astype(f32)
        for k in range(1, links.shards):
            final = final + links.across(results[k], k).astype(f32)
        outputs.append(final.astype(bf16))
        kept.append((attn, unit_two, scale_two, row_parts, grad_parts, row_grads, pieces))

    expert_grads = expert_weights(
        sum([k[3] for k in kept], []), sum([k[4] for k in kept], []), [k[6] for k in kept], held
    )

    expand_total = jnp.zeros((held * MODEL_WIDTH, 2 * F), f32)
    reduce_total = jnp.zeros((held * F, MODEL_WIDTH), f32)
    gate_grad, up_grad, down_grad = [g.reshape(-1, g.shape[-1]) for g in expert_grads]
    expand_total = links.place_rows(links.sum_over_chips(links.core_halves(gate_grad)), expand_total, 0)
    expand_total = links.place_rows(links.sum_over_chips(links.core_halves(up_grad)), expand_total, F)
    reduce_total = links.place_rows(links.sum_over_chips(links.core_halves(down_grad)), reduce_total, 0)

    input_grads, query_lows, pair_lows, middle_lows = [], [], [], []
    gain_one_grad, gain_two_grad = 0.0, 0.0
    for m in range(MB):
        own = slice(m * rows, (m + 1) * rows)
        attn, unit_two, scale_two, _, _, row_grads, _ = kept[m]
        moe_in_grad = row_grads[0].astype(f32)
        for k in range(1, links.shards):
            moe_in_grad = moe_in_grad + links.across(row_grads[k], k).astype(f32)
        gain_two_grad = gain_two_grad + jnp.sum(moe_in_grad * unit_two, axis=0)
        weighted = moe_in_grad * gain_two
        inner = jnp.mean(weighted * unit_two, axis=-1, keepdims=True)
        middle_grad = cotangent[m, 0].astype(f32) + (weighted - unit_two * inner) * scale_two
        middle_low = middle_grad.astype(bf16)
        attn_grad = links.to_absolute(dot(middle_low, output_weight, NT).astype(bf16))
        query_low, pair_grad = attention_backward(
            query_pre[own], cosine, sine, all_pairs[m], biases_turned[m], attn_grad
        )
        near = links.chips * rows
        part = pair_grad[:near].astype(f32) + links.other_core(pair_grad[near:]).astype(f32)
        part = part.astype(bf16)
        parts = [part[:rows]]
        for s in range(1, links.chips):
            parts.append(links.shift(part[s * rows : (s + 1) * rows], -s))
        pair_low = pair_gradient(parts, cosine, sine)
        normed_grad = dot(query_low, query_weight, NT) + dot(pair_low, pair_weight, NT)
        gain_one_grad = gain_one_grad + jnp.sum(normed_grad * unit_one[own], axis=0)
        weighted = normed_grad * gain_one
        inner = jnp.mean(weighted * unit_one[own], axis=-1, keepdims=True)
        residual_grad = (weighted - unit_one[own] * inner) * scale_one[own]
        input_grads.append(middle_grad + links.to_absolute(residual_grad))
        query_lows.append(query_low)
        pair_lows.append(pair_low)
        middle_lows.append(middle_low)

    join = lambda items: jnp.concatenate(items, axis=0)
    width = w_q.shape[0]

    def dense_total(grad):
        blocks = links.sum_over_chips(links.scatter_rows(grad))
        return links.place_rows(blocks, jnp.zeros((width, grad.shape[1]), f32), 0)

    output_grad = dot(join([k[0] for k in kept]), join(middle_lows), TN).astype(bf16)
    output_total = dense_total(output_grad)
    query_total = dense_total(dot(normed, join(query_lows), TN).astype(bf16))
    pair_weight_grad = dot(normed, join(pair_lows), TN).astype(bf16)
    gain_grads = jnp.stack([gain_one_grad, links.to_relative(gain_two_grad)], axis=1)
    gain_grads = jnp.pad(gain_grads, ((0, 0), (0, LANES - 2))).astype(bf16)
    pair_total = dense_total(jnp.concatenate([pair_weight_grad, gain_grads], axis=1))

    return (
        jnp.stack(outputs)[:, None],
        jnp.stack(input_grads)[:, None],
        pair_total[:, 2 * KEY_WIDTH],
        query_total,
        pair_total[:, : 2 * KEY_WIDTH],
        output_total,
        pair_total[:, 2 * KEY_WIDTH + 1],
        expand_total.reshape(held, MODEL_WIDTH, 2 * F),
        reduce_total.reshape(held, F, MODEL_WIDTH),
    )


def solution(mesh):
    return jax.shard_map(
        shards,
        mesh=mesh,
        in_specs=(
            P(None, "fsdp", "ctx", None),
            P(None, "fsdp", None),
            P(None, "fsdp", "ctx", None),
            P(None, "fsdp", "ctx", None),
            P("fsdp"),
            P("fsdp", None),
            P("fsdp", None),
            P("fsdp", None),
            P("fsdp"),
            P("fsdp", None, None),
            P("fsdp", None, None),
            P(None, "fsdp", "ctx", None),
        ),
        out_specs=(
            P(None, "fsdp", "ctx", None),
            P(None, "fsdp", "ctx", None),
            P("fsdp"),
            P("fsdp", None),
            P("fsdp", None),
            P("fsdp", None),
            P("fsdp"),
            P("fsdp", None, None),
            P("fsdp", None, None),
        ),
        check_vma=False,
    )
```

```python
import functools

import jax
import jax.numpy as jnp
from jax import lax
from jax.experimental import pallas as pl
from jax.experimental.pallas import tpu as pltpu
from jax.sharding import PartitionSpec as P

MODEL_WIDTH = 1536
QUERY_HEADS = 24
KEY_VALUE_HEADS = 8
HEAD_SIZE = 64
GROUP = QUERY_HEADS // KEY_VALUE_HEADS
KEY_WIDTH = KEY_VALUE_HEADS * HEAD_SIZE
F = 512
E = 8
TOP = 4
MB = 2
LANES = 128
PAIRS = KEY_WIDTH // LANES
PAIR_QUERY = 2 * GROUP * HEAD_SIZE
F_BLOCK = 256
VMEM_LIMIT = 60 * 1024 * 1024

eps = 1e-05
theta = 10000.0

NT = (((1,), (1,)), ((), ()))
TN = (((0,), (0,)), ((), ()))
bf16 = jnp.bfloat16
f32 = jnp.float32


def dot(left, right, dims=(((1,), (0,)), ((), ()))):
    return lax.dot_general(left, right, dims, preferred_element_type=f32)


def rotation_tables(positions):
    frequency = theta ** (-jnp.arange(0, HEAD_SIZE, 2, dtype=f32) / HEAD_SIZE)
    angles = positions.astype(f32)[:, None] * frequency[None, :]
    cosine, sine = jnp.cos(angles), jnp.sin(angles)
    repeat = LANES // HEAD_SIZE
    cosine = jnp.concatenate([cosine, cosine] * repeat, axis=1)
    sine = jnp.concatenate([-sine, sine] * repeat, axis=1)
    return cosine, sine


def lane_index(shape):
    return lax.broadcasted_iota(jnp.int32, shape, 1)


def rotate(tile, cosine, sine):
    half = HEAD_SIZE // 2
    ahead = pltpu.roll(tile, LANES - half, 1)
    behind = pltpu.roll(tile, half, 1)
    first = lane_index(tile.shape) % HEAD_SIZE < half
    return tile * cosine + jnp.where(first, ahead, behind) * sine


def rotate_pairs_kernel(pair_ref, cosine_ref, sine_ref, out_ref):
    cosine, sine = cosine_ref[...], sine_ref[...]
    for i in range(2 * KEY_WIDTH // LANES):
        cols = slice(i * LANES, (i + 1) * LANES)
        tile = pair_ref[:, cols]
        if i < KEY_WIDTH // LANES:
            tile = rotate(tile, cosine, sine)
        out_ref[:, cols] = tile.astype(bf16)


def rotate_pairs(pair_pre, cosine, sine):
    return pl.pallas_call(
        rotate_pairs_kernel,
        out_shape=jax.ShapeDtypeStruct(pair_pre.shape, bf16),
        compiler_params=pltpu.CompilerParams(vmem_limit_bytes=VMEM_LIMIT),
        name="rotate_pairs",
    )(pair_pre, cosine, sine)


def pair_gradient_kernel(count, cosine_ref, sine_ref, *refs):
    out_ref = refs[-1]
    cosine, sine = cosine_ref[...], sine_ref[...]
    for i in range(2 * KEY_WIDTH // LANES):
        cols = slice(i * LANES, (i + 1) * LANES)
        total = refs[0][:, cols].astype(f32)
        for ref in refs[1:count]:
            total = total + ref[:, cols].astype(f32)
        if i < KEY_WIDTH // LANES:
            total = rotate(total, cosine, -sine)
        out_ref[:, cols] = total.astype(bf16)


def pair_gradient(parts, cosine, sine):
    return pl.pallas_call(
        functools.partial(pair_gradient_kernel, len(parts)),
        out_shape=jax.ShapeDtypeStruct(parts[0].shape, bf16),
        compiler_params=pltpu.CompilerParams(vmem_limit_bytes=VMEM_LIMIT),
        name="pair_gradient",
    )(cosine, sine, *parts)


def grouped(tiles, half):
    mine = lane_index(tiles[0].shape) // HEAD_SIZE == half
    rows = []
    for j in range(GROUP * half, GROUP * half + GROUP):
        tile = tiles[j // 2]
        if j % 2 != half:
            tile = pltpu.roll(tile, HEAD_SIZE, 1)
        rows.append(jnp.where(mine, tile, 0.0))
    return jnp.concatenate(rows, axis=0).astype(bf16)


def ungrouped(per_half, rows):
    heads = []
    for j in range(2 * GROUP):
        half, place = j // GROUP, j % GROUP
        tile = per_half[half][place * rows : (place + 1) * rows]
        if j % 2 != half:
            tile = pltpu.roll(tile, HEAD_SIZE, 1)
        heads.append(tile)
    low = lane_index(heads[0].shape) < HEAD_SIZE
    return [jnp.where(low, heads[2 * i], heads[2 * i + 1]) for i in range(GROUP)]


def query_tiles(query_ref, cosine, sine):
    tiles = []
    for i in range(GROUP):
        tile = rotate(query_ref[:, i * LANES : (i + 1) * LANES], cosine, sine)
        tiles.append(tile.astype(bf16).astype(f32) * (1.0 / HEAD_SIZE))
    return tiles


def attention_forward_kernel(query_ref, cosine_ref, sine_ref, key_ref, value_ref, bias_ref, out_ref):
    rows = query_ref.shape[0]
    tiles = query_tiles(query_ref, cosine_ref[...], sine_ref[...])
    key, value = key_ref[...], value_ref[...]
    bias = bias_ref[...]
    results = []
    for half in range(2):
        scores = dot(grouped(tiles, half), key, NT)
        scores = jnp.concatenate(
            [scores[g * rows : (g + 1) * rows] + bias for g in range(GROUP)], axis=0
        )
        peak = jnp.max(scores, axis=1, keepdims=True)
        weights = jnp.exp(scores - peak)
        total = jnp.sum(weights, axis=1, keepdims=True)
        results.append(dot(weights.astype(bf16), value) / total)
    for i, tile in enumerate(ungrouped(results, rows)):
        out_ref[:, i * LANES : (i + 1) * LANES] = tile.astype(bf16)


def attention_forward(query_pre, cosine, sine, pairs, bias):
    rows, length = bias.shape
    whole = lambda shape: pl.BlockSpec(shape, lambda p: (0, 0))
    return pl.pallas_call(
        attention_forward_kernel,
        grid=(PAIRS,),
        in_specs=[
            pl.BlockSpec((rows, PAIR_QUERY), lambda p: (0, p)),
            whole((rows, LANES)),
            whole((rows, LANES)),
            pl.BlockSpec((length, LANES), lambda p: (0, p)),
            pl.BlockSpec((length, LANES), lambda p: (0, p + PAIRS)),
            whole((rows, length)),
        ],
        out_specs=pl.BlockSpec((rows, PAIR_QUERY), lambda p: (0, p)),
        out_shape=jax.ShapeDtypeStruct((rows, MODEL_WIDTH), bf16),
        compiler_params=pltpu.CompilerParams(vmem_limit_bytes=VMEM_LIMIT),
        cost_estimate=pl.CostEstimate(
            flops=16 * rows * length * MODEL_WIDTH,
            bytes_accessed=4 * length * MODEL_WIDTH,
            transcendentals=rows * length * QUERY_HEADS,
        ),
        name="attention_forward",
    )(query_pre, cosine, sine, pairs, pairs, bias)


def attention_backward_kernel(
    query_ref, cosine_ref, sine_ref, key_ref, value_ref, bias_ref, grad_ref, query_out, pair_out
):
    rows = query_ref.shape[0]
    cosine, sine = cosine_ref[...], sine_ref[...]
    tiles = query_tiles(query_ref, cosine, sine)
    grads = [grad_ref[:, i * LANES : (i + 1) * LANES].astype(f32) for i in range(GROUP)]
    key, value = key_ref[...], value_ref[...]
    key_grad, value_grad = None, None
    query_grads = []
    for half in range(2):
        query = grouped(tiles, half)
        grad = grouped(grads, half)
        scores = dot(key, query, NT) + bias_ref[...]
        weights = jnp.exp(scores - jnp.max(scores, axis=0, keepdims=True))
        prob = weights * (1.0 / jnp.sum(weights, axis=0, keepdims=True))
        prob_grad = dot(value, grad, NT)
        delta = jnp.sum(prob * prob_grad, axis=0, keepdims=True)
        score_grad = (prob * (prob_grad - delta)).astype(bf16)
        value_part = dot(prob.astype(bf16), grad)
        key_part = dot(score_grad, query)
        value_grad = value_part if half == 0 else value_grad + value_part
        key_grad = key_part if half == 0 else key_grad + key_part
        query_grads.append(dot(score_grad, key, TN))
    for i, tile in enumerate(ungrouped(query_grads, rows)):
        tile = rotate(tile * (1.0 / HEAD_SIZE), cosine, -sine)
        query_out[:, i * LANES : (i + 1) * LANES] = tile.astype(bf16)
    first = pl.multiple_of(pl.program_id(0) * LANES, LANES)
    pair_out[:, pl.ds(first, LANES)] = key_grad.astype(bf16)
    pair_out[:, pl.ds(first + KEY_WIDTH, LANES)] = value_grad.astype(bf16)


def attention_backward(query_pre, cosine, sine, pairs, bias, grad):
    rows = query_pre.shape[0]
    length = pairs.shape[0]
    whole = lambda shape: pl.BlockSpec(shape, lambda p: (0, 0))
    return pl.pallas_call(
        attention_backward_kernel,
        grid=(PAIRS,),
        in_specs=[
            pl.BlockSpec((rows, PAIR_QUERY), lambda p: (0, p)),
            whole((rows, LANES)),
            whole((rows, LANES)),
            pl.BlockSpec((length, LANES), lambda p: (0, p)),
            pl.BlockSpec((length, LANES), lambda p: (0, p + PAIRS)),
            whole(bias.shape),
            pl.BlockSpec((rows, PAIR_QUERY), lambda p: (0, p)),
        ],
        out_specs=[
            pl.BlockSpec((rows, PAIR_QUERY), lambda p: (0, p)),
            whole((length, 2 * KEY_WIDTH)),
        ],
        out_shape=[
            jax.ShapeDtypeStruct((rows, MODEL_WIDTH), bf16),
            jax.ShapeDtypeStruct((length, 2 * KEY_WIDTH), bf16),
        ],
        compiler_params=pltpu.CompilerParams(vmem_limit_bytes=VMEM_LIMIT),
        cost_estimate=pl.CostEstimate(
            flops=40 * rows * length * MODEL_WIDTH,
            bytes_accessed=8 * length * MODEL_WIDTH,
            transcendentals=rows * length * QUERY_HEADS,
        ),
        name="attention_backward",
    )(query_pre, cosine, sine, pairs, pairs, bias, grad)


def experts_kernel(parts, rows, steps, combine_ref, gate_ref, up_ref, down_ref, *refs):
    rows_in, grads_in = refs[:parts], refs[parts : 2 * parts]
    refs = refs[2 * parts :]
    results, row_grads = refs[:parts], refs[parts : 2 * parts]
    active_out, gate_out, up_out, rows_all, grads_all, result_sum, grad_sum = refs[2 * parts :]
    step = pl.program_id(0) * pl.num_programs(1) + pl.program_id(1)

    @pl.when(step == 0)
    def _():
        for k in range(parts):
            place = slice(k * rows, (k + 1) * rows)
            rows_all[place] = rows_in[k][...]
            grads_all[place] = grads_in[k][...]
        result_sum[...] = jnp.zeros_like(result_sum)
        grad_sum[...] = jnp.zeros_like(grad_sum)

    inputs, out_grad, combine = rows_all[...], grads_all[...], combine_ref[0]
    gate_weight, up_weight, down_weight = gate_ref[0], up_ref[0], down_ref[0]
    gate = dot(inputs, gate_weight)
    up = dot(inputs, up_weight)
    sigmoid = jax.nn.sigmoid(gate)
    silu = gate * sigmoid
    active = (silu * up * combine).astype(bf16)
    active_grad = dot(out_grad, down_weight, NT) * combine
    gate_grad = (active_grad * up * sigmoid * (1.0 + gate * (1.0 - sigmoid))).astype(bf16)
    up_grad = (active_grad * silu).astype(bf16)
    active_out[...] = active
    gate_out[...] = gate_grad
    up_out[...] = up_grad
    result_sum[...] += dot(active, down_weight)
    grad_sum[...] += dot(gate_grad, gate_weight, NT) + dot(up_grad, up_weight, NT)

    @pl.when(step == steps - 1)
    def _():
        for k in range(parts):
            place = slice(k * rows, (k + 1) * rows)
            results[k][...] = result_sum[place].astype(bf16)
            row_grads[k][...] = grad_sum[place].astype(bf16)


def experts(row_parts, grad_parts, combine, expert_in, expert_out):
    parts = len(row_parts)
    rows = row_parts[0].shape[0]
    held = expert_in.shape[0]
    tokens = parts * rows
    blocks = F // F_BLOCK
    whole = pl.BlockSpec((rows, MODEL_WIDTH), lambda e, b: (0, 0))
    piece = pl.BlockSpec((tokens, F_BLOCK), lambda e, b: (0, e * blocks + b))
    row_shape = jax.ShapeDtypeStruct((rows, MODEL_WIDTH), bf16)
    piece_shape = jax.ShapeDtypeStruct((tokens, held * F), bf16)
    out = pl.pallas_call(
        functools.partial(experts_kernel, parts, rows, held * blocks),
        grid=(held, blocks),
        in_specs=[
            pl.BlockSpec((1, tokens, 1), lambda e, b: (e, 0, 0)),
            pl.BlockSpec((1, MODEL_WIDTH, F_BLOCK), lambda e, b: (e, 0, b)),
            pl.BlockSpec((1, MODEL_WIDTH, F_BLOCK), lambda e, b: (e, 0, b + blocks)),
            pl.BlockSpec((1, F_BLOCK, MODEL_WIDTH), lambda e, b: (e, b, 0)),
        ]
        + [whole] * (2 * parts),
        out_specs=[whole] * (2 * parts) + [piece] * 3,
        out_shape=[row_shape] * (2 * parts) + [piece_shape] * 3,
        scratch_shapes=[
            pltpu.VMEM((tokens, MODEL_WIDTH), bf16),
            pltpu.VMEM((tokens, MODEL_WIDTH), bf16),
            pltpu.VMEM((tokens, MODEL_WIDTH), f32),
            pltpu.VMEM((tokens, MODEL_WIDTH), f32),
        ],
        compiler_params=pltpu.CompilerParams(vmem_limit_bytes=VMEM_LIMIT),
        cost_estimate=pl.CostEstimate(
            flops=12 * tokens * held * MODEL_WIDTH * F,
            bytes_accessed=6 * held * MODEL_WIDTH * F + 20 * tokens * MODEL_WIDTH,
            transcendentals=tokens * held * F,
        ),
        name="experts",
    )(combine, expert_in, expert_in, expert_out, *row_parts, *grad_parts)
    return out[:parts], out[parts : 2 * parts], out[2 * parts :]


def expert_weights_kernel(parts, rows, *refs):
    row_refs, grad_refs = refs[: MB * parts], refs[MB * parts : 2 * MB * parts]
    refs = refs[2 * MB * parts :]
    active_refs, gate_refs, up_refs = refs[:MB], refs[MB : 2 * MB], refs[2 * MB : 3 * MB]
    gate_out, up_out, down_out, turned, grads_all = refs[3 * MB :]
    step = pl.program_id(0) * pl.num_programs(1) + pl.program_id(1)

    @pl.when(step == 0)
    def _():
        for k in range(MB * parts):
            place = slice(k * rows, (k + 1) * rows)
            turned[:, place] = row_refs[k][...].T
            grads_all[place] = grad_refs[k][...]

    join = lambda items: jnp.concatenate([item[...] for item in items], axis=0)
    gate_out[0] = dot(turned[...], join(gate_refs)).astype(bf16)
    up_out[0] = dot(turned[...], join(up_refs)).astype(bf16)
    down_out[0] = dot(join(active_refs), grads_all[...], TN).astype(bf16)


def expert_weights(row_parts, grad_parts, pieces, held):
    rows = row_parts[0].shape[0]
    parts = len(row_parts) // MB
    tokens = parts * rows
    blocks = F // F_BLOCK
    whole = pl.BlockSpec((rows, MODEL_WIDTH), lambda e, b: (0, 0))
    piece = pl.BlockSpec((tokens, F_BLOCK), lambda e, b: (0, e * blocks + b))
    wide = pl.BlockSpec((1, MODEL_WIDTH, F_BLOCK), lambda e, b: (e, 0, b))
    return pl.pallas_call(
        functools.partial(expert_weights_kernel, parts, rows),
        grid=(held, blocks),
        in_specs=[whole] * (2 * MB * parts) + [piece] * (3 * MB),
        out_specs=[wide, wide, pl.BlockSpec((1, F_BLOCK, MODEL_WIDTH), lambda e, b: (e, b, 0))],
        out_shape=[
            jax.ShapeDtypeStruct((held, MODEL_WIDTH, F), bf16),
            jax.ShapeDtypeStruct((held, MODEL_WIDTH, F), bf16),
            jax.ShapeDtypeStruct((held, F, MODEL_WIDTH), bf16),
        ],
        scratch_shapes=[
            pltpu.VMEM((MODEL_WIDTH, MB * tokens), bf16),
            pltpu.VMEM((MB * tokens, MODEL_WIDTH), bf16),
        ],
        compiler_params=pltpu.CompilerParams(vmem_limit_bytes=VMEM_LIMIT),
        cost_estimate=pl.CostEstimate(
            flops=6 * MB * tokens * held * MODEL_WIDTH * F,
            bytes_accessed=6 * held * MODEL_WIDTH * F + 8 * MB * tokens * MODEL_WIDTH,
            transcendentals=0,
        ),
        name="expert_weights",
    )(*row_parts, *grad_parts, *[pieces[m][i] for i in range(3) for m in range(MB)])


class Links:
    def __init__(self):
        self.shards = lax.axis_size("fsdp")
        self.contexts = lax.axis_size("ctx")
        self.chips = self.contexts // 2
        self.shard = lax.axis_index("fsdp")
        self.context = lax.axis_index("ctx")
        self.chip = self.context // 2
        self.core = self.context % 2

    def across(self, array, k):
        return lax.ppermute(array, "fsdp", [(i, i ^ k) for i in range(self.shards)])

    def other_core(self, array):
        return lax.ppermute(array, "ctx", [(i, i ^ 1) for i in range(self.contexts)])

    def shift(self, array, s):
        n = self.contexts
        return lax.ppermute(array, "ctx", [(i, (i + 2 * s) % n) for i in range(n)])

    def step(self, array, first, last, direction):
        pairs = [
            (2 * i + core, 2 * (i + direction) + core) for i in range(first, last + 1) for core in range(2)
        ]
        return lax.ppermute(array, "ctx", pairs)

    def to_relative(self, array):
        width = array.shape[-1] // (2 * self.shards)
        pieces = [[array[..., (2 * b + h) * width : (2 * b + h + 1) * width] for b in range(self.shards)] for h in range(2)]
        return jnp.concatenate(sum(self._swapped(pieces), []), axis=-1)

    def to_absolute(self, array):
        width = array.shape[-1] // (2 * self.shards)
        pieces = [
            [array[..., (h * self.shards + b) * width : (h * self.shards + b + 1) * width] for b in range(self.shards)]
            for h in range(2)
        ]
        pieces = self._swapped(pieces)
        return jnp.concatenate([pieces[h][b] for b in range(self.shards) for h in range(2)], axis=-1)

    def _swapped(self, pieces):
        bit = 1
        while bit < self.shards:
            flag = (self.shard & bit) != 0
            pieces = [[jnp.where(flag, row[b ^ bit], row[b]) for b in range(self.shards)] for row in pieces]
            bit *= 2
        flag = self.core == 1
        return [
            [jnp.where(flag, pieces[1 - h][b], pieces[h][b]) for b in range(self.shards)] for h in range(2)
        ]

    def gather_rows(self, weight):
        half = weight.shape[0] // 2
        mine = lax.dynamic_slice_in_dim(weight, self.core * half, half, 0)
        rest = lax.dynamic_slice_in_dim(weight, (1 - self.core) * half, half, 0)
        arrived = [self.across(mine, k) for k in range(1, self.shards)]
        passed = [self.other_core(part) for part in arrived]
        return jnp.concatenate([mine] + arrived + [rest] + passed, axis=0)

    def scatter_rows(self, grad):
        half = grad.shape[0] // 2
        mine = grad[:half].astype(f32) + self.other_core(grad[half:]).astype(f32)
        mine = mine.astype(bf16)
        size = half // self.shards
        total = mine[:size].astype(f32)
        for k in range(1, self.shards):
            total = total + self.across(mine[k * size : (k + 1) * size], k).astype(f32)
        return total.astype(bf16)

    def core_halves(self, grad):
        half = grad.shape[0] // 2
        mine = lax.dynamic_slice_in_dim(grad, self.core * half, half, 0)
        rest = lax.dynamic_slice_in_dim(grad, (1 - self.core) * half, half, 0)
        return (mine.astype(f32) + self.other_core(rest).astype(f32)).astype(bf16)

    def sum_over_chips(self, half):
        n = self.chips
        size = half.shape[0] // n
        block = lambda j: lax.dynamic_slice_in_dim(half, jnp.clip(j, 0, n - 1) * size, size, 0).astype(f32)
        from_left, from_right = None, None
        for t in range(1, n):
            right, left = block(n - t + self.chip), block(t - n + self.chip)
            if t > 1:
                right = right + from_left.astype(f32)
                left = left + from_right.astype(f32)
            from_left = self.step(right.astype(bf16), 0, t - 1, 1)
            from_right = self.step(left.astype(bf16), n - t, n - 1, -1)
        total = block(self.chip) + from_left.astype(f32) + from_right.astype(f32)
        total = total.astype(bf16)
        going_right, going_left = [total], [total]
        for t in range(1, n):
            going_right.append(self.step(going_right[-1], t - 1, n - 2, 1))
            going_left.append(self.step(going_left[-1], 1, n - t, -1))
        return [total] + [going_right[t] + going_left[n - t] for t in range(1, n)]

    def place_rows(self, blocks, out, column):
        size = blocks[0].shape[0]
        others = [self.other_core(block) for block in blocks]
        for core, items in ((self.core, blocks), (1 - self.core, others)):
            for t, item in enumerate(items):
                row = (core * self.chips + (self.chip - t + self.chips) % self.chips) * size
                out = lax.dynamic_update_slice(out, item.astype(f32), (row, column))
        return out


MESH = pl.DeviceIdType.MESH
LINE = 4
PIECES = 4
DENSE_PIECES = 2
ADD_ROWS = 64


def add_into(out, *parts):
    rows = out.shape[0]
    size = max(d for d in range(16, ADD_ROWS + 1, 16) if rows % d == 0)

    def body(i, carry):
        place = pl.ds(pl.multiple_of(i * size, size), size)
        total = parts[0][place].astype(f32)
        for part in parts[1:]:
            total = total + part[place].astype(f32)
        out[place] = total.astype(out.dtype)
        return carry

    lax.fori_loop(0, rows // size, body, 0)


class Piece:
    def __init__(self, own, near, far, out, out_rows):
        self.own, self.near, self.far, self.out, self.out_rows = own, near, far, out, out_rows


def reduce_kernel(experts_n, dense_n, shards_n, *refs):
    count = experts_n + dense_n
    sources, outs = refs[:count], refs[count : 2 * count]
    refs = list(refs[2 * count :])
    take = lambda n: [refs.pop(0) for _ in range(n)]
    own, other = take(count), take(count)
    across = take(dense_n)
    near, far = take(count), take(count)
    load_sem, core_sem, across_sem, near_sem, far_sem, back_sem, pass_sem, store_sem = refs

    shard, context = lax.axis_index("fsdp"), lax.axis_index("ctx")
    core, chip = context % 2, context // 2
    partner = {"ctx": 2 * chip + 1 - core}
    inner = (chip == 1) | (chip == 2)
    outer_device = {"ctx": 2 * (3 * (chip // 2)) + core}
    inner_device = {"ctx": 2 * (1 + chip // 2) + core}
    facing_device = {"ctx": 2 * (3 - chip) + core}

    def peer(k):
        x, y = (shard % 2 + k % 2) % 2, (shard // 2 + k // 2) % 2
        return {"fsdp": 2 * y + x}

    def send(source, target, sems, index, device):
        return pltpu.make_async_remote_copy(
            src_ref=source,
            dst_ref=target,
            send_sem=sems.at[0, index],
            recv_sem=sems.at[1, index],
            device_id=device,
            device_id_type=MESH,
        )

    barrier = pltpu.get_barrier_semaphore()
    greet = lambda device: pl.semaphore_signal(barrier, inc=1, device_id=device, device_id_type=MESH)
    greet(partner)
    for k in range(1, shards_n):
        greet(peer(k))

    @pl.when(inner)
    def _():
        greet(outer_device)
        greet(facing_device)

    @pl.when(jnp.logical_not(inner))
    def _():
        greet(inner_device)

    pl.semaphore_wait(barrier, shards_n + jnp.where(inner, 2, 1))

    loads, trades = [], []
    pieces = []
    for a in range(count):
        rows = own[a].shape[0]
        if a < experts_n:
            mine = pl.multiple_of(core * rows, rows)
            rest = pl.multiple_of((1 - core) * rows, rows)
            parts = PIECES
        else:
            mine, rest = 0, rows
            parts = 1
        size = rows // parts
        for j in range(parts):
            i = len(loads)
            place = slice(j * size, (j + 1) * size)
            loads.append(
                pltpu.make_async_copy(
                    sources[a].at[pl.ds(mine + j * size, size)], own[a].at[place], load_sem.at[i]
                )
            )
            trades.append(
                send(
                    sources[a].at[pl.ds(rest + j * size, size)], other[a].at[place], core_sem, i, partner
                )
            )
        total = near[a].shape[0]
        parts = PIECES if a < experts_n else DENSE_PIECES
        size = total // parts
        for j in range(parts):
            place = slice(j * size, (j + 1) * size)
            at = pl.multiple_of(core * total, total) + j * size
            pieces.append(
                Piece(own[a].at[place], near[a].at[place], far[a].at[place], outs[a], pl.ds(at, size))
            )
    expert_pieces = experts_n * PIECES
    order = list(range(2)) + list(range(expert_pieces, expert_pieces + dense_n)) + list(range(2, expert_pieces))
    for i in order:
        loads[i].start()
        trades[i].start()

    crossings = []

    def meet_expert(i):
        a, j = i // PIECES, i % PIECES
        size = own[a].shape[0] // PIECES
        place = slice(j * size, (j + 1) * size)
        loads[i].wait()
        trades[i].wait_recv()
        add_into(own[a].at[place], own[a].at[place], other[a].at[place])

    def meet_dense(d):
        a, i = experts_n + d, expert_pieces + d
        loads[i].wait()
        trades[i].wait_recv()
        add_into(own[a], own[a], other[a])
        size = own[a].shape[0] // shards_n
        for k in range(1, shards_n):
            copy = send(
                own[a].at[k * size : (k + 1) * size],
                across[d].at[k - 1],
                across_sem,
                d * (shards_n - 1) + k - 1,
                peer(k),
            )
            copy.start()
            crossings.append(copy)

    def gather_dense(d):
        a = experts_n + d
        size = own[a].shape[0] // shards_n
        for k in range(1, shards_n):
            crossings[d * (shards_n - 1) + k - 1].wait_recv()
        add_into(own[a].at[0:size], own[a].at[0:size], *[across[d].at[k - 1] for k in range(1, shards_n)])

    number = len(pieces)
    inward = [send(p.own, p.near, near_sem, i, inner_device) for i, p in enumerate(pieces)]
    facing = [send(p.own, p.far, far_sem, i, facing_device) for i, p in enumerate(pieces)]
    outward = [send(p.near, p.out.at[p.out_rows], back_sem, i, outer_device) for i, p in enumerate(pieces)]
    passed_inner = [send(p.near, p.out.at[p.out_rows], pass_sem, i, partner) for i, p in enumerate(pieces)]
    passed_outer = [
        send(p.out.at[p.out_rows], p.out.at[p.out_rows], pass_sem, i, partner) for i, p in enumerate(pieces)
    ]
    stores = [
        pltpu.make_async_copy(p.near, p.out.at[p.out_rows], store_sem.at[i]) for i, p in enumerate(pieces)
    ]

    def ready(i):
        if i < expert_pieces:
            meet_expert(i)
            if 1 <= i <= dense_n:
                meet_dense(i - 1)
        elif (i - expert_pieces) % DENSE_PIECES == 0:
            gather_dense((i - expert_pieces) // DENSE_PIECES)

        @pl.when(jnp.logical_not(inner))
        def _():
            inward[i].start()

    def halfway(i):
        inward[i].wait_recv()
        add_into(pieces[i].own, pieces[i].own, pieces[i].near)
        facing[i].start()

    def finish(i):
        facing[i].wait_recv()
        add_into(pieces[i].near, pieces[i].own, pieces[i].far)
        outward[i].start()
        passed_inner[i].start()
        stores[i].start()

    def forward(i):
        outward[i].wait_recv()
        passed_outer[i].start()

    lag = 6
    for i in range(number + lag):
        if i < number:
            ready(i)

        @pl.when(inner)
        def _():
            if i < number:
                halfway(i)
            if 1 <= i <= number:
                finish(i - 1)

        @pl.when(jnp.logical_not(inner))
        def _():
            if i >= lag:
                forward(i - lag)

    for trade in trades:
        trade.wait_send()
    for crossing in crossings:
        crossing.wait_send()

    @pl.when(inner)
    def _():
        for i in range(number):
            facing[i].wait_send()
            outward[i].wait_send()
            stores[i].wait()
            passed_inner[i].wait_send()

    @pl.when(jnp.logical_not(inner))
    def _():
        for i in range(number):
            inward[i].wait_send()
            passed_outer[i].wait_send()

    for i in range(number):
        passed_outer[i].wait_recv()


def reduce_weights(expert_grads, dense_grads, shards_n):
    arrays = list(expert_grads) + list(dense_grads)
    experts_n, dense_n = len(expert_grads), len(dense_grads)
    out_rows = [g.shape[0] for g in expert_grads] + [g.shape[0] // shards_n for g in dense_grads]
    half = lambda g: pltpu.VMEM((g.shape[0] // 2, g.shape[1]), bf16)
    line = [pltpu.VMEM((r // 2, g.shape[1]), bf16) for r, g in zip(out_rows, arrays)]
    across = [pltpu.VMEM((shards_n - 1, g.shape[0] // (2 * shards_n), g.shape[1]), bf16) for g in dense_grads]
    first = experts_n * PIECES + dense_n
    number = experts_n * PIECES + dense_n * DENSE_PIECES
    dma = pltpu.SemaphoreType.DMA
    anywhere = pl.BlockSpec(memory_space=pl.ANY)
    return pl.pallas_call(
        functools.partial(reduce_kernel, experts_n, dense_n, shards_n),
        in_specs=[anywhere] * len(arrays),
        out_specs=[anywhere] * len(arrays),
        out_shape=[jax.ShapeDtypeStruct((r, g.shape[1]), bf16) for r, g in zip(out_rows, arrays)],
        scratch_shapes=[half(g) for g in arrays]
        + [half(g) for g in arrays]
        + across
        + line
        + line
        + [
            dma((first,)),
            dma((2, first)),
            dma((2, dense_n * (shards_n - 1))),
            dma((2, number)),
            dma((2, number)),
            dma((2, number)),
            dma((2, number)),
            dma((number,)),
        ],
        compiler_params=pltpu.CompilerParams(
            collective_id=0, has_side_effects=True, vmem_limit_bytes=VMEM_LIMIT
        ),
        name="reduce_weights",
    )(*arrays)


def shards(
    tokens,
    doc_starts,
    routes,
    gates,
    attn_gain,
    w_q,
    key_value_weight,
    w_o,
    moe_gain,
    expert_in,
    expert_out,
    cotangent,
):
    links = Links()
    rows = tokens.shape[2]
    length = rows * links.contexts
    held = expert_in.shape[0]
    positions = links.context * rows + jnp.arange(rows, dtype=jnp.int32)
    cosine, sine = rotation_tables(positions)
    chips_back = (links.chip - jnp.arange(links.chips, dtype=jnp.int32) + links.chips) % links.chips
    chunk_ids = jnp.concatenate([2 * chips_back + links.core, 2 * chips_back + 1 - links.core])
    key_places = (chunk_ids[:, None] * rows + jnp.arange(rows, dtype=jnp.int32)[None, :]).reshape(length)

    gains = lax.all_gather(jnp.stack([attn_gain, moe_gain]), "fsdp", axis=1, tiled=True).astype(f32)
    gain_one, gain_two = links.to_relative(gains[0]), gains[1]

    pair_weight = links.gather_rows(key_value_weight)
    query_weight = links.gather_rows(w_q)
    output_weight = links.gather_rows(w_o)

    flat_tokens = tokens.reshape(MB * rows, MODEL_WIDTH)
    relative = links.to_relative(flat_tokens).astype(f32)
    scale_one = lax.rsqrt(jnp.mean(relative * relative, axis=-1, keepdims=True) + eps)
    unit_one = relative * scale_one
    normed = (unit_one * gain_one).astype(bf16)
    pairs = rotate_pairs(
        dot(normed, pair_weight), jnp.concatenate([cosine] * MB), jnp.concatenate([sine] * MB)
    )
    query_pre = dot(normed, query_weight)

    expert_ids = jnp.arange(E, dtype=jnp.int32)
    chosen = (routes.reshape(MB, rows, TOP)[..., None] == expert_ids).astype(f32)
    combine = jnp.sum(gates.reshape(MB, rows, TOP)[..., None] * chosen, axis=2)
    combine = jnp.concatenate([combine] + [links.across(combine, k) for k in range(1, links.shards)], axis=1)
    combine = lax.dynamic_slice_in_dim(combine, links.shard * held, held, 2)
    combine = combine.transpose(0, 2, 1)[..., None]

    all_pairs, biases, biases_turned = [], [], []
    for m in range(MB):
        own = pairs[m * rows : (m + 1) * rows]
        near = jnp.concatenate([own] + [links.shift(own, s) for s in range(1, links.chips)], axis=0)
        all_pairs.append(jnp.concatenate([near, links.other_core(near)], axis=0))
        starts = doc_starts[m, 0]
        begin = jnp.max(jnp.where(starts[None, :] <= positions[:, None], starts[None, :], 0), axis=1)
        seen = (key_places[None, :] <= positions[:, None]) & (key_places[None, :] >= begin[:, None])
        biases.append(jnp.where(seen, 0.0, -1e30).astype(f32))
        places, begins = jnp.tile(positions, GROUP), jnp.tile(begin, GROUP)
        seen = (key_places[:, None] <= places[None, :]) & (key_places[:, None] >= begins[None, :])
        biases_turned.append(jnp.where(seen, 0.0, -1e30).astype(f32))

    kept = []
    outputs = []
    for m in range(MB):
        own = slice(m * rows, (m + 1) * rows)
        attn = attention_forward(query_pre[own], cosine, sine, all_pairs[m], biases[m])
        attn = links.to_relative(attn)
        middle = flat_tokens[own].astype(f32) + dot(attn, output_weight)
        scale_two = lax.rsqrt(jnp.mean(middle * middle, axis=-1, keepdims=True) + eps)
        unit_two = middle * scale_two
        moe_in = (unit_two * gain_two).astype(bf16)
        out_grad = cotangent[m, 0]
        row_parts = [moe_in] + [links.across(moe_in, k) for k in range(1, links.shards)]
        grad_parts = [out_grad] + [links.across(out_grad, k) for k in range(1, links.shards)]
        results, row_grads, pieces = experts(row_parts, grad_parts, combine[m], expert_in, expert_out)
        final = middle + results[0].astype(f32)
        for k in range(1, links.shards):
            final = final + links.across(results[k], k).astype(f32)
        outputs.append(final.astype(bf16))
        kept.append((attn, unit_two, scale_two, row_parts, grad_parts, row_grads, pieces))

    expert_grads = expert_weights(
        sum([k[3] for k in kept], []), sum([k[4] for k in kept], []), [k[6] for k in kept], held
    )

    expert_grads = [g.reshape(-1, g.shape[-1]) for g in expert_grads]

    input_grads, query_lows, pair_lows, middle_lows = [], [], [], []
    gain_one_grad, gain_two_grad = 0.0, 0.0
    for m in range(MB):
        own = slice(m * rows, (m + 1) * rows)
        attn, unit_two, scale_two, _, _, row_grads, _ = kept[m]
        moe_in_grad = row_grads[0].astype(f32)
        for k in range(1, links.shards):
            moe_in_grad = moe_in_grad + links.across(row_grads[k], k).astype(f32)
        gain_two_grad = gain_two_grad + jnp.sum(moe_in_grad * unit_two, axis=0)
        weighted = moe_in_grad * gain_two
        inner = jnp.mean(weighted * unit_two, axis=-1, keepdims=True)
        middle_grad = cotangent[m, 0].astype(f32) + (weighted - unit_two * inner) * scale_two
        middle_low = middle_grad.astype(bf16)
        attn_grad = links.to_absolute(dot(middle_low, output_weight, NT).astype(bf16))
        query_low, pair_grad = attention_backward(
            query_pre[own], cosine, sine, all_pairs[m], biases_turned[m], attn_grad
        )
        near = links.chips * rows
        part = pair_grad[:near].astype(f32) + links.other_core(pair_grad[near:]).astype(f32)
        part = part.astype(bf16)
        parts = [part[:rows]]
        for s in range(1, links.chips):
            parts.append(links.shift(part[s * rows : (s + 1) * rows], -s))
        pair_low = pair_gradient(parts, cosine, sine)
        normed_grad = dot(query_low, query_weight, NT) + dot(pair_low, pair_weight, NT)
        gain_one_grad = gain_one_grad + jnp.sum(normed_grad * unit_one[own], axis=0)
        weighted = normed_grad * gain_one
        inner = jnp.mean(weighted * unit_one[own], axis=-1, keepdims=True)
        residual_grad = (weighted - unit_one[own] * inner) * scale_one[own]
        input_grads.append(middle_grad + links.to_absolute(residual_grad))
        query_lows.append(query_low)
        pair_lows.append(pair_low)
        middle_lows.append(middle_low)

    join = lambda items: jnp.concatenate(items, axis=0)
    width = w_q.shape[0]

    output_grad = dot(join([k[0] for k in kept]), join(middle_lows), TN).astype(bf16)
    query_grad = dot(normed, join(query_lows), TN).astype(bf16)
    pair_weight_grad = dot(normed, join(pair_lows), TN).astype(bf16)
    gain_grads = jnp.stack([gain_one_grad, links.to_relative(gain_two_grad)], axis=1)
    gain_grads = jnp.pad(gain_grads, ((0, 0), (0, LANES - 2))).astype(bf16)
    dense_grads = [output_grad, query_grad, jnp.concatenate([pair_weight_grad, gain_grads], axis=1)]
    if links.chips == LINE and links.shards == 4 and held == 2:
        totals = reduce_weights(expert_grads, dense_grads, links.shards)
        gate_total, up_total, down_total, output_total, query_total, pair_total = [t.astype(f32) for t in totals]
        expand_total = jnp.concatenate([gate_total, up_total], axis=1)
    else:
        expand_total = jnp.zeros((held * MODEL_WIDTH, 2 * F), f32)
        down_total = jnp.zeros((held * F, MODEL_WIDTH), f32)
        sums = [links.sum_over_chips(links.core_halves(g)) for g in expert_grads]
        expand_total = links.place_rows(sums[0], expand_total, 0)
        expand_total = links.place_rows(sums[1], expand_total, F)
        down_total = links.place_rows(sums[2], down_total, 0)
        output_total, query_total, pair_total = [
            links.place_rows(
                links.sum_over_chips(links.scatter_rows(g)), jnp.zeros((width, g.shape[1]), f32), 0
            )
            for g in dense_grads
        ]

    return (
        jnp.stack(outputs)[:, None],
        jnp.stack(input_grads)[:, None],
        pair_total[:, 2 * KEY_WIDTH],
        query_total,
        pair_total[:, : 2 * KEY_WIDTH],
        output_total,
        pair_total[:, 2 * KEY_WIDTH + 1],
        expand_total.reshape(held, MODEL_WIDTH, 2 * F),
        down_total.reshape(held, F, MODEL_WIDTH),
    )


def solution(mesh):
    return jax.shard_map(
        shards,
        mesh=mesh,
        in_specs=(
            P(None, "fsdp", "ctx", None),
            P(None, "fsdp", None),
            P(None, "fsdp", "ctx", None),
            P(None, "fsdp", "ctx", None),
            P("fsdp"),
            P("fsdp", None),
            P("fsdp", None),
            P("fsdp", None),
            P("fsdp"),
            P("fsdp", None, None),
            P("fsdp", None, None),
            P(None, "fsdp", "ctx", None),
        ),
        out_specs=(
            P(None, "fsdp", "ctx", None),
            P(None, "fsdp", "ctx", None),
            P("fsdp"),
            P("fsdp", None),
            P("fsdp", None),
            P("fsdp", None),
            P("fsdp"),
            P("fsdp", None, None),
            P("fsdp", None, None),
        ),
        check_vma=False,
    )
```

```python
import functools

import jax
import jax.numpy as jnp
from jax import lax
from jax.experimental import pallas as pl
from jax.experimental.pallas import tpu as pltpu
from jax.sharding import PartitionSpec as P

MODEL_WIDTH = 1536
QUERY_HEADS = 24
KEY_VALUE_HEADS = 8
HEAD_SIZE = 64
GROUP = QUERY_HEADS // KEY_VALUE_HEADS
KEY_WIDTH = KEY_VALUE_HEADS * HEAD_SIZE
F = 512
E = 8
TOP = 4
MB = 2
LANES = 128
PAIRS = KEY_WIDTH // LANES
PAIR_QUERY = 2 * GROUP * HEAD_SIZE
F_BLOCK = 256
VMEM_LIMIT = 60 * 1024 * 1024

eps = 1e-05
theta = 10000.0

NT = (((1,), (1,)), ((), ()))
TN = (((0,), (0,)), ((), ()))
bf16 = jnp.bfloat16
f32 = jnp.float32


def dot(left, right, dims=(((1,), (0,)), ((), ()))):
    return lax.dot_general(left, right, dims, preferred_element_type=f32)


def rotation_tables(positions):
    frequency = theta ** (-jnp.arange(0, HEAD_SIZE, 2, dtype=f32) / HEAD_SIZE)
    angles = positions.astype(f32)[:, None] * frequency[None, :]
    cosine, sine = jnp.cos(angles), jnp.sin(angles)
    repeat = LANES // HEAD_SIZE
    cosine = jnp.concatenate([cosine, cosine] * repeat, axis=1)
    sine = jnp.concatenate([-sine, sine] * repeat, axis=1)
    return cosine, sine


def lane_index(shape):
    return lax.broadcasted_iota(jnp.int32, shape, 1)


def rotate(tile, cosine, sine):
    half = HEAD_SIZE // 2
    ahead = pltpu.roll(tile, LANES - half, 1)
    behind = pltpu.roll(tile, half, 1)
    first = lane_index(tile.shape) % HEAD_SIZE < half
    return tile * cosine + jnp.where(first, ahead, behind) * sine


def rotate_columns_kernel(rotated, values_ref, cosine_ref, sine_ref, out_ref):
    cosine, sine = cosine_ref[...], sine_ref[...]
    for i in range(values_ref.shape[1] // LANES):
        cols = slice(i * LANES, (i + 1) * LANES)
        tile = values_ref[:, cols]
        if i < rotated // LANES:
            tile = rotate(tile, cosine, sine)
        out_ref[:, cols] = tile.astype(bf16)


def rotate_columns(values, cosine, sine, rotated):
    return pl.pallas_call(
        functools.partial(rotate_columns_kernel, rotated),
        out_shape=jax.ShapeDtypeStruct(values.shape, bf16),
        compiler_params=pltpu.CompilerParams(vmem_limit_bytes=VMEM_LIMIT),
        name="rotate_columns",
    )(values, cosine, sine)


def pair_gradient_kernel(count, cosine_ref, sine_ref, *refs):
    out_ref = refs[-1]
    cosine, sine = cosine_ref[...], sine_ref[...]
    for i in range(2 * KEY_WIDTH // LANES):
        cols = slice(i * LANES, (i + 1) * LANES)
        total = refs[0][:, cols].astype(f32)
        for ref in refs[1:count]:
            total = total + ref[:, cols].astype(f32)
        if i < KEY_WIDTH // LANES:
            total = rotate(total, cosine, -sine)
        out_ref[:, cols] = total.astype(bf16)


def pair_gradient(parts, cosine, sine):
    return pl.pallas_call(
        functools.partial(pair_gradient_kernel, len(parts)),
        out_shape=jax.ShapeDtypeStruct(parts[0].shape, bf16),
        compiler_params=pltpu.CompilerParams(vmem_limit_bytes=VMEM_LIMIT),
        name="pair_gradient",
    )(cosine, sine, *parts)


def grouped(tiles, half):
    mine = lane_index(tiles[0].shape) // HEAD_SIZE == half
    rows = []
    for j in range(GROUP * half, GROUP * half + GROUP):
        tile = tiles[j // 2]
        if j % 2 != half:
            tile = pltpu.roll(tile, HEAD_SIZE, 1)
        rows.append(jnp.where(mine, tile, 0.0))
    return jnp.concatenate(rows, axis=0).astype(bf16)


def ungrouped(per_half, rows):
    heads = []
    for j in range(2 * GROUP):
        half, place = j // GROUP, j % GROUP
        tile = per_half[half][place * rows : (place + 1) * rows]
        if j % 2 != half:
            tile = pltpu.roll(tile, HEAD_SIZE, 1)
        heads.append(tile)
    low = lane_index(heads[0].shape) < HEAD_SIZE
    return [jnp.where(low, heads[2 * i], heads[2 * i + 1]) for i in range(GROUP)]


def query_tiles(query_ref):
    scale = 1.0 / HEAD_SIZE
    return [query_ref[:, i * LANES : (i + 1) * LANES].astype(f32) * scale for i in range(GROUP)]


def attention_forward_kernel(query_ref, key_ref, value_ref, bias_ref, out_ref):
    rows = query_ref.shape[0]
    tiles = query_tiles(query_ref)
    key, value = key_ref[...], value_ref[...]
    bias = bias_ref[...]
    results = []
    for half in range(2):
        scores = dot(grouped(tiles, half), key, NT)
        scores = jnp.concatenate(
            [scores[g * rows : (g + 1) * rows] + bias for g in range(GROUP)], axis=0
        )
        peak = jnp.max(scores, axis=1, keepdims=True)
        weights = jnp.exp(scores - peak)
        total = jnp.sum(weights, axis=1, keepdims=True)
        results.append(dot(weights.astype(bf16), value) / total)
    for i, tile in enumerate(ungrouped(results, rows)):
        out_ref[:, i * LANES : (i + 1) * LANES] = tile.astype(bf16)


def attention_forward(m, query, pairs, bias):
    rows, length = bias.shape
    return pl.pallas_call(
        attention_forward_kernel,
        grid=(PAIRS,),
        in_specs=[
            pl.BlockSpec((rows, PAIR_QUERY), lambda p: (m, p)),
            pl.BlockSpec((None, length, LANES), lambda p: (m, 0, p)),
            pl.BlockSpec((None, length, LANES), lambda p: (m, 0, p + PAIRS)),
            pl.BlockSpec((rows, length), lambda p: (0, 0)),
        ],
        out_specs=pl.BlockSpec((rows, PAIR_QUERY), lambda p: (0, p)),
        out_shape=jax.ShapeDtypeStruct((rows, MODEL_WIDTH), bf16),
        compiler_params=pltpu.CompilerParams(vmem_limit_bytes=VMEM_LIMIT),
        cost_estimate=pl.CostEstimate(
            flops=16 * rows * length * MODEL_WIDTH,
            bytes_accessed=4 * length * MODEL_WIDTH,
            transcendentals=rows * length * QUERY_HEADS,
        ),
        name="attention_forward",
    )(query, pairs, pairs, bias)


def attention_backward_kernel(
    query_ref, cosine_ref, sine_ref, key_ref, value_ref, bias_ref, grad_ref, query_out, pair_out
):
    rows = query_ref.shape[0]
    cosine, sine = cosine_ref[...], sine_ref[...]
    tiles = query_tiles(query_ref)
    grads = [grad_ref[:, i * LANES : (i + 1) * LANES].astype(f32) for i in range(GROUP)]
    key, value = key_ref[...], value_ref[...]
    key_grad, value_grad = None, None
    query_grads = []
    for half in range(2):
        query = grouped(tiles, half)
        grad = grouped(grads, half)
        scores = dot(key, query, NT) + bias_ref[...]
        weights = jnp.exp(scores - jnp.max(scores, axis=0, keepdims=True))
        prob = weights * (1.0 / jnp.sum(weights, axis=0, keepdims=True))
        prob_grad = dot(value, grad, NT)
        delta = jnp.sum(prob * prob_grad, axis=0, keepdims=True)
        score_grad = (prob * (prob_grad - delta)).astype(bf16)
        value_part = dot(prob.astype(bf16), grad)
        key_part = dot(score_grad, query)
        value_grad = value_part if half == 0 else value_grad + value_part
        key_grad = key_part if half == 0 else key_grad + key_part
        query_grads.append(dot(score_grad, key, TN))
    for i, tile in enumerate(ungrouped(query_grads, rows)):
        tile = rotate(tile * (1.0 / HEAD_SIZE), cosine, -sine)
        query_out[:, i * LANES : (i + 1) * LANES] = tile.astype(bf16)
    first = pl.multiple_of(pl.program_id(0) * LANES, LANES)
    pair_out[:, pl.ds(first, LANES)] = key_grad.astype(bf16)
    pair_out[:, pl.ds(first + KEY_WIDTH, LANES)] = value_grad.astype(bf16)


def attention_backward(m, query, cosine, sine, pairs, bias, grad):
    rows = cosine.shape[0]
    length = pairs.shape[1]
    whole = lambda shape: pl.BlockSpec(shape, lambda p: (0, 0))
    return pl.pallas_call(
        attention_backward_kernel,
        grid=(PAIRS,),
        in_specs=[
            pl.BlockSpec((rows, PAIR_QUERY), lambda p: (m, p)),
            whole((rows, LANES)),
            whole((rows, LANES)),
            pl.BlockSpec((None, length, LANES), lambda p: (m, 0, p)),
            pl.BlockSpec((None, length, LANES), lambda p: (m, 0, p + PAIRS)),
            whole(bias.shape),
            pl.BlockSpec((rows, PAIR_QUERY), lambda p: (0, p)),
        ],
        out_specs=[
            pl.BlockSpec((rows, PAIR_QUERY), lambda p: (0, p)),
            whole((length, 2 * KEY_WIDTH)),
        ],
        out_shape=[
            jax.ShapeDtypeStruct((rows, MODEL_WIDTH), bf16),
            jax.ShapeDtypeStruct((length, 2 * KEY_WIDTH), bf16),
        ],
        compiler_params=pltpu.CompilerParams(vmem_limit_bytes=VMEM_LIMIT),
        cost_estimate=pl.CostEstimate(
            flops=40 * rows * length * MODEL_WIDTH,
            bytes_accessed=8 * length * MODEL_WIDTH,
            transcendentals=rows * length * QUERY_HEADS,
        ),
        name="attention_backward",
    )(query, cosine, sine, pairs, pairs, bias, grad)


def experts_kernel(parts, rows, steps, combine_ref, gate_ref, up_ref, down_ref, *refs):
    rows_in, grads_in = refs[:parts], refs[parts : 2 * parts]
    refs = refs[2 * parts :]
    results, row_grads = refs[:parts], refs[parts : 2 * parts]
    active_out, gate_out, up_out, rows_all, grads_all, result_sum, grad_sum = refs[2 * parts :]
    step = pl.program_id(0) * pl.num_programs(1) + pl.program_id(1)

    @pl.when(step == 0)
    def _():
        for k in range(parts):
            place = slice(k * rows, (k + 1) * rows)
            rows_all[place] = rows_in[k][...]
            grads_all[place] = grads_in[k][...]
        result_sum[...] = jnp.zeros_like(result_sum)
        grad_sum[...] = jnp.zeros_like(grad_sum)

    inputs, out_grad, combine = rows_all[...], grads_all[...], combine_ref[0]
    gate_weight, up_weight, down_weight = gate_ref[0], up_ref[0], down_ref[0]
    gate = dot(inputs, gate_weight)
    up = dot(inputs, up_weight)
    sigmoid = jax.nn.sigmoid(gate)
    silu = gate * sigmoid
    active = (silu * up * combine).astype(bf16)
    active_grad = dot(out_grad, down_weight, NT) * combine
    gate_grad = (active_grad * up * sigmoid * (1.0 + gate * (1.0 - sigmoid))).astype(bf16)
    up_grad = (active_grad * silu).astype(bf16)
    active_out[...] = active
    gate_out[...] = gate_grad
    up_out[...] = up_grad
    result_sum[...] += dot(active, down_weight)
    grad_sum[...] += dot(gate_grad, gate_weight, NT) + dot(up_grad, up_weight, NT)

    @pl.when(step == steps - 1)
    def _():
        for k in range(parts):
            place = slice(k * rows, (k + 1) * rows)
            results[k][...] = result_sum[place].astype(bf16)
            row_grads[k][...] = grad_sum[place].astype(bf16)


def experts(row_parts, grad_parts, combine, expert_in, expert_out):
    parts = len(row_parts)
    rows = row_parts[0].shape[0]
    held = expert_in.shape[0]
    tokens = parts * rows
    blocks = F // F_BLOCK
    whole = pl.BlockSpec((rows, MODEL_WIDTH), lambda e, b: (0, 0))
    piece = pl.BlockSpec((tokens, F_BLOCK), lambda e, b: (0, e * blocks + b))
    row_shape = jax.ShapeDtypeStruct((rows, MODEL_WIDTH), bf16)
    piece_shape = jax.ShapeDtypeStruct((tokens, held * F), bf16)
    out = pl.pallas_call(
        functools.partial(experts_kernel, parts, rows, held * blocks),
        grid=(held, blocks),
        in_specs=[
            pl.BlockSpec((1, tokens, 1), lambda e, b: (e, 0, 0)),
            pl.BlockSpec((1, MODEL_WIDTH, F_BLOCK), lambda e, b: (e, 0, b)),
            pl.BlockSpec((1, MODEL_WIDTH, F_BLOCK), lambda e, b: (e, 0, b + blocks)),
            pl.BlockSpec((1, F_BLOCK, MODEL_WIDTH), lambda e, b: (e, b, 0)),
        ]
        + [whole] * (2 * parts),
        out_specs=[whole] * (2 * parts) + [piece] * 3,
        out_shape=[row_shape] * (2 * parts) + [piece_shape] * 3,
        scratch_shapes=[
            pltpu.VMEM((tokens, MODEL_WIDTH), bf16),
            pltpu.VMEM((tokens, MODEL_WIDTH), bf16),
            pltpu.VMEM((tokens, MODEL_WIDTH), f32),
            pltpu.VMEM((tokens, MODEL_WIDTH), f32),
        ],
        compiler_params=pltpu.CompilerParams(vmem_limit_bytes=VMEM_LIMIT),
        cost_estimate=pl.CostEstimate(
            flops=12 * tokens * held * MODEL_WIDTH * F,
            bytes_accessed=6 * held * MODEL_WIDTH * F + 20 * tokens * MODEL_WIDTH,
            transcendentals=tokens * held * F,
        ),
        name="experts",
    )(combine, expert_in, expert_in, expert_out, *row_parts, *grad_parts)
    return out[:parts], out[parts : 2 * parts], out[2 * parts :]


def expert_weights_kernel(parts, rows, *refs):
    row_refs, grad_refs = refs[: MB * parts], refs[MB * parts : 2 * MB * parts]
    refs = refs[2 * MB * parts :]
    active_refs, gate_refs, up_refs = refs[:MB], refs[MB : 2 * MB], refs[2 * MB : 3 * MB]
    gate_out, up_out, down_out, turned, grads_all = refs[3 * MB :]
    step = pl.program_id(0) * pl.num_programs(1) + pl.program_id(1)

    @pl.when(step == 0)
    def _():
        for k in range(MB * parts):
            place = slice(k * rows, (k + 1) * rows)
            turned[:, place] = row_refs[k][...].T
            grads_all[place] = grad_refs[k][...]

    join = lambda items: jnp.concatenate([item[...] for item in items], axis=0)
    gate_out[0] = dot(turned[...], join(gate_refs)).astype(bf16)
    up_out[0] = dot(turned[...], join(up_refs)).astype(bf16)
    down_out[0] = dot(join(active_refs), grads_all[...], TN).astype(bf16)


def expert_weights(row_parts, grad_parts, pieces, held):
    rows = row_parts[0].shape[0]
    parts = len(row_parts) // MB
    tokens = parts * rows
    blocks = F // F_BLOCK
    whole = pl.BlockSpec((rows, MODEL_WIDTH), lambda e, b: (0, 0))
    piece = pl.BlockSpec((tokens, F_BLOCK), lambda e, b: (0, e * blocks + b))
    wide = pl.BlockSpec((1, MODEL_WIDTH, F_BLOCK), lambda e, b: (e, 0, b))
    return pl.pallas_call(
        functools.partial(expert_weights_kernel, parts, rows),
        grid=(held, blocks),
        in_specs=[whole] * (2 * MB * parts) + [piece] * (3 * MB),
        out_specs=[wide, wide, pl.BlockSpec((1, F_BLOCK, MODEL_WIDTH), lambda e, b: (e, b, 0))],
        out_shape=[
            jax.ShapeDtypeStruct((held, MODEL_WIDTH, F), bf16),
            jax.ShapeDtypeStruct((held, MODEL_WIDTH, F), bf16),
            jax.ShapeDtypeStruct((held, F, MODEL_WIDTH), bf16),
        ],
        scratch_shapes=[
            pltpu.VMEM((MODEL_WIDTH, MB * tokens), bf16),
            pltpu.VMEM((MB * tokens, MODEL_WIDTH), bf16),
        ],
        compiler_params=pltpu.CompilerParams(vmem_limit_bytes=VMEM_LIMIT),
        cost_estimate=pl.CostEstimate(
            flops=6 * MB * tokens * held * MODEL_WIDTH * F,
            bytes_accessed=6 * held * MODEL_WIDTH * F + 8 * MB * tokens * MODEL_WIDTH,
            transcendentals=0,
        ),
        name="expert_weights",
    )(*row_parts, *grad_parts, *[pieces[m][i] for i in range(3) for m in range(MB)])


class Links:
    def __init__(self):
        self.shards = lax.axis_size("fsdp")
        self.contexts = lax.axis_size("ctx")
        self.chips = self.contexts // 2
        self.shard = lax.axis_index("fsdp")
        self.context = lax.axis_index("ctx")
        self.chip = self.context // 2
        self.core = self.context % 2

    def across(self, array, k):
        return lax.ppermute(array, "fsdp", [(i, i ^ k) for i in range(self.shards)])

    def other_core(self, array):
        return lax.ppermute(array, "ctx", [(i, i ^ 1) for i in range(self.contexts)])

    def shift(self, array, s):
        n = self.contexts
        return lax.ppermute(array, "ctx", [(i, (i + 2 * s) % n) for i in range(n)])


MESH = pl.DeviceIdType.MESH
LINE = 4


class Place:
    def __init__(self):
        self.shard, self.context = lax.axis_index("fsdp"), lax.axis_index("ctx")
        self.core, self.chip = self.context % 2, self.context // 2
        self.partner = {"ctx": 2 * self.chip + 1 - self.core}

    def peer_index(self, k):
        x, y = (self.shard % 2 + k % 2) % 2, (self.shard // 2 + k // 2) % 2
        return 2 * y + x

    def peer(self, k):
        return {"fsdp": self.peer_index(k)}

    def chip_device(self, chip):
        return {"ctx": 2 * chip + self.core}


def remote(source, target, sems, index, device):
    return pltpu.make_async_remote_copy(
        src_ref=source,
        dst_ref=target,
        send_sem=sems.at[0, index],
        recv_sem=sems.at[1, index],
        device_id=device,
        device_id_type=MESH,
    )


def greet(device):
    pl.semaphore_signal(pltpu.get_barrier_semaphore(), inc=1, device_id=device, device_id_type=MESH)


SHARDS = 4
GAIN_ROWS = 16


def project_kernel(
    tokens_ref, cosine_ref, sine_ref, gain_ref, pair_src, query_src, output_src, *refs
):
    outs, refs = refs[:6], refs[6:]
    normed_out, query_out, gains, pair_out, query_weight_out, output_weight_out = outs[0], outs[1], outs[2], *outs[3:6]
    pairs_out = refs[0]
    weights, own_pairs = refs[1:4], refs[4]
    load_sem, store_sem, gain_sem, direct_sem, relay_sem, pass_sem, right_sem, left_sem, core_sem, own_sem = refs[5:]
    sources = (pair_src, query_src, output_src)
    weight_outs = (pair_out, query_weight_out, output_weight_out)
    place = Place()
    core, chip, shard = place.core, place.chip, place.shard
    rows = cosine_ref.shape[0]
    held = pair_src.shape[0]
    half, quarter = held // 2, held // 4

    has_left, has_right = chip > 0, chip < LINE - 1
    greet(place.partner)
    for k in range(1, SHARDS):
        greet(place.peer(k))

    @pl.when(has_left)
    def _():
        greet(place.chip_device(chip - 1))

    @pl.when(has_right)
    def _():
        greet(place.chip_device(chip + 1))

    neighbours = jnp.where(has_left, 1, 0) + jnp.where(has_right, 1, 0)
    pl.semaphore_wait(pltpu.get_barrier_semaphore(), SHARDS + neighbours)

    def rows_of(owner, piece, size):
        return pl.ds(pl.multiple_of(owner * held + core * half, half) + piece, size)

    gains[pl.ds(pl.multiple_of(shard * GAIN_ROWS, GAIN_ROWS), GAIN_ROWS)] = gain_ref[...]
    gain_copies = []
    for k in range(1, SHARDS):
        target = gains.at[pl.ds(pl.multiple_of(shard * GAIN_ROWS, GAIN_ROWS), GAIN_ROWS)]
        gain_copies.append(remote(gain_ref, target, gain_sem, k - 1, place.peer(k)))

    loads, directs, relays, passes = [], [], [], []
    for w in range(3):
        weight = weights[w]
        own_rows = pl.ds(pl.multiple_of(shard * held, held), held)
        loads.append(pltpu.make_async_copy(sources[w], weight.at[own_rows], load_sem.at[w]))
        mine = sources[w].at[pl.ds(pl.multiple_of(core * half, half), half)]
        spot = weight.at[rows_of(shard, 0, half)]
        directs.append([remote(mine, spot, direct_sem, 2 * w + k - 1, place.peer(k)) for k in (1, 2)])
        relay, onward = [], []
        for k in (1, 2):
            spot = weight.at[rows_of(place.peer_index(k), (k - 1) * quarter, quarter)]
            relay.append(remote(spot, spot, relay_sem, 2 * w + k - 1, place.peer(3 - k)))
            spot = weight.at[rows_of(place.peer_index(k), 0, half)]
            onward.append(remote(spot, spot, pass_sem, 4 * w + k - 1, place.partner))
        for k in (1, 2):
            spot = weight.at[rows_of(place.peer_index(3), (k - 1) * quarter, quarter)]
            onward.append(remote(spot, spot, pass_sem, 4 * w + k + 1, place.partner))
        relays.append(relay)
        passes.append(onward)

    def send_weight(w):
        for copy in directs[w]:
            copy.start()

    def relay_weight(w):
        for k in (1, 2):
            directs[w][k - 1].wait_recv()
            relays[w][k - 1].start()
        for k in (1, 2):
            passes[w][k - 1].start()

    def pass_weight(w):
        for k in (1, 2):
            relays[w][k - 1].wait_recv()
            passes[w][k + 1].start()

    def store(w):
        return pltpu.make_async_copy(weights[w], weight_outs[w], store_sem.at[w])

    def settle_weight(w):
        loads[w].wait()
        for copy in passes[w]:
            copy.wait_recv()
        store(w).start()

    for copy in gain_copies:
        copy.start()
    send_weight(0)
    for load in loads:
        load.start()

    values = tokens_ref[...].astype(f32)
    scale = lax.rsqrt(jnp.mean(values * values, axis=-1, keepdims=True) + eps)
    for copy in gain_copies:
        copy.wait_recv()
    for b in range(SHARDS):
        columns = slice(b * held, (b + 1) * held)
        gain = gains[b * GAIN_ROWS : b * GAIN_ROWS + 1].astype(f32)
        normed_out[:, columns] = (values[:, columns] * scale * gain).astype(bf16)

    relay_weight(0)
    send_weight(1)
    pass_weight(0)
    settle_weight(0)
    cosine, sine = cosine_ref[...], sine_ref[...]

    def project(weight, column, rotated):
        result = dot(normed_out[...], weight[:, pl.ds(column, 2 * LANES)])
        tiles = []
        for m in range(MB):
            for i in range(2):
                tile = result[m * rows : (m + 1) * rows, i * LANES : (i + 1) * LANES]
                tiles.append((m, i, rotate(tile, cosine, sine) if rotated else tile))
        return tiles

    def pair_block(b, rotated):
        column = pl.multiple_of(b * 2 * LANES, 2 * LANES)
        for m, i, tile in project(weights[0], column, rotated):
            own_pairs[m, :, pl.ds(column + i * LANES, LANES)] = tile.astype(bf16)

    blocks = KEY_WIDTH // (2 * LANES)
    for b in range(blocks):
        pair_block(b, True)
    for b in range(blocks, 2 * blocks):
        pair_block(b, False)

    def chunk(m, owner):
        return pairs_out.at[m, pl.ds(pl.multiple_of((2 * owner + core) * rows, rows), rows)]

    def moves(m, t, direction):
        owner = chip - direction * (t - 1)
        source = own_pairs.at[m] if t == 1 else chunk(m, jnp.clip(owner, 0, LANES_CHIP))
        sems = right_sem if direction > 0 else left_sem
        target = chunk(m, jnp.clip(owner, 0, LANES_CHIP))
        device = place.chip_device(jnp.clip(chip + direction, 0, LANES_CHIP))
        return remote(source, target, sems, m * (LINE - 1) + t - 1, device)

    def sends(t, direction):
        owner = chip - direction * (t - 1)
        if direction > 0:
            return (chip < LINE - 1) & (owner >= 0)
        return (chip > 0) & (owner <= LINE - 1)

    def gets(t, direction):
        owner = chip - direction * t
        return owner >= 0 if direction > 0 else owner <= LINE - 1

    def from_far(m, t, direction):
        owner = jnp.clip(chip - direction * t, 0, LANES_CHIP)
        sems = right_sem if direction > 0 else left_sem
        return remote(chunk(m, owner), chunk(m, owner), sems, m * (LINE - 1) + t - 1, place.partner)

    def pass_chunk(m, t, direction):
        owner = jnp.clip(chip - direction * t, 0, LANES_CHIP)
        index = (m * LINE + t) * 2 + (1 if direction > 0 else 0)
        return remote(chunk(m, owner), chunk(m, owner), core_sem, index, place.partner)

    def send_step(m, t):
        for direction in (1, -1):

            @pl.when(sends(t, direction))
            def _():
                moves(m, t, direction).start()

    def take_step(m, t):
        for direction in (1, -1):

            @pl.when(gets(t, direction))
            def _():
                from_far(m, t, direction).wait_recv()
                if t < LINE - 1:

                    @pl.when(sends(t + 1, direction))
                    def _():
                        moves(m, t + 1, direction).start()

                pass_chunk(m, t, direction).start()

    own_copies = []
    for m in range(MB):
        send_step(m, 1)
        own_copies.append(
            (
                pltpu.make_async_copy(own_pairs.at[m], chunk(m, chip), own_sem.at[m]),
                remote(own_pairs.at[m], chunk(m, chip), core_sem, m * LINE * 2, place.partner),
            )
        )
        own_copies[-1][0].start()
        own_copies[-1][1].start()

    relay_weight(1)
    send_weight(2)
    take_step(0, 1)
    take_step(1, 1)
    pass_weight(1)
    take_step(0, 2)
    settle_weight(1)

    def query_block(b, carry):
        column = pl.multiple_of(b * 2 * LANES, 2 * LANES)
        for m, i, tile in project(weights[1], column, True):
            query_out[m * rows : (m + 1) * rows, pl.ds(column + i * LANES, LANES)] = tile.astype(bf16)
        return carry

    lax.fori_loop(0, MODEL_WIDTH // (2 * LANES), query_block, 0)
    take_step(1, 2)
    relay_weight(2)
    take_step(0, 3)
    take_step(1, 3)
    pass_weight(2)
    settle_weight(2)

    for copy in gain_copies:
        copy.wait_send()
    for w in range(3):
        for copy in directs[w] + relays[w] + passes[w]:
            copy.wait_send()
        store(w).wait()
    for m in range(MB):
        own_copies[m][0].wait()
        own_copies[m][1].wait()
        for t in range(1, LINE):
            for direction in (1, -1):

                @pl.when(sends(t, direction))
                def _():
                    moves(m, t, direction).wait_send()

                @pl.when(gets(t, direction))
                def _():
                    pass_chunk(m, t, direction).wait()


LANES_CHIP = LINE - 1


def project_all(tokens, cosine, sine, gains, pair_weight, query_weight, output_weight, length):
    held = pair_weight.shape[0]
    rows = cosine.shape[0]
    dma = pltpu.SemaphoreType.DMA
    anywhere = pl.BlockSpec(memory_space=pl.ANY)
    vmem = pl.BlockSpec(memory_space=pltpu.VMEM)
    sources = (pair_weight, query_weight, output_weight)
    full = [jax.ShapeDtypeStruct((SHARDS * held, w.shape[1]), bf16) for w in sources]
    return pl.pallas_call(
        project_kernel,
        in_specs=[vmem] * 4 + [anywhere] * 3,
        out_specs=[vmem] * 3 + [anywhere] * 4,
        out_shape=[
            jax.ShapeDtypeStruct(tokens.shape, bf16),
            jax.ShapeDtypeStruct((tokens.shape[0], query_weight.shape[1]), bf16),
            jax.ShapeDtypeStruct((SHARDS * GAIN_ROWS, held), bf16),
        ]
        + full
        + [jax.ShapeDtypeStruct((MB, length, 2 * KEY_WIDTH), bf16)],
        scratch_shapes=[pltpu.VMEM(f.shape, bf16) for f in full]
        + [
            pltpu.VMEM((MB, rows, 2 * KEY_WIDTH), bf16),
            dma((3,)),
            dma((3,)),
            dma((2, SHARDS - 1)),
            dma((2, 6)),
            dma((2, 6)),
            dma((2, 12)),
            dma((2, MB * (LINE - 1))),
            dma((2, MB * (LINE - 1))),
            dma((2, 2 * MB * LINE)),
            dma((MB,)),
        ],
        compiler_params=pltpu.CompilerParams(
            collective_id=1, has_side_effects=True, vmem_limit_bytes=VMEM_LIMIT
        ),
        name="project",
    )(tokens, cosine, sine, gains, *sources)


PIECES = 4
DENSE_PIECES = 2
ADD_ROWS = 64


def add_into(out, *parts):
    rows = out.shape[0]
    size = max(d for d in range(16, ADD_ROWS + 1, 16) if rows % d == 0)

    def body(i, carry):
        place = pl.ds(pl.multiple_of(i * size, size), size)
        total = parts[0][place].astype(f32)
        for part in parts[1:]:
            total = total + part[place].astype(f32)
        out[place] = total.astype(out.dtype)
        return carry

    lax.fori_loop(0, rows // size, body, 0)


class Piece:
    def __init__(self, own, near, far, out, out_rows):
        self.own, self.near, self.far, self.out, self.out_rows = own, near, far, out, out_rows


def reduce_kernel(experts_n, dense_n, shards_n, *refs):
    count = experts_n + dense_n
    sources, outs = refs[:count], refs[count : 2 * count]
    refs = list(refs[2 * count :])
    take = lambda n: [refs.pop(0) for _ in range(n)]
    own, other = take(count), take(count)
    across, crossed = take(dense_n), take(dense_n)
    near, far = take(count), take(count)
    load_sem, core_sem, across_sem, near_sem, far_sem, back_sem, pass_sem, store_sem = refs

    place = Place()
    core, chip, shard = place.core, place.chip, place.shard
    partner = place.partner
    inner = (chip == 1) | (chip == 2)
    outer_device = place.chip_device(3 * (chip // 2))
    inner_device = place.chip_device(1 + chip // 2)
    facing_device = place.chip_device(3 - chip)
    send = remote

    greet(partner)
    for k in range(1, shards_n):
        greet(place.peer(k))

    @pl.when(inner)
    def _():
        greet(outer_device)
        greet(facing_device)

    @pl.when(jnp.logical_not(inner))
    def _():
        greet(inner_device)

    pl.semaphore_wait(pltpu.get_barrier_semaphore(), shards_n + jnp.where(inner, 2, 1))

    loads, trades = [], []
    pieces = []
    for a in range(count):
        if a < experts_n:
            rows = own[a].shape[0]
            size = rows // PIECES
            views = [
                (
                    sources[a].at[pl.ds(pl.multiple_of(core * rows, rows) + j * size, size)],
                    sources[a].at[pl.ds(pl.multiple_of((1 - core) * rows, rows) + j * size, size)],
                    slice(j * size, (j + 1) * size),
                )
                for j in range(PIECES)
            ]
        else:
            views = [(sources[a].at[:, core], sources[a].at[:, 1 - core], slice(0, shards_n))]
        for mine, rest, spot in views:
            i = len(loads)
            loads.append(pltpu.make_async_copy(mine, own[a].at[spot], load_sem.at[i]))
            trades.append(send(rest, other[a].at[spot], core_sem, i, partner))
        total = near[a].shape[0]
        parts = PIECES if a < experts_n else DENSE_PIECES
        size = total // parts
        for j in range(parts):
            spot = slice(j * size, (j + 1) * size)
            at = pl.multiple_of(core * total, total) + j * size
            start = own[a] if a < experts_n else crossed[a - experts_n]
            pieces.append(Piece(start.at[spot], near[a].at[spot], far[a].at[spot], outs[a], pl.ds(at, size)))
    expert_pieces = experts_n * PIECES
    order = list(range(2)) + list(range(expert_pieces, expert_pieces + dense_n)) + list(range(2, expert_pieces))
    for i in order:
        loads[i].start()
        trades[i].start()

    crossings = []

    def meet_expert(i):
        a, j = i // PIECES, i % PIECES
        size = own[a].shape[0] // PIECES
        spot = slice(j * size, (j + 1) * size)
        loads[i].wait()
        trades[i].wait_recv()
        add_into(own[a].at[spot], own[a].at[spot], other[a].at[spot])

    def meet_dense(d):
        a, i = experts_n + d, expert_pieces + d
        loads[i].wait()
        trades[i].wait_recv()
        for b in range(shards_n):
            add_into(own[a].at[b], own[a].at[b], other[a].at[b])
        for k in range(1, shards_n):
            index = d * (shards_n - 1) + k - 1
            copy = send(own[a].at[place.peer_index(k)], across[d].at[k - 1], across_sem, index, place.peer(k))
            copy.start()
            crossings.append(copy)

    def gather_dense(d):
        for k in range(1, shards_n):
            crossings[d * (shards_n - 1) + k - 1].wait_recv()
        arrived = [across[d].at[k - 1] for k in range(1, shards_n)]
        add_into(crossed[d], own[experts_n + d].at[shard], *arrived)

    number = len(pieces)
    inward = [send(p.own, p.near, near_sem, i, inner_device) for i, p in enumerate(pieces)]
    facing = [send(p.own, p.far, far_sem, i, facing_device) for i, p in enumerate(pieces)]
    outward = [send(p.near, p.out.at[p.out_rows], back_sem, i, outer_device) for i, p in enumerate(pieces)]
    passed_inner = [send(p.near, p.out.at[p.out_rows], pass_sem, i, partner) for i, p in enumerate(pieces)]
    passed_outer = [
        send(p.out.at[p.out_rows], p.out.at[p.out_rows], pass_sem, i, partner) for i, p in enumerate(pieces)
    ]
    stores = [
        pltpu.make_async_copy(p.near, p.out.at[p.out_rows], store_sem.at[i]) for i, p in enumerate(pieces)
    ]

    def ready(i):
        if i < expert_pieces:
            meet_expert(i)
            if 1 <= i <= dense_n:
                meet_dense(i - 1)
        elif (i - expert_pieces) % DENSE_PIECES == 0:
            gather_dense((i - expert_pieces) // DENSE_PIECES)

        @pl.when(jnp.logical_not(inner))
        def _():
            inward[i].start()

    def halfway(i):
        inward[i].wait_recv()
        add_into(pieces[i].own, pieces[i].own, pieces[i].near)
        facing[i].start()

    def finish(i):
        facing[i].wait_recv()
        add_into(pieces[i].near, pieces[i].own, pieces[i].far)
        outward[i].start()
        passed_inner[i].start()
        stores[i].start()

    def forward(i):
        outward[i].wait_recv()
        passed_outer[i].start()

    lag = 6
    for i in range(number + lag):
        if i < number:
            ready(i)

        @pl.when(inner)
        def _():
            if i < number:
                halfway(i)
            if 1 <= i <= number:
                finish(i - 1)

        @pl.when(jnp.logical_not(inner))
        def _():
            if i >= lag:
                forward(i - lag)

    for trade in trades:
        trade.wait_send()
    for crossing in crossings:
        crossing.wait_send()

    @pl.when(inner)
    def _():
        for i in range(number):
            facing[i].wait_send()
            outward[i].wait_send()
            stores[i].wait()
            passed_inner[i].wait_send()

    @pl.when(jnp.logical_not(inner))
    def _():
        for i in range(number):
            inward[i].wait_send()
            passed_outer[i].wait_send()

    for i in range(number):
        passed_outer[i].wait_recv()


def reduce_weights(expert_grads, dense_grads, shards_n):
    experts_n, dense_n = len(expert_grads), len(dense_grads)
    columns = [g.shape[1] for g in (*expert_grads, *dense_grads)]
    out_rows = [g.shape[0] for g in expert_grads] + [g.shape[0] // shards_n for g in dense_grads]
    halves = [pltpu.VMEM((g.shape[0] // 2, g.shape[1]), bf16) for g in expert_grads]
    dense_grads = [g.reshape(shards_n, 2, g.shape[0] // (2 * shards_n), g.shape[1]) for g in dense_grads]
    arrays = list(expert_grads) + dense_grads
    halves += [pltpu.VMEM((g.shape[0],) + g.shape[2:], bf16) for g in dense_grads]
    line = [pltpu.VMEM((r // 2, c), bf16) for r, c in zip(out_rows, columns)]
    across = [pltpu.VMEM((shards_n - 1,) + g.shape[2:], bf16) for g in dense_grads]
    first = experts_n * PIECES + dense_n
    number = experts_n * PIECES + dense_n * DENSE_PIECES
    dma = pltpu.SemaphoreType.DMA
    anywhere = pl.BlockSpec(memory_space=pl.ANY)
    return pl.pallas_call(
        functools.partial(reduce_kernel, experts_n, dense_n, shards_n),
        in_specs=[anywhere] * len(arrays),
        out_specs=[anywhere] * len(arrays),
        out_shape=[jax.ShapeDtypeStruct((r, c), bf16) for r, c in zip(out_rows, columns)],
        scratch_shapes=halves + halves + across + line[experts_n:] + line + line
        + [
            dma((first,)),
            dma((2, first)),
            dma((2, dense_n * (shards_n - 1))),
            dma((2, number)),
            dma((2, number)),
            dma((2, number)),
            dma((2, number)),
            dma((number,)),
        ],
        compiler_params=pltpu.CompilerParams(
            collective_id=0, has_side_effects=True, vmem_limit_bytes=VMEM_LIMIT
        ),
        name="reduce_weights",
    )(*arrays)


def shards(
    tokens,
    doc_starts,
    routes,
    gates,
    attn_gain,
    w_q,
    key_value_weight,
    w_o,
    moe_gain,
    expert_in,
    expert_out,
    cotangent,
):
    links = Links()
    rows = tokens.shape[2]
    length = rows * links.contexts
    held = expert_in.shape[0]
    chained = links.chips == LINE and links.shards == SHARDS and held == 2
    positions = links.context * rows + jnp.arange(rows, dtype=jnp.int32)
    cosine, sine = rotation_tables(positions)
    key_places = jnp.arange(length, dtype=jnp.int32)
    width = w_q.shape[0]
    flat_tokens = tokens.reshape(MB * rows, MODEL_WIDTH)
    flat_values = flat_tokens.astype(f32)
    scale_one = lax.rsqrt(jnp.mean(flat_values * flat_values, axis=-1, keepdims=True) + eps)
    unit_one = flat_values * scale_one

    if chained:
        packed = jnp.pad(jnp.stack([attn_gain, moe_gain]), ((0, GAIN_ROWS - 2), (0, 0)))
        normed, query, gains, pair_weight, query_weight, output_weight, pairs = project_all(
            flat_tokens, cosine, sine, packed, key_value_weight, w_q, w_o, length
        )
        gains = gains.reshape(SHARDS, GAIN_ROWS, width).astype(f32)
        gain_one, gain_two = gains[:, 0].reshape(MODEL_WIDTH), gains[:, 1].reshape(MODEL_WIDTH)
    else:
        gather = lambda w: lax.all_gather(w, "fsdp", axis=0, tiled=True)
        pair_weight, query_weight, output_weight = gather(key_value_weight), gather(w_q), gather(w_o)
        gain_one, gain_two = gather(attn_gain).astype(f32), gather(moe_gain).astype(f32)
        normed = (unit_one * gain_one).astype(bf16)
        both = lambda table: jnp.concatenate([table] * MB)
        own_pairs = rotate_columns(dot(normed, pair_weight), both(cosine), both(sine), KEY_WIDTH)
        query = rotate_columns(dot(normed, query_weight), both(cosine), both(sine), MODEL_WIDTH)
        own_pairs = own_pairs.reshape(MB, rows, 2 * KEY_WIDTH)
        pairs = lax.all_gather(own_pairs, "ctx", axis=1, tiled=True)

    expert_ids = jnp.arange(E, dtype=jnp.int32)
    chosen = (routes.reshape(MB, rows, TOP)[..., None] == expert_ids).astype(f32)
    combine = jnp.sum(gates.reshape(MB, rows, TOP)[..., None] * chosen, axis=2)
    combine = jnp.concatenate([combine] + [links.across(combine, k) for k in range(1, links.shards)], axis=1)
    combine = lax.dynamic_slice_in_dim(combine, links.shard * held, held, 2)
    combine = combine.transpose(0, 2, 1)[..., None]

    biases, biases_turned = [], []
    for m in range(MB):
        starts = doc_starts[m, 0]
        begin = jnp.max(jnp.where(starts[None, :] <= positions[:, None], starts[None, :], 0), axis=1)
        seen = (key_places[None, :] <= positions[:, None]) & (key_places[None, :] >= begin[:, None])
        biases.append(jnp.where(seen, 0.0, -1e30).astype(f32))
        places, begins = jnp.tile(positions, GROUP), jnp.tile(begin, GROUP)
        seen = (key_places[:, None] <= places[None, :]) & (key_places[:, None] >= begins[None, :])
        biases_turned.append(jnp.where(seen, 0.0, -1e30).astype(f32))

    kept = []
    outputs = []
    for m in range(MB):
        own = slice(m * rows, (m + 1) * rows)
        attn = attention_forward(m, query, pairs, biases[m])
        middle = flat_tokens[own].astype(f32) + dot(attn, output_weight)
        scale_two = lax.rsqrt(jnp.mean(middle * middle, axis=-1, keepdims=True) + eps)
        unit_two = middle * scale_two
        moe_in = (unit_two * gain_two).astype(bf16)
        out_grad = cotangent[m, 0]
        row_parts = [moe_in] + [links.across(moe_in, k) for k in range(1, links.shards)]
        grad_parts = [out_grad] + [links.across(out_grad, k) for k in range(1, links.shards)]
        results, row_grads, pieces = experts(row_parts, grad_parts, combine[m], expert_in, expert_out)
        final = middle + results[0].astype(f32)
        for k in range(1, links.shards):
            final = final + links.across(results[k], k).astype(f32)
        outputs.append(final.astype(bf16))
        kept.append((attn, unit_two, scale_two, row_parts, grad_parts, row_grads, pieces))

    expert_grads = expert_weights(
        sum([k[3] for k in kept], []), sum([k[4] for k in kept], []), [k[6] for k in kept], held
    )

    expert_grads = [g.reshape(-1, g.shape[-1]) for g in expert_grads]

    input_grads, query_lows, pair_lows, middle_lows = [], [], [], []
    gain_one_grad, gain_two_grad = 0.0, 0.0
    for m in range(MB):
        own = slice(m * rows, (m + 1) * rows)
        attn, unit_two, scale_two, _, _, row_grads, _ = kept[m]
        moe_in_grad = row_grads[0].astype(f32)
        for k in range(1, links.shards):
            moe_in_grad = moe_in_grad + links.across(row_grads[k], k).astype(f32)
        gain_two_grad = gain_two_grad + jnp.sum(moe_in_grad * unit_two, axis=0)
        weighted = moe_in_grad * gain_two
        inner = jnp.mean(weighted * unit_two, axis=-1, keepdims=True)
        middle_grad = cotangent[m, 0].astype(f32) + (weighted - unit_two * inner) * scale_two
        middle_low = middle_grad.astype(bf16)
        attn_grad = dot(middle_low, output_weight, NT).astype(bf16)
        query_low, pair_grad = attention_backward(
            m, query, cosine, sine, pairs, biases_turned[m], attn_grad
        )
        if chained:
            pair_grad = pair_grad.reshape(links.chips, 2, rows, 2 * KEY_WIDTH)
            core_part = lambda core: lax.dynamic_index_in_dim(pair_grad, core, 1, keepdims=False)
            part = core_part(links.core).astype(f32)
            part = (part + links.other_core(core_part(1 - links.core)).astype(f32)).astype(bf16)
            chip_part = lambda s: lax.dynamic_index_in_dim(
                part, (links.chip - s + links.chips) % links.chips, 0, keepdims=False
            )
            parts = [chip_part(0)]
            for s in range(1, links.chips):
                parts.append(links.shift(chip_part(s), -s))
        else:
            parts = [lax.psum_scatter(pair_grad, "ctx", scatter_dimension=0, tiled=True)]
        pair_low = pair_gradient(parts, cosine, sine)
        normed_grad = dot(query_low, query_weight, NT) + dot(pair_low, pair_weight, NT)
        gain_one_grad = gain_one_grad + jnp.sum(normed_grad * unit_one[own], axis=0)
        weighted = normed_grad * gain_one
        inner = jnp.mean(weighted * unit_one[own], axis=-1, keepdims=True)
        residual_grad = (weighted - unit_one[own] * inner) * scale_one[own]
        input_grads.append(middle_grad + residual_grad)
        query_lows.append(query_low)
        pair_lows.append(pair_low)
        middle_lows.append(middle_low)

    join = lambda items: jnp.concatenate(items, axis=0)

    output_grad = dot(join([k[0] for k in kept]), join(middle_lows), TN).astype(bf16)
    query_grad = dot(normed, join(query_lows), TN).astype(bf16)
    pair_weight_grad = dot(normed, join(pair_lows), TN).astype(bf16)
    gain_grads = jnp.stack([gain_one_grad, gain_two_grad], axis=1)
    gain_grads = jnp.pad(gain_grads, ((0, 0), (0, LANES - 2))).astype(bf16)
    dense_grads = [output_grad, query_grad, jnp.concatenate([pair_weight_grad, gain_grads], axis=1)]
    if chained:
        totals = reduce_weights(expert_grads, dense_grads, links.shards)
    else:
        totals = [lax.psum(g, "ctx") for g in expert_grads]
        for g in dense_grads:
            part = lax.psum_scatter(g, "fsdp", scatter_dimension=0, tiled=True)
            totals.append(lax.psum(part, "ctx"))
    gate_total, up_total, down_total, output_total, query_total, pair_total = [t.astype(f32) for t in totals]
    expand_total = jnp.concatenate([gate_total, up_total], axis=1)

    return (
        jnp.stack(outputs)[:, None],
        jnp.stack(input_grads)[:, None],
        pair_total[:, 2 * KEY_WIDTH],
        query_total,
        pair_total[:, : 2 * KEY_WIDTH],
        output_total,
        pair_total[:, 2 * KEY_WIDTH + 1],
        expand_total.reshape(held, MODEL_WIDTH, 2 * F),
        down_total.reshape(held, F, MODEL_WIDTH),
    )


def solution(mesh):
    return jax.shard_map(
        shards,
        mesh=mesh,
        in_specs=(
            P(None, "fsdp", "ctx", None),
            P(None, "fsdp", None),
            P(None, "fsdp", "ctx", None),
            P(None, "fsdp", "ctx", None),
            P("fsdp"),
            P("fsdp", None),
            P("fsdp", None),
            P("fsdp", None),
            P("fsdp"),
            P("fsdp", None, None),
            P("fsdp", None, None),
            P(None, "fsdp", "ctx", None),
        ),
        out_specs=(
            P(None, "fsdp", "ctx", None),
            P(None, "fsdp", "ctx", None),
            P("fsdp"),
            P("fsdp", None),
            P("fsdp", None),
            P("fsdp", None),
            P("fsdp"),
            P("fsdp", None, None),
            P("fsdp", None, None),
        ),
        check_vma=False,
    )
```

```python
import functools

import jax
import jax.numpy as jnp
from jax import lax
from jax.experimental import pallas as pl
from jax.experimental.pallas import tpu as pltpu
from jax.sharding import PartitionSpec as P

MODEL_WIDTH = 1536
QUERY_HEADS = 24
KEY_VALUE_HEADS = 8
HEAD_SIZE = 64
GROUP = QUERY_HEADS // KEY_VALUE_HEADS
KEY_WIDTH = KEY_VALUE_HEADS * HEAD_SIZE
F = 512
E = 8
TOP = 4
MB = 2
LANES = 128
PAIRS = KEY_WIDTH // LANES
PAIR_QUERY = 2 * GROUP * HEAD_SIZE
F_BLOCK = 256
VMEM_LIMIT = 60 * 1024 * 1024

eps = 1e-05
theta = 10000.0

NT = (((1,), (1,)), ((), ()))
TN = (((0,), (0,)), ((), ()))
bf16 = jnp.bfloat16
f32 = jnp.float32


def dot(left, right, dims=(((1,), (0,)), ((), ()))):
    return lax.dot_general(left, right, dims, preferred_element_type=f32)


def rotation_tables(positions):
    frequency = theta ** (-jnp.arange(0, HEAD_SIZE, 2, dtype=f32) / HEAD_SIZE)
    angles = positions.astype(f32)[:, None] * frequency[None, :]
    cosine, sine = jnp.cos(angles), jnp.sin(angles)
    repeat = LANES // HEAD_SIZE
    cosine = jnp.concatenate([cosine, cosine] * repeat, axis=1)
    sine = jnp.concatenate([-sine, sine] * repeat, axis=1)
    return cosine, sine


def lane_index(shape):
    return lax.broadcasted_iota(jnp.int32, shape, 1)


def rotate(tile, cosine, sine):
    half = HEAD_SIZE // 2
    ahead = pltpu.roll(tile, LANES - half, 1)
    behind = pltpu.roll(tile, half, 1)
    first = lane_index(tile.shape) % HEAD_SIZE < half
    return tile * cosine + jnp.where(first, ahead, behind) * sine


def rotate_columns_kernel(rotated, values_ref, cosine_ref, sine_ref, out_ref):
    cosine, sine = cosine_ref[...], sine_ref[...]
    for i in range(values_ref.shape[1] // LANES):
        cols = slice(i * LANES, (i + 1) * LANES)
        tile = values_ref[:, cols]
        if i < rotated // LANES:
            tile = rotate(tile, cosine, sine)
        out_ref[:, cols] = tile.astype(bf16)


def rotate_columns(values, cosine, sine, rotated):
    return pl.pallas_call(
        functools.partial(rotate_columns_kernel, rotated),
        out_shape=jax.ShapeDtypeStruct(values.shape, bf16),
        compiler_params=pltpu.CompilerParams(vmem_limit_bytes=VMEM_LIMIT),
        name="rotate_columns",
    )(values, cosine, sine)


def pair_gradient_kernel(count, cosine_ref, sine_ref, *refs):
    out_ref = refs[-1]
    cosine, sine = cosine_ref[...], sine_ref[...]
    for i in range(2 * KEY_WIDTH // LANES):
        cols = slice(i * LANES, (i + 1) * LANES)
        total = refs[0][:, cols].astype(f32)
        for ref in refs[1:count]:
            total = total + ref[:, cols].astype(f32)
        if i < KEY_WIDTH // LANES:
            total = rotate(total, cosine, -sine)
        out_ref[:, cols] = total.astype(bf16)


def pair_gradient(parts, cosine, sine):
    return pl.pallas_call(
        functools.partial(pair_gradient_kernel, len(parts)),
        out_shape=jax.ShapeDtypeStruct(parts[0].shape, bf16),
        compiler_params=pltpu.CompilerParams(vmem_limit_bytes=VMEM_LIMIT),
        name="pair_gradient",
    )(cosine, sine, *parts)


def grouped(tiles, half):
    mine = lane_index(tiles[0].shape) // HEAD_SIZE == half
    rows = []
    for j in range(GROUP * half, GROUP * half + GROUP):
        tile = tiles[j // 2]
        if j % 2 != half:
            tile = pltpu.roll(tile, HEAD_SIZE, 1)
        rows.append(jnp.where(mine, tile, 0.0))
    return jnp.concatenate(rows, axis=0).astype(bf16)


def ungrouped(per_half, rows):
    heads = []
    for j in range(2 * GROUP):
        half, place = j // GROUP, j % GROUP
        tile = per_half[half][place * rows : (place + 1) * rows]
        if j % 2 != half:
            tile = pltpu.roll(tile, HEAD_SIZE, 1)
        heads.append(tile)
    low = lane_index(heads[0].shape) < HEAD_SIZE
    return [jnp.where(low, heads[2 * i], heads[2 * i + 1]) for i in range(GROUP)]


def query_tiles(query_ref):
    scale = 1.0 / HEAD_SIZE
    return [query_ref[:, i * LANES : (i + 1) * LANES].astype(f32) * scale for i in range(GROUP)]


def attention_pair(tiles, key, value, bias):
    rows = bias.shape[0]
    results = []
    for half in range(2):
        scores = dot(grouped(tiles, half), key, NT)
        scores = jnp.concatenate(
            [scores[g * rows : (g + 1) * rows] + bias for g in range(GROUP)], axis=0
        )
        peak = jnp.max(scores, axis=1, keepdims=True)
        weights = jnp.exp(scores - peak)
        total = jnp.sum(weights, axis=1, keepdims=True)
        results.append(dot(weights.astype(bf16), value) / total)
    return ungrouped(results, rows)


def attention_forward_kernel(query_ref, key_ref, value_ref, bias_ref, out_ref):
    tiles = attention_pair(query_tiles(query_ref), key_ref[...], value_ref[...], bias_ref[...])
    for i, tile in enumerate(tiles):
        out_ref[:, i * LANES : (i + 1) * LANES] = tile.astype(bf16)


def attention_forward(m, query, pairs, bias):
    rows, length = bias.shape
    return pl.pallas_call(
        attention_forward_kernel,
        grid=(PAIRS,),
        in_specs=[
            pl.BlockSpec((rows, PAIR_QUERY), lambda p: (m, p)),
            pl.BlockSpec((None, length, LANES), lambda p: (m, 0, p)),
            pl.BlockSpec((None, length, LANES), lambda p: (m, 0, p + PAIRS)),
            pl.BlockSpec((rows, length), lambda p: (0, 0)),
        ],
        out_specs=pl.BlockSpec((rows, PAIR_QUERY), lambda p: (0, p)),
        out_shape=jax.ShapeDtypeStruct((rows, MODEL_WIDTH), bf16),
        compiler_params=pltpu.CompilerParams(vmem_limit_bytes=VMEM_LIMIT),
        cost_estimate=pl.CostEstimate(
            flops=16 * rows * length * MODEL_WIDTH,
            bytes_accessed=4 * length * MODEL_WIDTH,
            transcendentals=rows * length * QUERY_HEADS,
        ),
        name="attention_forward",
    )(query, pairs, pairs, bias)


def attention_backward_kernel(
    query_ref, cosine_ref, sine_ref, key_ref, value_ref, bias_ref, grad_ref, query_out, pair_out
):
    rows = query_ref.shape[0]
    cosine, sine = cosine_ref[...], sine_ref[...]
    tiles = query_tiles(query_ref)
    grads = [grad_ref[:, i * LANES : (i + 1) * LANES].astype(f32) for i in range(GROUP)]
    key, value = key_ref[...], value_ref[...]
    key_grad, value_grad = None, None
    query_grads = []
    for half in range(2):
        query = grouped(tiles, half)
        grad = grouped(grads, half)
        scores = dot(key, query, NT) + bias_ref[...]
        weights = jnp.exp(scores - jnp.max(scores, axis=0, keepdims=True))
        prob = weights * (1.0 / jnp.sum(weights, axis=0, keepdims=True))
        prob_grad = dot(value, grad, NT)
        delta = jnp.sum(prob * prob_grad, axis=0, keepdims=True)
        score_grad = (prob * (prob_grad - delta)).astype(bf16)
        value_part = dot(prob.astype(bf16), grad)
        key_part = dot(score_grad, query)
        value_grad = value_part if half == 0 else value_grad + value_part
        key_grad = key_part if half == 0 else key_grad + key_part
        query_grads.append(dot(score_grad, key, TN))
    for i, tile in enumerate(ungrouped(query_grads, rows)):
        tile = rotate(tile * (1.0 / HEAD_SIZE), cosine, -sine)
        query_out[:, i * LANES : (i + 1) * LANES] = tile.astype(bf16)
    first = pl.multiple_of(pl.program_id(0) * LANES, LANES)
    pair_out[:, pl.ds(first, LANES)] = key_grad.astype(bf16)
    pair_out[:, pl.ds(first + KEY_WIDTH, LANES)] = value_grad.astype(bf16)


def attention_backward(m, query, cosine, sine, pairs, bias, grad):
    rows = cosine.shape[0]
    length = pairs.shape[1]
    whole = lambda shape: pl.BlockSpec(shape, lambda p: (0, 0))
    return pl.pallas_call(
        attention_backward_kernel,
        grid=(PAIRS,),
        in_specs=[
            pl.BlockSpec((rows, PAIR_QUERY), lambda p: (m, p)),
            whole((rows, LANES)),
            whole((rows, LANES)),
            pl.BlockSpec((None, length, LANES), lambda p: (m, 0, p)),
            pl.BlockSpec((None, length, LANES), lambda p: (m, 0, p + PAIRS)),
            whole(bias.shape),
            pl.BlockSpec((rows, PAIR_QUERY), lambda p: (0, p)),
        ],
        out_specs=[
            pl.BlockSpec((rows, PAIR_QUERY), lambda p: (0, p)),
            whole((length, 2 * KEY_WIDTH)),
        ],
        out_shape=[
            jax.ShapeDtypeStruct((rows, MODEL_WIDTH), bf16),
            jax.ShapeDtypeStruct((length, 2 * KEY_WIDTH), bf16),
        ],
        compiler_params=pltpu.CompilerParams(vmem_limit_bytes=VMEM_LIMIT),
        cost_estimate=pl.CostEstimate(
            flops=40 * rows * length * MODEL_WIDTH,
            bytes_accessed=8 * length * MODEL_WIDTH,
            transcendentals=rows * length * QUERY_HEADS,
        ),
        name="attention_backward",
    )(query, cosine, sine, pairs, pairs, bias, grad)


def expert_block(inputs, out_grad, combine, gate_weight, up_weight, down_weight):
    gate = dot(inputs, gate_weight)
    up = dot(inputs, up_weight)
    sigmoid = jax.nn.sigmoid(gate)
    silu = gate * sigmoid
    active = (silu * up * combine).astype(bf16)
    active_grad = dot(out_grad, down_weight, NT) * combine
    gate_grad = (active_grad * up * sigmoid * (1.0 + gate * (1.0 - sigmoid))).astype(bf16)
    up_grad = (active_grad * silu).astype(bf16)
    result = dot(active, down_weight)
    row_grad = dot(gate_grad, gate_weight, NT) + dot(up_grad, up_weight, NT)
    return active, gate_grad, up_grad, result, row_grad


def experts_kernel(parts, rows, steps, combine_ref, gate_ref, up_ref, down_ref, *refs):
    rows_in, grads_in = refs[:parts], refs[parts : 2 * parts]
    refs = refs[2 * parts :]
    results, row_grads = refs[:parts], refs[parts : 2 * parts]
    active_out, gate_out, up_out, rows_all, grads_all, result_sum, grad_sum = refs[2 * parts :]
    step = pl.program_id(0) * pl.num_programs(1) + pl.program_id(1)

    @pl.when(step == 0)
    def _():
        for k in range(parts):
            place = slice(k * rows, (k + 1) * rows)
            rows_all[place] = rows_in[k][...]
            grads_all[place] = grads_in[k][...]
        result_sum[...] = jnp.zeros_like(result_sum)
        grad_sum[...] = jnp.zeros_like(grad_sum)

    inputs, out_grad, combine = rows_all[...], grads_all[...], combine_ref[0]
    active, gate_grad, up_grad, result, row_grad = expert_block(
        inputs, out_grad, combine, gate_ref[0], up_ref[0], down_ref[0]
    )
    active_out[...] = active
    gate_out[...] = gate_grad
    up_out[...] = up_grad
    result_sum[...] += result
    grad_sum[...] += row_grad

    @pl.when(step == steps - 1)
    def _():
        for k in range(parts):
            place = slice(k * rows, (k + 1) * rows)
            results[k][...] = result_sum[place].astype(bf16)
            row_grads[k][...] = grad_sum[place].astype(bf16)


def experts(row_parts, grad_parts, combine, expert_in, expert_out):
    parts = len(row_parts)
    rows = row_parts[0].shape[0]
    held = expert_in.shape[0]
    tokens = parts * rows
    blocks = F // F_BLOCK
    whole = pl.BlockSpec((rows, MODEL_WIDTH), lambda e, b: (0, 0))
    piece = pl.BlockSpec((tokens, F_BLOCK), lambda e, b: (0, e * blocks + b))
    row_shape = jax.ShapeDtypeStruct((rows, MODEL_WIDTH), bf16)
    piece_shape = jax.ShapeDtypeStruct((tokens, held * F), bf16)
    out = pl.pallas_call(
        functools.partial(experts_kernel, parts, rows, held * blocks),
        grid=(held, blocks),
        in_specs=[
            pl.BlockSpec((1, tokens, 1), lambda e, b: (e, 0, 0)),
            pl.BlockSpec((1, MODEL_WIDTH, F_BLOCK), lambda e, b: (e, 0, b)),
            pl.BlockSpec((1, MODEL_WIDTH, F_BLOCK), lambda e, b: (e, 0, b + blocks)),
            pl.BlockSpec((1, F_BLOCK, MODEL_WIDTH), lambda e, b: (e, b, 0)),
        ]
        + [whole] * (2 * parts),
        out_specs=[whole] * (2 * parts) + [piece] * 3,
        out_shape=[row_shape] * (2 * parts) + [piece_shape] * 3,
        scratch_shapes=[
            pltpu.VMEM((tokens, MODEL_WIDTH), bf16),
            pltpu.VMEM((tokens, MODEL_WIDTH), bf16),
            pltpu.VMEM((tokens, MODEL_WIDTH), f32),
            pltpu.VMEM((tokens, MODEL_WIDTH), f32),
        ],
        compiler_params=pltpu.CompilerParams(vmem_limit_bytes=VMEM_LIMIT),
        cost_estimate=pl.CostEstimate(
            flops=12 * tokens * held * MODEL_WIDTH * F,
            bytes_accessed=6 * held * MODEL_WIDTH * F + 20 * tokens * MODEL_WIDTH,
            transcendentals=tokens * held * F,
        ),
        name="experts",
    )(combine, expert_in, expert_in, expert_out, *row_parts, *grad_parts)
    return out[:parts], out[parts : 2 * parts], out[2 * parts :]


def expert_weights_kernel(rows_ref, grads_ref, active_ref, gate_ref, up_ref, gate_out, up_out, down_out, turned):
    step = pl.program_id(0) * pl.num_programs(1) + pl.program_id(1)

    @pl.when(step == 0)
    def _():
        turned[...] = rows_ref[...].T

    gate_out[0] = dot(turned[...], gate_ref[...]).astype(bf16)
    up_out[0] = dot(turned[...], up_ref[...]).astype(bf16)
    down_out[0] = dot(active_ref[...], grads_ref[...], TN).astype(bf16)


def expert_weights(rows, grads, active, gate, up, held):
    tokens = rows.shape[0]
    blocks = F // F_BLOCK
    whole = pl.BlockSpec((tokens, MODEL_WIDTH), lambda e, b: (0, 0))
    piece = pl.BlockSpec((tokens, F_BLOCK), lambda e, b: (0, e * blocks + b))
    wide = pl.BlockSpec((1, MODEL_WIDTH, F_BLOCK), lambda e, b: (e, 0, b))
    return pl.pallas_call(
        expert_weights_kernel,
        grid=(held, blocks),
        in_specs=[whole] * 2 + [piece] * 3,
        out_specs=[wide, wide, pl.BlockSpec((1, F_BLOCK, MODEL_WIDTH), lambda e, b: (e, b, 0))],
        out_shape=[
            jax.ShapeDtypeStruct((held, MODEL_WIDTH, F), bf16),
            jax.ShapeDtypeStruct((held, MODEL_WIDTH, F), bf16),
            jax.ShapeDtypeStruct((held, F, MODEL_WIDTH), bf16),
        ],
        scratch_shapes=[pltpu.VMEM((MODEL_WIDTH, tokens), bf16)],
        compiler_params=pltpu.CompilerParams(vmem_limit_bytes=VMEM_LIMIT),
        cost_estimate=pl.CostEstimate(
            flops=6 * tokens * held * MODEL_WIDTH * F,
            bytes_accessed=6 * held * MODEL_WIDTH * F + 8 * tokens * MODEL_WIDTH,
            transcendentals=0,
        ),
        name="expert_weights",
    )(rows, grads, active, gate, up)


class Links:
    def __init__(self):
        self.shards = lax.axis_size("fsdp")
        self.contexts = lax.axis_size("ctx")
        self.chips = self.contexts // 2
        self.shard = lax.axis_index("fsdp")
        self.context = lax.axis_index("ctx")
        self.chip = self.context // 2
        self.core = self.context % 2

    def across(self, array, k):
        return lax.ppermute(array, "fsdp", [(i, i ^ k) for i in range(self.shards)])

    def other_core(self, array):
        return lax.ppermute(array, "ctx", [(i, i ^ 1) for i in range(self.contexts)])

    def shift(self, array, s):
        n = self.contexts
        return lax.ppermute(array, "ctx", [(i, (i + 2 * s) % n) for i in range(n)])


MESH = pl.DeviceIdType.MESH
LINE = 4


class Place:
    def __init__(self):
        self.shard, self.context = lax.axis_index("fsdp"), lax.axis_index("ctx")
        self.core, self.chip = self.context % 2, self.context // 2
        self.partner = {"ctx": 2 * self.chip + 1 - self.core}

    def peer_index(self, k):
        x, y = (self.shard % 2 + k % 2) % 2, (self.shard // 2 + k // 2) % 2
        return 2 * y + x

    def peer(self, k):
        return {"fsdp": self.peer_index(k)}

    def chip_device(self, chip):
        return {"ctx": 2 * chip + self.core}


def remote(source, target, sems, index, device):
    return pltpu.make_async_remote_copy(
        src_ref=source,
        dst_ref=target,
        send_sem=sems.at[0, index],
        recv_sem=sems.at[1, index],
        device_id=device,
        device_id_type=MESH,
    )


def greet(device):
    pl.semaphore_signal(pltpu.get_barrier_semaphore(), inc=1, device_id=device, device_id_type=MESH)


SHARDS = 4
GAIN_ROWS = 16


class Square:
    def __init__(self, place, blocks, direct_sem, relay_sem, base=0):
        half = blocks.shape[1] // 2
        own = blocks.at[place.shard]
        self.directs = [remote(own, own, direct_sem, base + k - 1, place.peer(k)) for k in (1, 2)]
        self.relays = []
        for k in (1, 2):
            spot = blocks.at[place.peer_index(k), (k - 1) * half : k * half]
            self.relays.append(remote(spot, spot, relay_sem, base + k - 1, place.peer(3 - k)))

    def start(self):
        for copy in self.directs:
            copy.start()

    def pass_on(self):
        for direct, relay in zip(self.directs, self.relays):
            direct.wait_recv()
            relay.start()

    def finish(self):
        for copy in self.relays:
            copy.wait_recv()

    def drain(self):
        for copy in self.directs + self.relays:
            copy.wait_send()


def project_kernel(
    tokens_ref, cosine_ref, sine_ref, gain_ref, combine_ref, grad_ref, pair_src, query_src, output_src, *refs
):
    normed_out, query_out, gains, combine_out, grads_out = refs[:5]
    pair_out, query_weight_out, output_weight_out, pairs_out = refs[5:9]
    weights, own_pairs = refs[9:12], refs[12]
    (
        load_sem,
        store_sem,
        gain_sem,
        combine_sem,
        direct_sem,
        relay_sem,
        pass_sem,
        right_sem,
        left_sem,
        core_sem,
        own_sem,
        square_direct_sem,
        square_relay_sem,
    ) = refs[13:]
    sources = (pair_src, query_src, output_src)
    weight_outs = (pair_out, query_weight_out, output_weight_out)
    place = Place()
    core, chip, shard = place.core, place.chip, place.shard
    rows = cosine_ref.shape[0]
    held = pair_src.shape[0]
    half, quarter = held // 2, held // 4

    has_left, has_right = chip > 0, chip < LINE - 1
    greet(place.partner)
    for k in range(1, SHARDS):
        greet(place.peer(k))

    @pl.when(has_left)
    def _():
        greet(place.chip_device(chip - 1))

    @pl.when(has_right)
    def _():
        greet(place.chip_device(chip + 1))

    neighbours = jnp.where(has_left, 1, 0) + jnp.where(has_right, 1, 0)
    pl.semaphore_wait(pltpu.get_barrier_semaphore(), SHARDS + neighbours)

    def rows_of(owner, piece, size):
        return pl.ds(pl.multiple_of(owner * held + core * half, half) + piece, size)

    gains[pl.ds(pl.multiple_of(shard * GAIN_ROWS, GAIN_ROWS), GAIN_ROWS)] = gain_ref[...]
    gain_copies = []
    for k in range(1, SHARDS):
        target = gains.at[pl.ds(pl.multiple_of(shard * GAIN_ROWS, GAIN_ROWS), GAIN_ROWS)]
        gain_copies.append(remote(gain_ref, target, gain_sem, k - 1, place.peer(k)))
    combine_out[shard] = combine_ref[...]
    combine_copies = [
        remote(combine_ref, combine_out.at[shard], combine_sem, k - 1, place.peer(k)) for k in range(1, SHARDS)
    ]
    grads_out[shard] = grad_ref[...]
    square = Square(place, grads_out, square_direct_sem, square_relay_sem)

    loads, directs, relays, passes = [], [], [], []
    for w in range(3):
        weight = weights[w]
        own_rows = pl.ds(pl.multiple_of(shard * held, held), held)
        loads.append(pltpu.make_async_copy(sources[w], weight.at[own_rows], load_sem.at[w]))
        mine = sources[w].at[pl.ds(pl.multiple_of(core * half, half), half)]
        spot = weight.at[rows_of(shard, 0, half)]
        directs.append([remote(mine, spot, direct_sem, 2 * w + k - 1, place.peer(k)) for k in (1, 2)])
        relay, onward = [], []
        for k in (1, 2):
            spot = weight.at[rows_of(place.peer_index(k), (k - 1) * quarter, quarter)]
            relay.append(remote(spot, spot, relay_sem, 2 * w + k - 1, place.peer(3 - k)))
            spot = weight.at[rows_of(place.peer_index(k), 0, half)]
            onward.append(remote(spot, spot, pass_sem, 4 * w + k - 1, place.partner))
        for k in (1, 2):
            spot = weight.at[rows_of(place.peer_index(3), (k - 1) * quarter, quarter)]
            onward.append(remote(spot, spot, pass_sem, 4 * w + k + 1, place.partner))
        relays.append(relay)
        passes.append(onward)

    def send_weight(w):
        for copy in directs[w]:
            copy.start()

    def relay_weight(w):
        for k in (1, 2):
            directs[w][k - 1].wait_recv()
            relays[w][k - 1].start()
        for k in (1, 2):
            passes[w][k - 1].start()

    def pass_weight(w):
        for k in (1, 2):
            relays[w][k - 1].wait_recv()
            passes[w][k + 1].start()

    def store(w):
        return pltpu.make_async_copy(weights[w], weight_outs[w], store_sem.at[w])

    def settle_weight(w):
        loads[w].wait()
        for copy in passes[w]:
            copy.wait_recv()
        store(w).start()

    for copy in gain_copies:
        copy.start()
    send_weight(0)
    for load in loads:
        load.start()

    values = tokens_ref[...].astype(f32)
    scale = lax.rsqrt(jnp.mean(values * values, axis=-1, keepdims=True) + eps)
    for copy in gain_copies:
        copy.wait_recv()
    for b in range(SHARDS):
        columns = slice(b * held, (b + 1) * held)
        gain = gains[b * GAIN_ROWS : b * GAIN_ROWS + 1].astype(f32)
        normed_out[:, columns] = (values[:, columns] * scale * gain).astype(bf16)

    relay_weight(0)
    send_weight(1)
    pass_weight(0)
    settle_weight(0)
    cosine, sine = cosine_ref[...], sine_ref[...]

    def project(weight, column, rotated):
        result = dot(normed_out[...], weight[:, pl.ds(column, 2 * LANES)])
        tiles = []
        for m in range(MB):
            for i in range(2):
                tile = result[m * rows : (m + 1) * rows, i * LANES : (i + 1) * LANES]
                tiles.append((m, i, rotate(tile, cosine, sine) if rotated else tile))
        return tiles

    def pair_block(b, rotated):
        column = pl.multiple_of(b * 2 * LANES, 2 * LANES)
        for m, i, tile in project(weights[0], column, rotated):
            own_pairs[m, :, pl.ds(column + i * LANES, LANES)] = tile.astype(bf16)

    blocks = KEY_WIDTH // (2 * LANES)
    for b in range(blocks):
        pair_block(b, True)
    for b in range(blocks, 2 * blocks):
        pair_block(b, False)

    def chunk(m, owner):
        return pairs_out.at[m, pl.ds(pl.multiple_of((2 * owner + core) * rows, rows), rows)]

    def moves(m, t, direction):
        owner = chip - direction * (t - 1)
        source = own_pairs.at[m] if t == 1 else chunk(m, jnp.clip(owner, 0, LANES_CHIP))
        sems = right_sem if direction > 0 else left_sem
        target = chunk(m, jnp.clip(owner, 0, LANES_CHIP))
        device = place.chip_device(jnp.clip(chip + direction, 0, LANES_CHIP))
        return remote(source, target, sems, m * (LINE - 1) + t - 1, device)

    def sends(t, direction):
        owner = chip - direction * (t - 1)
        if direction > 0:
            return (chip < LINE - 1) & (owner >= 0)
        return (chip > 0) & (owner <= LINE - 1)

    def gets(t, direction):
        owner = chip - direction * t
        return owner >= 0 if direction > 0 else owner <= LINE - 1

    def from_far(m, t, direction):
        owner = jnp.clip(chip - direction * t, 0, LANES_CHIP)
        sems = right_sem if direction > 0 else left_sem
        return remote(chunk(m, owner), chunk(m, owner), sems, m * (LINE - 1) + t - 1, place.partner)

    def pass_chunk(m, t, direction):
        owner = jnp.clip(chip - direction * t, 0, LANES_CHIP)
        index = (m * LINE + t) * 2 + (1 if direction > 0 else 0)
        return remote(chunk(m, owner), chunk(m, owner), core_sem, index, place.partner)

    def send_step(m, t):
        for direction in (1, -1):

            @pl.when(sends(t, direction))
            def _():
                moves(m, t, direction).start()

    def take_step(m, t):
        for direction in (1, -1):

            @pl.when(gets(t, direction))
            def _():
                from_far(m, t, direction).wait_recv()
                if t < LINE - 1:

                    @pl.when(sends(t + 1, direction))
                    def _():
                        moves(m, t + 1, direction).start()

                pass_chunk(m, t, direction).start()

    own_copies = []
    for m in range(MB):
        send_step(m, 1)
        own_copies.append(
            (
                pltpu.make_async_copy(own_pairs.at[m], chunk(m, chip), own_sem.at[m]),
                remote(own_pairs.at[m], chunk(m, chip), core_sem, m * LINE * 2, place.partner),
            )
        )
        own_copies[-1][0].start()
        own_copies[-1][1].start()

    relay_weight(1)
    send_weight(2)
    take_step(0, 1)
    take_step(1, 1)
    pass_weight(1)
    take_step(0, 2)
    settle_weight(1)

    def query_block(b, carry):
        column = pl.multiple_of(b * 2 * LANES, 2 * LANES)
        for m, i, tile in project(weights[1], column, True):
            query_out[m * rows : (m + 1) * rows, pl.ds(column + i * LANES, LANES)] = tile.astype(bf16)
        return carry

    lax.fori_loop(0, MODEL_WIDTH // (2 * LANES), query_block, 0)
    take_step(1, 2)
    relay_weight(2)
    square.start()
    for copy in combine_copies:
        copy.start()
    take_step(0, 3)
    pass_weight(2)
    square.pass_on()
    take_step(1, 3)
    settle_weight(2)
    square.finish()

    square.drain()
    for copy in combine_copies:
        copy.wait()
    for copy in gain_copies:
        copy.wait_send()
    for w in range(3):
        for copy in directs[w] + relays[w] + passes[w]:
            copy.wait_send()
        store(w).wait()
    for m in range(MB):
        own_copies[m][0].wait()
        own_copies[m][1].wait()
        for t in range(1, LINE):
            for direction in (1, -1):

                @pl.when(sends(t, direction))
                def _():
                    moves(m, t, direction).wait_send()

                @pl.when(gets(t, direction))
                def _():
                    pass_chunk(m, t, direction).wait()


LANES_CHIP = LINE - 1


def project_all(tokens, cosine, sine, gains, combine, grads, pair_weight, query_weight, output_weight, length):
    held = pair_weight.shape[0]
    rows = cosine.shape[0]
    dma = pltpu.SemaphoreType.DMA
    anywhere = pl.BlockSpec(memory_space=pl.ANY)
    vmem = pl.BlockSpec(memory_space=pltpu.VMEM)
    sources = (pair_weight, query_weight, output_weight)
    full = [jax.ShapeDtypeStruct((SHARDS * held, w.shape[1]), bf16) for w in sources]
    return pl.pallas_call(
        project_kernel,
        in_specs=[vmem] * 6 + [anywhere] * 3,
        out_specs=[vmem] * 5 + [anywhere] * 4,
        out_shape=[
            jax.ShapeDtypeStruct(tokens.shape, bf16),
            jax.ShapeDtypeStruct((tokens.shape[0], query_weight.shape[1]), bf16),
            jax.ShapeDtypeStruct((SHARDS * GAIN_ROWS, held), bf16),
            jax.ShapeDtypeStruct((SHARDS,) + combine.shape, f32),
            jax.ShapeDtypeStruct((SHARDS,) + grads.shape, bf16),
        ]
        + full
        + [jax.ShapeDtypeStruct((MB, length, 2 * KEY_WIDTH), bf16)],
        scratch_shapes=[pltpu.VMEM(f.shape, bf16) for f in full]
        + [
            pltpu.VMEM((MB, rows, 2 * KEY_WIDTH), bf16),
            dma((3,)),
            dma((3,)),
            dma((2, SHARDS - 1)),
            dma((2, SHARDS - 1)),
            dma((2, 6)),
            dma((2, 6)),
            dma((2, 12)),
            dma((2, MB * (LINE - 1))),
            dma((2, MB * (LINE - 1))),
            dma((2, 2 * MB * LINE)),
            dma((MB,)),
            dma((2, 2)),
            dma((2, 2)),
        ],
        compiler_params=pltpu.CompilerParams(
            collective_id=1, has_side_effects=True, vmem_limit_bytes=VMEM_LIMIT
        ),
        name="project",
    )(tokens, cosine, sine, gains, combine, grads, *sources)


def layer_kernel(
    query_ref,
    pairs_ref,
    bias_ref,
    tokens_ref,
    gain_ref,
    grads_ref,
    own_grad_ref,
    combine_ref,
    output_src,
    expand_src,
    shrink_src,
    attn_out,
    middle_out,
    rows_out,
    grads_out,
    results_out,
    row_grads_out,
    active_out,
    gate_out,
    up_out,
    output_weight,
    expand,
    shrink,
    rows_all,
    grads_all,
    result_sum,
    grad_sum,
    results,
    row_grads,
    active,
    gate,
    up,
    load_sem,
    direct_sem,
    relay_sem,
    emit_sem,
):
    place = Place()
    shard = place.shard
    rows = bias_ref.shape[1]
    held = expand.shape[0]
    tokens = SHARDS * rows
    loads = [
        pltpu.make_async_copy(source, target, load_sem.at[i])
        for i, (source, target) in enumerate(
            ((output_src, output_weight), (expand_src, expand), (shrink_src, shrink))
        )
    ]
    for load in loads:
        load.start()
    for k in (1, 2):
        greet(place.peer(k))
    pl.semaphore_wait(pltpu.get_barrier_semaphore(), 2)

    grads_all[shard] = own_grad_ref[...]
    grad_square = Square(place, grads_all, direct_sem, relay_sem)
    row_squares = [Square(place, rows_all.at[m], direct_sem, relay_sem, 2 + 2 * m) for m in range(MB)]
    grad_square.start()

    def attend(m):
        own = slice(m * rows, (m + 1) * rows)

        def pair(p, carry):
            column = pl.multiple_of(p * PAIR_QUERY, PAIR_QUERY)
            lane = pl.multiple_of(p * LANES, LANES)
            scale = 1.0 / HEAD_SIZE
            tiles = [
                query_ref[own, pl.ds(column + i * LANES, LANES)].astype(f32) * scale for i in range(GROUP)
            ]
            key = pairs_ref[m, :, pl.ds(lane, LANES)]
            value = pairs_ref[m, :, pl.ds(lane + KEY_WIDTH, LANES)]
            for i, tile in enumerate(attention_pair(tiles, key, value, bias_ref[m])):
                attn_out[own, pl.ds(column + i * LANES, LANES)] = tile.astype(bf16)
            return carry

        lax.fori_loop(0, PAIRS, pair, 0)

    def project(m):
        own = slice(m * rows, (m + 1) * rows)
        middle = tokens_ref[own].astype(f32) + dot(attn_out[own], output_weight[...])
        middle_out[own] = middle
        scale = lax.rsqrt(jnp.mean(middle * middle, axis=-1, keepdims=True) + eps)
        rows_all[m, shard] = (middle * scale * gain_ref[...]).astype(bf16)

    def emits(m):
        pairs = (
            (rows_all.at[m], rows_out.at[m]),
            (results, results_out.at[m]),
            (row_grads, row_grads_out.at[m]),
            (active, active_out.at[m]),
            (gate, gate_out.at[m]),
            (up, up_out.at[m]),
        )
        return [pltpu.make_async_copy(a, b, emit_sem.at[m * len(pairs) + i]) for i, (a, b) in enumerate(pairs)]

    def expert_steps(m, between):
        inputs = rows_all.at[m]
        out_grads = grads_ref if m == 0 else grads_all
        steps = [(e, b) for e in range(held) for b in range(F // F_BLOCK)]
        for i, (e, b) in enumerate(steps):
            weights = combine_ref[:, m * rows : (m + 1) * rows, :].reshape(tokens, LANES)
            combine = jnp.sum(
                jnp.where(lane_index(weights.shape) == shard * held + e, weights, 0.0), axis=1, keepdims=True
            )
            columns = slice(b * F_BLOCK, (b + 1) * F_BLOCK)
            up_columns = slice(F + b * F_BLOCK, F + (b + 1) * F_BLOCK)
            a, g, u, result, row_grad = expert_block(
                inputs[...].reshape(tokens, MODEL_WIDTH),
                out_grads[...].reshape(tokens, MODEL_WIDTH),
                combine,
                expand[e, :, columns],
                expand[e, :, up_columns],
                shrink[e, columns, :],
            )
            spot = slice(e * F + b * F_BLOCK, e * F + (b + 1) * F_BLOCK)
            active[:, spot], gate[:, spot], up[:, spot] = a, g, u
            if i == 0:
                result_sum[...] = result
                grad_sum[...] = row_grad
            elif i < len(steps) - 1:
                result_sum[...] += result
                grad_sum[...] += row_grad
            else:
                shape = (SHARDS, rows, MODEL_WIDTH)
                results[...] = (result_sum[...] + result).astype(bf16).reshape(shape)
                row_grads[...] = (grad_sum[...] + row_grad).astype(bf16).reshape(shape)
            if i in between:
                between[i]()

    attend(0)
    grad_square.pass_on()
    loads[0].wait()
    project(0)
    row_squares[0].start()
    attend(1)
    row_squares[0].pass_on()
    project(1)
    row_squares[1].start()
    loads[1].wait()
    loads[2].wait()
    row_squares[0].finish()
    expert_steps(0, {1: row_squares[1].pass_on})
    for emit in emits(0):
        emit.start()
    row_squares[1].finish()
    grad_square.finish()
    grads_emit = pltpu.make_async_copy(grads_all, grads_out, load_sem.at[3])
    grads_emit.start()
    for emit in emits(0):
        emit.wait()
    expert_steps(1, {})
    for emit in emits(1):
        emit.start()
    grads_emit.wait()
    grad_square.drain()
    for square in row_squares:
        square.drain()
    for emit in emits(1):
        emit.wait()


def layer(query, pairs, bias, tokens, gain, grads, own_grad, combine, output_weight, expert_in, expert_out):
    held = expert_in.shape[0]
    rows = own_grad.shape[0]
    wide = SHARDS * rows
    dma = pltpu.SemaphoreType.DMA
    anywhere = pl.BlockSpec(memory_space=pl.ANY)
    vmem = pl.BlockSpec(memory_space=pltpu.VMEM)
    blocks = jax.ShapeDtypeStruct((MB, SHARDS, rows, MODEL_WIDTH), bf16)
    pieces = jax.ShapeDtypeStruct((MB, wide, held * F), bf16)
    block = pltpu.VMEM((SHARDS, rows, MODEL_WIDTH), bf16)
    total = pltpu.VMEM((wide, MODEL_WIDTH), f32)
    piece = pltpu.VMEM((wide, held * F), bf16)
    return pl.pallas_call(
        layer_kernel,
        in_specs=[vmem] * 8 + [anywhere] * 3,
        out_specs=[vmem] * 2 + [anywhere] * 7,
        out_shape=[
            jax.ShapeDtypeStruct(tokens.shape, bf16),
            jax.ShapeDtypeStruct(tokens.shape, f32),
            blocks,
            jax.ShapeDtypeStruct(blocks.shape[1:], bf16),
            blocks,
            blocks,
            pieces,
            pieces,
            pieces,
        ],
        scratch_shapes=[
            pltpu.VMEM(output_weight.shape, bf16),
            pltpu.VMEM(expert_in.shape, bf16),
            pltpu.VMEM(expert_out.shape, bf16),
            pltpu.VMEM((MB, SHARDS, rows, MODEL_WIDTH), bf16),
            block,
            total,
            total,
            block,
            block,
            piece,
            piece,
            piece,
            dma((4,)),
            dma((2, 2 + 2 * MB)),
            dma((2, 2 + 2 * MB)),
            dma((6 * MB,)),
        ],
        compiler_params=pltpu.CompilerParams(
            collective_id=2, has_side_effects=True, vmem_limit_bytes=VMEM_LIMIT
        ),
        name="layer",
    )(query, pairs, bias, tokens, gain, grads, own_grad, combine, output_weight, expert_in, expert_out)


PIECES = 4
DENSE_PIECES = 2
ADD_ROWS = 64


def add_into(out, *parts):
    rows = out.shape[0]
    size = max(d for d in range(16, ADD_ROWS + 1, 16) if rows % d == 0)

    def body(i, carry):
        place = pl.ds(pl.multiple_of(i * size, size), size)
        total = parts[0][place].astype(f32)
        for part in parts[1:]:
            total = total + part[place].astype(f32)
        out[place] = total.astype(out.dtype)
        return carry

    lax.fori_loop(0, rows // size, body, 0)


class Piece:
    def __init__(self, own, near, far, out, out_rows):
        self.own, self.near, self.far, self.out, self.out_rows = own, near, far, out, out_rows


def reduce_kernel(experts_n, dense_n, shards_n, *refs):
    count = experts_n + dense_n
    sources, outs = refs[:count], refs[count : 2 * count]
    refs = list(refs[2 * count :])
    take = lambda n: [refs.pop(0) for _ in range(n)]
    own, other = take(count), take(count)
    across, crossed = take(dense_n), take(dense_n)
    near, far = take(count), take(count)
    load_sem, core_sem, across_sem, near_sem, far_sem, back_sem, pass_sem, store_sem = refs

    place = Place()
    core, chip, shard = place.core, place.chip, place.shard
    partner = place.partner
    inner = (chip == 1) | (chip == 2)
    outer_device = place.chip_device(3 * (chip // 2))
    inner_device = place.chip_device(1 + chip // 2)
    facing_device = place.chip_device(3 - chip)
    send = remote

    greet(partner)
    for k in range(1, shards_n):
        greet(place.peer(k))

    @pl.when(inner)
    def _():
        greet(outer_device)
        greet(facing_device)

    @pl.when(jnp.logical_not(inner))
    def _():
        greet(inner_device)

    pl.semaphore_wait(pltpu.get_barrier_semaphore(), shards_n + jnp.where(inner, 2, 1))

    loads, trades = [], []
    pieces = []
    for a in range(count):
        if a < experts_n:
            rows = own[a].shape[0]
            size = rows // PIECES
            views = [
                (
                    sources[a].at[pl.ds(pl.multiple_of(core * rows, rows) + j * size, size)],
                    sources[a].at[pl.ds(pl.multiple_of((1 - core) * rows, rows) + j * size, size)],
                    slice(j * size, (j + 1) * size),
                )
                for j in range(PIECES)
            ]
        else:
            views = [(sources[a].at[:, core], sources[a].at[:, 1 - core], slice(0, shards_n))]
        for mine, rest, spot in views:
            i = len(loads)
            loads.append(pltpu.make_async_copy(mine, own[a].at[spot], load_sem.at[i]))
            trades.append(send(rest, other[a].at[spot], core_sem, i, partner))
        total = near[a].shape[0]
        parts = PIECES if a < experts_n else DENSE_PIECES
        size = total // parts
        for j in range(parts):
            spot = slice(j * size, (j + 1) * size)
            at = pl.multiple_of(core * total, total) + j * size
            start = own[a] if a < experts_n else crossed[a - experts_n]
            pieces.append(Piece(start.at[spot], near[a].at[spot], far[a].at[spot], outs[a], pl.ds(at, size)))
    expert_pieces = experts_n * PIECES
    order = list(range(2)) + list(range(expert_pieces, expert_pieces + dense_n)) + list(range(2, expert_pieces))
    for i in order:
        loads[i].start()
        trades[i].start()

    crossings = []

    def meet_expert(i):
        a, j = i // PIECES, i % PIECES
        size = own[a].shape[0] // PIECES
        spot = slice(j * size, (j + 1) * size)
        loads[i].wait()
        trades[i].wait_recv()
        add_into(own[a].at[spot], own[a].at[spot], other[a].at[spot])

    def meet_dense(d):
        a, i = experts_n + d, expert_pieces + d
        loads[i].wait()
        trades[i].wait_recv()
        for b in range(shards_n):
            add_into(own[a].at[b], own[a].at[b], other[a].at[b])
        for k in range(1, shards_n):
            index = d * (shards_n - 1) + k - 1
            copy = send(own[a].at[place.peer_index(k)], across[d].at[k - 1], across_sem, index, place.peer(k))
            copy.start()
            crossings.append(copy)

    def gather_dense(d):
        for k in range(1, shards_n):
            crossings[d * (shards_n - 1) + k - 1].wait_recv()
        arrived = [across[d].at[k - 1] for k in range(1, shards_n)]
        add_into(crossed[d], own[experts_n + d].at[shard], *arrived)

    number = len(pieces)
    inward = [send(p.own, p.near, near_sem, i, inner_device) for i, p in enumerate(pieces)]
    facing = [send(p.own, p.far, far_sem, i, facing_device) for i, p in enumerate(pieces)]
    outward = [send(p.near, p.out.at[p.out_rows], back_sem, i, outer_device) for i, p in enumerate(pieces)]
    passed_inner = [send(p.near, p.out.at[p.out_rows], pass_sem, i, partner) for i, p in enumerate(pieces)]
    passed_outer = [
        send(p.out.at[p.out_rows], p.out.at[p.out_rows], pass_sem, i, partner) for i, p in enumerate(pieces)
    ]
    stores = [
        pltpu.make_async_copy(p.near, p.out.at[p.out_rows], store_sem.at[i]) for i, p in enumerate(pieces)
    ]

    def ready(i):
        if i < expert_pieces:
            meet_expert(i)
            if 1 <= i <= dense_n:
                meet_dense(i - 1)
        elif (i - expert_pieces) % DENSE_PIECES == 0:
            gather_dense((i - expert_pieces) // DENSE_PIECES)

        @pl.when(jnp.logical_not(inner))
        def _():
            inward[i].start()

    def halfway(i):
        inward[i].wait_recv()
        add_into(pieces[i].own, pieces[i].own, pieces[i].near)
        facing[i].start()

    def finish(i):
        facing[i].wait_recv()
        add_into(pieces[i].near, pieces[i].own, pieces[i].far)
        outward[i].start()
        passed_inner[i].start()
        stores[i].start()

    def forward(i):
        outward[i].wait_recv()
        passed_outer[i].start()

    lag = 6
    for i in range(number + lag):
        if i < number:
            ready(i)

        @pl.when(inner)
        def _():
            if i < number:
                halfway(i)
            if 1 <= i <= number:
                finish(i - 1)

        @pl.when(jnp.logical_not(inner))
        def _():
            if i >= lag:
                forward(i - lag)

    for trade in trades:
        trade.wait_send()
    for crossing in crossings:
        crossing.wait_send()

    @pl.when(inner)
    def _():
        for i in range(number):
            facing[i].wait_send()
            outward[i].wait_send()
            stores[i].wait()
            passed_inner[i].wait_send()

    @pl.when(jnp.logical_not(inner))
    def _():
        for i in range(number):
            inward[i].wait_send()
            passed_outer[i].wait_send()

    for i in range(number):
        passed_outer[i].wait_recv()


def reduce_weights(expert_grads, dense_grads, shards_n):
    experts_n, dense_n = len(expert_grads), len(dense_grads)
    columns = [g.shape[1] for g in (*expert_grads, *dense_grads)]
    out_rows = [g.shape[0] for g in expert_grads] + [g.shape[0] // shards_n for g in dense_grads]
    halves = [pltpu.VMEM((g.shape[0] // 2, g.shape[1]), bf16) for g in expert_grads]
    dense_grads = [g.reshape(shards_n, 2, g.shape[0] // (2 * shards_n), g.shape[1]) for g in dense_grads]
    arrays = list(expert_grads) + dense_grads
    halves += [pltpu.VMEM((g.shape[0],) + g.shape[2:], bf16) for g in dense_grads]
    line = [pltpu.VMEM((r // 2, c), bf16) for r, c in zip(out_rows, columns)]
    across = [pltpu.VMEM((shards_n - 1,) + g.shape[2:], bf16) for g in dense_grads]
    first = experts_n * PIECES + dense_n
    number = experts_n * PIECES + dense_n * DENSE_PIECES
    dma = pltpu.SemaphoreType.DMA
    anywhere = pl.BlockSpec(memory_space=pl.ANY)
    return pl.pallas_call(
        functools.partial(reduce_kernel, experts_n, dense_n, shards_n),
        in_specs=[anywhere] * len(arrays),
        out_specs=[anywhere] * len(arrays),
        out_shape=[jax.ShapeDtypeStruct((r, c), bf16) for r, c in zip(out_rows, columns)],
        scratch_shapes=halves + halves + across + line[experts_n:] + line + line
        + [
            dma((first,)),
            dma((2, first)),
            dma((2, dense_n * (shards_n - 1))),
            dma((2, number)),
            dma((2, number)),
            dma((2, number)),
            dma((2, number)),
            dma((number,)),
        ],
        compiler_params=pltpu.CompilerParams(
            collective_id=0, has_side_effects=True, vmem_limit_bytes=VMEM_LIMIT
        ),
        name="reduce_weights",
    )(*arrays)


def shards(
    tokens,
    doc_starts,
    routes,
    gates,
    attn_gain,
    w_q,
    key_value_weight,
    w_o,
    moe_gain,
    expert_in,
    expert_out,
    cotangent,
):
    links = Links()
    rows = tokens.shape[2]
    length = rows * links.contexts
    held = expert_in.shape[0]
    chained = links.chips == LINE and links.shards == SHARDS and held == 2
    positions = links.context * rows + jnp.arange(rows, dtype=jnp.int32)
    cosine, sine = rotation_tables(positions)
    key_places = jnp.arange(length, dtype=jnp.int32)
    width = w_q.shape[0]
    flat_tokens = tokens.reshape(MB * rows, MODEL_WIDTH)
    flat_values = flat_tokens.astype(f32)
    scale_one = lax.rsqrt(jnp.mean(flat_values * flat_values, axis=-1, keepdims=True) + eps)
    unit_one = flat_values * scale_one

    expert_ids = jnp.arange(E, dtype=jnp.int32)
    chosen = (routes.reshape(MB, rows, TOP)[..., None] == expert_ids).astype(f32)
    combine = jnp.sum(gates.reshape(MB, rows, TOP)[..., None] * chosen, axis=2)

    if chained:
        packed = jnp.pad(jnp.stack([attn_gain, moe_gain]), ((0, GAIN_ROWS - 2), (0, 0)))
        spread = jnp.pad(combine.reshape(MB * rows, E), ((0, 0), (0, LANES - E)))
        projected = project_all(
            flat_tokens,
            cosine,
            sine,
            packed,
            spread,
            cotangent[0, 0],
            key_value_weight,
            w_q,
            w_o,
            length,
        )
        normed, query, gains, combine, grads, pair_weight, query_weight, output_weight, pairs = projected
        gains = gains.reshape(SHARDS, GAIN_ROWS, width).astype(f32)
        gain_one, gain_two = gains[:, 0].reshape(MODEL_WIDTH), gains[:, 1].reshape(MODEL_WIDTH)
    else:
        gather = lambda w: lax.all_gather(w, "fsdp", axis=0, tiled=True)
        pair_weight, query_weight, output_weight = gather(key_value_weight), gather(w_q), gather(w_o)
        gain_one, gain_two = gather(attn_gain).astype(f32), gather(moe_gain).astype(f32)
        normed = (unit_one * gain_one).astype(bf16)
        both = lambda table: jnp.concatenate([table] * MB)
        own_pairs = rotate_columns(dot(normed, pair_weight), both(cosine), both(sine), KEY_WIDTH)
        query = rotate_columns(dot(normed, query_weight), both(cosine), both(sine), MODEL_WIDTH)
        own_pairs = own_pairs.reshape(MB, rows, 2 * KEY_WIDTH)
        pairs = lax.all_gather(own_pairs, "ctx", axis=1, tiled=True)

        combine = jnp.concatenate([combine] + [links.across(combine, k) for k in range(1, links.shards)], axis=1)
        combine = lax.dynamic_slice_in_dim(combine, links.shard * held, held, 2)
        combine = combine.transpose(0, 2, 1)[..., None]

    biases, biases_turned = [], []
    for m in range(MB):
        starts = doc_starts[m, 0]
        begin = jnp.max(jnp.where(starts[None, :] <= positions[:, None], starts[None, :], 0), axis=1)
        seen = (key_places[None, :] <= positions[:, None]) & (key_places[None, :] >= begin[:, None])
        biases.append(jnp.where(seen, 0.0, -1e30).astype(f32))
        places, begins = jnp.tile(positions, GROUP), jnp.tile(begin, GROUP)
        seen = (key_places[:, None] <= places[None, :]) & (key_places[:, None] >= begins[None, :])
        biases_turned.append(jnp.where(seen, 0.0, -1e30).astype(f32))

    middles, attns, results, row_grads = [], [], [], []
    if chained:
        (
            attn_all,
            middle_all,
            row_blocks,
            grad_blocks,
            result_blocks,
            row_grad_blocks,
            active,
            gate,
            up,
        ) = layer(
            query,
            pairs,
            jnp.stack(biases),
            flat_tokens,
            gain_two[None],
            grads,
            cotangent[1, 0],
            combine,
            output_weight,
            expert_in,
            expert_out,
        )
        flat = lambda a: a.reshape(-1, a.shape[-1])
        expert_grads = expert_weights(
            flat(row_blocks),
            jnp.concatenate([flat(grads), flat(grad_blocks)], axis=0),
            flat(active),
            flat(gate),
            flat(up),
            held,
        )
        for m in range(MB):
            own = slice(m * rows, (m + 1) * rows)
            middles.append(middle_all[own])
            attns.append(attn_all[own])
            pick = lambda blocks, k: lax.dynamic_index_in_dim(blocks[m], links.shard ^ k, 0, keepdims=False)
            for blocks, sums in ((result_blocks, results), (row_grad_blocks, row_grads)):
                total = pick(blocks, 0).astype(f32)
                for k in range(1, links.shards):
                    total = total + links.across(pick(blocks, k), k).astype(f32)
                sums.append(total)
    else:
        rows_kept, grads_kept, pieces_kept = [], [], []
        for m in range(MB):
            own = slice(m * rows, (m + 1) * rows)
            attn = attention_forward(m, query, pairs, biases[m])
            middle = flat_tokens[own].astype(f32) + dot(attn, output_weight)
            scale_two = lax.rsqrt(jnp.mean(middle * middle, axis=-1, keepdims=True) + eps)
            moe_in = (middle * scale_two * gain_two).astype(bf16)
            out_grad = cotangent[m, 0]
            row_parts = [moe_in] + [links.across(moe_in, k) for k in range(1, links.shards)]
            grad_parts = [out_grad] + [links.across(out_grad, k) for k in range(1, links.shards)]
            result, row_grad, pieces = experts(row_parts, grad_parts, combine[m], expert_in, expert_out)
            for parts, sums in ((result, results), (row_grad, row_grads)):
                total = parts[0].astype(f32)
                for k in range(1, links.shards):
                    total = total + links.across(parts[k], k).astype(f32)
                sums.append(total)
            middles.append(middle)
            attns.append(attn)
            rows_kept += row_parts
            grads_kept += grad_parts
            pieces_kept.append(pieces)
        merge = lambda items: jnp.concatenate(items, axis=0)
        expert_grads = expert_weights(
            merge(rows_kept), merge(grads_kept), *[merge([p[i] for p in pieces_kept]) for i in range(3)], held
        )
    expert_grads = [g.reshape(-1, g.shape[-1]) for g in expert_grads]
    outputs = [(middles[m] + results[m]).astype(bf16) for m in range(MB)]

    input_grads, query_lows, pair_lows, middle_lows = [], [], [], []
    gain_one_grad, gain_two_grad = 0.0, 0.0
    for m in range(MB):
        own = slice(m * rows, (m + 1) * rows)
        scale_two = lax.rsqrt(jnp.mean(middles[m] * middles[m], axis=-1, keepdims=True) + eps)
        unit_two = middles[m] * scale_two
        moe_in_grad = row_grads[m]
        gain_two_grad = gain_two_grad + jnp.sum(moe_in_grad * unit_two, axis=0)
        weighted = moe_in_grad * gain_two
        inner = jnp.mean(weighted * unit_two, axis=-1, keepdims=True)
        middle_grad = cotangent[m, 0].astype(f32) + (weighted - unit_two * inner) * scale_two
        middle_low = middle_grad.astype(bf16)
        attn_grad = dot(middle_low, output_weight, NT).astype(bf16)
        query_low, pair_grad = attention_backward(
            m, query, cosine, sine, pairs, biases_turned[m], attn_grad
        )
        if chained:
            pair_grad = pair_grad.reshape(links.chips, 2, rows, 2 * KEY_WIDTH)
            core_part = lambda core: lax.dynamic_index_in_dim(pair_grad, core, 1, keepdims=False)
            part = core_part(links.core).astype(f32)
            part = (part + links.other_core(core_part(1 - links.core)).astype(f32)).astype(bf16)
            chip_part = lambda s: lax.dynamic_index_in_dim(
                part, (links.chip - s + links.chips) % links.chips, 0, keepdims=False
            )
            parts = [chip_part(0)]
            for s in range(1, links.chips):
                parts.append(links.shift(chip_part(s), -s))
        else:
            parts = [lax.psum_scatter(pair_grad, "ctx", scatter_dimension=0, tiled=True)]
        pair_low = pair_gradient(parts, cosine, sine)
        normed_grad = dot(query_low, query_weight, NT) + dot(pair_low, pair_weight, NT)
        gain_one_grad = gain_one_grad + jnp.sum(normed_grad * unit_one[own], axis=0)
        weighted = normed_grad * gain_one
        inner = jnp.mean(weighted * unit_one[own], axis=-1, keepdims=True)
        residual_grad = (weighted - unit_one[own] * inner) * scale_one[own]
        input_grads.append(middle_grad + residual_grad)
        query_lows.append(query_low)
        pair_lows.append(pair_low)
        middle_lows.append(middle_low)

    join = lambda items: jnp.concatenate(items, axis=0)

    output_grad = dot(join(attns), join(middle_lows), TN).astype(bf16)
    query_grad = dot(normed, join(query_lows), TN).astype(bf16)
    pair_weight_grad = dot(normed, join(pair_lows), TN).astype(bf16)
    gain_grads = jnp.stack([gain_one_grad, gain_two_grad], axis=1)
    gain_grads = jnp.pad(gain_grads, ((0, 0), (0, LANES - 2))).astype(bf16)
    dense_grads = [output_grad, query_grad, jnp.concatenate([pair_weight_grad, gain_grads], axis=1)]
    if chained:
        totals = reduce_weights(expert_grads, dense_grads, links.shards)
    else:
        totals = [lax.psum(g, "ctx") for g in expert_grads]
        for g in dense_grads:
            part = lax.psum_scatter(g, "fsdp", scatter_dimension=0, tiled=True)
            totals.append(lax.psum(part, "ctx"))
    gate_total, up_total, down_total, output_total, query_total, pair_total = [t.astype(f32) for t in totals]
    expand_total = jnp.concatenate([gate_total, up_total], axis=1)

    return (
        jnp.stack(outputs)[:, None],
        jnp.stack(input_grads)[:, None],
        pair_total[:, 2 * KEY_WIDTH],
        query_total,
        pair_total[:, : 2 * KEY_WIDTH],
        output_total,
        pair_total[:, 2 * KEY_WIDTH + 1],
        expand_total.reshape(held, MODEL_WIDTH, 2 * F),
        down_total.reshape(held, F, MODEL_WIDTH),
    )


def solution(mesh):
    return jax.shard_map(
        shards,
        mesh=mesh,
        in_specs=(
            P(None, "fsdp", "ctx", None),
            P(None, "fsdp", None),
            P(None, "fsdp", "ctx", None),
            P(None, "fsdp", "ctx", None),
            P("fsdp"),
            P("fsdp", None),
            P("fsdp", None),
            P("fsdp", None),
            P("fsdp"),
            P("fsdp", None, None),
            P("fsdp", None, None),
            P(None, "fsdp", "ctx", None),
        ),
        out_specs=(
            P(None, "fsdp", "ctx", None),
            P(None, "fsdp", "ctx", None),
            P("fsdp"),
            P("fsdp", None),
            P("fsdp", None),
            P("fsdp", None),
            P("fsdp"),
            P("fsdp", None, None),
            P("fsdp", None, None),
        ),
        check_vma=False,
    )
```

```python
import functools
import types

import jax
import jax.numpy as jnp
import numpy as np
from jax import lax
from jax.experimental import pallas as pl
from jax.experimental.pallas import tpu as pltpu
from jax.sharding import PartitionSpec as P

MODEL_WIDTH = 1536
QUERY_HEADS = 24
KEY_VALUE_HEADS = 8
HEAD_SIZE = 64
GROUP = QUERY_HEADS // KEY_VALUE_HEADS
KEY_WIDTH = KEY_VALUE_HEADS * HEAD_SIZE
F = 512
E = 8
TOP = 4
MB = 2
LANES = 128
PAIRS = KEY_WIDTH // LANES
PAIR_QUERY = 2 * GROUP * HEAD_SIZE
F_BLOCK = 256
VMEM_LIMIT = 60 * 1024 * 1024

eps = 1e-05
theta = 10000.0

NT = (((1,), (1,)), ((), ()))
TN = (((0,), (0,)), ((), ()))
bf16 = jnp.bfloat16
f32 = jnp.float32


def dot(left, right, dims=(((1,), (0,)), ((), ()))):
    return lax.dot_general(left, right, dims, preferred_element_type=f32)


def rotation_tables(positions):
    frequency = theta ** (-jnp.arange(0, HEAD_SIZE, 2, dtype=f32) / HEAD_SIZE)
    angles = positions.astype(f32)[:, None] * frequency[None, :]
    cosine, sine = jnp.cos(angles), jnp.sin(angles)
    repeat = LANES // HEAD_SIZE
    cosine = jnp.concatenate([cosine, cosine] * repeat, axis=1)
    sine = jnp.concatenate([-sine, sine] * repeat, axis=1)
    return cosine, sine


def rotation_constants(length):
    frequency = theta ** (-np.arange(0, HEAD_SIZE, 2, dtype=np.float64) / HEAD_SIZE)
    angles = np.arange(length, dtype=np.float64)[:, None] * frequency[None, :]
    cosine, sine = np.cos(angles), np.sin(angles)
    repeat = LANES // HEAD_SIZE
    cosine = np.concatenate([cosine, cosine] * repeat, axis=1)
    sine = np.concatenate([-sine, sine] * repeat, axis=1)
    return jnp.asarray(np.stack([cosine, sine]).astype(np.float32))


def visible_bias(starts, m, context, shape, query_axis):
    rows = shape[query_axis]
    narrow = (rows, 1) if query_axis == 0 else (1, rows)
    query = context * rows + lax.broadcasted_iota(jnp.int32, narrow, query_axis)
    begin = jnp.zeros(narrow, jnp.int32)
    for i in range(starts.shape[1]):
        begin = jnp.maximum(begin, jnp.where(query >= starts[m, i], starts[m, i], 0))
    key = lax.broadcasted_iota(jnp.int32, shape, 1 - query_axis)
    return jnp.where((key <= query) & (key >= begin), 0.0, -1e30).astype(f32)


def lane_index(shape):
    return lax.broadcasted_iota(jnp.int32, shape, 1)


def rotate(tile, cosine, sine):
    half = HEAD_SIZE // 2
    ahead = pltpu.roll(tile, LANES - half, 1)
    behind = pltpu.roll(tile, half, 1)
    first = lane_index(tile.shape) % HEAD_SIZE < half
    return tile * cosine + jnp.where(first, ahead, behind) * sine


def rotate_columns_kernel(rotated, values_ref, cosine_ref, sine_ref, out_ref):
    cosine, sine = cosine_ref[...], sine_ref[...]
    for i in range(values_ref.shape[1] // LANES):
        cols = slice(i * LANES, (i + 1) * LANES)
        tile = values_ref[:, cols]
        if i < rotated // LANES:
            tile = rotate(tile, cosine, sine)
        out_ref[:, cols] = tile.astype(bf16)


def rotate_columns(values, cosine, sine, rotated):
    return pl.pallas_call(
        functools.partial(rotate_columns_kernel, rotated),
        out_shape=jax.ShapeDtypeStruct(values.shape, bf16),
        compiler_params=pltpu.CompilerParams(vmem_limit_bytes=VMEM_LIMIT),
        name="rotate_columns",
    )(values, cosine, sine)


def pair_gradient_kernel(count, cosine_ref, sine_ref, *refs):
    out_ref = refs[-1]
    cosine, sine = cosine_ref[...], sine_ref[...]
    for i in range(2 * KEY_WIDTH // LANES):
        cols = slice(i * LANES, (i + 1) * LANES)
        total = refs[0][:, cols].astype(f32)
        for ref in refs[1:count]:
            total = total + ref[:, cols].astype(f32)
        if i < KEY_WIDTH // LANES:
            total = rotate(total, cosine, -sine)
        out_ref[:, cols] = total.astype(bf16)


def pair_gradient(parts, cosine, sine):
    return pl.pallas_call(
        functools.partial(pair_gradient_kernel, len(parts)),
        out_shape=jax.ShapeDtypeStruct(parts[0].shape, bf16),
        compiler_params=pltpu.CompilerParams(vmem_limit_bytes=VMEM_LIMIT),
        name="pair_gradient",
    )(cosine, sine, *parts)


def grouped(tiles, half):
    mine = lane_index(tiles[0].shape) // HEAD_SIZE == half
    rows = []
    for j in range(GROUP * half, GROUP * half + GROUP):
        tile = tiles[j // 2]
        if j % 2 != half:
            tile = pltpu.roll(tile, HEAD_SIZE, 1)
        rows.append(jnp.where(mine, tile, 0.0))
    return jnp.concatenate(rows, axis=0).astype(bf16)


def ungrouped(per_half, rows):
    heads = []
    for j in range(2 * GROUP):
        half, place = j // GROUP, j % GROUP
        tile = per_half[half][place * rows : (place + 1) * rows]
        if j % 2 != half:
            tile = pltpu.roll(tile, HEAD_SIZE, 1)
        heads.append(tile)
    low = lane_index(heads[0].shape) < HEAD_SIZE
    return [jnp.where(low, heads[2 * i], heads[2 * i + 1]) for i in range(GROUP)]


def query_tiles(query_ref):
    scale = 1.0 / HEAD_SIZE
    return [query_ref[:, i * LANES : (i + 1) * LANES].astype(f32) * scale for i in range(GROUP)]


def attention_pair(tiles, key, value, bias):
    rows = bias.shape[0]
    results = []
    for half in range(2):
        scores = dot(grouped(tiles, half), key, NT)
        scores = jnp.concatenate(
            [scores[g * rows : (g + 1) * rows] + bias for g in range(GROUP)], axis=0
        )
        peak = jnp.max(scores, axis=1, keepdims=True)
        weights = jnp.exp(scores - peak)
        total = jnp.sum(weights, axis=1, keepdims=True)
        results.append(dot(weights.astype(bf16), value) / total)
    return ungrouped(results, rows)


def attention_forward_kernel(query_ref, key_ref, value_ref, bias_ref, out_ref):
    tiles = attention_pair(query_tiles(query_ref), key_ref[...], value_ref[...], bias_ref[...])
    for i, tile in enumerate(tiles):
        out_ref[:, i * LANES : (i + 1) * LANES] = tile.astype(bf16)


def attention_forward(m, query, pairs, bias):
    rows, length = bias.shape
    return pl.pallas_call(
        attention_forward_kernel,
        grid=(PAIRS,),
        in_specs=[
            pl.BlockSpec((rows, PAIR_QUERY), lambda p: (m, p)),
            pl.BlockSpec((None, length, LANES), lambda p: (m, 0, p)),
            pl.BlockSpec((None, length, LANES), lambda p: (m, 0, p + PAIRS)),
            pl.BlockSpec((rows, length), lambda p: (0, 0)),
        ],
        out_specs=pl.BlockSpec((rows, PAIR_QUERY), lambda p: (0, p)),
        out_shape=jax.ShapeDtypeStruct((rows, MODEL_WIDTH), bf16),
        compiler_params=pltpu.CompilerParams(vmem_limit_bytes=VMEM_LIMIT),
        cost_estimate=pl.CostEstimate(
            flops=16 * rows * length * MODEL_WIDTH,
            bytes_accessed=4 * length * MODEL_WIDTH,
            transcendentals=rows * length * QUERY_HEADS,
        ),
        name="attention_forward",
    )(query, pairs, pairs, bias)


def attention_pair_gradient(tiles, grads, key, value, bias):
    rows = tiles[0].shape[0]
    key_grad, value_grad = None, None
    query_grads = []
    for half in range(2):
        query = grouped(tiles, half)
        grad = grouped(grads, half)
        scores = dot(key, query, NT) + bias
        weights = jnp.exp(scores - jnp.max(scores, axis=0, keepdims=True))
        prob = weights * (1.0 / jnp.sum(weights, axis=0, keepdims=True))
        prob_grad = dot(value, grad, NT)
        delta = jnp.sum(prob * prob_grad, axis=0, keepdims=True)
        score_grad = (prob * (prob_grad - delta)).astype(bf16)
        value_part = dot(prob.astype(bf16), grad)
        key_part = dot(score_grad, query)
        value_grad = value_part if half == 0 else value_grad + value_part
        key_grad = key_part if half == 0 else key_grad + key_part
        query_grads.append(dot(score_grad, key, TN))
    return ungrouped(query_grads, rows), key_grad, value_grad


def attention_backward_kernel(
    query_ref, cosine_ref, sine_ref, key_ref, value_ref, bias_ref, grad_ref, query_out, pair_out
):
    cosine, sine = cosine_ref[...], sine_ref[...]
    grads = [grad_ref[:, i * LANES : (i + 1) * LANES].astype(f32) for i in range(GROUP)]
    query_grads, key_grad, value_grad = attention_pair_gradient(
        query_tiles(query_ref), grads, key_ref[...], value_ref[...], bias_ref[...]
    )
    for i, tile in enumerate(query_grads):
        tile = rotate(tile * (1.0 / HEAD_SIZE), cosine, -sine)
        query_out[:, i * LANES : (i + 1) * LANES] = tile.astype(bf16)
    first = pl.multiple_of(pl.program_id(0) * LANES, LANES)
    pair_out[:, pl.ds(first, LANES)] = key_grad.astype(bf16)
    pair_out[:, pl.ds(first + KEY_WIDTH, LANES)] = value_grad.astype(bf16)


def attention_backward(m, query, cosine, sine, pairs, bias, grad):
    rows = cosine.shape[0]
    length = pairs.shape[1]
    whole = lambda shape: pl.BlockSpec(shape, lambda p: (0, 0))
    return pl.pallas_call(
        attention_backward_kernel,
        grid=(PAIRS,),
        in_specs=[
            pl.BlockSpec((rows, PAIR_QUERY), lambda p: (m, p)),
            whole((rows, LANES)),
            whole((rows, LANES)),
            pl.BlockSpec((None, length, LANES), lambda p: (m, 0, p)),
            pl.BlockSpec((None, length, LANES), lambda p: (m, 0, p + PAIRS)),
            whole(bias.shape),
            pl.BlockSpec((rows, PAIR_QUERY), lambda p: (0, p)),
        ],
        out_specs=[
            pl.BlockSpec((rows, PAIR_QUERY), lambda p: (0, p)),
            whole((length, 2 * KEY_WIDTH)),
        ],
        out_shape=[
            jax.ShapeDtypeStruct((rows, MODEL_WIDTH), bf16),
            jax.ShapeDtypeStruct((length, 2 * KEY_WIDTH), bf16),
        ],
        compiler_params=pltpu.CompilerParams(vmem_limit_bytes=VMEM_LIMIT),
        cost_estimate=pl.CostEstimate(
            flops=40 * rows * length * MODEL_WIDTH,
            bytes_accessed=8 * length * MODEL_WIDTH,
            transcendentals=rows * length * QUERY_HEADS,
        ),
        name="attention_backward",
    )(query, cosine, sine, pairs, pairs, bias, grad)


def expert_block(inputs, out_grad, combine, gate_weight, up_weight, down_weight):
    gate = dot(inputs, gate_weight)
    up = dot(inputs, up_weight)
    sigmoid = jax.nn.sigmoid(gate)
    silu = gate * sigmoid
    active = (silu * up * combine).astype(bf16)
    active_grad = dot(out_grad, down_weight, NT) * combine
    gate_grad = (active_grad * up * sigmoid * (1.0 + gate * (1.0 - sigmoid))).astype(bf16)
    up_grad = (active_grad * silu).astype(bf16)
    result = dot(active, down_weight)
    row_grad = dot(gate_grad, gate_weight, NT) + dot(up_grad, up_weight, NT)
    return active, gate_grad, up_grad, result, row_grad


def experts_kernel(parts, rows, steps, combine_ref, gate_ref, up_ref, down_ref, *refs):
    rows_in, grads_in = refs[:parts], refs[parts : 2 * parts]
    refs = refs[2 * parts :]
    results, row_grads = refs[:parts], refs[parts : 2 * parts]
    active_out, gate_out, up_out, rows_all, grads_all, result_sum, grad_sum = refs[2 * parts :]
    step = pl.program_id(0) * pl.num_programs(1) + pl.program_id(1)

    @pl.when(step == 0)
    def _():
        for k in range(parts):
            place = slice(k * rows, (k + 1) * rows)
            rows_all[place] = rows_in[k][...]
            grads_all[place] = grads_in[k][...]
        result_sum[...] = jnp.zeros_like(result_sum)
        grad_sum[...] = jnp.zeros_like(grad_sum)

    inputs, out_grad, combine = rows_all[...], grads_all[...], combine_ref[0]
    active, gate_grad, up_grad, result, row_grad = expert_block(
        inputs, out_grad, combine, gate_ref[0], up_ref[0], down_ref[0]
    )
    active_out[...] = active
    gate_out[...] = gate_grad
    up_out[...] = up_grad
    result_sum[...] += result
    grad_sum[...] += row_grad

    @pl.when(step == steps - 1)
    def _():
        for k in range(parts):
            place = slice(k * rows, (k + 1) * rows)
            results[k][...] = result_sum[place].astype(bf16)
            row_grads[k][...] = grad_sum[place].astype(bf16)


def experts(row_parts, grad_parts, combine, expert_in, expert_out):
    parts = len(row_parts)
    rows = row_parts[0].shape[0]
    held = expert_in.shape[0]
    tokens = parts * rows
    blocks = F // F_BLOCK
    whole = pl.BlockSpec((rows, MODEL_WIDTH), lambda e, b: (0, 0))
    piece = pl.BlockSpec((tokens, F_BLOCK), lambda e, b: (0, e * blocks + b))
    row_shape = jax.ShapeDtypeStruct((rows, MODEL_WIDTH), bf16)
    piece_shape = jax.ShapeDtypeStruct((tokens, held * F), bf16)
    out = pl.pallas_call(
        functools.partial(experts_kernel, parts, rows, held * blocks),
        grid=(held, blocks),
        in_specs=[
            pl.BlockSpec((1, tokens, 1), lambda e, b: (e, 0, 0)),
            pl.BlockSpec((1, MODEL_WIDTH, F_BLOCK), lambda e, b: (e, 0, b)),
            pl.BlockSpec((1, MODEL_WIDTH, F_BLOCK), lambda e, b: (e, 0, b + blocks)),
            pl.BlockSpec((1, F_BLOCK, MODEL_WIDTH), lambda e, b: (e, b, 0)),
        ]
        + [whole] * (2 * parts),
        out_specs=[whole] * (2 * parts) + [piece] * 3,
        out_shape=[row_shape] * (2 * parts) + [piece_shape] * 3,
        scratch_shapes=[
            pltpu.VMEM((tokens, MODEL_WIDTH), bf16),
            pltpu.VMEM((tokens, MODEL_WIDTH), bf16),
            pltpu.VMEM((tokens, MODEL_WIDTH), f32),
            pltpu.VMEM((tokens, MODEL_WIDTH), f32),
        ],
        compiler_params=pltpu.CompilerParams(vmem_limit_bytes=VMEM_LIMIT),
        cost_estimate=pl.CostEstimate(
            flops=12 * tokens * held * MODEL_WIDTH * F,
            bytes_accessed=6 * held * MODEL_WIDTH * F + 20 * tokens * MODEL_WIDTH,
            transcendentals=tokens * held * F,
        ),
        name="experts",
    )(combine, expert_in, expert_in, expert_out, *row_parts, *grad_parts)
    return out[:parts], out[parts : 2 * parts], out[2 * parts :]


def expert_weights_kernel(rows_ref, grads_ref, active_ref, gate_ref, up_ref, gate_out, up_out, down_out, turned):
    step = pl.program_id(0) * pl.num_programs(1) + pl.program_id(1)

    @pl.when(step == 0)
    def _():
        turned[...] = rows_ref[...].T

    gate_out[0] = dot(turned[...], gate_ref[...]).astype(bf16)
    up_out[0] = dot(turned[...], up_ref[...]).astype(bf16)
    down_out[0] = dot(active_ref[...], grads_ref[...], TN).astype(bf16)


def expert_weights(rows, grads, active, gate, up, held):
    tokens = rows.shape[0]
    blocks = F // F_BLOCK
    whole = pl.BlockSpec((tokens, MODEL_WIDTH), lambda e, b: (0, 0))
    piece = pl.BlockSpec((tokens, F_BLOCK), lambda e, b: (0, e * blocks + b))
    wide = pl.BlockSpec((1, MODEL_WIDTH, F_BLOCK), lambda e, b: (e, 0, b))
    return pl.pallas_call(
        expert_weights_kernel,
        grid=(held, blocks),
        in_specs=[whole] * 2 + [piece] * 3,
        out_specs=[wide, wide, pl.BlockSpec((1, F_BLOCK, MODEL_WIDTH), lambda e, b: (e, b, 0))],
        out_shape=[
            jax.ShapeDtypeStruct((held, MODEL_WIDTH, F), bf16),
            jax.ShapeDtypeStruct((held, MODEL_WIDTH, F), bf16),
            jax.ShapeDtypeStruct((held, F, MODEL_WIDTH), bf16),
        ],
        scratch_shapes=[pltpu.VMEM((MODEL_WIDTH, tokens), bf16)],
        compiler_params=pltpu.CompilerParams(vmem_limit_bytes=VMEM_LIMIT),
        cost_estimate=pl.CostEstimate(
            flops=6 * tokens * held * MODEL_WIDTH * F,
            bytes_accessed=6 * held * MODEL_WIDTH * F + 8 * tokens * MODEL_WIDTH,
            transcendentals=0,
        ),
        name="expert_weights",
    )(rows, grads, active, gate, up)


class Links:
    def __init__(self):
        self.shards = lax.axis_size("fsdp")
        self.contexts = lax.axis_size("ctx")
        self.chips = self.contexts // 2
        self.shard = lax.axis_index("fsdp")
        self.context = lax.axis_index("ctx")
        self.chip = self.context // 2
        self.core = self.context % 2

    def across(self, array, k):
        return lax.ppermute(array, "fsdp", [(i, i ^ k) for i in range(self.shards)])

    def other_core(self, array):
        return lax.ppermute(array, "ctx", [(i, i ^ 1) for i in range(self.contexts)])

    def shift(self, array, s):
        n = self.contexts
        return lax.ppermute(array, "ctx", [(i, (i + 2 * s) % n) for i in range(n)])


MESH = pl.DeviceIdType.MESH
LINE = 4


class Place:
    def __init__(self):
        self.shard, self.context = lax.axis_index("fsdp"), lax.axis_index("ctx")
        self.core, self.chip = self.context % 2, self.context // 2
        self.partner = {"ctx": 2 * self.chip + 1 - self.core}

    def peer_index(self, k):
        x, y = (self.shard % 2 + k % 2) % 2, (self.shard // 2 + k // 2) % 2
        return 2 * y + x

    def peer(self, k):
        return {"fsdp": self.peer_index(k)}

    def chip_device(self, chip):
        return {"ctx": 2 * chip + self.core}


def remote(source, target, sems, index, device):
    return pltpu.make_async_remote_copy(
        src_ref=source,
        dst_ref=target,
        send_sem=sems.at[0, index],
        recv_sem=sems.at[1, index],
        device_id=device,
        device_id_type=MESH,
    )


def greet(device):
    pl.semaphore_signal(pltpu.get_barrier_semaphore(), inc=1, device_id=device, device_id_type=MESH)


SHARDS = 4
GAIN_ROWS = 16


class Square:
    def __init__(self, place, blocks, direct_sem, relay_sem, base=0):
        half = blocks.shape[1] // 2
        own = blocks.at[place.shard]
        self.directs = [remote(own, own, direct_sem, base + k - 1, place.peer(k)) for k in (1, 2)]
        self.relays = []
        for k in (1, 2):
            spot = blocks.at[place.peer_index(k), (k - 1) * half : k * half]
            self.relays.append(remote(spot, spot, relay_sem, base + k - 1, place.peer(3 - k)))

    def start(self):
        for copy in self.directs:
            copy.start()

    def pass_on(self):
        for direct, relay in zip(self.directs, self.relays):
            direct.wait_recv()
            relay.start()

    def finish(self):
        for copy in self.relays:
            copy.wait_recv()

    def drain(self):
        for copy in self.directs + self.relays:
            copy.wait_send()


LAST = LINE - 1
WIDE = 4


def forward_kernel(
    tokens,
    routes,
    gates,
    gain_pair,
    cotangent,
    starts,
    tables,
    pair_src,
    query_src,
    output_src,
    expand_src,
    shrink_src,
    turned_normed,
    query,
    turned_attn,
    middle,
    gains,
    cosine,
    sine,
    pair_out,
    query_out,
    output_out,
    pairs,
    rows_out,
    grads_out,
    results_out,
    row_grads_out,
    active_out,
    gate_out,
    up_out,
    pair_weight,
    query_weight,
    output_weight,
    expand,
    shrink,
    own_pairs,
    normed,
    combine_in,
    combine_own,
    attn,
    bias,
    combine,
    rows_all,
    grads_all,
    result_sum,
    grad_sum,
    key_value,
    load_sem,
    table_sem,
    store_sem,
    expert_sem,
    gain_sem,
    combine_sem,
    direct_sem,
    relay_sem,
    pass_sem,
    right_sem,
    left_sem,
    core_sem,
    own_sem,
    square_direct_sem,
    square_relay_sem,
    key_sem,
    emit_sem,
):
    r = types.SimpleNamespace(**locals())
    place = Place()
    core, chip, shard = place.core, place.chip, place.shard
    local = pltpu.make_async_copy
    rows = r.cosine.shape[0]
    wide = SHARDS * rows
    held = r.pair_src.shape[0]
    half, quarter = held // 2, held // 4
    greet_line(place)
    length = r.bias.shape[2]

    def rows_of(owner, piece, size):
        return pl.ds(pl.multiple_of(owner * held + core * half, half) + piece, size)

    sources = (r.pair_src, r.query_src, r.output_src)
    weights = (r.pair_weight, r.query_weight, r.output_weight)
    weight_outs = (r.pair_out, r.query_out, r.output_out)
    loads, directs, relays, passes, stores = [], [], [], [], []
    for w in range(3):
        weight = weights[w]
        own_rows = pl.ds(pl.multiple_of(shard * held, held), held)
        loads.append(local(sources[w], weight.at[own_rows], r.load_sem.at[w]))
        stores.append(local(weight, weight_outs[w], r.store_sem.at[w]))
        mine = sources[w].at[pl.ds(pl.multiple_of(core * half, half), half)]
        spot = weight.at[rows_of(shard, 0, half)]
        directs.append([remote(mine, spot, r.direct_sem, 2 * w + k - 1, place.peer(k)) for k in (1, 2)])
        relay, onward = [], []
        for k in (1, 2):
            spot = weight.at[rows_of(place.peer_index(k), (k - 1) * quarter, quarter)]
            relay.append(remote(spot, spot, r.relay_sem, 2 * w + k - 1, place.peer(3 - k)))
            spot = weight.at[rows_of(place.peer_index(k), 0, half)]
            onward.append(remote(spot, spot, r.pass_sem, 4 * w + k - 1, place.partner))
        for k in (1, 2):
            spot = weight.at[rows_of(place.peer_index(3), (k - 1) * quarter, quarter)]
            onward.append(remote(spot, spot, r.pass_sem, 4 * w + k + 1, place.partner))
        relays.append(relay)
        passes.append(onward)

    def send_weight(w):
        for copy in directs[w]:
            copy.start()

    def relay_weight(w):
        for k in (1, 2):
            directs[w][k - 1].wait_recv()
            relays[w][k - 1].start()
        for k in (1, 2):
            passes[w][k - 1].start()

    def pass_weight(w):
        for k in (1, 2):
            relays[w][k - 1].wait_recv()
            passes[w][k + 1].start()

    def settle_weight(w):
        loads[w].wait()
        for copy in passes[w]:
            copy.wait_recv()
        stores[w].start()

    def sent_weight(w):
        for copy in directs[w] + relays[w] + passes[w]:
            copy.wait_send()
        stores[w].wait()

    send_weight(0)

    gain_rows = r.gains.at[pl.ds(pl.multiple_of(shard * GAIN_ROWS, GAIN_ROWS), GAIN_ROWS)]
    gain_rows[...] = jnp.concatenate([r.gain_pair[...], jnp.zeros((GAIN_ROWS - 2, held), bf16)], axis=0)
    expert_row = lax.broadcasted_iota(jnp.int32, (E, rows), 0)
    for m in range(MB):
        combine = jnp.zeros((E, rows), f32)
        for k in range(TOP):
            combine += jnp.where(expert_row == r.routes[m, k : k + 1], r.gates[m, k : k + 1], 0.0)
        r.combine_own[:, m * rows : (m + 1) * rows] = combine
    r.combine_in[shard] = r.combine_own[...]
    small_copies = []
    for k in range(1, SHARDS):
        small_copies.append(remote(gain_rows, gain_rows, r.gain_sem, k - 1, place.peer(k)))
        small_copies.append(remote(r.combine_own, r.combine_in.at[shard], r.combine_sem, k - 1, place.peer(k)))

    for copy in small_copies:
        copy.start()
    at = pl.ds(pl.multiple_of(place.context * rows, rows), rows)
    table_loads = [
        local(r.tables.at[i, at], table, r.table_sem.at[i]) for i, table in enumerate((r.cosine, r.sine))
    ]
    for load in table_loads + loads:
        load.start()
    expert_loads = [
        local(r.expand_src, r.expand, r.expert_sem.at[0]),
        local(r.shrink_src, r.shrink, r.expert_sem.at[1]),
    ]
    for load in expert_loads:
        load.start()
    for m in range(MB):
        r.grads_all[m, shard] = r.cotangent[m * rows : (m + 1) * rows]
    grad_squares = [Square(place, r.grads_all.at[m], r.square_direct_sem, r.square_relay_sem, 2 * m) for m in range(MB)]
    row_squares = [
        Square(place, r.rows_all.at[m], r.square_direct_sem, r.square_relay_sem, 2 * (MB + m)) for m in range(MB)
    ]

    def gain_times(values, row, write):
        for b in range(SHARDS):
            columns = slice(b * held, (b + 1) * held)
            at = b * GAIN_ROWS + row
            write(columns, (values[:, columns] * r.gains[at : at + 1].astype(f32)).astype(bf16))

    values = r.tokens[...].astype(f32)
    unit = values * lax.rsqrt(jnp.mean(values * values, axis=-1, keepdims=True) + eps)
    for copy in small_copies:
        copy.wait_recv()

    def write_normed(columns, value):
        r.normed[:, columns] = value

    gain_times(unit, 0, write_normed)
    r.turned_normed[...] = r.normed[...].T
    for b in range(SHARDS):
        spread = jnp.concatenate([r.combine_in[b], jnp.zeros((LANES - E, MB * rows), f32)], axis=0)
        r.combine[b] = spread.T
    for m in range(MB):
        r.bias[m] = visible_bias(r.starts, m, place.context, (rows, length), 0)
    for load in table_loads:
        load.wait()

    relay_weight(0)
    send_weight(1)
    pass_weight(0)
    settle_weight(0)
    cosine, sine = r.cosine[...], r.sine[...]

    def project(weight, column, rotated):
        result = dot(r.normed[...], weight[:, pl.ds(column, WIDE * LANES)])
        tiles = []
        for m in range(MB):
            for i in range(WIDE):
                tile = result[m * rows : (m + 1) * rows, i * LANES : (i + 1) * LANES]
                tiles.append((m, i, rotate(tile, cosine, sine) if rotated else tile))
        return tiles

    blocks = KEY_WIDTH // (WIDE * LANES)
    for b in range(2 * blocks):
        column = b * WIDE * LANES
        for m, i, tile in project(r.pair_weight, column, b < blocks):
            r.own_pairs[m, :, pl.ds(column + i * LANES, LANES)] = tile.astype(bf16)

    def chunk(m, owner):
        owner = jnp.clip(owner, 0, LAST)
        return r.pairs.at[m, pl.ds(pl.multiple_of((2 * owner + core) * rows, rows), rows)]

    def move(m, t, direction):
        target = chunk(m, chip - direction * (t - 1))
        source = r.own_pairs.at[m] if t == 1 else target
        sems = r.right_sem if direction > 0 else r.left_sem
        device = place.chip_device(jnp.clip(chip + direction, 0, LAST))
        return remote(source, target, sems, m * LAST + t - 1, device)

    def sends(t, direction):
        owner = chip - direction * (t - 1)
        if direction > 0:
            return (chip < LAST) & (owner >= 0)
        return (chip > 0) & (owner <= LAST)

    def gets(t, direction):
        owner = chip - direction * t
        return owner >= 0 if direction > 0 else owner <= LAST

    def came(m, t, direction):
        spot = chunk(m, chip - direction * t)
        sems = r.right_sem if direction > 0 else r.left_sem
        return remote(spot, spot, sems, m * LAST + t - 1, place.partner)

    def pass_chunk(m, t, direction):
        spot = chunk(m, chip - direction * t)
        index = (m * LINE + t) * 2 + (1 if direction > 0 else 0)
        return remote(spot, spot, r.core_sem, index, place.partner)

    def take_step(m, t):
        for direction in (1, -1):

            @pl.when(gets(t, direction))
            def _():
                came(m, t, direction).wait_recv()
                if t < LAST:

                    @pl.when(sends(t + 1, direction))
                    def _():
                        move(m, t + 1, direction).start()

                pass_chunk(m, t, direction).start()

    own_copies = []
    for m in range(MB):
        for direction in (1, -1):

            @pl.when(sends(1, direction))
            def _():
                move(m, 1, direction).start()

        own_copies.append(
            (
                local(r.own_pairs.at[m], chunk(m, chip), r.own_sem.at[m]),
                remote(r.own_pairs.at[m], chunk(m, chip), r.core_sem, m * LINE * 2, place.partner),
            )
        )
        for copy in own_copies[m]:
            copy.start()

    def settle_pairs(m):
        own_copies[m][0].wait()
        own_copies[m][1].wait()
        for t in range(1, LINE):
            for direction in (1, -1):

                @pl.when(gets(t, direction))
                def _():
                    pass_chunk(m, t, direction).wait()

    def query_block(b, carry):
        column = pl.multiple_of(b * WIDE * LANES, WIDE * LANES)
        for m, i, tile in project(r.query_weight, column, True):
            r.query[m * rows : (m + 1) * rows, pl.ds(column + i * LANES, LANES)] = tile.astype(bf16)
        return carry

    def key_load(m, p, slot, i):
        lane = pl.multiple_of(p * LANES, LANES) + i * KEY_WIDTH
        return local(r.pairs.at[m, :, pl.ds(lane, LANES)], r.key_value.at[slot, i], r.key_sem.at[slot, i])

    def attend(m):
        own = slice(m * rows, (m + 1) * rows)
        for i in range(2):
            key_load(m, 0, 0, i).start()

        def pair(p, carry):
            slot = p % 2
            for i in range(2):
                key_load(m, p, slot, i).wait()

            @pl.when(p + 1 < PAIRS)
            def _():
                for i in range(2):
                    key_load(m, p + 1, 1 - slot, i).start()

            column = pl.multiple_of(p * PAIR_QUERY, PAIR_QUERY)
            columns = [pl.ds(column + i * LANES, LANES) for i in range(GROUP)]
            tiles = [r.query[own, c].astype(f32) * (1.0 / HEAD_SIZE) for c in columns]
            results = attention_pair(tiles, r.key_value[slot, 0], r.key_value[slot, 1], r.bias[m])
            for c, tile in zip(columns, results):
                r.attn[own, c] = tile.astype(bf16)
            return carry

        lax.fori_loop(0, PAIRS, pair, 0)
        r.turned_attn[:, own] = r.attn[own].T

    def finish_attention(m):
        own = slice(m * rows, (m + 1) * rows)
        middle = r.tokens[own].astype(f32) + dot(r.attn[own], r.output_weight[...])
        r.middle[own] = middle
        unit = middle * lax.rsqrt(jnp.mean(middle * middle, axis=-1, keepdims=True) + eps)

        def write(columns, value):
            r.rows_all[m, shard, :, columns] = value

        gain_times(unit, 1, write)

    active, gate, up = [r.pair_weight.at[i * wide : (i + 1) * wide] for i in range(3)]
    results, row_grads = [r.query_weight.at[i * wide : (i + 1) * wide] for i in range(2)]

    def emits(m):
        pairs = (
            (r.rows_all.at[m], r.rows_out.at[m]),
            (r.grads_all.at[m], r.grads_out.at[m]),
            (results, r.results_out.at[m]),
            (row_grads, r.row_grads_out.at[m]),
            (active, r.active_out.at[m]),
            (gate, r.gate_out.at[m]),
            (up, r.up_out.at[m]),
        )
        return [local(a, b, r.emit_sem.at[m * len(pairs) + i]) for i, (a, b) in enumerate(pairs)]

    def expert_steps(m, between):
        steps = [(e, b) for e in range(r.expand.shape[0]) for b in range(F // F_BLOCK)]
        for i, (e, b) in enumerate(steps):
            weight = r.combine[:, m * rows : (m + 1) * rows, :].reshape(wide, LANES)
            expert = shard * r.expand.shape[0] + e
            chosen = jnp.where(lane_index(weight.shape) == expert, weight, 0.0)
            columns = slice(b * F_BLOCK, (b + 1) * F_BLOCK)
            up_columns = slice(F + b * F_BLOCK, F + (b + 1) * F_BLOCK)
            a, g, u, result, row_grad = expert_block(
                r.rows_all[m].reshape(wide, MODEL_WIDTH),
                r.grads_all[m].reshape(wide, MODEL_WIDTH),
                jnp.sum(chosen, axis=1, keepdims=True),
                r.expand[e, :, columns],
                r.expand[e, :, up_columns],
                r.shrink[e, columns, :],
            )
            spot = slice(e * F + b * F_BLOCK, e * F + (b + 1) * F_BLOCK)
            active[:, spot], gate[:, spot], up[:, spot] = a, g, u
            if i == 0:
                r.result_sum[...] = result
                r.grad_sum[...] = row_grad
            elif i < len(steps) - 1:
                r.result_sum[...] += result
                r.grad_sum[...] += row_grad
            else:
                results[...] = (r.result_sum[...] + result).astype(bf16)
                row_grads[...] = (r.grad_sum[...] + row_grad).astype(bf16)
            if i in between:
                between[i]()

    relay_weight(1)
    send_weight(2)
    take_step(0, 1)
    take_step(1, 1)
    pass_weight(1)
    take_step(0, 2)
    settle_weight(1)
    lax.fori_loop(0, MODEL_WIDTH // (WIDE * LANES), query_block, 0)
    relay_weight(2)
    grad_squares[0].start()
    take_step(1, 2)
    take_step(0, 3)
    settle_pairs(0)
    attend(0)
    pass_weight(2)
    grad_squares[0].pass_on()
    take_step(1, 3)
    settle_weight(2)
    finish_attention(0)
    row_squares[0].start()
    settle_pairs(1)
    attend(1)
    row_squares[0].pass_on()
    finish_attention(1)
    row_squares[1].start()
    grad_squares[1].start()
    for load in expert_loads:
        load.wait()
    sent_weight(0)
    sent_weight(1)
    grad_squares[0].finish()
    row_squares[0].finish()
    expert_steps(0, {1: row_squares[1].pass_on})
    for emit in emits(0):
        emit.start()
    grad_squares[1].pass_on()
    row_squares[1].finish()
    for emit in emits(0):
        emit.wait()
    grad_squares[1].finish()
    expert_steps(1, {})
    for emit in emits(1):
        emit.start()

    for copy in small_copies:
        copy.wait_send()
    sent_weight(2)
    for m in range(MB):
        for t in range(1, LINE):
            for direction in (1, -1):

                @pl.when(sends(t, direction))
                def _():
                    move(m, t, direction).wait_send()

    for square in grad_squares + row_squares:
        square.drain()
    for emit in emits(1):
        emit.wait()


def forward(tokens, routes, gates, gain_pair, cotangent, starts, tables, weights, expert_in, expert_out):
    rows = tokens.shape[0] // MB
    length = tables.shape[1]
    wide = SHARDS * rows
    held = weights[0].shape[0]
    dma = pltpu.SemaphoreType.DMA
    anywhere = pl.BlockSpec(memory_space=pl.ANY)
    vmem = pl.BlockSpec(memory_space=pltpu.VMEM)
    shape = jax.ShapeDtypeStruct
    low = lambda *s: pltpu.VMEM(s, bf16)
    full = [(SHARDS * held, w.shape[1]) for w in weights]
    blocks = (MB, SHARDS, rows, MODEL_WIDTH)
    return pl.pallas_call(
        forward_kernel,
        in_specs=[vmem] * 5 + [pl.BlockSpec(memory_space=pltpu.SMEM)] + [anywhere] * 6,
        out_specs=[vmem] * 7 + [anywhere] * 11,
        out_shape=[
            shape(tokens.shape[::-1], bf16),
            shape(tokens.shape, bf16),
            shape(tokens.shape[::-1], bf16),
            shape(tokens.shape, f32),
            shape((SHARDS * GAIN_ROWS, held), bf16),
            shape((rows, LANES), f32),
            shape((rows, LANES), f32),
        ]
        + [shape(f, bf16) for f in full]
        + [
            shape((MB, length, 2 * KEY_WIDTH), bf16),
            shape(blocks, bf16),
            shape(blocks, bf16),
            shape((MB, wide, MODEL_WIDTH), bf16),
            shape((MB, wide, MODEL_WIDTH), bf16),
        ]
        + [shape((MB, wide, 2 * F), bf16)] * 3,
        scratch_shapes=[low(*f) for f in full]
        + [
            low(*expert_in.shape),
            low(*expert_out.shape),
            low(MB, rows, 2 * KEY_WIDTH),
            low(*tokens.shape),
            pltpu.VMEM((SHARDS, E, MB * rows), f32),
            pltpu.VMEM((E, MB * rows), f32),
            low(*tokens.shape),
            pltpu.VMEM((MB, rows, length), f32),
            pltpu.VMEM((SHARDS, MB * rows, LANES), f32),
            low(*blocks),
            low(*blocks),
            pltpu.VMEM((wide, MODEL_WIDTH), f32),
            pltpu.VMEM((wide, MODEL_WIDTH), f32),
            low(2, 2, length, LANES),
            dma((3,)),
            dma((2,)),
            dma((3,)),
            dma((2,)),
            dma((2, SHARDS - 1)),
            dma((2, SHARDS - 1)),
            dma((2, 6)),
            dma((2, 6)),
            dma((2, 12)),
            dma((2, MB * LAST)),
            dma((2, MB * LAST)),
            dma((2, 2 * MB * LINE)),
            dma((MB,)),
            dma((2, 4 * MB)),
            dma((2, 4 * MB)),
            dma((2, 2)),
            dma((7 * MB,)),
        ],
        compiler_params=pltpu.CompilerParams(
            collective_id=1, has_side_effects=True, vmem_limit_bytes=VMEM_LIMIT
        ),
        name="forward",
    )(tokens, routes, gates, gain_pair, cotangent, starts, tables, *weights, expert_in, expert_out)


ADD_ROWS = 64


def add_into(out, *parts):
    rows = out.shape[0]
    size = max(d for d in range(16, ADD_ROWS + 1, 16) if rows % d == 0)

    def body(i, carry):
        spot = pl.ds(pl.multiple_of(i * size, size), size)
        total = parts[0][spot].astype(f32)
        for part in parts[1:]:
            total = total + part[spot].astype(f32)
        out[spot] = total.astype(out.dtype)
        return carry

    lax.fori_loop(0, rows // size, body, 0)


def greet_line(place):
    has_left, has_right = place.chip > 0, place.chip < LINE - 1
    greet(place.partner)
    for k in range(1, SHARDS):
        greet(place.peer(k))

    @pl.when(has_left)
    def _():
        greet(place.chip_device(place.chip - 1))

    @pl.when(has_right)
    def _():
        greet(place.chip_device(place.chip + 1))

    neighbours = jnp.where(has_left, 1, 0) + jnp.where(has_right, 1, 0)
    pl.semaphore_wait(pltpu.get_barrier_semaphore(), SHARDS + neighbours)


class Line:
    def __init__(self, place, pieces, sems):
        near_sem, far_sem, back_sem, pass_sem, store_sem = sems
        chip = place.chip
        self.inner = (chip == 1) | (chip == 2)
        outer = place.chip_device(3 * (chip // 2))
        inner = place.chip_device(1 + chip // 2)
        facing = place.chip_device(3 - chip)
        self.pieces = pieces
        numbered = list(enumerate(pieces))
        self.inward = [remote(p[0], p[1], near_sem, i, inner) for i, p in numbered]
        self.facing = [remote(p[0], p[2], far_sem, i, facing) for i, p in numbered]
        self.outward = [remote(p[1], p[3], back_sem, i, outer) for i, p in numbered]
        self.pass_inner = [remote(p[1], p[3], pass_sem, i, place.partner) for i, p in numbered]
        self.pass_outer = [remote(p[3], p[3], pass_sem, i, place.partner) for i, p in numbered]
        self.stores = [pltpu.make_async_copy(p[1], p[3], store_sem.at[i]) for i, p in numbered]

    def ready(self, *items):
        @pl.when(jnp.logical_not(self.inner))
        def _():
            for i in items:
                self.inward[i].start()

    def serve(self, halfway=(), finish=(), forward=()):
        @pl.when(self.inner)
        def _():
            for i in halfway:
                self.inward[i].wait_recv()
                own, near = self.pieces[i][:2]
                add_into(own, own, near)
                self.facing[i].start()
            for i in finish:
                self.facing[i].wait_recv()
                own, near, far = self.pieces[i][:3]
                add_into(near, own, far)
                self.outward[i].start()
                self.pass_inner[i].start()
                self.stores[i].start()

        @pl.when(jnp.logical_not(self.inner))
        def _():
            for i in forward:
                self.outward[i].wait_recv()
                self.pass_outer[i].start()

    def drain(self):
        @pl.when(self.inner)
        def _():
            for i in range(len(self.pieces)):
                self.facing[i].wait_send()
                self.outward[i].wait_send()
                self.pass_inner[i].wait_send()
                self.stores[i].wait()

        @pl.when(jnp.logical_not(self.inner))
        def _():
            for i in range(len(self.pieces)):
                self.inward[i].wait_send()
                self.pass_outer[i].wait_send()

        for copy in self.pass_outer:
            copy.wait_recv()


def line_sems(number):
    dma = pltpu.SemaphoreType.DMA
    return [dma((2, number))] * 4 + [dma((number,))]


def split_rows(ref, parts):
    size = ref.shape[0] // parts
    return [ref.at[j * size : (j + 1) * size] for j in range(parts)]


def out_halves(place, ref, parts):
    half = ref.shape[0] // 2
    size = half // parts
    first = pl.multiple_of(place.core * half, half)
    return [ref.at[pl.ds(first + j * size, size)] for j in range(parts)]


def line_pieces(place, own, near, far, out, parts):
    return list(
        zip(split_rows(own, parts), split_rows(near, parts), split_rows(far, parts), out_halves(place, out, parts))
    )


class PairSum:
    def __init__(self, place, own, sources, others, lands, core_sem, left_sem):
        self.place, self.own, self.others, self.lands, self.left_sem = place, own, others, lands, left_sem
        self.trades = [remote(sources(j), others.at[j], core_sem, j, place.partner) for j in range(LINE)]
        self.past = LAST - place.chip

    def trade(self):
        for copy in self.trades:
            copy.start()

    def move(self, t):
        owner = jnp.clip(self.place.chip - (LINE - t), 0, LAST)
        device = self.place.chip_device(jnp.clip(self.place.chip - 1, 0, LAST))
        return remote(self.own(owner), self.lands.at[t - 1], self.left_sem, t - 1, device)

    def meet(self):
        for j in range(LINE):
            self.trades[j].wait_recv()
            add_into(self.own(j), self.own(j), self.others.at[j])

        @pl.when(self.past == 0)
        def _():
            for t in range(1, LINE):
                self.move(t).start()

    def take(self, t):
        self.move(t).wait_recv()
        owner = jnp.clip(self.place.chip - (LAST - t), 0, LAST)
        add_into(self.own(owner), self.own(owner), self.lands.at[t - 1])

    def step(self, t):
        @pl.when((self.past >= 1) & (self.past <= min(t - 1, LINE - 2)))
        def _():
            self.take(t - 1)
            self.move(t).start()

    def finish(self, out, cosine, sine):
        @pl.when(self.past >= 1)
        def _():
            self.take(LAST)

        mine = self.own(self.place.chip)
        for i in range(2 * KEY_WIDTH // LANES):
            columns = slice(i * LANES, (i + 1) * LANES)
            tile = mine[:, columns]
            if i < KEY_WIDTH // LANES:
                tile = rotate(tile.astype(f32), cosine[...], -sine[...]).astype(bf16)
            out[:, columns] = tile

    def drain(self):
        for copy in self.trades:
            copy.wait_send()
        for t in range(1, LINE):

            @pl.when((self.past <= t - 1) & (self.past <= LINE - 2))
            def _():
                self.move(t).wait_send()


PARTS = 4


def backward_kernel(
    query,
    starts,
    cosine,
    sine,
    middle,
    cotangent,
    gain,
    pairs,
    rows_src,
    grads_src,
    active_src,
    gate_src,
    up_src,
    results_src,
    row_grads_src,
    output_src,
    query_low,
    pair_low,
    middle_low,
    middle_grad,
    gain_grad,
    block_output,
    gate_total,
    up_total,
    gate_rest,
    up_rest,
    down_rest,
    pair_grad,
    rows,
    turned,
    grads,
    pool,
    send_gate,
    send_up,
    send_down,
    own_gate,
    own_up,
    own_down,
    other_gate,
    other_up,
    other_down,
    near_gate,
    near_up,
    far_gate,
    far_up,
    row_grad_own,
    row_grad_in,
    result_own,
    result_in,
    attn_grad,
    key_value,
    bias,
    pair_other,
    land_left,
    load_sem,
    weight_sem,
    trade_sem,
    rest_sem,
    row_sem,
    result_sem,
    key_sem,
    core_sem,
    left_sem,
    near_sem,
    far_sem,
    back_sem,
    pass_sem,
    store_sem,
):
    r = types.SimpleNamespace(**locals())
    place = Place()
    core, chip, shard = place.core, place.chip, place.shard
    rows = r.cosine.shape[0]
    tokens = MB * SHARDS * rows
    side = MODEL_WIDTH // 2
    local = pltpu.make_async_copy

    wide = SHARDS * rows
    loads = []

    def load(source, target):
        loads.append(local(source, target, r.load_sem.at[len(loads)]))
        loads[-1].start()
        return loads[-1]

    flat = lambda ref, m: [(ref.at[m, k], m * wide + k * rows) for k in range(SHARDS)]
    row_loads, grad_loads, piece_loads = [], [], []
    for m in range(MB):
        for source, at in flat(r.rows_src, m):
            row_loads.append(load(source, r.rows.at[at : at + rows]))
        for source, at in flat(r.grads_src, m):
            grad_loads.append(load(source, r.grads.at[at : at + rows]))
    for i, ref in enumerate((r.active_src, r.gate_src, r.up_src)):
        for m in range(MB):
            at = i * tokens + m * wide
            piece_loads.append(load(ref.at[m], r.pool.at[at : at + wide]))
    own_loads = [load(r.row_grads_src.at[m, shard], r.row_grad_own.at[m]) for m in range(MB)]
    own_loads.append(load(r.results_src.at[0, shard], r.result_own))

    greet_line(place)

    row_copies, result_copies = [], []
    for m in range(MB):
        for k in range(1, SHARDS):
            i = m * (SHARDS - 1) + k - 1
            at = place.peer_index(k)
            row_copies.append(
                remote(r.row_grads_src.at[m, at], r.row_grad_in.at[m, k - 1], r.row_sem, i, place.peer(k))
            )
            if m == 0:
                result_copies.append(
                    remote(r.results_src.at[m, at], r.result_in.at[k - 1], r.result_sem, i, place.peer(k))
                )
    for copy in row_copies:
        copy.start()

    for m in range(MB):
        r.bias[m] = visible_bias(r.starts, m, place.context, r.bias.shape[1:], 1)

    for copy in row_loads:
        copy.wait()
    r.turned[...] = r.rows[...].T
    sends = (r.send_gate, r.send_up, r.send_down)
    owns = (r.own_gate, r.own_up, r.own_down)
    others = (r.other_gate, r.other_up, r.other_down)
    trades = [
        [remote(sends[i], others[i].at[b], r.trade_sem, b * 3 + i, place.partner) for i in range(3)]
        for b in range(2)
    ]

    def weight_block(b, expert, outs):
        column = pl.ds(pl.multiple_of(expert * F + b * F_BLOCK, F_BLOCK), F_BLOCK)
        for i in range(2):
            outs[i][...] = dot(r.turned[...], r.pool[(i + 1) * tokens : (i + 2) * tokens, column]).astype(bf16)

    def down_block(b, expert, out):
        column = pl.ds(pl.multiple_of(expert * F + b * F_BLOCK, F_BLOCK), F_BLOCK)
        out[...] = dot(r.pool[0:tokens, column], r.grads[...], TN).astype(bf16)

    def meet(b, i):
        trades[b][i].wait_recv()
        add_into(owns[i].at[b], owns[i].at[b], others[i].at[b])

    pieces = []
    for own, near, far, out in (
        (r.own_gate.at[0], r.near_gate, r.far_gate, r.gate_total),
        (r.own_up.at[0], r.near_up, r.far_up, r.up_total),
    ):
        pieces += line_pieces(place, own, near, far, out, PARTS)
    line = Line(place, pieces, (r.near_sem, r.far_sem, r.back_sem, r.pass_sem, r.store_sem))

    for copy in piece_loads[MB:]:
        copy.wait()
    for b in range(2):
        if b == 1:
            for i in range(2):
                trades[0][i].wait_send()
        weight_block(b, 1 - core, sends)
        for i in range(2):
            trades[b][i].start()
        weight_block(b, core, [own.at[b] for own in owns[:2]])
        if b == 0:
            for i in range(2):
                meet(0, i)
                line.ready(*range(i * PARTS, (i + 1) * PARTS))
            for copy in piece_loads[:MB] + grad_loads:
                copy.wait()
        else:
            trades[0][2].wait_send()
        down_block(b, 1 - core, sends[2])
        trades[b][2].start()
        down_block(b, core, owns[2].at[b])
        if b == 0:
            meet(0, 2)

    weight_loads = []
    for i in range(2):
        source = r.output_src.at[:, i * side : (i + 1) * side]
        target = r.pool.at[i * MODEL_WIDTH : (i + 1) * MODEL_WIDTH, 0:side]
        weight_loads.append(local(source, target, r.weight_sem.at[i]))
        weight_loads[-1].start()
    for copy in result_copies:
        copy.start()
    for i in range(3):
        meet(1, i)
    rests = [
        local(r.own_gate.at[1], r.gate_rest, r.rest_sem.at[0]),
        local(r.own_up.at[1], r.up_rest, r.rest_sem.at[1]),
        local(r.own_down, r.down_rest, r.rest_sem.at[2]),
    ]
    for copy in rests:
        copy.start()

    r.gain_grad[...] = jnp.zeros_like(r.gain_grad)

    def prepare(m):
        own = slice(m * rows, (m + 1) * rows)
        own_loads[m].wait()
        moe_in_grad = r.row_grad_own[m].astype(f32)
        for k in range(1, SHARDS):
            row_copies[m * (SHARDS - 1) + k - 1].wait_recv()
            moe_in_grad = moe_in_grad + r.row_grad_in[m, k - 1].astype(f32)
        middle = r.middle[own]
        scale = lax.rsqrt(jnp.mean(middle * middle, axis=-1, keepdims=True) + eps)
        unit = middle * scale
        r.gain_grad[m : m + 1] = jnp.sum(moe_in_grad * unit, axis=0, keepdims=True)
        weighted = moe_in_grad * r.gain[...]
        inner = jnp.mean(weighted * unit, axis=-1, keepdims=True)
        middle_grad = r.cotangent[own].astype(f32) + (weighted - unit * inner) * scale
        r.middle_grad[own] = middle_grad
        r.middle_low[own] = middle_grad.astype(bf16)
        if m == 0:
            for copy in weight_loads:
                copy.wait()
        total = dot(r.middle_low[own, 0:side], r.pool[0:MODEL_WIDTH, 0:side], NT)
        total = total + dot(r.middle_low[own, side:], r.pool[MODEL_WIDTH : 2 * MODEL_WIDTH, 0:side], NT)
        r.attn_grad[m] = total.astype(bf16)

    def key_load(step, slot, i):
        m, p = step // PAIRS, step % PAIRS
        lane = pl.multiple_of(p * LANES, LANES) + i * KEY_WIDTH
        return local(r.pairs.at[m, :, pl.ds(lane, LANES)], r.key_value.at[slot, i], r.key_sem.at[slot, i])

    pair_grads = (r.rows.at[:, 0 : 2 * KEY_WIDTH], r.grads.at[:, 0 : 2 * KEY_WIDTH])

    def chunk(of_chip, of_core):
        return pair_grads[0].at[pl.ds(pl.multiple_of((2 * of_chip + of_core) * rows, rows), rows)]

    pair_sum = PairSum(
        place,
        lambda j: chunk(j, core),
        lambda j: chunk(j, 1 - core),
        r.pair_other,
        r.land_left,
        r.core_sem,
        r.left_sem,
    )

    def pair_step(step, carry):
        m, p = step // PAIRS, step % PAIRS
        slot = step % 2
        for i in range(2):
            key_load(step, slot, i).wait()

        @pl.when(step + 1 < MB * PAIRS)
        def _():
            for i in range(2):
                key_load(step + 1, 1 - slot, i).start()

        at = pl.multiple_of(m * rows, rows)
        column = pl.multiple_of(p * PAIR_QUERY, PAIR_QUERY)
        lane = pl.multiple_of(p * LANES, LANES)
        columns = [pl.ds(column + i * LANES, LANES) for i in range(GROUP)]
        scale = 1.0 / HEAD_SIZE
        tiles = [r.query[pl.ds(at, rows), c].astype(f32) * scale for c in columns]
        grads = [r.attn_grad[m, :, c].astype(f32) for c in columns]
        bias = jnp.concatenate([r.bias[m]] * GROUP, axis=1)
        query_grads, key_grad, value_grad = attention_pair_gradient(
            tiles, grads, r.key_value[slot, 0], r.key_value[slot, 1], bias
        )
        for c, tile in zip(columns, query_grads):
            tile = rotate(tile * scale, r.cosine[...], -r.sine[...])
            r.query_low[pl.ds(at, rows), c] = tile.astype(bf16)
        key_low, value_low = key_grad.astype(bf16), value_grad.astype(bf16)
        for micro in range(MB):

            @pl.when(m == micro)
            def _():
                pair_grads[micro][:, pl.ds(lane, LANES)] = key_low
                pair_grads[micro][:, pl.ds(lane + KEY_WIDTH, LANES)] = value_low

        for at_step, actions in SERVICE:

            @pl.when(step == at_step)
            def _():
                for action in actions:
                    action()

        return carry

    serve = line.serve
    SERVICE = (
        (0, (lambda: serve([3], [0]),)),
        (1, (lambda: serve([], [1]),)),
        (2, (lambda: serve([4], [2, 3]),)),
        (3, (pair_sum.trade, lambda: prepare(1), lambda: serve([5, 6], [4], [0, 1]), pair_sum.meet)),
        (4, (lambda: serve([7], [], [2]),)),
        (5, (lambda: pair_sum.step(2), lambda: serve([], [5, 6], [3]))),
        (6, (lambda: serve([], [7], [4]),)),
        (7, (lambda: pair_sum.step(3), lambda: serve([], [], [5]))),
    )
    for i in range(2):
        key_load(0, 0, i).start()
    serve([0])
    prepare(0)
    serve([1, 2])
    lax.fori_loop(0, MB * PAIRS, pair_step, 0)
    second = local(pair_grads[1], r.pair_grad, r.rest_sem.at[3])
    second.start()
    own_loads[MB].wait()
    total = r.middle[0:rows] + r.result_own[...].astype(f32)
    for k in range(1, SHARDS):
        result_copies[k - 1].wait_recv()
        total = total + r.result_in[k - 1].astype(f32)
    r.block_output[...] = total.astype(bf16)
    serve([], [], [6])
    pair_sum.finish(r.pair_low, r.cosine, r.sine)
    serve([], [], [7])
    second.wait()

    for copy in trades[1]:
        copy.wait_send()
    for copy in rests:
        copy.wait()
    for copy in row_copies:
        copy.wait_send()
    for copy in result_copies:
        copy.wait_send()
    pair_sum.drain()
    line.drain()


def backward(query, starts, cosine, sine, middle, cotangent, gain, pairs, row_blocks, grad_blocks, pieces, results, row_grads, output_weight):
    rows = cosine.shape[0]
    length = pairs.shape[1]
    held_rows = 2 * MODEL_WIDTH
    tokens = MB * SHARDS * rows
    dma = pltpu.SemaphoreType.DMA
    anywhere = pl.BlockSpec(memory_space=pl.ANY)
    vmem = pl.BlockSpec(memory_space=pltpu.VMEM)
    shape = jax.ShapeDtypeStruct
    tall, flat = (MODEL_WIDTH, F_BLOCK), (F_BLOCK, MODEL_WIDTH)
    two = lambda s: (2,) + s
    low = lambda s: pltpu.VMEM(s, bf16)
    number = 2 * PARTS
    return pl.pallas_call(
        backward_kernel,
        in_specs=[vmem, pl.BlockSpec(memory_space=pltpu.SMEM)] + [vmem] * 5 + [anywhere] * 9,
        out_specs=[vmem] * 6 + [anywhere] * 6,
        out_shape=[
            shape(query.shape, bf16),
            shape((rows, 2 * KEY_WIDTH), bf16),
            shape((MB * rows, MODEL_WIDTH), bf16),
            shape((MB * rows, MODEL_WIDTH), f32),
            shape((8, MODEL_WIDTH), f32),
            shape((rows, MODEL_WIDTH), bf16),
            shape((held_rows, F_BLOCK), bf16),
            shape((held_rows, F_BLOCK), bf16),
            shape(tall, bf16),
            shape(tall, bf16),
            shape(two(flat), bf16),
            shape((length, 2 * KEY_WIDTH), bf16),
        ],
        scratch_shapes=[
            low((tokens, MODEL_WIDTH)),
            low((MODEL_WIDTH, tokens)),
            low((tokens, MODEL_WIDTH)),
            low((3 * tokens, 2 * F)),
            low(tall),
            low(tall),
            low(flat),
            low(two(tall)),
            low(two(tall)),
            low(two(flat)),
            low(two(tall)),
            low(two(tall)),
            low(two(flat)),
            low(tall),
            low(tall),
            low(tall),
            low(tall),
            low((MB, rows, MODEL_WIDTH)),
            low((MB, SHARDS - 1, rows, MODEL_WIDTH)),
            low((rows, MODEL_WIDTH)),
            low((SHARDS - 1, rows, MODEL_WIDTH)),
            low((MB, rows, MODEL_WIDTH)),
            low((2, 2, length, LANES)),
            pltpu.VMEM((MB, length, rows), f32),
            low((LINE, rows, 2 * KEY_WIDTH)),
            low((LINE - 1, rows, 2 * KEY_WIDTH)),
            dma((4 * MB * SHARDS,)),
            dma((2,)),
            dma((2, 6)),
            dma((4,)),
            dma((2, MB * (SHARDS - 1))),
            dma((2, SHARDS - 1)),
            dma((2, 2)),
            dma((2, LINE)),
            dma((2, LINE - 1)),
        ]
        + line_sems(number),
        compiler_params=pltpu.CompilerParams(
            collective_id=3, has_side_effects=True, vmem_limit_bytes=VMEM_LIMIT
        ),
        name="backward",
    )(query, starts, cosine, sine, middle, cotangent, gain, pairs, row_blocks, grad_blocks, *pieces, results, row_grads, output_weight)


DENSE = ("output", "query", "pair", "gain")
DENSE_PARTS = 4
FINE = 4
GATHER_AFTER = {4: ("output",), 9: ("query",), 13: ("pair", "gain")}
OUTPUT_AFTER = 19


def dense_kernel(
    turned_normed,
    turned_attn,
    query_low,
    pair_low_first,
    middle_low,
    middle_grad,
    tokens,
    gain,
    gain_grad,
    cosine,
    sine,
    middle,
    query_src,
    pair_src,
    pair_grad,
    results_src,
    gate_rest,
    up_rest,
    down_rest,
    input_grad,
    block_output,
    results_in,
    output_total,
    query_total,
    pair_total,
    gain_total,
    gate_total,
    up_total,
    down_total,
    pair_low,
    pair_own,
    pair_other,
    land_left,
    query_weight,
    pair_weight,
    gains,
    send_output,
    send_query,
    own_output,
    own_query,
    own_pair,
    own_gain,
    other_output,
    other_query,
    other_pair,
    other_gain,
    across_output,
    across_query,
    across_pair,
    across_gain,
    sum_output,
    sum_query,
    sum_pair,
    sum_gain,
    near_output,
    near_query,
    near_pair,
    near_gain,
    far_output,
    far_query,
    far_pair,
    far_gain,
    own_gate,
    own_up,
    own_down,
    near_gate,
    near_up,
    near_down,
    far_gate,
    far_up,
    far_down,
    load_sem,
    core_sem,
    left_sem,
    result_sem,
    trade_sem,
    across_sem,
    near_sem,
    far_sem,
    back_sem,
    pass_sem,
    store_sem,
):
    r = types.SimpleNamespace(**locals())
    at = lambda kind, name: getattr(r, kind + "_" + name)
    place = Place()
    core, shard = place.core, place.shard
    rows = r.tokens.shape[0] // MB
    held = MODEL_WIDTH // SHARDS
    half = held // 2
    loads = [
        pltpu.make_async_copy(source, target, r.load_sem.at[i])
        for i, (source, target) in enumerate(
            (
                (r.gate_rest, r.own_gate),
                (r.up_rest, r.own_up),
                (r.down_rest, r.own_down),
                (r.query_src, r.query_weight),
                (r.pair_src, r.pair_weight),
                (r.pair_grad.at[:, core], r.pair_own),
            )
        )
    ]
    for load in loads:
        load.start()
    greet_line(place)
    pair_sum = PairSum(
        place,
        lambda j: r.pair_own.at[j],
        lambda j: r.pair_grad.at[j, 1 - core],
        r.pair_other,
        r.land_left,
        r.core_sem,
        r.left_sem,
    )
    pair_sum.trade()

    pieces = []
    for name, parts in (("gate", FINE), ("up", FINE), ("down", 2 * FINE)):
        pieces += line_pieces(place, at("own", name), at("near", name), at("far", name), getattr(r, name + "_total"), parts)
    expert_pieces = len(pieces)
    for name in DENSE:
        parts = 1 if name == "gain" else DENSE_PARTS
        pieces += line_pieces(
            place, at("sum", name), at("near", name), at("far", name), getattr(r, name + "_total"), parts
        )
    line = Line(place, pieces, (r.near_sem, r.far_sem, r.back_sem, r.pass_sem, r.store_sem))
    for i in range(3):
        loads[i].wait()
    line.ready(0)
    loads[5].wait()
    pair_sum.meet()
    line.ready(*range(1, expert_pieces))

    def block(b, of_core):
        return pl.ds(pl.multiple_of(b * held + of_core * half, half), half)

    trades = {}

    def dense(name, turned, right, sent):
        index = DENSE.index(name)
        trades[name] = []
        for b in range(SHARDS):
            sent[b] = dot(turned[block(b, 1 - core)], right[...]).astype(bf16)
            copy = remote(sent.at[b], at("other", name).at[b], r.trade_sem, index * SHARDS + b, place.partner)
            copy.start()
            trades[name].append(copy)
        for b in range(SHARDS):
            at("own", name)[b] = dot(turned[block(b, core)], right[...]).astype(bf16)

    crossings = {}

    def meet(name):
        own, other, across = at("own", name), at("other", name), at("across", name)
        for b in range(SHARDS):
            trades[name][b].wait_recv()
            add_into(own.at[b], own.at[b], other.at[b])
        crossings[name] = []
        for k in range(1, SHARDS):
            index = DENSE.index(name) * (SHARDS - 1) + k - 1
            copy = remote(own.at[place.peer_index(k)], across.at[k - 1], r.across_sem, index, place.peer(k))
            copy.start()
            crossings[name].append(copy)

    def gather(name):
        for copy in crossings[name]:
            copy.wait_recv()
        across = at("across", name)
        add_into(at("sum", name), at("own", name).at[shard], *[across.at[k] for k in range(SHARDS - 1)])

    dense("output", r.turned_attn, r.middle_low, r.send_output)
    dense("query", r.turned_normed, r.query_low, r.send_query)
    meet("output")
    line.serve([0])
    pair_sum.step(2)
    meet("query")
    pair_sum.step(3)
    for copy in trades["output"]:
        copy.wait_send()
    r.pair_low[0:rows] = r.pair_low_first[...]
    pair_sum.finish(r.pair_low.at[rows : 2 * rows], r.cosine, r.sine)
    dense("pair", r.turned_normed, r.pair_low, r.send_output.at[:, :, 0 : 2 * KEY_WIDTH])
    line.serve([1], [0])
    for load in loads[3:5]:
        load.wait()

    gain_one_grad = jnp.zeros((1, MODEL_WIDTH), f32)
    for m in range(MB):
        own = slice(m * rows, (m + 1) * rows)
        values = r.tokens[own].astype(f32)
        scale = lax.rsqrt(jnp.mean(values * values, axis=-1, keepdims=True) + eps)
        unit = values * scale
        normed_grad = dot(r.query_low[own], r.query_weight[...], NT) + dot(r.pair_low[own], r.pair_weight[...], NT)
        gain_one_grad = gain_one_grad + jnp.sum(normed_grad * unit, axis=0, keepdims=True)
        weighted = normed_grad * r.gain[...]
        inner = jnp.mean(weighted * unit, axis=-1, keepdims=True)
        r.input_grad[own] = r.middle_grad[own] + (weighted - unit * inner) * scale
        if m == 0:
            meet("pair")
            line.serve([2], [1])
    line.serve([3], [2])
    gain_two_grad = jnp.sum(r.gain_grad[...], axis=0, keepdims=True)
    stacked = jnp.concatenate(
        [gain_one_grad, gain_two_grad, jnp.zeros((LANES - 2, MODEL_WIDTH), f32)], axis=0
    )
    r.gains[...] = stacked.T.astype(bf16)
    trades["gain"] = []
    for b in range(SHARDS):
        source = r.gains.at[block(b, 1 - core)]
        index = DENSE.index("gain") * SHARDS + b
        trades["gain"].append(remote(source, r.other_gain.at[b], r.trade_sem, index, place.partner))
        trades["gain"][b].start()
        r.own_gain[b] = r.gains[block(b, core)]
    meet("gain")

    result_copies = []
    for k in range(1, SHARDS):
        source = r.results_src.at[1, place.peer_index(k)]
        result_copies.append(remote(source, r.results_in.at[k - 1], r.result_sem, k - 1, place.peer(k)))
        result_copies[-1].start()
    for copy in trades["pair"]:
        copy.wait_send()
    result_parts = [r.send_output.at[k, 0:rows] for k in range(SHARDS)]
    result_loads = [
        pltpu.make_async_copy(source, target, r.load_sem.at[6 + k])
        for k, (source, target) in enumerate(
            zip([r.results_src.at[1, shard]] + [r.results_in.at[k] for k in range(SHARDS - 1)], result_parts)
        )
    ]
    result_loads[0].start()

    def output_rows():
        for copy, load in zip(result_copies, result_loads[1:]):
            copy.wait_recv()
            load.start()
        total = r.middle[...]
        for load, part in zip(result_loads, result_parts):
            load.wait()
            total = total + part[...].astype(f32)
        r.block_output[...] = total.astype(bf16)

    number = len(pieces)
    first = expert_pieces
    spans = {}
    for name in DENSE:
        parts = 1 if name == "gain" else DENSE_PARTS
        spans[name] = range(first, first + parts)
        first += parts
    lag = 4
    for i in range(number + lag):
        line.serve(
            [i] if 4 <= i < number else [],
            [i - 1] if 4 <= i <= number else [],
            [i - lag] if i >= lag else [],
        )
        for name in GATHER_AFTER.get(i, ()):
            gather(name)
            line.ready(*spans[name])
        if i == OUTPUT_AFTER:
            output_rows()

    for name in DENSE:
        for copy in crossings[name]:
            copy.wait_send()
        if name in ("query", "gain"):
            for copy in trades[name]:
                copy.wait_send()
    for copy in result_copies:
        copy.wait_send()
    pair_sum.drain()
    line.drain()


def dense_weights(vectors, query_weight, pair_weight, pair_grad, results, rests):
    dma = pltpu.SemaphoreType.DMA
    anywhere = pl.BlockSpec(memory_space=pl.ANY)
    vmem = pl.BlockSpec(memory_space=pltpu.VMEM)
    shape = jax.ShapeDtypeStruct
    rows = pair_grad.shape[2]
    low = lambda *s: pltpu.VMEM(s, bf16)
    held = MODEL_WIDTH // SHARDS
    half = held // 2
    widths = (MODEL_WIDTH, MODEL_WIDTH, 2 * KEY_WIDTH, LANES)
    tall = (MODEL_WIDTH, F_BLOCK)
    number = 4 * FINE + 3 * DENSE_PARTS + 1
    return pl.pallas_call(
        dense_kernel,
        in_specs=[vmem] * len(vectors) + [anywhere] * 7,
        out_specs=[vmem] * 2 + [anywhere] * 8,
        out_shape=[
            shape((MB * rows, MODEL_WIDTH), f32),
            shape((rows, MODEL_WIDTH), bf16),
            shape((SHARDS - 1, rows, MODEL_WIDTH), bf16),
        ]
        + [shape((held, w), bf16) for w in widths]
        + [
            shape((2 * MODEL_WIDTH, F_BLOCK), bf16),
            shape((2 * MODEL_WIDTH, F_BLOCK), bf16),
            shape((2 * F, MODEL_WIDTH), bf16),
        ],
        scratch_shapes=[
            low(MB * rows, 2 * KEY_WIDTH),
            low(LINE, rows, 2 * KEY_WIDTH),
            low(LINE, rows, 2 * KEY_WIDTH),
            low(LINE - 1, rows, 2 * KEY_WIDTH),
            low(*query_weight.shape),
            low(*pair_weight.shape),
            low(MODEL_WIDTH, LANES),
            low(SHARDS, half, MODEL_WIDTH),
            low(SHARDS, half, MODEL_WIDTH),
        ]
        + [low(SHARDS, half, w) for w in widths] * 2
        + [low(SHARDS - 1, half, w) for w in widths]
        + [low(half, w) for w in widths] * 3
        + [low(*tall), low(*tall), low(F, MODEL_WIDTH)] * 3
        + [dma((6 + SHARDS,)), dma((2, LINE)), dma((2, LINE - 1)), dma((2, SHARDS - 1)), dma((2, 4 * SHARDS)), dma((2, 4 * (SHARDS - 1)))]
        + line_sems(number),
        compiler_params=pltpu.CompilerParams(
            collective_id=4, has_side_effects=True, vmem_limit_bytes=VMEM_LIMIT
        ),
        name="dense_weights",
    )(*vectors, query_weight, pair_weight, pair_grad, results, *rests)


def widen_kernel(gate_first, gate_second, up_first, up_second, *refs):
    count = len(refs) // 2
    expand_out = refs[count]
    for i, ref in enumerate((gate_first, gate_second, up_first, up_second)):
        expand_out[:, i * F_BLOCK : (i + 1) * F_BLOCK] = ref[...].astype(f32)
    for source, target in zip(refs[:count], refs[count + 1 :]):
        target[...] = source[...].astype(f32)


def widen(expand_parts, arrays):
    steps = 8
    block = lambda a, c: pl.BlockSpec((a.shape[0] // steps, c), lambda i: (i, 0))
    rows = expand_parts[0].shape[0]
    outs = [jax.ShapeDtypeStruct((rows, 2 * F), f32)] + [jax.ShapeDtypeStruct(a.shape, f32) for a in arrays]
    return pl.pallas_call(
        widen_kernel,
        grid=(steps,),
        in_specs=[block(a, a.shape[1]) for a in (*expand_parts, *arrays)],
        out_specs=[block(a, a.shape[1]) for a in outs],
        out_shape=outs,
        compiler_params=pltpu.CompilerParams(vmem_limit_bytes=VMEM_LIMIT),
        name="widen",
    )(*expand_parts, *arrays)


def shards(
    tokens,
    doc_starts,
    routes,
    gates,
    attn_gain,
    w_q,
    key_value_weight,
    w_o,
    moe_gain,
    expert_in,
    expert_out,
    cotangent,
):
    links = Links()
    rows = tokens.shape[2]
    length = rows * links.contexts
    held = expert_in.shape[0]
    chained = links.chips == LINE and links.shards == SHARDS and held == 2
    width = w_q.shape[0]
    flat_tokens = tokens.reshape(MB * rows, MODEL_WIDTH)
    if chained:
        flat_cotangent = cotangent.reshape(MB * rows, MODEL_WIDTH)
        starts = doc_starts[:, 0]
        (
            turned_normed,
            query,
            turned_attn,
            middle,
            gains,
            cosine,
            sine,
            pair_weight,
            query_weight,
            output_weight,
            pairs,
            row_blocks,
            grad_blocks,
            result_blocks,
            row_grad_blocks,
            active,
            gate,
            up,
        ) = forward(
            flat_tokens,
            routes[:, 0].transpose(0, 2, 1),
            gates[:, 0].transpose(0, 2, 1),
            jnp.stack([attn_gain, moe_gain]),
            flat_cotangent,
            starts,
            rotation_constants(length),
            (key_value_weight, w_q, w_o),
            expert_in,
            expert_out,
        )
        result_blocks = result_blocks.reshape(row_blocks.shape)
        row_grad_blocks = row_grad_blocks.reshape(row_blocks.shape)
        gains = gains.reshape(SHARDS, GAIN_ROWS, width).astype(f32)
        gain_one, gain_two = gains[:, 0].reshape(1, MODEL_WIDTH), gains[:, 1].reshape(1, MODEL_WIDTH)
        (
            query_low,
            pair_low,
            middle_low,
            middle_grad,
            gain_two_grad,
            output_first,
            gate_first,
            up_first,
            gate_rest,
            up_rest,
            down_rest,
            pair_grad,
        ) = backward(
            query,
            starts,
            cosine,
            sine,
            middle,
            flat_cotangent,
            gain_two,
            pairs,
            row_blocks,
            grad_blocks,
            (active, gate, up),
            result_blocks,
            row_grad_blocks,
            output_weight,
        )
        (
            input_grad,
            output_second,
            _,
            output_total,
            query_total,
            pair_total,
            gain_total,
            gate_second,
            up_second,
            shrink_total,
        ) = dense_weights(
            (
                turned_normed,
                turned_attn,
                query_low,
                pair_low,
                middle_low,
                middle_grad,
                flat_tokens,
                gain_one,
                gain_two_grad,
                cosine,
                sine,
                middle[rows:],
            ),
            query_weight,
            pair_weight,
            pair_grad.reshape(LINE, 2, rows, 2 * KEY_WIDTH),
            result_blocks,
            (gate_rest, up_rest, down_rest.reshape(F, MODEL_WIDTH)),
        )
        expand_total, shrink_total, output_total, query_total, pair_total = widen(
            (gate_first, gate_second, up_first, up_second),
            (shrink_total, output_total, query_total, pair_total),
        )
        return (
            jnp.stack([output_first, output_second])[:, None],
            input_grad.reshape(MB, 1, rows, MODEL_WIDTH),
            gain_total[:, 0].astype(f32),
            query_total,
            pair_total,
            output_total,
            gain_total[:, 1].astype(f32),
            expand_total.reshape(held, MODEL_WIDTH, 2 * F),
            shrink_total.reshape(held, F, MODEL_WIDTH),
        )

    positions = links.context * rows + jnp.arange(rows, dtype=jnp.int32)
    cosine, sine = rotation_tables(positions)
    key_places = jnp.arange(length, dtype=jnp.int32)
    flat_values = flat_tokens.astype(f32)
    scale_one = lax.rsqrt(jnp.mean(flat_values * flat_values, axis=-1, keepdims=True) + eps)
    unit_one = flat_values * scale_one
    expert_ids = jnp.arange(E, dtype=jnp.int32)
    chosen = (routes.reshape(MB, rows, TOP)[..., None] == expert_ids).astype(f32)
    combine = jnp.sum(gates.reshape(MB, rows, TOP)[..., None] * chosen, axis=2)
    gather = lambda w: lax.all_gather(w, "fsdp", axis=0, tiled=True)
    pair_weight, query_weight, output_weight = gather(key_value_weight), gather(w_q), gather(w_o)
    gain_one, gain_two = gather(attn_gain).astype(f32), gather(moe_gain).astype(f32)
    normed = (unit_one * gain_one).astype(bf16)
    both = lambda table: jnp.concatenate([table] * MB)
    own_pairs = rotate_columns(dot(normed, pair_weight), both(cosine), both(sine), KEY_WIDTH)
    query = rotate_columns(dot(normed, query_weight), both(cosine), both(sine), MODEL_WIDTH)
    own_pairs = own_pairs.reshape(MB, rows, 2 * KEY_WIDTH)
    pairs = lax.all_gather(own_pairs, "ctx", axis=1, tiled=True)

    combine = jnp.concatenate([combine] + [links.across(combine, k) for k in range(1, links.shards)], axis=1)
    combine = lax.dynamic_slice_in_dim(combine, links.shard * held, held, 2)
    combine = combine.transpose(0, 2, 1)[..., None]

    biases, biases_turned = [], []
    for m in range(MB):
        starts = doc_starts[m, 0]
        begin = jnp.max(jnp.where(starts[None, :] <= positions[:, None], starts[None, :], 0), axis=1)
        seen = (key_places[None, :] <= positions[:, None]) & (key_places[None, :] >= begin[:, None])
        biases.append(jnp.where(seen, 0.0, -1e30).astype(f32))
        places, begins = jnp.tile(positions, GROUP), jnp.tile(begin, GROUP)
        seen = (key_places[:, None] <= places[None, :]) & (key_places[:, None] >= begins[None, :])
        biases_turned.append(jnp.where(seen, 0.0, -1e30).astype(f32))

    middles, attns, results, row_grads = [], [], [], []
    rows_kept, grads_kept, pieces_kept = [], [], []
    for m in range(MB):
        own = slice(m * rows, (m + 1) * rows)
        attn = attention_forward(m, query, pairs, biases[m])
        middle = flat_tokens[own].astype(f32) + dot(attn, output_weight)
        scale_two = lax.rsqrt(jnp.mean(middle * middle, axis=-1, keepdims=True) + eps)
        moe_in = (middle * scale_two * gain_two).astype(bf16)
        out_grad = cotangent[m, 0]
        row_parts = [moe_in] + [links.across(moe_in, k) for k in range(1, links.shards)]
        grad_parts = [out_grad] + [links.across(out_grad, k) for k in range(1, links.shards)]
        result, row_grad, pieces = experts(row_parts, grad_parts, combine[m], expert_in, expert_out)
        for parts, sums in ((result, results), (row_grad, row_grads)):
            total = parts[0].astype(f32)
            for k in range(1, links.shards):
                total = total + links.across(parts[k], k).astype(f32)
            sums.append(total)
        middles.append(middle)
        attns.append(attn)
        rows_kept += row_parts
        grads_kept += grad_parts
        pieces_kept.append(pieces)
    merge = lambda items: jnp.concatenate(items, axis=0)
    expert_grads = expert_weights(
        merge(rows_kept), merge(grads_kept), *[merge([p[i] for p in pieces_kept]) for i in range(3)], held
    )
    expert_grads = [g.reshape(-1, g.shape[-1]) for g in expert_grads]
    outputs = [(middles[m] + results[m]).astype(bf16) for m in range(MB)]

    input_grads, query_lows, pair_lows, middle_lows = [], [], [], []
    gain_one_grad, gain_two_grad = 0.0, 0.0
    for m in range(MB):
        own = slice(m * rows, (m + 1) * rows)
        scale_two = lax.rsqrt(jnp.mean(middles[m] * middles[m], axis=-1, keepdims=True) + eps)
        unit_two = middles[m] * scale_two
        moe_in_grad = row_grads[m]
        gain_two_grad = gain_two_grad + jnp.sum(moe_in_grad * unit_two, axis=0)
        weighted = moe_in_grad * gain_two
        inner = jnp.mean(weighted * unit_two, axis=-1, keepdims=True)
        middle_grad = cotangent[m, 0].astype(f32) + (weighted - unit_two * inner) * scale_two
        middle_low = middle_grad.astype(bf16)
        attn_grad = dot(middle_low, output_weight, NT).astype(bf16)
        query_low, pair_grad = attention_backward(
            m, query, cosine, sine, pairs, biases_turned[m], attn_grad
        )
        parts = [lax.psum_scatter(pair_grad, "ctx", scatter_dimension=0, tiled=True)]
        pair_low = pair_gradient(parts, cosine, sine)
        normed_grad = dot(query_low, query_weight, NT) + dot(pair_low, pair_weight, NT)
        gain_one_grad = gain_one_grad + jnp.sum(normed_grad * unit_one[own], axis=0)
        weighted = normed_grad * gain_one
        inner = jnp.mean(weighted * unit_one[own], axis=-1, keepdims=True)
        residual_grad = (weighted - unit_one[own] * inner) * scale_one[own]
        input_grads.append(middle_grad + residual_grad)
        query_lows.append(query_low)
        pair_lows.append(pair_low)
        middle_lows.append(middle_low)

    join = lambda items: jnp.concatenate(items, axis=0)

    output_grad = dot(join(attns), join(middle_lows), TN).astype(bf16)
    query_grad = dot(normed, join(query_lows), TN).astype(bf16)
    pair_weight_grad = dot(normed, join(pair_lows), TN).astype(bf16)
    gain_grads = jnp.stack([gain_one_grad, gain_two_grad], axis=1)
    gain_grads = jnp.pad(gain_grads, ((0, 0), (0, LANES - 2))).astype(bf16)
    dense_grads = [output_grad, query_grad, jnp.concatenate([pair_weight_grad, gain_grads], axis=1)]
    totals = [lax.psum(g, "ctx") for g in expert_grads]
    for g in dense_grads:
        part = lax.psum_scatter(g, "fsdp", scatter_dimension=0, tiled=True)
        totals.append(lax.psum(part, "ctx"))
    gate_total, up_total, down_total, output_total, query_total, pair_total = [t.astype(f32) for t in totals]
    expand_total = jnp.concatenate([gate_total, up_total], axis=1)

    return (
        jnp.stack(outputs)[:, None],
        jnp.stack(input_grads)[:, None],
        pair_total[:, 2 * KEY_WIDTH],
        query_total,
        pair_total[:, : 2 * KEY_WIDTH],
        output_total,
        pair_total[:, 2 * KEY_WIDTH + 1],
        expand_total.reshape(held, MODEL_WIDTH, 2 * F),
        down_total.reshape(held, F, MODEL_WIDTH),
    )


def solution(mesh):
    return jax.shard_map(
        shards,
        mesh=mesh,
        in_specs=(
            P(None, "fsdp", "ctx", None),
            P(None, "fsdp", None),
            P(None, "fsdp", "ctx", None),
            P(None, "fsdp", "ctx", None),
            P("fsdp"),
            P("fsdp", None),
            P("fsdp", None),
            P("fsdp", None),
            P("fsdp"),
            P("fsdp", None, None),
            P("fsdp", None, None),
            P(None, "fsdp", "ctx", None),
        ),
        out_specs=(
            P(None, "fsdp", "ctx", None),
            P(None, "fsdp", "ctx", None),
            P("fsdp"),
            P("fsdp", None),
            P("fsdp", None),
            P("fsdp", None),
            P("fsdp"),
            P("fsdp", None, None),
            P("fsdp", None, None),
        ),
        check_vma=False,
    )
```

```python
import functools
import types

import jax
import jax.numpy as jnp
import numpy as np
from jax import lax
from jax.experimental import pallas as pl
from jax.experimental.pallas import tpu as pltpu
from jax.sharding import PartitionSpec as P

MODEL_WIDTH = 1536
QUERY_HEADS = 24
KEY_VALUE_HEADS = 8
HEAD_SIZE = 64
GROUP = QUERY_HEADS // KEY_VALUE_HEADS
KEY_WIDTH = KEY_VALUE_HEADS * HEAD_SIZE
F = 512
E = 8
TOP = 4
MB = 2
LANES = 128
PAIRS = KEY_WIDTH // LANES
PAIR_QUERY = 2 * GROUP * HEAD_SIZE
F_BLOCK = 256
VMEM_LIMIT = 60 * 1024 * 1024

eps = 1e-05
theta = 10000.0

NT = (((1,), (1,)), ((), ()))
TN = (((0,), (0,)), ((), ()))
bf16 = jnp.bfloat16
f32 = jnp.float32


def dot(left, right, dims=(((1,), (0,)), ((), ()))):
    return lax.dot_general(left, right, dims, preferred_element_type=f32)


def rotation_tables(positions):
    frequency = theta ** (-jnp.arange(0, HEAD_SIZE, 2, dtype=f32) / HEAD_SIZE)
    angles = positions.astype(f32)[:, None] * frequency[None, :]
    cosine, sine = jnp.cos(angles), jnp.sin(angles)
    repeat = LANES // HEAD_SIZE
    cosine = jnp.concatenate([cosine, cosine] * repeat, axis=1)
    sine = jnp.concatenate([-sine, sine] * repeat, axis=1)
    return cosine, sine


def rotation_constants(length):
    frequency = theta ** (-np.arange(0, HEAD_SIZE, 2, dtype=np.float64) / HEAD_SIZE)
    angles = np.arange(length, dtype=np.float64)[:, None] * frequency[None, :]
    cosine, sine = np.cos(angles), np.sin(angles)
    repeat = LANES // HEAD_SIZE
    cosine = np.concatenate([cosine, cosine] * repeat, axis=1)
    sine = np.concatenate([-sine, sine] * repeat, axis=1)
    return jnp.asarray(np.stack([cosine, sine]).astype(np.float32))


def visible_bias(starts, m, context, shape, query_axis):
    rows = shape[query_axis]
    narrow = (rows, 1) if query_axis == 0 else (1, rows)
    query = context * rows + lax.broadcasted_iota(jnp.int32, narrow, query_axis)
    begin = jnp.zeros(narrow, jnp.int32)
    for i in range(starts.shape[1]):
        begin = jnp.maximum(begin, jnp.where(query >= starts[m, i], starts[m, i], 0))
    key = lax.broadcasted_iota(jnp.int32, shape, 1 - query_axis)
    return jnp.where((key <= query) & (key >= begin), 0.0, -1e30).astype(f32)


def lane_index(shape):
    return lax.broadcasted_iota(jnp.int32, shape, 1)


def rotate(tile, cosine, sine):
    half = HEAD_SIZE // 2
    ahead = pltpu.roll(tile, LANES - half, 1)
    behind = pltpu.roll(tile, half, 1)
    first = lane_index(tile.shape) % HEAD_SIZE < half
    return tile * cosine + jnp.where(first, ahead, behind) * sine


def rotate_columns_kernel(rotated, values_ref, cosine_ref, sine_ref, out_ref):
    cosine, sine = cosine_ref[...], sine_ref[...]
    for i in range(values_ref.shape[1] // LANES):
        cols = slice(i * LANES, (i + 1) * LANES)
        tile = values_ref[:, cols]
        if i < rotated // LANES:
            tile = rotate(tile, cosine, sine)
        out_ref[:, cols] = tile.astype(bf16)


def rotate_columns(values, cosine, sine, rotated):
    return pl.pallas_call(
        functools.partial(rotate_columns_kernel, rotated),
        out_shape=jax.ShapeDtypeStruct(values.shape, bf16),
        compiler_params=pltpu.CompilerParams(vmem_limit_bytes=VMEM_LIMIT),
        name="rotate_columns",
    )(values, cosine, sine)


def pair_gradient_kernel(count, cosine_ref, sine_ref, *refs):
    out_ref = refs[-1]
    cosine, sine = cosine_ref[...], sine_ref[...]
    for i in range(2 * KEY_WIDTH // LANES):
        cols = slice(i * LANES, (i + 1) * LANES)
        total = refs[0][:, cols].astype(f32)
        for ref in refs[1:count]:
            total = total + ref[:, cols].astype(f32)
        if i < KEY_WIDTH // LANES:
            total = rotate(total, cosine, -sine)
        out_ref[:, cols] = total.astype(bf16)


def pair_gradient(parts, cosine, sine):
    return pl.pallas_call(
        functools.partial(pair_gradient_kernel, len(parts)),
        out_shape=jax.ShapeDtypeStruct(parts[0].shape, bf16),
        compiler_params=pltpu.CompilerParams(vmem_limit_bytes=VMEM_LIMIT),
        name="pair_gradient",
    )(cosine, sine, *parts)


def grouped(tiles, half):
    mine = lane_index(tiles[0].shape) // HEAD_SIZE == half
    rows = []
    for j in range(GROUP * half, GROUP * half + GROUP):
        tile = tiles[j // 2]
        if j % 2 != half:
            tile = pltpu.roll(tile, HEAD_SIZE, 1)
        rows.append(jnp.where(mine, tile, 0.0))
    return jnp.concatenate(rows, axis=0).astype(bf16)


def ungrouped(per_half, rows):
    heads = []
    for j in range(2 * GROUP):
        half, place = j // GROUP, j % GROUP
        tile = per_half[half][place * rows : (place + 1) * rows]
        if j % 2 != half:
            tile = pltpu.roll(tile, HEAD_SIZE, 1)
        heads.append(tile)
    low = lane_index(heads[0].shape) < HEAD_SIZE
    return [jnp.where(low, heads[2 * i], heads[2 * i + 1]) for i in range(GROUP)]


def query_tiles(query_ref):
    scale = 1.0 / HEAD_SIZE
    return [query_ref[:, i * LANES : (i + 1) * LANES].astype(f32) * scale for i in range(GROUP)]


def attention_pair(tiles, key, value, bias):
    rows = bias.shape[0]
    results = []
    for half in range(2):
        scores = dot(grouped(tiles, half), key, NT)
        scores = jnp.concatenate(
            [scores[g * rows : (g + 1) * rows] + bias for g in range(GROUP)], axis=0
        )
        peak = jnp.max(scores, axis=1, keepdims=True)
        weights = jnp.exp(scores - peak)
        total = jnp.sum(weights, axis=1, keepdims=True)
        results.append(dot(weights.astype(bf16), value) / total)
    return ungrouped(results, rows)


def attention_forward_kernel(query_ref, key_ref, value_ref, bias_ref, out_ref):
    tiles = attention_pair(query_tiles(query_ref), key_ref[...], value_ref[...], bias_ref[...])
    for i, tile in enumerate(tiles):
        out_ref[:, i * LANES : (i + 1) * LANES] = tile.astype(bf16)


def attention_forward(m, query, pairs, bias):
    rows, length = bias.shape
    return pl.pallas_call(
        attention_forward_kernel,
        grid=(PAIRS,),
        in_specs=[
            pl.BlockSpec((rows, PAIR_QUERY), lambda p: (m, p)),
            pl.BlockSpec((None, length, LANES), lambda p: (m, 0, p)),
            pl.BlockSpec((None, length, LANES), lambda p: (m, 0, p + PAIRS)),
            pl.BlockSpec((rows, length), lambda p: (0, 0)),
        ],
        out_specs=pl.BlockSpec((rows, PAIR_QUERY), lambda p: (0, p)),
        out_shape=jax.ShapeDtypeStruct((rows, MODEL_WIDTH), bf16),
        compiler_params=pltpu.CompilerParams(vmem_limit_bytes=VMEM_LIMIT),
        cost_estimate=pl.CostEstimate(
            flops=16 * rows * length * MODEL_WIDTH,
            bytes_accessed=4 * length * MODEL_WIDTH,
            transcendentals=rows * length * QUERY_HEADS,
        ),
        name="attention_forward",
    )(query, pairs, pairs, bias)


def attention_pair_gradient(tiles, grads, key, value, bias):
    rows = tiles[0].shape[0]
    key_grad, value_grad = None, None
    query_grads = []
    for half in range(2):
        query = grouped(tiles, half)
        grad = grouped(grads, half)
        scores = dot(key, query, NT) + bias
        weights = jnp.exp(scores - jnp.max(scores, axis=0, keepdims=True))
        prob = weights * (1.0 / jnp.sum(weights, axis=0, keepdims=True))
        prob_grad = dot(value, grad, NT)
        delta = jnp.sum(prob * prob_grad, axis=0, keepdims=True)
        score_grad = (prob * (prob_grad - delta)).astype(bf16)
        value_part = dot(prob.astype(bf16), grad)
        key_part = dot(score_grad, query)
        value_grad = value_part if half == 0 else value_grad + value_part
        key_grad = key_part if half == 0 else key_grad + key_part
        query_grads.append(dot(score_grad, key, TN))
    return ungrouped(query_grads, rows), key_grad, value_grad


def attention_backward_kernel(
    query_ref, cosine_ref, sine_ref, key_ref, value_ref, bias_ref, grad_ref, query_out, pair_out
):
    cosine, sine = cosine_ref[...], sine_ref[...]
    grads = [grad_ref[:, i * LANES : (i + 1) * LANES].astype(f32) for i in range(GROUP)]
    query_grads, key_grad, value_grad = attention_pair_gradient(
        query_tiles(query_ref), grads, key_ref[...], value_ref[...], bias_ref[...]
    )
    for i, tile in enumerate(query_grads):
        tile = rotate(tile * (1.0 / HEAD_SIZE), cosine, -sine)
        query_out[:, i * LANES : (i + 1) * LANES] = tile.astype(bf16)
    first = pl.multiple_of(pl.program_id(0) * LANES, LANES)
    pair_out[:, pl.ds(first, LANES)] = key_grad.astype(bf16)
    pair_out[:, pl.ds(first + KEY_WIDTH, LANES)] = value_grad.astype(bf16)


def attention_backward(m, query, cosine, sine, pairs, bias, grad):
    rows = cosine.shape[0]
    length = pairs.shape[1]
    whole = lambda shape: pl.BlockSpec(shape, lambda p: (0, 0))
    return pl.pallas_call(
        attention_backward_kernel,
        grid=(PAIRS,),
        in_specs=[
            pl.BlockSpec((rows, PAIR_QUERY), lambda p: (m, p)),
            whole((rows, LANES)),
            whole((rows, LANES)),
            pl.BlockSpec((None, length, LANES), lambda p: (m, 0, p)),
            pl.BlockSpec((None, length, LANES), lambda p: (m, 0, p + PAIRS)),
            whole(bias.shape),
            pl.BlockSpec((rows, PAIR_QUERY), lambda p: (0, p)),
        ],
        out_specs=[
            pl.BlockSpec((rows, PAIR_QUERY), lambda p: (0, p)),
            whole((length, 2 * KEY_WIDTH)),
        ],
        out_shape=[
            jax.ShapeDtypeStruct((rows, MODEL_WIDTH), bf16),
            jax.ShapeDtypeStruct((length, 2 * KEY_WIDTH), bf16),
        ],
        compiler_params=pltpu.CompilerParams(vmem_limit_bytes=VMEM_LIMIT),
        cost_estimate=pl.CostEstimate(
            flops=40 * rows * length * MODEL_WIDTH,
            bytes_accessed=8 * length * MODEL_WIDTH,
            transcendentals=rows * length * QUERY_HEADS,
        ),
        name="attention_backward",
    )(query, cosine, sine, pairs, pairs, bias, grad)


def expert_block(inputs, out_grad, combine, gate_weight, up_weight, down_weight):
    gate = dot(inputs, gate_weight)
    up = dot(inputs, up_weight)
    sigmoid = jax.nn.sigmoid(gate)
    silu = gate * sigmoid
    active = (silu * up * combine).astype(bf16)
    active_grad = dot(out_grad, down_weight, NT) * combine
    gate_grad = (active_grad * up * sigmoid * (1.0 + gate * (1.0 - sigmoid))).astype(bf16)
    up_grad = (active_grad * silu).astype(bf16)
    result = dot(active, down_weight)
    row_grad = dot(gate_grad, gate_weight, NT) + dot(up_grad, up_weight, NT)
    return active, gate_grad, up_grad, result, row_grad


def experts_kernel(parts, rows, steps, combine_ref, gate_ref, up_ref, down_ref, *refs):
    rows_in, grads_in = refs[:parts], refs[parts : 2 * parts]
    refs = refs[2 * parts :]
    results, row_grads = refs[:parts], refs[parts : 2 * parts]
    active_out, gate_out, up_out, rows_all, grads_all, result_sum, grad_sum = refs[2 * parts :]
    step = pl.program_id(0) * pl.num_programs(1) + pl.program_id(1)

    @pl.when(step == 0)
    def _():
        for k in range(parts):
            place = slice(k * rows, (k + 1) * rows)
            rows_all[place] = rows_in[k][...]
            grads_all[place] = grads_in[k][...]
        result_sum[...] = jnp.zeros_like(result_sum)
        grad_sum[...] = jnp.zeros_like(grad_sum)

    inputs, out_grad, combine = rows_all[...], grads_all[...], combine_ref[0]
    active, gate_grad, up_grad, result, row_grad = expert_block(
        inputs, out_grad, combine, gate_ref[0], up_ref[0], down_ref[0]
    )
    active_out[...] = active
    gate_out[...] = gate_grad
    up_out[...] = up_grad
    result_sum[...] += result
    grad_sum[...] += row_grad

    @pl.when(step == steps - 1)
    def _():
        for k in range(parts):
            place = slice(k * rows, (k + 1) * rows)
            results[k][...] = result_sum[place].astype(bf16)
            row_grads[k][...] = grad_sum[place].astype(bf16)


def experts(row_parts, grad_parts, combine, expert_in, expert_out):
    parts = len(row_parts)
    rows = row_parts[0].shape[0]
    held = expert_in.shape[0]
    tokens = parts * rows
    blocks = F // F_BLOCK
    whole = pl.BlockSpec((rows, MODEL_WIDTH), lambda e, b: (0, 0))
    piece = pl.BlockSpec((tokens, F_BLOCK), lambda e, b: (0, e * blocks + b))
    row_shape = jax.ShapeDtypeStruct((rows, MODEL_WIDTH), bf16)
    piece_shape = jax.ShapeDtypeStruct((tokens, held * F), bf16)
    out = pl.pallas_call(
        functools.partial(experts_kernel, parts, rows, held * blocks),
        grid=(held, blocks),
        in_specs=[
            pl.BlockSpec((1, tokens, 1), lambda e, b: (e, 0, 0)),
            pl.BlockSpec((1, MODEL_WIDTH, F_BLOCK), lambda e, b: (e, 0, b)),
            pl.BlockSpec((1, MODEL_WIDTH, F_BLOCK), lambda e, b: (e, 0, b + blocks)),
            pl.BlockSpec((1, F_BLOCK, MODEL_WIDTH), lambda e, b: (e, b, 0)),
        ]
        + [whole] * (2 * parts),
        out_specs=[whole] * (2 * parts) + [piece] * 3,
        out_shape=[row_shape] * (2 * parts) + [piece_shape] * 3,
        scratch_shapes=[
            pltpu.VMEM((tokens, MODEL_WIDTH), bf16),
            pltpu.VMEM((tokens, MODEL_WIDTH), bf16),
            pltpu.VMEM((tokens, MODEL_WIDTH), f32),
            pltpu.VMEM((tokens, MODEL_WIDTH), f32),
        ],
        compiler_params=pltpu.CompilerParams(vmem_limit_bytes=VMEM_LIMIT),
        cost_estimate=pl.CostEstimate(
            flops=12 * tokens * held * MODEL_WIDTH * F,
            bytes_accessed=6 * held * MODEL_WIDTH * F + 20 * tokens * MODEL_WIDTH,
            transcendentals=tokens * held * F,
        ),
        name="experts",
    )(combine, expert_in, expert_in, expert_out, *row_parts, *grad_parts)
    return out[:parts], out[parts : 2 * parts], out[2 * parts :]


def expert_weights_kernel(rows_ref, grads_ref, active_ref, gate_ref, up_ref, gate_out, up_out, down_out, turned):
    step = pl.program_id(0) * pl.num_programs(1) + pl.program_id(1)

    @pl.when(step == 0)
    def _():
        turned[...] = rows_ref[...].T

    gate_out[0] = dot(turned[...], gate_ref[...]).astype(bf16)
    up_out[0] = dot(turned[...], up_ref[...]).astype(bf16)
    down_out[0] = dot(active_ref[...], grads_ref[...], TN).astype(bf16)


def expert_weights(rows, grads, active, gate, up, held):
    tokens = rows.shape[0]
    blocks = F // F_BLOCK
    whole = pl.BlockSpec((tokens, MODEL_WIDTH), lambda e, b: (0, 0))
    piece = pl.BlockSpec((tokens, F_BLOCK), lambda e, b: (0, e * blocks + b))
    wide = pl.BlockSpec((1, MODEL_WIDTH, F_BLOCK), lambda e, b: (e, 0, b))
    return pl.pallas_call(
        expert_weights_kernel,
        grid=(held, blocks),
        in_specs=[whole] * 2 + [piece] * 3,
        out_specs=[wide, wide, pl.BlockSpec((1, F_BLOCK, MODEL_WIDTH), lambda e, b: (e, b, 0))],
        out_shape=[
            jax.ShapeDtypeStruct((held, MODEL_WIDTH, F), bf16),
            jax.ShapeDtypeStruct((held, MODEL_WIDTH, F), bf16),
            jax.ShapeDtypeStruct((held, F, MODEL_WIDTH), bf16),
        ],
        scratch_shapes=[pltpu.VMEM((MODEL_WIDTH, tokens), bf16)],
        compiler_params=pltpu.CompilerParams(vmem_limit_bytes=VMEM_LIMIT),
        cost_estimate=pl.CostEstimate(
            flops=6 * tokens * held * MODEL_WIDTH * F,
            bytes_accessed=6 * held * MODEL_WIDTH * F + 8 * tokens * MODEL_WIDTH,
            transcendentals=0,
        ),
        name="expert_weights",
    )(rows, grads, active, gate, up)


class Links:
    def __init__(self):
        self.shards = lax.axis_size("fsdp")
        self.contexts = lax.axis_size("ctx")
        self.chips = self.contexts // 2
        self.shard = lax.axis_index("fsdp")
        self.context = lax.axis_index("ctx")
        self.chip = self.context // 2
        self.core = self.context % 2

    def across(self, array, k):
        return lax.ppermute(array, "fsdp", [(i, i ^ k) for i in range(self.shards)])

    def other_core(self, array):
        return lax.ppermute(array, "ctx", [(i, i ^ 1) for i in range(self.contexts)])

    def shift(self, array, s):
        n = self.contexts
        return lax.ppermute(array, "ctx", [(i, (i + 2 * s) % n) for i in range(n)])


MESH = pl.DeviceIdType.MESH
LINE = 4


class Place:
    def __init__(self):
        self.shard, self.context = lax.axis_index("fsdp"), lax.axis_index("ctx")
        self.core, self.chip = self.context % 2, self.context // 2
        self.partner = {"ctx": 2 * self.chip + 1 - self.core}

    def peer_index(self, k):
        x, y = (self.shard % 2 + k % 2) % 2, (self.shard // 2 + k // 2) % 2
        return 2 * y + x

    def peer(self, k):
        return {"fsdp": self.peer_index(k)}

    def chip_device(self, chip):
        return {"ctx": 2 * chip + self.core}


def remote(source, target, sems, index, device):
    return pltpu.make_async_remote_copy(
        src_ref=source,
        dst_ref=target,
        send_sem=sems.at[0, index],
        recv_sem=sems.at[1, index],
        device_id=device,
        device_id_type=MESH,
    )


def greet(device):
    pl.semaphore_signal(pltpu.get_barrier_semaphore(), inc=1, device_id=device, device_id_type=MESH)


SHARDS = 4
GAIN_ROWS = 16


class Square:
    def __init__(self, place, blocks, direct_sem, relay_sem, base=0):
        half = blocks.shape[1] // 2
        own = blocks.at[place.shard]
        self.directs = [remote(own, own, direct_sem, base + k - 1, place.peer(k)) for k in (1, 2)]
        self.relays = []
        for k in (1, 2):
            spot = blocks.at[place.peer_index(k), (k - 1) * half : k * half]
            self.relays.append(remote(spot, spot, relay_sem, base + k - 1, place.peer(3 - k)))

    def start(self):
        for copy in self.directs:
            copy.start()

    def pass_on(self):
        for direct, relay in zip(self.directs, self.relays):
            direct.wait_recv()
            relay.start()

    def finish(self):
        for copy in self.relays:
            copy.wait_recv()

    def drain(self):
        for copy in self.directs + self.relays:
            copy.wait_send()


LAST = LINE - 1
WIDE = 4


def forward_kernel(
    tokens,
    routes,
    gates,
    gain_pair,
    cotangent,
    starts,
    tables,
    pair_src,
    query_src,
    output_src,
    expand_src,
    shrink_src,
    turned_normed_out,
    query_rows_out,
    turned_attn_out,
    middle_out,
    gain_rows_out,
    cosine,
    sine,
    pair_out,
    query_out,
    output_out,
    pairs,
    turned_out,
    grads_out,
    results_out,
    row_grads_out,
    active_out,
    gate_out,
    up_out,
    turned_normed,
    query,
    turned_attn,
    middle,
    gains,
    turned_rows,
    pair_weight,
    query_weight,
    output_weight,
    expand,
    shrink,
    own_pairs,
    normed,
    combine_in,
    combine_own,
    attn,
    bias,
    combine,
    rows_all,
    grads_all,
    result_sum,
    grad_sum,
    key_value,
    load_sem,
    table_sem,
    store_sem,
    expert_sem,
    gain_sem,
    combine_sem,
    direct_sem,
    relay_sem,
    pass_sem,
    right_sem,
    left_sem,
    core_sem,
    own_sem,
    square_direct_sem,
    square_relay_sem,
    key_sem,
    emit_sem,
    last_sem,
):
    r = types.SimpleNamespace(**locals())
    place = Place()
    core, chip, shard = place.core, place.chip, place.shard
    local = pltpu.make_async_copy
    rows = r.cosine.shape[0]
    wide = SHARDS * rows
    held = r.pair_src.shape[0]
    half, quarter = held // 2, held // 4
    greet_line(place)
    length = r.bias.shape[2]

    def rows_of(owner, piece, size):
        return pl.ds(pl.multiple_of(owner * held + core * half, half) + piece, size)

    sources = (r.pair_src, r.query_src, r.output_src)
    weights = (r.pair_weight, r.query_weight, r.output_weight)
    weight_outs = (r.pair_out, r.query_out, r.output_out)
    loads, directs, relays, passes, stores = [], [], [], [], []
    for w in range(3):
        weight = weights[w]
        own_rows = pl.ds(pl.multiple_of(shard * held, held), held)
        loads.append(local(sources[w], weight.at[own_rows], r.load_sem.at[w]))
        stores.append(local(weight, weight_outs[w], r.store_sem.at[w]))
        mine = sources[w].at[pl.ds(pl.multiple_of(core * half, half), half)]
        spot = weight.at[rows_of(shard, 0, half)]
        directs.append([remote(mine, spot, r.direct_sem, 2 * w + k - 1, place.peer(k)) for k in (1, 2)])
        relay, onward = [], []
        for k in (1, 2):
            spot = weight.at[rows_of(place.peer_index(k), (k - 1) * quarter, quarter)]
            relay.append(remote(spot, spot, r.relay_sem, 2 * w + k - 1, place.peer(3 - k)))
            spot = weight.at[rows_of(place.peer_index(k), 0, half)]
            onward.append(remote(spot, spot, r.pass_sem, 4 * w + k - 1, place.partner))
        for k in (1, 2):
            spot = weight.at[rows_of(place.peer_index(3), (k - 1) * quarter, quarter)]
            onward.append(remote(spot, spot, r.pass_sem, 4 * w + k + 1, place.partner))
        relays.append(relay)
        passes.append(onward)

    def send_weight(w):
        for copy in directs[w]:
            copy.start()

    def relay_weight(w):
        for k in (1, 2):
            directs[w][k - 1].wait_recv()
            relays[w][k - 1].start()
        for k in (1, 2):
            passes[w][k - 1].start()

    def pass_weight(w):
        for k in (1, 2):
            relays[w][k - 1].wait_recv()
            passes[w][k + 1].start()

    def settle_weight(w):
        loads[w].wait()
        for copy in passes[w]:
            copy.wait_recv()
        stores[w].start()

    def sent_weight(w):
        for copy in directs[w] + relays[w] + passes[w]:
            copy.wait_send()
        stores[w].wait()

    send_weight(0)

    gain_rows = r.gains.at[pl.ds(pl.multiple_of(shard * GAIN_ROWS, GAIN_ROWS), GAIN_ROWS)]
    gain_rows[...] = jnp.concatenate([r.gain_pair[...], jnp.zeros((GAIN_ROWS - 2, held), bf16)], axis=0)
    expert_row = lax.broadcasted_iota(jnp.int32, (E, rows), 0)
    for m in range(MB):
        combine = jnp.zeros((E, rows), f32)
        for k in range(TOP):
            combine += jnp.where(expert_row == r.routes[m, 0, k : k + 1], r.gates[m, 0, k : k + 1], 0.0)
        r.combine_own[:, m * rows : (m + 1) * rows] = combine
    r.combine_in[shard] = r.combine_own[...]
    small_copies = []
    for k in range(1, SHARDS):
        small_copies.append(remote(gain_rows, gain_rows, r.gain_sem, k - 1, place.peer(k)))
        small_copies.append(remote(r.combine_own, r.combine_in.at[shard], r.combine_sem, k - 1, place.peer(k)))

    for copy in small_copies:
        copy.start()
    at = pl.ds(pl.multiple_of(place.context * rows, rows), rows)
    table_loads = [
        local(r.tables.at[i, at], table, r.table_sem.at[i]) for i, table in enumerate((r.cosine, r.sine))
    ]
    for load in table_loads + loads:
        load.start()
    expert_loads = [
        local(r.expand_src, r.expand, r.expert_sem.at[0]),
        local(r.shrink_src, r.shrink, r.expert_sem.at[1]),
    ]
    for load in expert_loads:
        load.start()
    for m in range(MB):
        r.grads_all[m, shard] = r.cotangent[m * rows : (m + 1) * rows]
    grad_squares = [Square(place, r.grads_all.at[m], r.square_direct_sem, r.square_relay_sem, 2 * m) for m in range(MB)]
    row_squares = [
        Square(place, r.rows_all.at[m], r.square_direct_sem, r.square_relay_sem, 2 * (MB + m)) for m in range(MB)
    ]

    def spread_gains():
        r.gain_rows_out[...] = jnp.zeros_like(r.gain_rows_out)
        for b in range(SHARDS):
            pair = r.gains[b * GAIN_ROWS : b * GAIN_ROWS + 2]
            r.gain_rows_out[0:2, b * held : (b + 1) * held] = pair.astype(f32)

    def gain_times(values, row, write):
        for b in range(SHARDS):
            columns = slice(b * held, (b + 1) * held)
            write(columns, (values[:, columns] * r.gain_rows_out[row : row + 1, columns]).astype(bf16))

    values = r.tokens[...].astype(f32)
    unit = values * lax.rsqrt(jnp.mean(values * values, axis=-1, keepdims=True) + eps)
    for copy in small_copies:
        copy.wait_recv()

    def write_normed(columns, value):
        r.normed[:, columns] = value

    spread_gains()
    gain_times(unit, 0, write_normed)
    r.turned_normed[...] = r.normed[...].T
    for b in range(SHARDS):
        spread = jnp.concatenate([r.combine_in[b], jnp.zeros((LANES - E, MB * rows), f32)], axis=0)
        r.combine[b] = spread.T
    for m in range(MB):
        r.bias[m] = visible_bias(r.starts, m, place.context, (rows, length), 0)
    for load in table_loads:
        load.wait()

    relay_weight(0)
    send_weight(1)
    pass_weight(0)
    settle_weight(0)
    cosine, sine = r.cosine[...], r.sine[...]

    def project(weight, column, rotated):
        result = dot(r.normed[...], weight[:, pl.ds(column, WIDE * LANES)])
        tiles = []
        for m in range(MB):
            for i in range(WIDE):
                tile = result[m * rows : (m + 1) * rows, i * LANES : (i + 1) * LANES]
                tiles.append((m, i, rotate(tile, cosine, sine) if rotated else tile))
        return tiles

    blocks = KEY_WIDTH // (WIDE * LANES)
    for b in range(2 * blocks):
        column = b * WIDE * LANES
        for m, i, tile in project(r.pair_weight, column, b < blocks):
            r.own_pairs[m, :, pl.ds(column + i * LANES, LANES)] = tile.astype(bf16)

    def chunk(m, owner):
        owner = jnp.clip(owner, 0, LAST)
        return r.pairs.at[m, pl.ds(pl.multiple_of((2 * owner + core) * rows, rows), rows)]

    def move(m, t, direction):
        target = chunk(m, chip - direction * (t - 1))
        source = r.own_pairs.at[m] if t == 1 else target
        sems = r.right_sem if direction > 0 else r.left_sem
        device = place.chip_device(jnp.clip(chip + direction, 0, LAST))
        return remote(source, target, sems, m * LAST + t - 1, device)

    def sends(t, direction):
        owner = chip - direction * (t - 1)
        if direction > 0:
            return (chip < LAST) & (owner >= 0)
        return (chip > 0) & (owner <= LAST)

    def gets(t, direction):
        owner = chip - direction * t
        return owner >= 0 if direction > 0 else owner <= LAST

    def came(m, t, direction):
        spot = chunk(m, chip - direction * t)
        sems = r.right_sem if direction > 0 else r.left_sem
        return remote(spot, spot, sems, m * LAST + t - 1, place.partner)

    def pass_chunk(m, t, direction):
        spot = chunk(m, chip - direction * t)
        index = (m * LINE + t) * 2 + (1 if direction > 0 else 0)
        return remote(spot, spot, r.core_sem, index, place.partner)

    def take_step(m, t):
        for direction in (1, -1):

            @pl.when(gets(t, direction))
            def _():
                came(m, t, direction).wait_recv()
                if t < LAST:

                    @pl.when(sends(t + 1, direction))
                    def _():
                        move(m, t + 1, direction).start()

                pass_chunk(m, t, direction).start()

    own_copies = []
    for m in range(MB):
        for direction in (1, -1):

            @pl.when(sends(1, direction))
            def _():
                move(m, 1, direction).start()

        own_copies.append(
            (
                local(r.own_pairs.at[m], chunk(m, chip), r.own_sem.at[m]),
                remote(r.own_pairs.at[m], chunk(m, chip), r.core_sem, m * LINE * 2, place.partner),
            )
        )
        for copy in own_copies[m]:
            copy.start()

    def settle_pairs(m):
        own_copies[m][0].wait()
        own_copies[m][1].wait()
        for t in range(1, LINE):
            for direction in (1, -1):

                @pl.when(gets(t, direction))
                def _():
                    pass_chunk(m, t, direction).wait()

    def query_block(b, carry):
        column = pl.multiple_of(b * WIDE * LANES, WIDE * LANES)
        for m, i, tile in project(r.query_weight, column, True):
            r.query[m * rows : (m + 1) * rows, pl.ds(column + i * LANES, LANES)] = tile.astype(bf16)
        return carry

    def key_load(m, p, slot, i):
        lane = pl.multiple_of(p * LANES, LANES) + i * KEY_WIDTH
        return local(r.pairs.at[m, :, pl.ds(lane, LANES)], r.key_value.at[slot, i], r.key_sem.at[slot, i])

    def attend(m):
        own = slice(m * rows, (m + 1) * rows)
        for i in range(2):
            key_load(m, 0, 0, i).start()

        def pair(p, carry):
            slot = p % 2
            for i in range(2):
                key_load(m, p, slot, i).wait()

            @pl.when(p + 1 < PAIRS)
            def _():
                for i in range(2):
                    key_load(m, p + 1, 1 - slot, i).start()

            column = pl.multiple_of(p * PAIR_QUERY, PAIR_QUERY)
            columns = [pl.ds(column + i * LANES, LANES) for i in range(GROUP)]
            tiles = [r.query[own, c].astype(f32) * (1.0 / HEAD_SIZE) for c in columns]
            results = attention_pair(tiles, r.key_value[slot, 0], r.key_value[slot, 1], r.bias[m])
            for c, tile in zip(columns, results):
                r.attn[own, c] = tile.astype(bf16)
            return carry

        lax.fori_loop(0, PAIRS, pair, 0)
        r.turned_attn[:, own] = r.attn[own].T

    def finish_attention(m):
        own = slice(m * rows, (m + 1) * rows)
        middle = r.tokens[own].astype(f32) + dot(r.attn[own], r.output_weight[...])
        r.middle[own] = middle
        unit = middle * lax.rsqrt(jnp.mean(middle * middle, axis=-1, keepdims=True) + eps)

        def write(columns, value):
            r.rows_all[m, shard, :, columns] = value

        gain_times(unit, 1, write)

    active, gate, up = [r.pair_weight.at[i * wide : (i + 1) * wide] for i in range(3)]
    results, row_grads = [r.query_weight.at[i * wide : (i + 1) * wide] for i in range(2)]

    turned = r.turned_rows

    def turn(m):
        turned[...] = r.rows_all[m].reshape(wide, MODEL_WIDTH).T

    def emits(m):
        pairs = (
            (turned, r.turned_out.at[:, m * wide : (m + 1) * wide]),
            (r.grads_all.at[m], r.grads_out.at[m]),
            (results, r.results_out.at[m]),
            (row_grads, r.row_grads_out.at[m]),
            (active, r.active_out.at[m]),
            (gate, r.gate_out.at[m]),
            (up, r.up_out.at[m]),
        )
        return [local(a, b, r.emit_sem.at[m * len(pairs) + i]) for i, (a, b) in enumerate(pairs)]

    def expert_steps(m, between):
        steps = [(e, b) for e in range(r.expand.shape[0]) for b in range(F // F_BLOCK)]
        for i, (e, b) in enumerate(steps):
            weight = r.combine[:, m * rows : (m + 1) * rows, :].reshape(wide, LANES)
            expert = shard * r.expand.shape[0] + e
            chosen = jnp.where(lane_index(weight.shape) == expert, weight, 0.0)
            columns = slice(b * F_BLOCK, (b + 1) * F_BLOCK)
            up_columns = slice(F + b * F_BLOCK, F + (b + 1) * F_BLOCK)
            a, g, u, result, row_grad = expert_block(
                r.rows_all[m].reshape(wide, MODEL_WIDTH),
                r.grads_all[m].reshape(wide, MODEL_WIDTH),
                jnp.sum(chosen, axis=1, keepdims=True),
                r.expand[e, :, columns],
                r.expand[e, :, up_columns],
                r.shrink[e, columns, :],
            )
            spot = slice(e * F + b * F_BLOCK, e * F + (b + 1) * F_BLOCK)
            active[:, spot], gate[:, spot], up[:, spot] = a, g, u
            if i == 0:
                r.result_sum[...] = result
                r.grad_sum[...] = row_grad
            elif i < len(steps) - 1:
                r.result_sum[...] += result
                r.grad_sum[...] += row_grad
            else:
                results[...] = (r.result_sum[...] + result).astype(bf16)
                row_grads[...] = (r.grad_sum[...] + row_grad).astype(bf16)
            if i in between:
                between[i]()

    relay_weight(1)
    send_weight(2)
    take_step(0, 1)
    take_step(1, 1)
    pass_weight(1)
    take_step(0, 2)
    settle_weight(1)
    lax.fori_loop(0, MODEL_WIDTH // (WIDE * LANES), query_block, 0)
    relay_weight(2)
    grad_squares[0].start()
    take_step(1, 2)
    take_step(0, 3)
    settle_pairs(0)
    attend(0)
    pass_weight(2)
    grad_squares[0].pass_on()
    take_step(1, 3)
    settle_weight(2)
    finish_attention(0)
    row_squares[0].start()
    settle_pairs(1)
    attend(1)
    row_squares[0].pass_on()
    finish_attention(1)
    row_squares[1].start()
    grad_squares[1].start()
    early = [
        local(source, target, r.last_sem.at[i])
        for i, (source, target) in enumerate(
            (
                (r.turned_normed, r.turned_normed_out),
                (r.query, r.query_rows_out),
                (r.turned_attn, r.turned_attn_out),
                (r.middle, r.middle_out),
            )
        )
    ]
    for emit in early:
        emit.start()
    for load in expert_loads:
        load.wait()
    sent_weight(0)
    sent_weight(1)
    grad_squares[0].finish()
    row_squares[0].finish()
    expert_steps(0, {1: row_squares[1].pass_on})
    turn(0)
    for emit in emits(0):
        emit.start()
    grad_squares[1].pass_on()
    row_squares[1].finish()
    for emit in emits(0):
        emit.wait()
    turn(1)
    grad_squares[1].finish()
    expert_steps(1, {})
    for emit in emits(1):
        emit.start()
    for emit in early:
        emit.wait()

    for copy in small_copies:
        copy.wait_send()
    sent_weight(2)
    for m in range(MB):
        for t in range(1, LINE):
            for direction in (1, -1):

                @pl.when(sends(t, direction))
                def _():
                    move(m, t, direction).wait_send()

    for square in grad_squares + row_squares:
        square.drain()
    for emit in emits(1):
        emit.wait()


def forward(tokens, routes, gates, gain_pair, cotangent, starts, tables, weights, expert_in, expert_out):
    rows = tokens.shape[0] // MB
    length = tables.shape[1]
    wide = SHARDS * rows
    held = weights[0].shape[0]
    dma = pltpu.SemaphoreType.DMA
    anywhere = pl.BlockSpec(memory_space=pl.ANY)
    vmem = pl.BlockSpec(memory_space=pltpu.VMEM)
    shape = jax.ShapeDtypeStruct
    low = lambda *s: pltpu.VMEM(s, bf16)
    full = [(SHARDS * held, w.shape[1]) for w in weights]
    blocks = (MB, SHARDS, rows, MODEL_WIDTH)
    return pl.pallas_call(
        forward_kernel,
        in_specs=[vmem] * 5 + [pl.BlockSpec(memory_space=pltpu.SMEM)] + [anywhere] * 6,
        out_specs=[anywhere] * 4 + [vmem] * 3 + [anywhere] * 11,
        out_shape=[
            shape(tokens.shape[::-1], bf16),
            shape(tokens.shape, bf16),
            shape(tokens.shape[::-1], bf16),
            shape(tokens.shape, f32),
            shape((8, MODEL_WIDTH), f32),
            shape((rows, LANES), f32),
            shape((rows, LANES), f32),
        ]
        + [shape(f, bf16) for f in full]
        + [
            shape((MB, length, 2 * KEY_WIDTH), bf16),
            shape((MODEL_WIDTH, MB * wide), bf16),
            shape(blocks, bf16),
            shape((MB, wide, MODEL_WIDTH), bf16),
            shape((MB, wide, MODEL_WIDTH), bf16),
        ]
        + [shape((MB, wide, 2 * F), bf16)] * 3,
        scratch_shapes=[
            low(*tokens.shape[::-1]),
            low(*tokens.shape),
            low(*tokens.shape[::-1]),
            pltpu.VMEM(tokens.shape, f32),
            low(SHARDS * GAIN_ROWS, held),
            low(MODEL_WIDTH, wide),
        ]
        + [low(*f) for f in full]
        + [
            low(*expert_in.shape),
            low(*expert_out.shape),
            low(MB, rows, 2 * KEY_WIDTH),
            low(*tokens.shape),
            pltpu.VMEM((SHARDS, E, MB * rows), f32),
            pltpu.VMEM((E, MB * rows), f32),
            low(*tokens.shape),
            pltpu.VMEM((MB, rows, length), f32),
            pltpu.VMEM((SHARDS, MB * rows, LANES), f32),
            low(*blocks),
            low(*blocks),
            pltpu.VMEM((wide, MODEL_WIDTH), f32),
            pltpu.VMEM((wide, MODEL_WIDTH), f32),
            low(2, 2, length, LANES),
            dma((3,)),
            dma((2,)),
            dma((3,)),
            dma((2,)),
            dma((2, SHARDS - 1)),
            dma((2, SHARDS - 1)),
            dma((2, 6)),
            dma((2, 6)),
            dma((2, 12)),
            dma((2, MB * LAST)),
            dma((2, MB * LAST)),
            dma((2, 2 * MB * LINE)),
            dma((MB,)),
            dma((2, 4 * MB)),
            dma((2, 4 * MB)),
            dma((2, 2)),
            dma((7 * MB,)),
            dma((4,)),
        ],
        compiler_params=pltpu.CompilerParams(
            collective_id=1, has_side_effects=True, vmem_limit_bytes=VMEM_LIMIT
        ),
        name="forward",
    )(tokens, routes, gates, gain_pair, cotangent, starts, tables, *weights, expert_in, expert_out)


ADD_ROWS = 64


def add_into(out, *parts):
    rows = out.shape[0]
    size = max(d for d in range(16, ADD_ROWS + 1, 16) if rows % d == 0)

    def body(i, carry):
        spot = pl.ds(pl.multiple_of(i * size, size), size)
        total = parts[0][spot].astype(f32)
        for part in parts[1:]:
            total = total + part[spot].astype(f32)
        out[spot] = total.astype(out.dtype)
        return carry

    lax.fori_loop(0, rows // size, body, 0)


def greet_line(place):
    has_left, has_right = place.chip > 0, place.chip < LINE - 1
    greet(place.partner)
    for k in range(1, SHARDS):
        greet(place.peer(k))

    @pl.when(has_left)
    def _():
        greet(place.chip_device(place.chip - 1))

    @pl.when(has_right)
    def _():
        greet(place.chip_device(place.chip + 1))

    neighbours = jnp.where(has_left, 1, 0) + jnp.where(has_right, 1, 0)
    pl.semaphore_wait(pltpu.get_barrier_semaphore(), SHARDS + neighbours)


class Line:
    def __init__(self, place, pieces, sems):
        near_sem, far_sem, back_sem, pass_sem, store_sem = sems
        chip = place.chip
        self.inner = (chip == 1) | (chip == 2)
        outer = place.chip_device(3 * (chip // 2))
        inner = place.chip_device(1 + chip // 2)
        facing = place.chip_device(3 - chip)
        self.pieces = pieces
        numbered = list(enumerate(pieces))
        self.inward = [remote(p[0], p[1], near_sem, i, inner) for i, p in numbered]
        self.facing = [remote(p[0], p[2], far_sem, i, facing) for i, p in numbered]
        self.outward = [remote(p[1], p[3], back_sem, i, outer) for i, p in numbered]
        self.pass_inner = [remote(p[1], p[3], pass_sem, i, place.partner) for i, p in numbered]
        self.pass_outer = [remote(p[3], p[3], pass_sem, i, place.partner) for i, p in numbered]
        self.stores = [pltpu.make_async_copy(p[1], p[3], store_sem.at[i]) for i, p in numbered]

    def ready(self, *items):
        @pl.when(jnp.logical_not(self.inner))
        def _():
            for i in items:
                self.inward[i].start()

    def serve(self, halfway=(), finish=(), forward=()):
        @pl.when(self.inner)
        def _():
            for i in halfway:
                self.inward[i].wait_recv()
                own, near = self.pieces[i][:2]
                add_into(own, own, near)
                self.facing[i].start()
            for i in finish:
                self.facing[i].wait_recv()
                own, near, far = self.pieces[i][:3]
                add_into(near, own, far)
                self.outward[i].start()
                self.pass_inner[i].start()
                self.stores[i].start()

        @pl.when(jnp.logical_not(self.inner))
        def _():
            for i in forward:
                self.outward[i].wait_recv()
                self.pass_outer[i].start()

    def drain(self):
        @pl.when(self.inner)
        def _():
            for i in range(len(self.pieces)):
                self.facing[i].wait_send()
                self.outward[i].wait_send()
                self.pass_inner[i].wait_send()
                self.stores[i].wait()

        @pl.when(jnp.logical_not(self.inner))
        def _():
            for i in range(len(self.pieces)):
                self.inward[i].wait_send()
                self.pass_outer[i].wait_send()

        for copy in self.pass_outer:
            copy.wait_recv()


def line_sems(number):
    dma = pltpu.SemaphoreType.DMA
    return [dma((2, number))] * 4 + [dma((number,))]


def split_rows(ref, parts):
    size = ref.shape[0] // parts
    return [ref.at[j * size : (j + 1) * size] for j in range(parts)]


def out_halves(place, ref, parts):
    half = ref.shape[0] // 2
    size = half // parts
    first = pl.multiple_of(place.core * half, half)
    return [ref.at[pl.ds(first + j * size, size)] for j in range(parts)]


def line_pieces(place, own, near, far, out, parts):
    return list(
        zip(split_rows(own, parts), split_rows(near, parts), split_rows(far, parts), out_halves(place, out, parts))
    )


class PairSum:
    def __init__(self, place, own, sources, others, lands, core_sem, left_sem):
        self.place, self.own, self.others, self.lands, self.left_sem = place, own, others, lands, left_sem
        self.trades = [remote(sources(j), others.at[j], core_sem, j, place.partner) for j in range(LINE)]
        self.past = LAST - place.chip

    def trade(self):
        for copy in self.trades:
            copy.start()

    def move(self, t):
        owner = jnp.clip(self.place.chip - (LINE - t), 0, LAST)
        device = self.place.chip_device(jnp.clip(self.place.chip - 1, 0, LAST))
        return remote(self.own(owner), self.lands.at[t - 1], self.left_sem, t - 1, device)

    def meet(self):
        for j in range(LINE):
            self.trades[j].wait_recv()
            add_into(self.own(j), self.own(j), self.others.at[j])

        @pl.when(self.past == 0)
        def _():
            for t in range(1, LINE):
                self.move(t).start()

    def take(self, t):
        self.move(t).wait_recv()
        owner = jnp.clip(self.place.chip - (LAST - t), 0, LAST)
        add_into(self.own(owner), self.own(owner), self.lands.at[t - 1])

    def step(self, t):
        @pl.when((self.past >= 1) & (self.past <= min(t - 1, LINE - 2)))
        def _():
            self.take(t - 1)
            self.move(t).start()

    def finish(self, out, cosine, sine):
        @pl.when(self.past >= 1)
        def _():
            self.take(LAST)

        mine = self.own(self.place.chip)
        for i in range(2 * KEY_WIDTH // LANES):
            columns = slice(i * LANES, (i + 1) * LANES)
            tile = mine[:, columns]
            if i < KEY_WIDTH // LANES:
                tile = rotate(tile.astype(f32), cosine[...], -sine[...]).astype(bf16)
            out[:, columns] = tile

    def drain(self):
        for copy in self.trades:
            copy.wait_send()
        for t in range(1, LINE):

            @pl.when((self.past <= t - 1) & (self.past <= LINE - 2))
            def _():
                self.move(t).wait_send()


PARTS = 4


def backward_kernel(
    query_src,
    starts,
    cosine,
    sine,
    middle_src,
    cotangent_src,
    gain,
    pairs,
    turned_src,
    grads_src,
    active_src,
    gate_src,
    up_src,
    results_src,
    row_grads_src,
    output_src,
    query_low_out,
    pair_low,
    middle_low_out,
    middle_grad_out,
    gain_grad,
    block_output,
    gate_total,
    up_total,
    gate_rest,
    up_rest,
    down_rest,
    pair_grad,
    query,
    middle,
    cotangent,
    query_low,
    middle_low,
    middle_grad,
    rows,
    turned,
    grads,
    pool,
    send_gate,
    send_up,
    send_down,
    own_gate,
    own_up,
    own_down,
    other_gate,
    other_up,
    other_down,
    near_gate,
    near_up,
    far_gate,
    far_up,
    row_grad_own,
    row_grad_in,
    result_own,
    result_in,
    attn_grad,
    key_value,
    bias,
    pair_other,
    land_left,
    load_sem,
    weight_sem,
    trade_sem,
    rest_sem,
    row_sem,
    result_sem,
    key_sem,
    core_sem,
    left_sem,
    near_sem,
    far_sem,
    back_sem,
    pass_sem,
    store_sem,
    emit_sem,
):
    r = types.SimpleNamespace(**locals())
    place = Place()
    core, chip, shard = place.core, place.chip, place.shard
    rows = r.cosine.shape[0]
    tokens = MB * SHARDS * rows
    side = MODEL_WIDTH // 2
    local = pltpu.make_async_copy

    wide = SHARDS * rows
    loads = []

    def load(source, target):
        loads.append(local(source, target, r.load_sem.at[len(loads)]))
        loads[-1].start()
        return loads[-1]

    flat = lambda ref, m: [(ref.at[m, k], m * wide + k * rows) for k in range(SHARDS)]
    grad_loads, piece_loads = [], []
    turned_load = load(r.turned_src, r.turned)
    for i, ref in ((1, r.gate_src), (2, r.up_src), (0, r.active_src)):
        for m in range(MB):
            at = i * tokens + m * wide
            piece_loads.append(load(ref.at[m], r.pool.at[at : at + wide]))
    for m in range(MB):
        for source, at in flat(r.grads_src, m):
            grad_loads.append(load(source, r.grads.at[at : at + rows]))
    own_loads = [load(r.row_grads_src.at[m, shard], r.row_grad_own.at[m]) for m in range(MB)]
    own_loads.append(load(r.results_src.at[0, shard], r.result_own))

    vector_loads = [
        load(source, target)
        for source, target in ((r.middle_src, r.middle), (r.cotangent_src, r.cotangent), (r.query_src, r.query))
    ]
    greet_line(place)

    row_copies, result_copies = [], []
    for m in range(MB):
        for k in range(1, SHARDS):
            i = m * (SHARDS - 1) + k - 1
            at = place.peer_index(k)
            row_copies.append(
                remote(r.row_grads_src.at[m, at], r.row_grad_in.at[m, k - 1], r.row_sem, i, place.peer(k))
            )
            if m == 0:
                result_copies.append(
                    remote(r.results_src.at[m, at], r.result_in.at[k - 1], r.result_sem, i, place.peer(k))
                )
    for copy in row_copies:
        copy.start()

    for m in range(MB):
        r.bias[m] = visible_bias(r.starts, m, place.context, r.bias.shape[1:], 1)

    turned_load.wait()
    sends = (r.send_gate, r.send_up, r.send_down)
    owns = (r.own_gate, r.own_up, r.own_down)
    others = (r.other_gate, r.other_up, r.other_down)
    trades = [
        [remote(sends[i], others[i].at[b], r.trade_sem, b * 3 + i, place.partner) for i in range(3)]
        for b in range(2)
    ]

    def weight_block(b, expert, outs):
        column = pl.ds(pl.multiple_of(expert * F + b * F_BLOCK, F_BLOCK), F_BLOCK)
        for i in range(2):
            outs[i][...] = dot(r.turned[...], r.pool[(i + 1) * tokens : (i + 2) * tokens, column]).astype(bf16)

    def down_block(b, expert, out):
        column = pl.ds(pl.multiple_of(expert * F + b * F_BLOCK, F_BLOCK), F_BLOCK)
        out[...] = dot(r.pool[0:tokens, column], r.grads[...], TN).astype(bf16)

    def meet(b, i):
        trades[b][i].wait_recv()
        add_into(owns[i].at[b], owns[i].at[b], others[i].at[b])

    pieces = []
    for own, near, far, out in (
        (r.own_gate.at[0], r.near_gate, r.far_gate, r.gate_total),
        (r.own_up.at[0], r.near_up, r.far_up, r.up_total),
    ):
        pieces += line_pieces(place, own, near, far, out, PARTS)
    line = Line(place, pieces, (r.near_sem, r.far_sem, r.back_sem, r.pass_sem, r.store_sem))

    for copy in piece_loads[: 2 * MB]:
        copy.wait()

    def else_serve(b):
        if b == 1:
            line.serve([0])

    for b in range(2):
        if b == 1:
            for i in range(2):
                trades[0][i].wait_send()
        weight_block(b, 1 - core, sends)
        for i in range(2):
            trades[b][i].start()
        weight_block(b, core, [own.at[b] for own in owns[:2]])
        if b == 0:
            for i in range(2):
                meet(0, i)
                line.ready(*range(i * PARTS, (i + 1) * PARTS))
            for copy in piece_loads[2 * MB :] + grad_loads:
                copy.wait()
        else:
            trades[0][2].wait_send()
        else_serve(b)
        down_block(b, 1 - core, sends[2])
        trades[b][2].start()
        down_block(b, core, owns[2].at[b])
        if b == 0:
            meet(0, 2)

    weight_loads = []
    for i in range(2):
        source = r.output_src.at[:, i * side : (i + 1) * side]
        target = r.pool.at[i * MODEL_WIDTH : (i + 1) * MODEL_WIDTH, 0:side]
        weight_loads.append(local(source, target, r.weight_sem.at[i]))
        weight_loads[-1].start()
    for copy in result_copies:
        copy.start()
    for i in range(3):
        meet(1, i)
    rests = [
        local(r.own_gate.at[1], r.gate_rest, r.rest_sem.at[0]),
        local(r.own_up.at[1], r.up_rest, r.rest_sem.at[1]),
        local(r.own_down, r.down_rest, r.rest_sem.at[2]),
    ]
    for copy in rests:
        copy.start()

    r.gain_grad[...] = jnp.zeros_like(r.gain_grad)

    def prepare(m):
        own = slice(m * rows, (m + 1) * rows)
        own_loads[m].wait()
        moe_in_grad = r.row_grad_own[m].astype(f32)
        for k in range(1, SHARDS):
            row_copies[m * (SHARDS - 1) + k - 1].wait_recv()
            moe_in_grad = moe_in_grad + r.row_grad_in[m, k - 1].astype(f32)
        middle = r.middle[own]
        scale = lax.rsqrt(jnp.mean(middle * middle, axis=-1, keepdims=True) + eps)
        unit = middle * scale
        r.gain_grad[m : m + 1] = jnp.sum(moe_in_grad * unit, axis=0, keepdims=True)
        weighted = moe_in_grad * r.gain[1:2]
        inner = jnp.mean(weighted * unit, axis=-1, keepdims=True)
        middle_grad = r.cotangent[own].astype(f32) + (weighted - unit * inner) * scale
        r.middle_grad[own] = middle_grad
        r.middle_low[own] = middle_grad.astype(bf16)
        if m == 0:
            for copy in weight_loads:
                copy.wait()
        total = dot(r.middle_low[own, 0:side], r.pool[0:MODEL_WIDTH, 0:side], NT)
        total = total + dot(r.middle_low[own, side:], r.pool[MODEL_WIDTH : 2 * MODEL_WIDTH, 0:side], NT)
        r.attn_grad[m] = total.astype(bf16)

    def key_load(step, slot, i):
        m, p = step // PAIRS, step % PAIRS
        lane = pl.multiple_of(p * LANES, LANES) + i * KEY_WIDTH
        return local(r.pairs.at[m, :, pl.ds(lane, LANES)], r.key_value.at[slot, i], r.key_sem.at[slot, i])

    pair_grads = (r.rows, r.grads.at[:, 0 : 2 * KEY_WIDTH])

    def chunk(of_chip, of_core):
        return pair_grads[0].at[pl.ds(pl.multiple_of((2 * of_chip + of_core) * rows, rows), rows)]

    pair_sum = PairSum(
        place,
        lambda j: chunk(j, core),
        lambda j: chunk(j, 1 - core),
        r.pair_other,
        r.land_left,
        r.core_sem,
        r.left_sem,
    )

    def pair_step(step, carry):
        m, p = step // PAIRS, step % PAIRS
        slot = step % 2
        for i in range(2):
            key_load(step, slot, i).wait()

        @pl.when(step + 1 < MB * PAIRS)
        def _():
            for i in range(2):
                key_load(step + 1, 1 - slot, i).start()

        at = pl.multiple_of(m * rows, rows)
        column = pl.multiple_of(p * PAIR_QUERY, PAIR_QUERY)
        lane = pl.multiple_of(p * LANES, LANES)
        columns = [pl.ds(column + i * LANES, LANES) for i in range(GROUP)]
        scale = 1.0 / HEAD_SIZE
        tiles = [r.query[pl.ds(at, rows), c].astype(f32) * scale for c in columns]
        grads = [r.attn_grad[m, :, c].astype(f32) for c in columns]
        bias = jnp.concatenate([r.bias[m]] * GROUP, axis=1)
        query_grads, key_grad, value_grad = attention_pair_gradient(
            tiles, grads, r.key_value[slot, 0], r.key_value[slot, 1], bias
        )
        for c, tile in zip(columns, query_grads):
            tile = rotate(tile * scale, r.cosine[...], -r.sine[...])
            r.query_low[pl.ds(at, rows), c] = tile.astype(bf16)
        key_low, value_low = key_grad.astype(bf16), value_grad.astype(bf16)
        for micro in range(MB):

            @pl.when(m == micro)
            def _():
                pair_grads[micro][:, pl.ds(lane, LANES)] = key_low
                pair_grads[micro][:, pl.ds(lane + KEY_WIDTH, LANES)] = value_low

        for at_step, actions in SERVICE:

            @pl.when(step == at_step)
            def _():
                for action in actions:
                    action()

        return carry

    serve = line.serve
    SERVICE = (
        (1, (lambda: serve([3], [1]),)),
        (2, (lambda: serve([4], [2], [0]),)),
        (3, (pair_sum.trade, lambda: prepare(1), lambda: serve([5], [3], [1]), pair_sum.meet)),
        (4, (lambda: serve([6], [4], [2]),)),
        (5, (lambda: serve([7], [5], [3]),)),
        (6, (lambda: serve([], [6], [4]), lambda: pair_sum.step(2))),
        (7, (lambda: serve([], [7], [5]),)),
    )
    for i in range(2):
        key_load(0, 0, i).start()
    for copy in vector_loads:
        copy.wait()
    serve([1])
    prepare(0)
    serve([2], [0])
    lax.fori_loop(0, MB * PAIRS, pair_step, 0)
    second = local(pair_grads[1], r.pair_grad, r.rest_sem.at[3])
    second.start()
    emits = [
        local(source, target, r.emit_sem.at[i])
        for i, (source, target) in enumerate(
            (
                (r.query_low, r.query_low_out),
                (r.middle_low, r.middle_low_out),
                (r.middle_grad, r.middle_grad_out),
            )
        )
    ]
    for copy in emits:
        copy.start()
    pair_sum.step(3)
    own_loads[MB].wait()
    total = r.middle[0:rows] + r.result_own[...].astype(f32)
    for k in range(1, SHARDS):
        result_copies[k - 1].wait_recv()
        total = total + r.result_in[k - 1].astype(f32)
    r.block_output[...] = total.astype(bf16)
    serve([], [], [6])
    pair_sum.finish(r.pair_low, r.cosine, r.sine)
    serve([], [], [7])
    for copy in [second] + emits:
        copy.wait()

    for copy in trades[1]:
        copy.wait_send()
    for copy in rests:
        copy.wait()
    for copy in row_copies:
        copy.wait_send()
    for copy in result_copies:
        copy.wait_send()
    pair_sum.drain()
    line.drain()


def backward(query, starts, cosine, sine, middle, cotangent, gain, pairs, turned_rows, grad_blocks, pieces, results, row_grads, output_weight):
    rows = cosine.shape[0]
    length = pairs.shape[1]
    held_rows = 2 * MODEL_WIDTH
    tokens = MB * SHARDS * rows
    dma = pltpu.SemaphoreType.DMA
    anywhere = pl.BlockSpec(memory_space=pl.ANY)
    vmem = pl.BlockSpec(memory_space=pltpu.VMEM)
    shape = jax.ShapeDtypeStruct
    tall, flat = (MODEL_WIDTH, F_BLOCK), (F_BLOCK, MODEL_WIDTH)
    two = lambda s: (2,) + s
    low = lambda s: pltpu.VMEM(s, bf16)
    number = 2 * PARTS
    return pl.pallas_call(
        backward_kernel,
        in_specs=[anywhere, pl.BlockSpec(memory_space=pltpu.SMEM), vmem, vmem, anywhere, anywhere, vmem]
        + [anywhere] * 9,
        out_specs=[anywhere, vmem, anywhere, anywhere, vmem, vmem] + [anywhere] * 6,
        out_shape=[
            shape(query.shape, bf16),
            shape((rows, 2 * KEY_WIDTH), bf16),
            shape((MB * rows, MODEL_WIDTH), bf16),
            shape((MB * rows, MODEL_WIDTH), f32),
            shape((8, MODEL_WIDTH), f32),
            shape((rows, MODEL_WIDTH), bf16),
            shape((held_rows, F_BLOCK), bf16),
            shape((held_rows, F_BLOCK), bf16),
            shape(tall, bf16),
            shape(tall, bf16),
            shape(two(flat), bf16),
            shape((length, 2 * KEY_WIDTH), bf16),
        ],
        scratch_shapes=[
            low((MB * rows, MODEL_WIDTH)),
            pltpu.VMEM((MB * rows, MODEL_WIDTH), f32),
            low((MB * rows, MODEL_WIDTH)),
            low((MB * rows, MODEL_WIDTH)),
            low((MB * rows, MODEL_WIDTH)),
            pltpu.VMEM((MB * rows, MODEL_WIDTH), f32),
            low((length, 2 * KEY_WIDTH)),
            low((MODEL_WIDTH, tokens)),
            low((tokens, MODEL_WIDTH)),
            low((3 * tokens, 2 * F)),
            low(tall),
            low(tall),
            low(flat),
            low(two(tall)),
            low(two(tall)),
            low(two(flat)),
            low(two(tall)),
            low(two(tall)),
            low(two(flat)),
            low(tall),
            low(tall),
            low(tall),
            low(tall),
            low((MB, rows, MODEL_WIDTH)),
            low((MB, SHARDS - 1, rows, MODEL_WIDTH)),
            low((rows, MODEL_WIDTH)),
            low((SHARDS - 1, rows, MODEL_WIDTH)),
            low((MB, rows, MODEL_WIDTH)),
            low((2, 2, length, LANES)),
            pltpu.VMEM((MB, length, rows), f32),
            low((LINE, rows, 2 * KEY_WIDTH)),
            low((LINE - 1, rows, 2 * KEY_WIDTH)),
            dma((4 * MB * SHARDS,)),
            dma((2,)),
            dma((2, 6)),
            dma((4,)),
            dma((2, MB * (SHARDS - 1))),
            dma((2, SHARDS - 1)),
            dma((2, 2)),
            dma((2, LINE)),
            dma((2, LINE - 1)),
        ]
        + line_sems(number)
        + [dma((3,))],
        compiler_params=pltpu.CompilerParams(
            collective_id=3, has_side_effects=True, vmem_limit_bytes=VMEM_LIMIT
        ),
        name="backward",
    )(query, starts, cosine, sine, middle, cotangent, gain, pairs, turned_rows, grad_blocks, *pieces, results, row_grads, output_weight)


DENSE = ("output", "query", "pair", "gain")
DENSE_PARTS = 4
FINE = 4
GATHER_AFTER = {4: ("output",), 9: ("query",), 13: ("pair", "gain")}
OUTPUT_AFTER = 19


def dense_kernel(
    turned_normed_src,
    turned_attn_src,
    query_low_src,
    pair_low_first,
    middle_low_src,
    gain,
    gain_grad,
    cosine,
    sine,
    middle_grad_src,
    tokens_src,
    middle_src,
    query_src,
    pair_src,
    pair_grad,
    results_src,
    gate_rest,
    up_rest,
    down_rest,
    input_grad_out,
    block_output,
    results_in,
    output_total,
    query_total,
    pair_total,
    gain_total,
    gate_total,
    up_total,
    down_total,
    turned_normed,
    turned_attn,
    query_low,
    middle_low,
    input_grad,
    middle_grad,
    tokens,
    middle,
    pair_low,
    pair_own,
    pair_other,
    land_left,
    query_weight,
    pair_weight,
    gains,
    send_output,
    send_query,
    own_output,
    own_query,
    own_pair,
    own_gain,
    other_output,
    other_query,
    other_pair,
    other_gain,
    across_output,
    across_query,
    across_pair,
    across_gain,
    sum_output,
    sum_query,
    sum_pair,
    sum_gain,
    near_output,
    near_query,
    near_pair,
    near_gain,
    far_output,
    far_query,
    far_pair,
    far_gain,
    own_gate,
    own_up,
    own_down,
    near_gate,
    near_up,
    near_down,
    far_gate,
    far_up,
    far_down,
    load_sem,
    core_sem,
    left_sem,
    result_sem,
    trade_sem,
    across_sem,
    near_sem,
    far_sem,
    back_sem,
    pass_sem,
    store_sem,
    emit_sem,
):
    r = types.SimpleNamespace(**locals())
    at = lambda kind, name: getattr(r, kind + "_" + name)
    place = Place()
    core, shard = place.core, place.shard
    rows = r.middle.shape[0]
    held = MODEL_WIDTH // SHARDS
    half = held // 2
    loads = [
        pltpu.make_async_copy(source, target, r.load_sem.at[i])
        for i, (source, target) in enumerate(
            (
                (r.gate_rest, r.own_gate),
                (r.up_rest, r.own_up),
                (r.down_rest, r.own_down),
                (r.query_src, r.query_weight),
                (r.pair_src, r.pair_weight),
                (r.pair_grad.at[:, core], r.pair_own),
                (r.middle_grad_src, r.middle_grad),
                (r.tokens_src, r.tokens),
                (r.middle_src.at[rows : 2 * rows], r.middle),
                (r.turned_attn_src, r.turned_attn),
                (r.middle_low_src, r.middle_low),
                (r.turned_normed_src, r.turned_normed),
                (r.query_low_src, r.query_low),
            )
        )
    ]
    for load in loads:
        load.start()
    greet_line(place)
    pair_sum = PairSum(
        place,
        lambda j: r.pair_own.at[j],
        lambda j: r.pair_grad.at[j, 1 - core],
        r.pair_other,
        r.land_left,
        r.core_sem,
        r.left_sem,
    )
    pair_sum.trade()

    pieces = []
    for name, parts in (("gate", FINE), ("up", FINE), ("down", 2 * FINE)):
        pieces += line_pieces(place, at("own", name), at("near", name), at("far", name), getattr(r, name + "_total"), parts)
    expert_pieces = len(pieces)
    for name in DENSE:
        parts = 1 if name == "gain" else DENSE_PARTS
        pieces += line_pieces(
            place, at("sum", name), at("near", name), at("far", name), getattr(r, name + "_total"), parts
        )
    line = Line(place, pieces, (r.near_sem, r.far_sem, r.back_sem, r.pass_sem, r.store_sem))
    loads[0].wait()
    line.ready(0)
    loads[5].wait()
    pair_sum.meet()
    for i in (1, 2):
        loads[i].wait()
    line.ready(*range(1, expert_pieces))

    def block(b, of_core):
        return pl.ds(pl.multiple_of(b * held + of_core * half, half), half)

    trades = {}

    def dense(name, turned, right, sent):
        index = DENSE.index(name)
        trades[name] = []
        for b in range(SHARDS):
            sent[b] = dot(turned[block(b, 1 - core)], right[...]).astype(bf16)
            copy = remote(sent.at[b], at("other", name).at[b], r.trade_sem, index * SHARDS + b, place.partner)
            copy.start()
            trades[name].append(copy)
        for b in range(SHARDS):
            at("own", name)[b] = dot(turned[block(b, core)], right[...]).astype(bf16)

    crossings = {}

    def meet(name):
        own, other, across = at("own", name), at("other", name), at("across", name)
        for b in range(SHARDS):
            trades[name][b].wait_recv()
            add_into(own.at[b], own.at[b], other.at[b])
        crossings[name] = []
        for k in range(1, SHARDS):
            index = DENSE.index(name) * (SHARDS - 1) + k - 1
            copy = remote(own.at[place.peer_index(k)], across.at[k - 1], r.across_sem, index, place.peer(k))
            copy.start()
            crossings[name].append(copy)

    def gather(name):
        for copy in crossings[name]:
            copy.wait_recv()
        across = at("across", name)
        add_into(at("sum", name), at("own", name).at[shard], *[across.at[k] for k in range(SHARDS - 1)])

    for load in loads[9:]:
        load.wait()
    dense("output", r.turned_attn, r.middle_low, r.send_output)
    dense("query", r.turned_normed, r.query_low, r.send_query)
    meet("output")
    line.serve([0])
    pair_sum.step(2)
    meet("query")
    pair_sum.step(3)
    for copy in trades["output"]:
        copy.wait_send()
    r.pair_low[0:rows] = r.pair_low_first[...]
    pair_sum.finish(r.pair_low.at[rows : 2 * rows], r.cosine, r.sine)
    dense("pair", r.turned_normed, r.pair_low, r.send_output.at[:, :, 0 : 2 * KEY_WIDTH])
    line.serve([1], [0])
    for load in loads[3:5] + loads[6:9]:
        load.wait()

    gain_one_grad = jnp.zeros((1, MODEL_WIDTH), f32)
    for m in range(MB):
        own = slice(m * rows, (m + 1) * rows)
        values = r.tokens[own].astype(f32)
        scale = lax.rsqrt(jnp.mean(values * values, axis=-1, keepdims=True) + eps)
        unit = values * scale
        normed_grad = dot(r.query_low[own], r.query_weight[...], NT) + dot(r.pair_low[own], r.pair_weight[...], NT)
        gain_one_grad = gain_one_grad + jnp.sum(normed_grad * unit, axis=0, keepdims=True)
        weighted = normed_grad * r.gain[0:1]
        inner = jnp.mean(weighted * unit, axis=-1, keepdims=True)
        r.input_grad[own] = r.middle_grad[own] + (weighted - unit * inner) * scale
        if m == 0:
            meet("pair")
            line.serve([2], [1])
    line.serve([3], [2])
    grad_emit = pltpu.make_async_copy(r.input_grad, r.input_grad_out, r.emit_sem.at[0])
    grad_emit.start()
    gain_two_grad = jnp.sum(r.gain_grad[...], axis=0, keepdims=True)
    stacked = jnp.concatenate(
        [gain_one_grad, gain_two_grad, jnp.zeros((LANES - 2, MODEL_WIDTH), f32)], axis=0
    )
    r.gains[...] = stacked.T.astype(bf16)
    trades["gain"] = []
    for b in range(SHARDS):
        source = r.gains.at[block(b, 1 - core)]
        index = DENSE.index("gain") * SHARDS + b
        trades["gain"].append(remote(source, r.other_gain.at[b], r.trade_sem, index, place.partner))
        trades["gain"][b].start()
        r.own_gain[b] = r.gains[block(b, core)]
    meet("gain")

    result_copies = []
    for k in range(1, SHARDS):
        source = r.results_src.at[1, place.peer_index(k)]
        result_copies.append(remote(source, r.results_in.at[k - 1], r.result_sem, k - 1, place.peer(k)))
        result_copies[-1].start()
    for copy in trades["pair"]:
        copy.wait_send()
    result_parts = [r.send_output.at[k, 0:rows] for k in range(SHARDS)]
    result_loads = [
        pltpu.make_async_copy(source, target, r.load_sem.at[13 + k])
        for k, (source, target) in enumerate(
            zip([r.results_src.at[1, shard]] + [r.results_in.at[k] for k in range(SHARDS - 1)], result_parts)
        )
    ]
    result_loads[0].start()

    def output_rows():
        for copy, load in zip(result_copies, result_loads[1:]):
            copy.wait_recv()
            load.start()
        total = r.middle[...]
        for load, part in zip(result_loads, result_parts):
            load.wait()
            total = total + part[...].astype(f32)
        r.block_output[...] = total.astype(bf16)

    number = len(pieces)
    first = expert_pieces
    spans = {}
    for name in DENSE:
        parts = 1 if name == "gain" else DENSE_PARTS
        spans[name] = range(first, first + parts)
        first += parts
    lag = 4
    for i in range(number + lag):
        line.serve(
            [i] if 4 <= i < number else [],
            [i - 1] if 4 <= i <= number else [],
            [i - lag] if i >= lag else [],
        )
        for name in GATHER_AFTER.get(i, ()):
            gather(name)
            line.ready(*spans[name])
        if i == OUTPUT_AFTER:
            output_rows()

    for name in DENSE:
        for copy in crossings[name]:
            copy.wait_send()
        if name in ("query", "gain"):
            for copy in trades[name]:
                copy.wait_send()
    for copy in result_copies:
        copy.wait_send()
    pair_sum.drain()
    grad_emit.wait()
    line.drain()


def dense_weights(vectors, streamed, query_weight, pair_weight, pair_grad, results, rests):
    dma = pltpu.SemaphoreType.DMA
    anywhere = pl.BlockSpec(memory_space=pl.ANY)
    vmem = pl.BlockSpec(memory_space=pltpu.VMEM)
    shape = jax.ShapeDtypeStruct
    rows = pair_grad.shape[2]
    low = lambda *s: pltpu.VMEM(s, bf16)
    held = MODEL_WIDTH // SHARDS
    half = held // 2
    widths = (MODEL_WIDTH, MODEL_WIDTH, 2 * KEY_WIDTH, LANES)
    tall = (MODEL_WIDTH, F_BLOCK)
    number = 4 * FINE + 3 * DENSE_PARTS + 1
    return pl.pallas_call(
        dense_kernel,
        in_specs=[anywhere] * 3 + [vmem, anywhere] + [vmem] * 4 + [anywhere] * (7 + len(streamed)),
        out_specs=[anywhere, vmem] + [anywhere] * 8,
        out_shape=[
            shape((MB * rows, MODEL_WIDTH), f32),
            shape((rows, MODEL_WIDTH), bf16),
            shape((SHARDS - 1, rows, MODEL_WIDTH), bf16),
        ]
        + [shape((held, w), bf16) for w in widths]
        + [
            shape((2 * MODEL_WIDTH, F_BLOCK), bf16),
            shape((2 * MODEL_WIDTH, F_BLOCK), bf16),
            shape((2 * F, MODEL_WIDTH), bf16),
        ],
        scratch_shapes=[
            low(MODEL_WIDTH, MB * rows),
            low(MODEL_WIDTH, MB * rows),
            low(MB * rows, MODEL_WIDTH),
            low(MB * rows, MODEL_WIDTH),
            pltpu.VMEM((MB * rows, MODEL_WIDTH), f32),
            pltpu.VMEM((MB * rows, MODEL_WIDTH), f32),
            low(MB * rows, MODEL_WIDTH),
            pltpu.VMEM((rows, MODEL_WIDTH), f32),
            low(MB * rows, 2 * KEY_WIDTH),
            low(LINE, rows, 2 * KEY_WIDTH),
            low(LINE, rows, 2 * KEY_WIDTH),
            low(LINE - 1, rows, 2 * KEY_WIDTH),
            low(*query_weight.shape),
            low(*pair_weight.shape),
            low(MODEL_WIDTH, LANES),
            low(SHARDS, half, MODEL_WIDTH),
            low(SHARDS, half, MODEL_WIDTH),
        ]
        + [low(SHARDS, half, w) for w in widths] * 2
        + [low(SHARDS - 1, half, w) for w in widths]
        + [low(half, w) for w in widths] * 3
        + [low(*tall), low(*tall), low(F, MODEL_WIDTH)] * 3
        + [dma((13 + SHARDS,)), dma((2, LINE)), dma((2, LINE - 1)), dma((2, SHARDS - 1)), dma((2, 4 * SHARDS)), dma((2, 4 * (SHARDS - 1)))]
        + line_sems(number)
        + [dma((1,))],
        compiler_params=pltpu.CompilerParams(
            collective_id=4, has_side_effects=True, vmem_limit_bytes=VMEM_LIMIT
        ),
        name="dense_weights",
    )(*vectors, *streamed, query_weight, pair_weight, pair_grad, results, *rests)


def widen_kernel(*refs):
    r = refs
    step = pl.program_id(0)
    parts, (shrink, dense, rows_in, gains, grad) = r[:4], (r[4], r[5:8], r[8:10], r[10], r[11])
    expand_out, shrink_out, dense_out, rows_out, gain_outs, grad_out = r[12], r[13], r[14:17], r[17], r[18:20], r[20]
    for i, ref in enumerate(parts):
        expand_out[:, i * F_BLOCK : (i + 1) * F_BLOCK] = ref[...].astype(f32)
    shrink_out[...] = shrink[...].astype(f32)
    grad_out[...] = grad[...]

    for source, target in zip(dense, dense_out):
        target[...] = source[...].astype(f32)

    for i in range(MB):

        @pl.when(step // (WIDEN_STEPS // MB) == i)
        def _():
            rows_out[...] = rows_in[i][...]

    @pl.when(step == 0)
    def _():
        turned = gains[...].astype(f32).T
        for i in range(2):
            gain_outs[i][...] = turned[i]


WIDEN_STEPS = 8


def widen(expand_parts, shrink, dense, rows, gains, grad):
    n = WIDEN_STEPS
    every = lambda a: pl.BlockSpec((a.shape[0] // n, a.shape[1]), lambda i: (i, 0))
    one = lambda a: pl.BlockSpec(a.shape, lambda i: (0, 0))
    size = MB * rows[0].shape[0] // n
    half = lambda m: pl.BlockSpec(
        (size, MODEL_WIDTH), lambda i: (jnp.clip(i - m * (n // MB), 0, n // MB - 1), 0)
    )
    shape = jax.ShapeDtypeStruct
    expand = shape((expand_parts[0].shape[0], 2 * F), f32)
    joined = shape((MB * rows[0].shape[0], MODEL_WIDTH), bf16)
    gain = shape((gains.shape[0],), f32)
    flat = pl.BlockSpec(gain.shape, lambda i: (0,))
    dense_out = [shape(a.shape, f32) for a in dense]
    return pl.pallas_call(
        widen_kernel,
        grid=(n,),
        in_specs=[every(a) for a in expand_parts]
        + [every(shrink)]
        + [every(a) for a in dense]
        + [half(m) for m in range(MB)]
        + [one(gains), every(grad)],
        out_specs=[every(expand), every(shrink)]
        + [every(a) for a in dense]
        + [every(joined), flat, flat, every(grad)],
        out_shape=[expand, shape(shrink.shape, f32), *dense_out, joined, gain, gain, shape(grad.shape, f32)],
        compiler_params=pltpu.CompilerParams(vmem_limit_bytes=VMEM_LIMIT),
        name="widen",
    )(*expand_parts, shrink, *dense, *rows, gains, grad)


def shards(
    tokens,
    doc_starts,
    routes,
    gates,
    attn_gain,
    w_q,
    key_value_weight,
    w_o,
    moe_gain,
    expert_in,
    expert_out,
    cotangent,
):
    links = Links()
    rows = tokens.shape[2]
    length = rows * links.contexts
    held = expert_in.shape[0]
    chained = links.chips == LINE and links.shards == SHARDS and held == 2
    width = w_q.shape[0]
    flat_tokens = tokens.reshape(MB * rows, MODEL_WIDTH)
    if chained:
        flat_cotangent = cotangent.reshape(MB * rows, MODEL_WIDTH)
        starts = doc_starts[:, 0]
        (
            turned_normed,
            query,
            turned_attn,
            middle,
            gains,
            cosine,
            sine,
            pair_weight,
            query_weight,
            output_weight,
            pairs,
            turned_rows,
            grad_blocks,
            result_blocks,
            row_grad_blocks,
            active,
            gate,
            up,
        ) = forward(
            flat_tokens,
            routes.transpose(0, 1, 3, 2),
            gates.transpose(0, 1, 3, 2),
            jnp.stack([attn_gain, moe_gain]),
            flat_cotangent,
            starts,
            rotation_constants(length),
            (key_value_weight, w_q, w_o),
            expert_in,
            expert_out,
        )
        result_blocks = result_blocks.reshape(grad_blocks.shape)
        row_grad_blocks = row_grad_blocks.reshape(grad_blocks.shape)
        (
            query_low,
            pair_low,
            middle_low,
            middle_grad,
            gain_two_grad,
            output_first,
            gate_first,
            up_first,
            gate_rest,
            up_rest,
            down_rest,
            pair_grad,
        ) = backward(
            query,
            starts,
            cosine,
            sine,
            middle,
            flat_cotangent,
            gains,
            pairs,
            turned_rows,
            grad_blocks,
            (active, gate, up),
            result_blocks,
            row_grad_blocks,
            output_weight,
        )
        (
            input_grad,
            output_second,
            _,
            output_total,
            query_total,
            pair_total,
            gain_total,
            gate_second,
            up_second,
            shrink_total,
        ) = dense_weights(
            (
                turned_normed,
                turned_attn,
                query_low,
                pair_low,
                middle_low,
                gains,
                gain_two_grad,
                cosine,
                sine,
            ),
            (middle_grad, flat_tokens, middle),
            query_weight,
            pair_weight,
            pair_grad.reshape(LINE, 2, rows, 2 * KEY_WIDTH),
            result_blocks,
            (gate_rest, up_rest, down_rest.reshape(F, MODEL_WIDTH)),
        )
        (
            expand_total,
            shrink_total,
            output_total,
            query_total,
            pair_total,
            block_output,
            gain_one_total,
            gain_two_total,
            input_grad,
        ) = widen(
            (gate_first, gate_second, up_first, up_second),
            shrink_total,
            (output_total, query_total, pair_total),
            (output_first, output_second),
            gain_total,
            input_grad,
        )
        return (
            block_output.reshape(MB, 1, rows, MODEL_WIDTH),
            input_grad.reshape(MB, 1, rows, MODEL_WIDTH),
            gain_one_total,
            query_total,
            pair_total,
            output_total,
            gain_two_total,
            expand_total.reshape(held, MODEL_WIDTH, 2 * F),
            shrink_total.reshape(held, F, MODEL_WIDTH),
        )

    positions = links.context * rows + jnp.arange(rows, dtype=jnp.int32)
    cosine, sine = rotation_tables(positions)
    key_places = jnp.arange(length, dtype=jnp.int32)
    flat_values = flat_tokens.astype(f32)
    scale_one = lax.rsqrt(jnp.mean(flat_values * flat_values, axis=-1, keepdims=True) + eps)
    unit_one = flat_values * scale_one
    expert_ids = jnp.arange(E, dtype=jnp.int32)
    chosen = (routes.reshape(MB, rows, TOP)[..., None] == expert_ids).astype(f32)
    combine = jnp.sum(gates.reshape(MB, rows, TOP)[..., None] * chosen, axis=2)
    gather = lambda w: lax.all_gather(w, "fsdp", axis=0, tiled=True)
    pair_weight, query_weight, output_weight = gather(key_value_weight), gather(w_q), gather(w_o)
    gain_one, gain_two = gather(attn_gain).astype(f32), gather(moe_gain).astype(f32)
    normed = (unit_one * gain_one).astype(bf16)
    both = lambda table: jnp.concatenate([table] * MB)
    own_pairs = rotate_columns(dot(normed, pair_weight), both(cosine), both(sine), KEY_WIDTH)
    query = rotate_columns(dot(normed, query_weight), both(cosine), both(sine), MODEL_WIDTH)
    own_pairs = own_pairs.reshape(MB, rows, 2 * KEY_WIDTH)
    pairs = lax.all_gather(own_pairs, "ctx", axis=1, tiled=True)

    combine = jnp.concatenate([combine] + [links.across(combine, k) for k in range(1, links.shards)], axis=1)
    combine = lax.dynamic_slice_in_dim(combine, links.shard * held, held, 2)
    combine = combine.transpose(0, 2, 1)[..., None]

    biases, biases_turned = [], []
    for m in range(MB):
        starts = doc_starts[m, 0]
        begin = jnp.max(jnp.where(starts[None, :] <= positions[:, None], starts[None, :], 0), axis=1)
        seen = (key_places[None, :] <= positions[:, None]) & (key_places[None, :] >= begin[:, None])
        biases.append(jnp.where(seen, 0.0, -1e30).astype(f32))
        places, begins = jnp.tile(positions, GROUP), jnp.tile(begin, GROUP)
        seen = (key_places[:, None] <= places[None, :]) & (key_places[:, None] >= begins[None, :])
        biases_turned.append(jnp.where(seen, 0.0, -1e30).astype(f32))

    middles, attns, results, row_grads = [], [], [], []
    rows_kept, grads_kept, pieces_kept = [], [], []
    for m in range(MB):
        own = slice(m * rows, (m + 1) * rows)
        attn = attention_forward(m, query, pairs, biases[m])
        middle = flat_tokens[own].astype(f32) + dot(attn, output_weight)
        scale_two = lax.rsqrt(jnp.mean(middle * middle, axis=-1, keepdims=True) + eps)
        moe_in = (middle * scale_two * gain_two).astype(bf16)
        out_grad = cotangent[m, 0]
        row_parts = [moe_in] + [links.across(moe_in, k) for k in range(1, links.shards)]
        grad_parts = [out_grad] + [links.across(out_grad, k) for k in range(1, links.shards)]
        result, row_grad, pieces = experts(row_parts, grad_parts, combine[m], expert_in, expert_out)
        for parts, sums in ((result, results), (row_grad, row_grads)):
            total = parts[0].astype(f32)
            for k in range(1, links.shards):
                total = total + links.across(parts[k], k).astype(f32)
            sums.append(total)
        middles.append(middle)
        attns.append(attn)
        rows_kept += row_parts
        grads_kept += grad_parts
        pieces_kept.append(pieces)
    merge = lambda items: jnp.concatenate(items, axis=0)
    expert_grads = expert_weights(
        merge(rows_kept), merge(grads_kept), *[merge([p[i] for p in pieces_kept]) for i in range(3)], held
    )
    expert_grads = [g.reshape(-1, g.shape[-1]) for g in expert_grads]
    outputs = [(middles[m] + results[m]).astype(bf16) for m in range(MB)]

    input_grads, query_lows, pair_lows, middle_lows = [], [], [], []
    gain_one_grad, gain_two_grad = 0.0, 0.0
    for m in range(MB):
        own = slice(m * rows, (m + 1) * rows)
        scale_two = lax.rsqrt(jnp.mean(middles[m] * middles[m], axis=-1, keepdims=True) + eps)
        unit_two = middles[m] * scale_two
        moe_in_grad = row_grads[m]
        gain_two_grad = gain_two_grad + jnp.sum(moe_in_grad * unit_two, axis=0)
        weighted = moe_in_grad * gain_two
        inner = jnp.mean(weighted * unit_two, axis=-1, keepdims=True)
        middle_grad = cotangent[m, 0].astype(f32) + (weighted - unit_two * inner) * scale_two
        middle_low = middle_grad.astype(bf16)
        attn_grad = dot(middle_low, output_weight, NT).astype(bf16)
        query_low, pair_grad = attention_backward(
            m, query, cosine, sine, pairs, biases_turned[m], attn_grad
        )
        parts = [lax.psum_scatter(pair_grad, "ctx", scatter_dimension=0, tiled=True)]
        pair_low = pair_gradient(parts, cosine, sine)
        normed_grad = dot(query_low, query_weight, NT) + dot(pair_low, pair_weight, NT)
        gain_one_grad = gain_one_grad + jnp.sum(normed_grad * unit_one[own], axis=0)
        weighted = normed_grad * gain_one
        inner = jnp.mean(weighted * unit_one[own], axis=-1, keepdims=True)
        residual_grad = (weighted - unit_one[own] * inner) * scale_one[own]
        input_grads.append(middle_grad + residual_grad)
        query_lows.append(query_low)
        pair_lows.append(pair_low)
        middle_lows.append(middle_low)

    join = lambda items: jnp.concatenate(items, axis=0)

    output_grad = dot(join(attns), join(middle_lows), TN).astype(bf16)
    query_grad = dot(normed, join(query_lows), TN).astype(bf16)
    pair_weight_grad = dot(normed, join(pair_lows), TN).astype(bf16)
    gain_grads = jnp.stack([gain_one_grad, gain_two_grad], axis=1)
    gain_grads = jnp.pad(gain_grads, ((0, 0), (0, LANES - 2))).astype(bf16)
    dense_grads = [output_grad, query_grad, jnp.concatenate([pair_weight_grad, gain_grads], axis=1)]
    totals = [lax.psum(g, "ctx") for g in expert_grads]
    for g in dense_grads:
        part = lax.psum_scatter(g, "fsdp", scatter_dimension=0, tiled=True)
        totals.append(lax.psum(part, "ctx"))
    gate_total, up_total, down_total, output_total, query_total, pair_total = [t.astype(f32) for t in totals]
    expand_total = jnp.concatenate([gate_total, up_total], axis=1)

    return (
        jnp.stack(outputs)[:, None],
        jnp.stack(input_grads)[:, None],
        pair_total[:, 2 * KEY_WIDTH],
        query_total,
        pair_total[:, : 2 * KEY_WIDTH],
        output_total,
        pair_total[:, 2 * KEY_WIDTH + 1],
        expand_total.reshape(held, MODEL_WIDTH, 2 * F),
        down_total.reshape(held, F, MODEL_WIDTH),
    )


def solution(mesh):
    return jax.shard_map(
        shards,
        mesh=mesh,
        in_specs=(
            P(None, "fsdp", "ctx", None),
            P(None, "fsdp", None),
            P(None, "fsdp", "ctx", None),
            P(None, "fsdp", "ctx", None),
            P("fsdp"),
            P("fsdp", None),
            P("fsdp", None),
            P("fsdp", None),
            P("fsdp"),
            P("fsdp", None, None),
            P("fsdp", None, None),
            P(None, "fsdp", "ctx", None),
        ),
        out_specs=(
            P(None, "fsdp", "ctx", None),
            P(None, "fsdp", "ctx", None),
            P("fsdp"),
            P("fsdp", None),
            P("fsdp", None),
            P("fsdp", None),
            P("fsdp"),
            P("fsdp", None, None),
            P("fsdp", None, None),
        ),
        check_vma=False,
    )
```

```python
import functools
import types

import jax
import jax.numpy as jnp
import numpy as np
from jax import lax
from jax.experimental import pallas as pl
from jax.experimental.pallas import tpu as pltpu
from jax.sharding import PartitionSpec as P

MODEL_WIDTH = 1536
QUERY_HEADS = 24
KEY_VALUE_HEADS = 8
HEAD_SIZE = 64
GROUP = QUERY_HEADS // KEY_VALUE_HEADS
KEY_WIDTH = KEY_VALUE_HEADS * HEAD_SIZE
F = 512
E = 8
TOP = 4
MB = 2
LANES = 128
PAIRS = KEY_WIDTH // LANES
PAIR_QUERY = 2 * GROUP * HEAD_SIZE
F_BLOCK = 256
VMEM_LIMIT = 60 * 1024 * 1024

eps = 1e-05
theta = 10000.0

NT = (((1,), (1,)), ((), ()))
TN = (((0,), (0,)), ((), ()))
bf16 = jnp.bfloat16
f32 = jnp.float32


def dot(left, right, dims=(((1,), (0,)), ((), ()))):
    return lax.dot_general(left, right, dims, preferred_element_type=f32)


def rotation_tables(positions):
    frequency = theta ** (-jnp.arange(0, HEAD_SIZE, 2, dtype=f32) / HEAD_SIZE)
    angles = positions.astype(f32)[:, None] * frequency[None, :]
    cosine, sine = jnp.cos(angles), jnp.sin(angles)
    repeat = LANES // HEAD_SIZE
    cosine = jnp.concatenate([cosine, cosine] * repeat, axis=1)
    sine = jnp.concatenate([-sine, sine] * repeat, axis=1)
    return cosine, sine


def rotation_constants(length):
    frequency = theta ** (-np.arange(0, HEAD_SIZE, 2, dtype=np.float64) / HEAD_SIZE)
    angles = np.arange(length, dtype=np.float64)[:, None] * frequency[None, :]
    cosine, sine = np.cos(angles), np.sin(angles)
    repeat = LANES // HEAD_SIZE
    cosine = np.concatenate([cosine, cosine] * repeat, axis=1)
    sine = np.concatenate([-sine, sine] * repeat, axis=1)
    return jnp.asarray(np.stack([cosine, sine]).astype(np.float32))


def visible_bias(starts, m, context, shape, query_axis):
    rows = shape[query_axis]
    narrow = (rows, 1) if query_axis == 0 else (1, rows)
    query = context * rows + lax.broadcasted_iota(jnp.int32, narrow, query_axis)
    begin = jnp.zeros(narrow, jnp.int32)
    for i in range(starts.shape[1]):
        begin = jnp.maximum(begin, jnp.where(query >= starts[m, i], starts[m, i], 0))
    key = lax.broadcasted_iota(jnp.int32, shape, 1 - query_axis)
    return jnp.where((key <= query) & (key >= begin), 0.0, -1e30).astype(f32)


def lane_index(shape):
    return lax.broadcasted_iota(jnp.int32, shape, 1)


def rotate(tile, cosine, sine):
    half = HEAD_SIZE // 2
    ahead = pltpu.roll(tile, LANES - half, 1)
    behind = pltpu.roll(tile, half, 1)
    first = lane_index(tile.shape) % HEAD_SIZE < half
    return tile * cosine + jnp.where(first, ahead, behind) * sine


def rotate_columns_kernel(rotated, values_ref, cosine_ref, sine_ref, out_ref):
    cosine, sine = cosine_ref[...], sine_ref[...]
    for i in range(values_ref.shape[1] // LANES):
        cols = slice(i * LANES, (i + 1) * LANES)
        tile = values_ref[:, cols]
        if i < rotated // LANES:
            tile = rotate(tile, cosine, sine)
        out_ref[:, cols] = tile.astype(bf16)


def rotate_columns(values, cosine, sine, rotated):
    return pl.pallas_call(
        functools.partial(rotate_columns_kernel, rotated),
        out_shape=jax.ShapeDtypeStruct(values.shape, bf16),
        compiler_params=pltpu.CompilerParams(vmem_limit_bytes=VMEM_LIMIT),
        name="rotate_columns",
    )(values, cosine, sine)


def pair_gradient_kernel(count, cosine_ref, sine_ref, *refs):
    out_ref = refs[-1]
    cosine, sine = cosine_ref[...], sine_ref[...]
    for i in range(2 * KEY_WIDTH // LANES):
        cols = slice(i * LANES, (i + 1) * LANES)
        total = refs[0][:, cols].astype(f32)
        for ref in refs[1:count]:
            total = total + ref[:, cols].astype(f32)
        if i < KEY_WIDTH // LANES:
            total = rotate(total, cosine, -sine)
        out_ref[:, cols] = total.astype(bf16)


def pair_gradient(parts, cosine, sine):
    return pl.pallas_call(
        functools.partial(pair_gradient_kernel, len(parts)),
        out_shape=jax.ShapeDtypeStruct(parts[0].shape, bf16),
        compiler_params=pltpu.CompilerParams(vmem_limit_bytes=VMEM_LIMIT),
        name="pair_gradient",
    )(cosine, sine, *parts)


def grouped(tiles, half):
    mine = lane_index(tiles[0].shape) // HEAD_SIZE == half
    rows = []
    for j in range(GROUP * half, GROUP * half + GROUP):
        tile = tiles[j // 2]
        if j % 2 != half:
            tile = pltpu.roll(tile, HEAD_SIZE, 1)
        rows.append(jnp.where(mine, tile, 0.0))
    return jnp.concatenate(rows, axis=0).astype(bf16)


def ungrouped(per_half, rows):
    heads = []
    for j in range(2 * GROUP):
        half, place = j // GROUP, j % GROUP
        tile = per_half[half][place * rows : (place + 1) * rows]
        if j % 2 != half:
            tile = pltpu.roll(tile, HEAD_SIZE, 1)
        heads.append(tile)
    low = lane_index(heads[0].shape) < HEAD_SIZE
    return [jnp.where(low, heads[2 * i], heads[2 * i + 1]) for i in range(GROUP)]


def query_tiles(query_ref):
    scale = 1.0 / HEAD_SIZE
    return [query_ref[:, i * LANES : (i + 1) * LANES].astype(f32) * scale for i in range(GROUP)]


def attention_pair(tiles, key, value, bias):
    rows = bias.shape[0]
    results = []
    for half in range(2):
        scores = dot(grouped(tiles, half), key, NT)
        scores = jnp.concatenate(
            [scores[g * rows : (g + 1) * rows] + bias for g in range(GROUP)], axis=0
        )
        peak = jnp.max(scores, axis=1, keepdims=True)
        weights = jnp.exp(scores - peak)
        total = jnp.sum(weights, axis=1, keepdims=True)
        results.append(dot(weights.astype(bf16), value) / total)
    return ungrouped(results, rows)


def attention_forward_kernel(query_ref, key_ref, value_ref, bias_ref, out_ref):
    tiles = attention_pair(query_tiles(query_ref), key_ref[...], value_ref[...], bias_ref[...])
    for i, tile in enumerate(tiles):
        out_ref[:, i * LANES : (i + 1) * LANES] = tile.astype(bf16)


def attention_forward(m, query, pairs, bias):
    rows, length = bias.shape
    return pl.pallas_call(
        attention_forward_kernel,
        grid=(PAIRS,),
        in_specs=[
            pl.BlockSpec((rows, PAIR_QUERY), lambda p: (m, p)),
            pl.BlockSpec((None, length, LANES), lambda p: (m, 0, p)),
            pl.BlockSpec((None, length, LANES), lambda p: (m, 0, p + PAIRS)),
            pl.BlockSpec((rows, length), lambda p: (0, 0)),
        ],
        out_specs=pl.BlockSpec((rows, PAIR_QUERY), lambda p: (0, p)),
        out_shape=jax.ShapeDtypeStruct((rows, MODEL_WIDTH), bf16),
        compiler_params=pltpu.CompilerParams(vmem_limit_bytes=VMEM_LIMIT),
        cost_estimate=pl.CostEstimate(
            flops=16 * rows * length * MODEL_WIDTH,
            bytes_accessed=4 * length * MODEL_WIDTH,
            transcendentals=rows * length * QUERY_HEADS,
        ),
        name="attention_forward",
    )(query, pairs, pairs, bias)


def attention_pair_gradient(tiles, grads, key, value, bias):
    rows = tiles[0].shape[0]
    key_grad, value_grad = None, None
    query_grads = []
    for half in range(2):
        query = grouped(tiles, half)
        grad = grouped(grads, half)
        scores = dot(key, query, NT) + bias
        weights = jnp.exp(scores - jnp.max(scores, axis=0, keepdims=True))
        prob = weights * (1.0 / jnp.sum(weights, axis=0, keepdims=True))
        prob_grad = dot(value, grad, NT)
        delta = jnp.sum(prob * prob_grad, axis=0, keepdims=True)
        score_grad = (prob * (prob_grad - delta)).astype(bf16)
        value_part = dot(prob.astype(bf16), grad)
        key_part = dot(score_grad, query)
        value_grad = value_part if half == 0 else value_grad + value_part
        key_grad = key_part if half == 0 else key_grad + key_part
        query_grads.append(dot(score_grad, key, TN))
    return ungrouped(query_grads, rows), key_grad, value_grad


def attention_backward_kernel(
    query_ref, cosine_ref, sine_ref, key_ref, value_ref, bias_ref, grad_ref, query_out, pair_out
):
    cosine, sine = cosine_ref[...], sine_ref[...]
    grads = [grad_ref[:, i * LANES : (i + 1) * LANES].astype(f32) for i in range(GROUP)]
    query_grads, key_grad, value_grad = attention_pair_gradient(
        query_tiles(query_ref), grads, key_ref[...], value_ref[...], bias_ref[...]
    )
    for i, tile in enumerate(query_grads):
        tile = rotate(tile * (1.0 / HEAD_SIZE), cosine, -sine)
        query_out[:, i * LANES : (i + 1) * LANES] = tile.astype(bf16)
    first = pl.multiple_of(pl.program_id(0) * LANES, LANES)
    pair_out[:, pl.ds(first, LANES)] = key_grad.astype(bf16)
    pair_out[:, pl.ds(first + KEY_WIDTH, LANES)] = value_grad.astype(bf16)


def attention_backward(m, query, cosine, sine, pairs, bias, grad):
    rows = cosine.shape[0]
    length = pairs.shape[1]
    whole = lambda shape: pl.BlockSpec(shape, lambda p: (0, 0))
    return pl.pallas_call(
        attention_backward_kernel,
        grid=(PAIRS,),
        in_specs=[
            pl.BlockSpec((rows, PAIR_QUERY), lambda p: (m, p)),
            whole((rows, LANES)),
            whole((rows, LANES)),
            pl.BlockSpec((None, length, LANES), lambda p: (m, 0, p)),
            pl.BlockSpec((None, length, LANES), lambda p: (m, 0, p + PAIRS)),
            whole(bias.shape),
            pl.BlockSpec((rows, PAIR_QUERY), lambda p: (0, p)),
        ],
        out_specs=[
            pl.BlockSpec((rows, PAIR_QUERY), lambda p: (0, p)),
            whole((length, 2 * KEY_WIDTH)),
        ],
        out_shape=[
            jax.ShapeDtypeStruct((rows, MODEL_WIDTH), bf16),
            jax.ShapeDtypeStruct((length, 2 * KEY_WIDTH), bf16),
        ],
        compiler_params=pltpu.CompilerParams(vmem_limit_bytes=VMEM_LIMIT),
        cost_estimate=pl.CostEstimate(
            flops=40 * rows * length * MODEL_WIDTH,
            bytes_accessed=8 * length * MODEL_WIDTH,
            transcendentals=rows * length * QUERY_HEADS,
        ),
        name="attention_backward",
    )(query, cosine, sine, pairs, pairs, bias, grad)


def expert_block(inputs, out_grad, combine, gate_weight, up_weight, down_weight):
    gate = dot(inputs, gate_weight)
    up = dot(inputs, up_weight)
    sigmoid = jax.nn.sigmoid(gate)
    silu = gate * sigmoid
    active = (silu * up * combine).astype(bf16)
    active_grad = dot(out_grad, down_weight, NT) * combine
    gate_grad = (active_grad * up * sigmoid * (1.0 + gate * (1.0 - sigmoid))).astype(bf16)
    up_grad = (active_grad * silu).astype(bf16)
    result = dot(active, down_weight)
    row_grad = dot(gate_grad, gate_weight, NT) + dot(up_grad, up_weight, NT)
    return active, gate_grad, up_grad, result, row_grad


def experts_kernel(parts, rows, steps, combine_ref, gate_ref, up_ref, down_ref, *refs):
    rows_in, grads_in = refs[:parts], refs[parts : 2 * parts]
    refs = refs[2 * parts :]
    results, row_grads = refs[:parts], refs[parts : 2 * parts]
    active_out, gate_out, up_out, rows_all, grads_all, result_sum, grad_sum = refs[2 * parts :]
    step = pl.program_id(0) * pl.num_programs(1) + pl.program_id(1)

    @pl.when(step == 0)
    def _():
        for k in range(parts):
            place = slice(k * rows, (k + 1) * rows)
            rows_all[place] = rows_in[k][...]
            grads_all[place] = grads_in[k][...]
        result_sum[...] = jnp.zeros_like(result_sum)
        grad_sum[...] = jnp.zeros_like(grad_sum)

    inputs, out_grad, combine = rows_all[...], grads_all[...], combine_ref[0]
    active, gate_grad, up_grad, result, row_grad = expert_block(
        inputs, out_grad, combine, gate_ref[0], up_ref[0], down_ref[0]
    )
    active_out[...] = active
    gate_out[...] = gate_grad
    up_out[...] = up_grad
    result_sum[...] += result
    grad_sum[...] += row_grad

    @pl.when(step == steps - 1)
    def _():
        for k in range(parts):
            place = slice(k * rows, (k + 1) * rows)
            results[k][...] = result_sum[place].astype(bf16)
            row_grads[k][...] = grad_sum[place].astype(bf16)


def experts(row_parts, grad_parts, combine, expert_in, expert_out):
    parts = len(row_parts)
    rows = row_parts[0].shape[0]
    held = expert_in.shape[0]
    tokens = parts * rows
    blocks = F // F_BLOCK
    whole = pl.BlockSpec((rows, MODEL_WIDTH), lambda e, b: (0, 0))
    piece = pl.BlockSpec((tokens, F_BLOCK), lambda e, b: (0, e * blocks + b))
    row_shape = jax.ShapeDtypeStruct((rows, MODEL_WIDTH), bf16)
    piece_shape = jax.ShapeDtypeStruct((tokens, held * F), bf16)
    out = pl.pallas_call(
        functools.partial(experts_kernel, parts, rows, held * blocks),
        grid=(held, blocks),
        in_specs=[
            pl.BlockSpec((1, tokens, 1), lambda e, b: (e, 0, 0)),
            pl.BlockSpec((1, MODEL_WIDTH, F_BLOCK), lambda e, b: (e, 0, b)),
            pl.BlockSpec((1, MODEL_WIDTH, F_BLOCK), lambda e, b: (e, 0, b + blocks)),
            pl.BlockSpec((1, F_BLOCK, MODEL_WIDTH), lambda e, b: (e, b, 0)),
        ]
        + [whole] * (2 * parts),
        out_specs=[whole] * (2 * parts) + [piece] * 3,
        out_shape=[row_shape] * (2 * parts) + [piece_shape] * 3,
        scratch_shapes=[
            pltpu.VMEM((tokens, MODEL_WIDTH), bf16),
            pltpu.VMEM((tokens, MODEL_WIDTH), bf16),
            pltpu.VMEM((tokens, MODEL_WIDTH), f32),
            pltpu.VMEM((tokens, MODEL_WIDTH), f32),
        ],
        compiler_params=pltpu.CompilerParams(vmem_limit_bytes=VMEM_LIMIT),
        cost_estimate=pl.CostEstimate(
            flops=12 * tokens * held * MODEL_WIDTH * F,
            bytes_accessed=6 * held * MODEL_WIDTH * F + 20 * tokens * MODEL_WIDTH,
            transcendentals=tokens * held * F,
        ),
        name="experts",
    )(combine, expert_in, expert_in, expert_out, *row_parts, *grad_parts)
    return out[:parts], out[parts : 2 * parts], out[2 * parts :]


def expert_weights_kernel(rows_ref, grads_ref, active_ref, gate_ref, up_ref, gate_out, up_out, down_out, turned):
    step = pl.program_id(0) * pl.num_programs(1) + pl.program_id(1)

    @pl.when(step == 0)
    def _():
        turned[...] = rows_ref[...].T

    gate_out[0] = dot(turned[...], gate_ref[...]).astype(bf16)
    up_out[0] = dot(turned[...], up_ref[...]).astype(bf16)
    down_out[0] = dot(active_ref[...], grads_ref[...], TN).astype(bf16)


def expert_weights(rows, grads, active, gate, up, held):
    tokens = rows.shape[0]
    blocks = F // F_BLOCK
    whole = pl.BlockSpec((tokens, MODEL_WIDTH), lambda e, b: (0, 0))
    piece = pl.BlockSpec((tokens, F_BLOCK), lambda e, b: (0, e * blocks + b))
    wide = pl.BlockSpec((1, MODEL_WIDTH, F_BLOCK), lambda e, b: (e, 0, b))
    return pl.pallas_call(
        expert_weights_kernel,
        grid=(held, blocks),
        in_specs=[whole] * 2 + [piece] * 3,
        out_specs=[wide, wide, pl.BlockSpec((1, F_BLOCK, MODEL_WIDTH), lambda e, b: (e, b, 0))],
        out_shape=[
            jax.ShapeDtypeStruct((held, MODEL_WIDTH, F), bf16),
            jax.ShapeDtypeStruct((held, MODEL_WIDTH, F), bf16),
            jax.ShapeDtypeStruct((held, F, MODEL_WIDTH), bf16),
        ],
        scratch_shapes=[pltpu.VMEM((MODEL_WIDTH, tokens), bf16)],
        compiler_params=pltpu.CompilerParams(vmem_limit_bytes=VMEM_LIMIT),
        cost_estimate=pl.CostEstimate(
            flops=6 * tokens * held * MODEL_WIDTH * F,
            bytes_accessed=6 * held * MODEL_WIDTH * F + 8 * tokens * MODEL_WIDTH,
            transcendentals=0,
        ),
        name="expert_weights",
    )(rows, grads, active, gate, up)


class Links:
    def __init__(self):
        self.shards = lax.axis_size("fsdp")
        self.contexts = lax.axis_size("ctx")
        self.chips = self.contexts // 2
        self.shard = lax.axis_index("fsdp")
        self.context = lax.axis_index("ctx")
        self.chip = self.context // 2
        self.core = self.context % 2

    def across(self, array, k):
        return lax.ppermute(array, "fsdp", [(i, i ^ k) for i in range(self.shards)])

    def other_core(self, array):
        return lax.ppermute(array, "ctx", [(i, i ^ 1) for i in range(self.contexts)])

    def shift(self, array, s):
        n = self.contexts
        return lax.ppermute(array, "ctx", [(i, (i + 2 * s) % n) for i in range(n)])


MESH = pl.DeviceIdType.MESH
LINE = 4


class Place:
    def __init__(self):
        self.shard, self.context = lax.axis_index("fsdp"), lax.axis_index("ctx")
        self.core, self.chip = self.context % 2, self.context // 2
        self.partner = {"ctx": 2 * self.chip + 1 - self.core}

    def peer_index(self, k):
        x, y = (self.shard % 2 + k % 2) % 2, (self.shard // 2 + k // 2) % 2
        return 2 * y + x

    def peer(self, k):
        return {"fsdp": self.peer_index(k)}

    def chip_device(self, chip):
        return {"ctx": 2 * chip + self.core}


def remote(source, target, sems, index, device):
    return pltpu.make_async_remote_copy(
        src_ref=source,
        dst_ref=target,
        send_sem=sems.at[0, index],
        recv_sem=sems.at[1, index],
        device_id=device,
        device_id_type=MESH,
    )


def greet(device):
    pl.semaphore_signal(pltpu.get_barrier_semaphore(), inc=1, device_id=device, device_id_type=MESH)


SHARDS = 4
GAIN_ROWS = 16


class Square:
    def __init__(self, place, blocks, direct_sem, relay_sem, base=0):
        half = blocks.shape[1] // 2
        own = blocks.at[place.shard]
        self.directs = [remote(own, own, direct_sem, base + k - 1, place.peer(k)) for k in (1, 2)]
        self.relays = []
        for k in (1, 2):
            spot = blocks.at[place.peer_index(k), (k - 1) * half : k * half]
            self.relays.append(remote(spot, spot, relay_sem, base + k - 1, place.peer(3 - k)))

    def start(self):
        for copy in self.directs:
            copy.start()

    def pass_on(self):
        for direct, relay in zip(self.directs, self.relays):
            direct.wait_recv()
            relay.start()

    def finish(self):
        for copy in self.relays:
            copy.wait_recv()

    def drain(self):
        for copy in self.directs + self.relays:
            copy.wait_send()


LAST = LINE - 1
WIDE = 4


def forward_kernel(
    tokens,
    routes,
    gates,
    gain_pair,
    cotangent,
    starts,
    tables,
    pair_src,
    query_src,
    output_src,
    expand_src,
    shrink_src,
    turned_normed_out,
    query_rows_out,
    turned_attn_out,
    middle_out,
    gain_rows_out,
    cosine,
    sine,
    pair_out,
    query_out,
    output_out,
    pairs,
    turned_out,
    grads_out,
    results_out,
    row_grads_out,
    active_out,
    gate_out,
    up_out,
    turned_normed,
    query,
    turned_attn,
    middle,
    gains,
    turned_rows,
    pair_weight,
    query_weight,
    output_weight,
    expand,
    shrink,
    own_pairs,
    normed,
    combine_in,
    combine_own,
    attn,
    bias,
    combine,
    rows_all,
    grads_all,
    result_sum,
    grad_sum,
    key_value,
    load_sem,
    table_sem,
    store_sem,
    expert_sem,
    gain_sem,
    combine_sem,
    direct_sem,
    relay_sem,
    pass_sem,
    right_sem,
    left_sem,
    core_sem,
    own_sem,
    square_direct_sem,
    square_relay_sem,
    key_sem,
    emit_sem,
    last_sem,
):
    r = types.SimpleNamespace(**locals())
    place = Place()
    core, chip, shard = place.core, place.chip, place.shard
    local = pltpu.make_async_copy
    rows = r.cosine.shape[0]
    wide = SHARDS * rows
    held = r.pair_src.shape[0]
    half, quarter = held // 2, held // 4
    greet_line(place)
    length = r.bias.shape[2]

    def rows_of(owner, piece, size):
        return pl.ds(pl.multiple_of(owner * held + core * half, half) + piece, size)

    sources = (r.pair_src, r.query_src, r.output_src)
    weights = (r.pair_weight, r.query_weight, r.output_weight)
    weight_outs = (r.pair_out, r.query_out, r.output_out)
    loads, directs, relays, passes, stores = [], [], [], [], []
    for w in range(3):
        weight = weights[w]
        own_rows = pl.ds(pl.multiple_of(shard * held, held), held)
        loads.append(local(sources[w], weight.at[own_rows], r.load_sem.at[w]))
        stores.append(local(weight, weight_outs[w], r.store_sem.at[w]))
        mine = sources[w].at[pl.ds(pl.multiple_of(core * half, half), half)]
        spot = weight.at[rows_of(shard, 0, half)]
        directs.append([remote(mine, spot, r.direct_sem, 2 * w + k - 1, place.peer(k)) for k in (1, 2)])
        relay, onward = [], []
        for k in (1, 2):
            spot = weight.at[rows_of(place.peer_index(k), (k - 1) * quarter, quarter)]
            relay.append(remote(spot, spot, r.relay_sem, 2 * w + k - 1, place.peer(3 - k)))
            spot = weight.at[rows_of(place.peer_index(k), 0, half)]
            onward.append(remote(spot, spot, r.pass_sem, 4 * w + k - 1, place.partner))
        for k in (1, 2):
            spot = weight.at[rows_of(place.peer_index(3), (k - 1) * quarter, quarter)]
            onward.append(remote(spot, spot, r.pass_sem, 4 * w + k + 1, place.partner))
        relays.append(relay)
        passes.append(onward)

    def send_weight(w):
        for copy in directs[w]:
            copy.start()

    def relay_weight(w):
        for k in (1, 2):
            directs[w][k - 1].wait_recv()
            relays[w][k - 1].start()
        for k in (1, 2):
            passes[w][k - 1].start()

    def pass_weight(w):
        for k in (1, 2):
            relays[w][k - 1].wait_recv()
            passes[w][k + 1].start()

    def settle_weight(w):
        loads[w].wait()
        for copy in passes[w]:
            copy.wait_recv()
        stores[w].start()

    def sent_weight(w):
        for copy in directs[w] + relays[w] + passes[w]:
            copy.wait_send()
        stores[w].wait()

    send_weight(0)

    gain_rows = r.gains.at[pl.ds(pl.multiple_of(shard * GAIN_ROWS, GAIN_ROWS), GAIN_ROWS)]
    gain_rows[...] = jnp.concatenate([r.gain_pair[...], jnp.zeros((GAIN_ROWS - 2, held), bf16)], axis=0)
    expert_row = lax.broadcasted_iota(jnp.int32, (E, rows), 0)
    for m in range(MB):
        combine = jnp.zeros((E, rows), f32)
        for k in range(TOP):
            combine += jnp.where(expert_row == r.routes[m, 0, k : k + 1], r.gates[m, 0, k : k + 1], 0.0)
        r.combine_own[:, m * rows : (m + 1) * rows] = combine
    r.combine_in[shard] = r.combine_own[...]
    small_copies = []
    for k in range(1, SHARDS):
        small_copies.append(remote(gain_rows, gain_rows, r.gain_sem, k - 1, place.peer(k)))
        small_copies.append(remote(r.combine_own, r.combine_in.at[shard], r.combine_sem, k - 1, place.peer(k)))

    for copy in small_copies:
        copy.start()
    at = pl.ds(pl.multiple_of(place.context * rows, rows), rows)
    table_loads = [
        local(r.tables.at[i, at], table, r.table_sem.at[i]) for i, table in enumerate((r.cosine, r.sine))
    ]
    for load in table_loads + loads:
        load.start()
    expert_loads = [
        local(r.expand_src, r.expand, r.expert_sem.at[0]),
        local(r.shrink_src, r.shrink, r.expert_sem.at[1]),
    ]
    for load in expert_loads:
        load.start()
    for m in range(MB):
        r.grads_all[m, shard] = r.cotangent[m * rows : (m + 1) * rows]
    grad_squares = [Square(place, r.grads_all.at[m], r.square_direct_sem, r.square_relay_sem, 2 * m) for m in range(MB)]
    row_squares = [
        Square(place, r.rows_all.at[m], r.square_direct_sem, r.square_relay_sem, 2 * (MB + m)) for m in range(MB)
    ]

    def spread_gains():
        r.gain_rows_out[...] = jnp.zeros_like(r.gain_rows_out)
        for b in range(SHARDS):
            pair = r.gains[b * GAIN_ROWS : b * GAIN_ROWS + 2]
            r.gain_rows_out[0:2, b * held : (b + 1) * held] = pair.astype(f32)

    def gain_times(values, row, write):
        for b in range(SHARDS):
            columns = slice(b * held, (b + 1) * held)
            write(columns, (values[:, columns] * r.gain_rows_out[row : row + 1, columns]).astype(bf16))

    values = r.tokens[...].astype(f32)
    unit = values * lax.rsqrt(jnp.mean(values * values, axis=-1, keepdims=True) + eps)
    for copy in small_copies:
        copy.wait_recv()

    def write_normed(columns, value):
        r.normed[:, columns] = value

    spread_gains()
    gain_times(unit, 0, write_normed)
    r.turned_normed[...] = r.normed[...].T
    for b in range(SHARDS):
        spread = jnp.concatenate([r.combine_in[b], jnp.zeros((LANES - E, MB * rows), f32)], axis=0)
        r.combine[b] = spread.T
    for m in range(MB):
        r.bias[m] = visible_bias(r.starts, m, place.context, (rows, length), 0)
    for load in table_loads:
        load.wait()

    relay_weight(0)
    send_weight(1)
    pass_weight(0)
    settle_weight(0)
    cosine, sine = r.cosine[...], r.sine[...]

    def project(weight, column, rotated):
        result = dot(r.normed[...], weight[:, pl.ds(column, WIDE * LANES)])
        tiles = []
        for m in range(MB):
            for i in range(WIDE):
                tile = result[m * rows : (m + 1) * rows, i * LANES : (i + 1) * LANES]
                tiles.append((m, i, rotate(tile, cosine, sine) if rotated else tile))
        return tiles

    blocks = KEY_WIDTH // (WIDE * LANES)
    for b in range(2 * blocks):
        column = b * WIDE * LANES
        for m, i, tile in project(r.pair_weight, column, b < blocks):
            r.own_pairs[m, :, pl.ds(column + i * LANES, LANES)] = tile.astype(bf16)

    def chunk(m, owner):
        owner = jnp.clip(owner, 0, LAST)
        return r.pairs.at[m, pl.ds(pl.multiple_of((2 * owner + core) * rows, rows), rows)]

    def move(m, t, direction):
        target = chunk(m, chip - direction * (t - 1))
        source = r.own_pairs.at[m] if t == 1 else target
        sems = r.right_sem if direction > 0 else r.left_sem
        device = place.chip_device(jnp.clip(chip + direction, 0, LAST))
        return remote(source, target, sems, m * LAST + t - 1, device)

    def sends(t, direction):
        owner = chip - direction * (t - 1)
        if direction > 0:
            return (chip < LAST) & (owner >= 0)
        return (chip > 0) & (owner <= LAST)

    def gets(t, direction):
        owner = chip - direction * t
        return owner >= 0 if direction > 0 else owner <= LAST

    def came(m, t, direction):
        spot = chunk(m, chip - direction * t)
        sems = r.right_sem if direction > 0 else r.left_sem
        return remote(spot, spot, sems, m * LAST + t - 1, place.partner)

    def pass_chunk(m, t, direction):
        spot = chunk(m, chip - direction * t)
        index = (m * LINE + t) * 2 + (1 if direction > 0 else 0)
        return remote(spot, spot, r.core_sem, index, place.partner)

    def take_step(m, t):
        for direction in (1, -1):

            @pl.when(gets(t, direction))
            def _():
                came(m, t, direction).wait_recv()
                if t < LAST:

                    @pl.when(sends(t + 1, direction))
                    def _():
                        move(m, t + 1, direction).start()

                pass_chunk(m, t, direction).start()

    own_copies = []
    for m in range(MB):
        for direction in (1, -1):

            @pl.when(sends(1, direction))
            def _():
                move(m, 1, direction).start()

        own_copies.append(
            (
                local(r.own_pairs.at[m], chunk(m, chip), r.own_sem.at[m]),
                remote(r.own_pairs.at[m], chunk(m, chip), r.core_sem, m * LINE * 2, place.partner),
            )
        )
        for copy in own_copies[m]:
            copy.start()

    def settle_pairs(m):
        own_copies[m][0].wait()
        own_copies[m][1].wait()
        for t in range(1, LINE):
            for direction in (1, -1):

                @pl.when(gets(t, direction))
                def _():
                    pass_chunk(m, t, direction).wait()

    def query_block(b, carry):
        column = pl.multiple_of(b * WIDE * LANES, WIDE * LANES)
        for m, i, tile in project(r.query_weight, column, True):
            r.query[m * rows : (m + 1) * rows, pl.ds(column + i * LANES, LANES)] = tile.astype(bf16)
        return carry

    def key_load(m, p, slot, i):
        lane = pl.multiple_of(p * LANES, LANES) + i * KEY_WIDTH
        return local(r.pairs.at[m, :, pl.ds(lane, LANES)], r.key_value.at[slot, i], r.key_sem.at[slot, i])

    def attend(m):
        own = slice(m * rows, (m + 1) * rows)
        for i in range(2):
            key_load(m, 0, 0, i).start()

        def pair(p, carry):
            slot = p % 2
            for i in range(2):
                key_load(m, p, slot, i).wait()

            @pl.when(p + 1 < PAIRS)
            def _():
                for i in range(2):
                    key_load(m, p + 1, 1 - slot, i).start()

            column = pl.multiple_of(p * PAIR_QUERY, PAIR_QUERY)
            columns = [pl.ds(column + i * LANES, LANES) for i in range(GROUP)]
            tiles = [r.query[own, c].astype(f32) * (1.0 / HEAD_SIZE) for c in columns]
            results = attention_pair(tiles, r.key_value[slot, 0], r.key_value[slot, 1], r.bias[m])
            for c, tile in zip(columns, results):
                r.attn[own, c] = tile.astype(bf16)
            return carry

        lax.fori_loop(0, PAIRS, pair, 0)
        r.turned_attn[:, own] = r.attn[own].T

    def finish_attention(m):
        own = slice(m * rows, (m + 1) * rows)
        middle = r.tokens[own].astype(f32) + dot(r.attn[own], r.output_weight[...])
        r.middle[own] = middle
        unit = middle * lax.rsqrt(jnp.mean(middle * middle, axis=-1, keepdims=True) + eps)

        def write(columns, value):
            r.rows_all[m, shard, :, columns] = value

        gain_times(unit, 1, write)

    active, gate, up = [r.pair_weight.at[i * wide : (i + 1) * wide] for i in range(3)]
    results, row_grads = [r.query_weight.at[i * wide : (i + 1) * wide] for i in range(2)]

    turned = r.turned_rows

    def turn(m):
        turned[...] = r.rows_all[m].reshape(wide, MODEL_WIDTH).T

    def emits(m):
        pairs = (
            (turned, r.turned_out.at[:, m * wide : (m + 1) * wide]),
            (r.grads_all.at[m], r.grads_out.at[m]),
            (results, r.results_out.at[m]),
            (row_grads, r.row_grads_out.at[m]),
        )
        for e in range(2):
            columns = slice(e * F, (e + 1) * F)
            pairs += tuple(
                (source.at[:, columns], target.at[m, :, columns])
                for source, target in ((active, r.active_out), (gate, r.gate_out), (up, r.up_out))
            )
        return [local(a, b, r.emit_sem.at[m * len(pairs) + i]) for i, (a, b) in enumerate(pairs)]

    def expert_steps(m, between):
        steps = [(e, b) for e in range(r.expand.shape[0]) for b in range(F // F_BLOCK)]
        for i, (e, b) in enumerate(steps):
            weight = r.combine[:, m * rows : (m + 1) * rows, :].reshape(wide, LANES)
            expert = shard * r.expand.shape[0] + e
            chosen = jnp.where(lane_index(weight.shape) == expert, weight, 0.0)
            columns = slice(b * F_BLOCK, (b + 1) * F_BLOCK)
            up_columns = slice(F + b * F_BLOCK, F + (b + 1) * F_BLOCK)
            a, g, u, result, row_grad = expert_block(
                r.rows_all[m].reshape(wide, MODEL_WIDTH),
                r.grads_all[m].reshape(wide, MODEL_WIDTH),
                jnp.sum(chosen, axis=1, keepdims=True),
                r.expand[e, :, columns],
                r.expand[e, :, up_columns],
                r.shrink[e, columns, :],
            )
            spot = slice(e * F + b * F_BLOCK, e * F + (b + 1) * F_BLOCK)
            active[:, spot], gate[:, spot], up[:, spot] = a, g, u
            if i == 0:
                r.result_sum[...] = result
                r.grad_sum[...] = row_grad
            elif i < len(steps) - 1:
                r.result_sum[...] += result
                r.grad_sum[...] += row_grad
            else:
                results[...] = (r.result_sum[...] + result).astype(bf16)
                row_grads[...] = (r.grad_sum[...] + row_grad).astype(bf16)
            if i in between:
                between[i]()

    relay_weight(1)
    send_weight(2)
    take_step(0, 1)
    take_step(1, 1)
    pass_weight(1)
    take_step(0, 2)
    settle_weight(1)
    lax.fori_loop(0, MODEL_WIDTH // (WIDE * LANES), query_block, 0)
    relay_weight(2)
    grad_squares[0].start()
    take_step(1, 2)
    take_step(0, 3)
    settle_pairs(0)
    attend(0)
    pass_weight(2)
    grad_squares[0].pass_on()
    take_step(1, 3)
    settle_weight(2)
    finish_attention(0)
    row_squares[0].start()
    settle_pairs(1)
    attend(1)
    row_squares[0].pass_on()
    finish_attention(1)
    row_squares[1].start()
    grad_squares[1].start()
    early = [
        local(source, target, r.last_sem.at[i])
        for i, (source, target) in enumerate(
            (
                (r.turned_normed, r.turned_normed_out),
                (r.query, r.query_rows_out),
                (r.turned_attn, r.turned_attn_out),
                (r.middle, r.middle_out),
            )
        )
    ]
    for emit in early:
        emit.start()
    for load in expert_loads:
        load.wait()
    sent_weight(0)
    sent_weight(1)
    grad_squares[0].finish()
    row_squares[0].finish()
    expert_steps(0, {1: row_squares[1].pass_on})
    turn(0)
    for emit in emits(0):
        emit.start()
    for emit in early:
        emit.wait()

    for copy in small_copies:
        copy.wait_send()
    sent_weight(2)
    for m in range(MB):
        for t in range(1, LINE):
            for direction in (1, -1):

                @pl.when(sends(t, direction))
                def _():
                    move(m, t, direction).wait_send()

    for square in grad_squares[:1] + row_squares[:1]:
        square.drain()
    grad_squares[1].pass_on()
    row_squares[1].finish()
    for emit in emits(0):
        emit.wait()
    turn(1)
    grad_squares[1].finish()
    last = emits(1)

    def emit_first():
        for emit in last[:2] + last[4:7]:
            emit.start()

    expert_steps(1, {1: emit_first})
    for emit in last[2:4] + last[7:]:
        emit.start()
    for square in grad_squares[1:] + row_squares[1:]:
        square.drain()
    for emit in last:
        emit.wait()


def forward(tokens, routes, gates, gain_pair, cotangent, starts, tables, weights, expert_in, expert_out):
    rows = tokens.shape[0] // MB
    length = tables.shape[1]
    wide = SHARDS * rows
    held = weights[0].shape[0]
    dma = pltpu.SemaphoreType.DMA
    anywhere = pl.BlockSpec(memory_space=pl.ANY)
    vmem = pl.BlockSpec(memory_space=pltpu.VMEM)
    shape = jax.ShapeDtypeStruct
    low = lambda *s: pltpu.VMEM(s, bf16)
    full = [(SHARDS * held, w.shape[1]) for w in weights]
    blocks = (MB, SHARDS, rows, MODEL_WIDTH)
    return pl.pallas_call(
        forward_kernel,
        in_specs=[vmem] * 5 + [pl.BlockSpec(memory_space=pltpu.SMEM)] + [anywhere] * 6,
        out_specs=[anywhere] * 4 + [vmem] * 3 + [anywhere] * 11,
        out_shape=[
            shape(tokens.shape[::-1], bf16),
            shape(tokens.shape, bf16),
            shape(tokens.shape[::-1], bf16),
            shape(tokens.shape, f32),
            shape((8, MODEL_WIDTH), f32),
            shape((rows, LANES), f32),
            shape((rows, LANES), f32),
        ]
        + [shape(f, bf16) for f in full]
        + [
            shape((MB, length, 2 * KEY_WIDTH), bf16),
            shape((MODEL_WIDTH, MB * wide), bf16),
            shape(blocks, bf16),
            shape((MB, wide, MODEL_WIDTH), bf16),
            shape((MB, wide, MODEL_WIDTH), bf16),
        ]
        + [shape((MB, wide, 2 * F), bf16)] * 3,
        scratch_shapes=[
            low(*tokens.shape[::-1]),
            low(*tokens.shape),
            low(*tokens.shape[::-1]),
            pltpu.VMEM(tokens.shape, f32),
            low(SHARDS * GAIN_ROWS, held),
            low(MODEL_WIDTH, wide),
        ]
        + [low(*f) for f in full]
        + [
            low(*expert_in.shape),
            low(*expert_out.shape),
            low(MB, rows, 2 * KEY_WIDTH),
            low(*tokens.shape),
            pltpu.VMEM((SHARDS, E, MB * rows), f32),
            pltpu.VMEM((E, MB * rows), f32),
            low(*tokens.shape),
            pltpu.VMEM((MB, rows, length), f32),
            pltpu.VMEM((SHARDS, MB * rows, LANES), f32),
            low(*blocks),
            low(*blocks),
            pltpu.VMEM((wide, MODEL_WIDTH), f32),
            pltpu.VMEM((wide, MODEL_WIDTH), f32),
            low(2, 2, length, LANES),
            dma((3,)),
            dma((2,)),
            dma((3,)),
            dma((2,)),
            dma((2, SHARDS - 1)),
            dma((2, SHARDS - 1)),
            dma((2, 6)),
            dma((2, 6)),
            dma((2, 12)),
            dma((2, MB * LAST)),
            dma((2, MB * LAST)),
            dma((2, 2 * MB * LINE)),
            dma((MB,)),
            dma((2, 4 * MB)),
            dma((2, 4 * MB)),
            dma((2, 2)),
            dma((10 * MB,)),
            dma((4,)),
        ],
        compiler_params=pltpu.CompilerParams(
            collective_id=1, has_side_effects=True, vmem_limit_bytes=VMEM_LIMIT
        ),
        name="forward",
    )(tokens, routes, gates, gain_pair, cotangent, starts, tables, *weights, expert_in, expert_out)


ADD_ROWS = 64


def add_into(out, *parts):
    rows = out.shape[0]
    size = max(d for d in range(16, ADD_ROWS + 1, 16) if rows % d == 0)

    def body(i, carry):
        spot = pl.ds(pl.multiple_of(i * size, size), size)
        total = parts[0][spot].astype(f32)
        for part in parts[1:]:
            total = total + part[spot].astype(f32)
        out[spot] = total.astype(out.dtype)
        return carry

    lax.fori_loop(0, rows // size, body, 0)


def greet_line(place):
    has_left, has_right = place.chip > 0, place.chip < LINE - 1
    greet(place.partner)
    for k in range(1, SHARDS):
        greet(place.peer(k))

    @pl.when(has_left)
    def _():
        greet(place.chip_device(place.chip - 1))

    @pl.when(has_right)
    def _():
        greet(place.chip_device(place.chip + 1))

    neighbours = jnp.where(has_left, 1, 0) + jnp.where(has_right, 1, 0)
    pl.semaphore_wait(pltpu.get_barrier_semaphore(), SHARDS + neighbours)


class Line:
    def __init__(self, place, pieces, sems):
        near_sem, far_sem, back_sem, pass_sem, store_sem = sems
        chip = place.chip
        self.inner = (chip == 1) | (chip == 2)
        outer = place.chip_device(3 * (chip // 2))
        inner = place.chip_device(1 + chip // 2)
        facing = place.chip_device(3 - chip)
        self.pieces = pieces
        numbered = list(enumerate(pieces))
        self.inward = [remote(p[0], p[1], near_sem, i, inner) for i, p in numbered]
        self.facing = [remote(p[0], p[2], far_sem, i, facing) for i, p in numbered]
        self.outward = [remote(p[1], p[3], back_sem, i, outer) for i, p in numbered]
        self.pass_inner = [remote(p[1], p[3], pass_sem, i, place.partner) for i, p in numbered]
        self.pass_outer = [remote(p[3], p[3], pass_sem, i, place.partner) for i, p in numbered]
        self.stores = [pltpu.make_async_copy(p[1], p[3], store_sem.at[i]) for i, p in numbered]

    def ready(self, *items):
        @pl.when(jnp.logical_not(self.inner))
        def _():
            for i in items:
                self.inward[i].start()

    def serve(self, halfway=(), finish=(), forward=()):
        @pl.when(self.inner)
        def _():
            for i in halfway:
                self.inward[i].wait_recv()
                own, near = self.pieces[i][:2]
                add_into(own, own, near)
                self.facing[i].start()
            for i in finish:
                self.facing[i].wait_recv()
                own, near, far = self.pieces[i][:3]
                add_into(near, own, far)
                self.outward[i].start()
                self.pass_inner[i].start()
                self.stores[i].start()

        @pl.when(jnp.logical_not(self.inner))
        def _():
            for i in forward:
                self.outward[i].wait_recv()
                self.pass_outer[i].start()

    def drain(self, items=None):
        items = range(len(self.pieces)) if items is None else items

        @pl.when(self.inner)
        def _():
            for i in items:
                self.facing[i].wait_send()
                self.outward[i].wait_send()
                self.pass_inner[i].wait_send()
                self.stores[i].wait()

        @pl.when(jnp.logical_not(self.inner))
        def _():
            for i in items:
                self.inward[i].wait_send()
                self.pass_outer[i].wait_send()

        for i in items:
            self.pass_outer[i].wait_recv()


def line_sems(number):
    dma = pltpu.SemaphoreType.DMA
    return [dma((2, number))] * 4 + [dma((number,))]


def split_rows(ref, parts):
    size = ref.shape[0] // parts
    return [ref.at[j * size : (j + 1) * size] for j in range(parts)]


def out_halves(place, ref, parts):
    half = ref.shape[0] // 2
    size = half // parts
    first = pl.multiple_of(place.core * half, half)
    return [ref.at[pl.ds(first + j * size, size)] for j in range(parts)]


def line_pieces(place, own, near, far, out, parts):
    return list(
        zip(split_rows(own, parts), split_rows(near, parts), split_rows(far, parts), out_halves(place, out, parts))
    )


class PairSum:
    def __init__(self, place, own, sources, others, lands, core_sem, left_sem):
        self.place, self.own, self.others, self.lands, self.left_sem = place, own, others, lands, left_sem
        self.trades = [remote(sources(j), others.at[j], core_sem, j, place.partner) for j in range(LINE)]
        self.past = LAST - place.chip

    def trade(self):
        for copy in self.trades:
            copy.start()

    def half(self, ref, h):
        size = ref.shape[0] // 2
        return ref.at[h * size : (h + 1) * size]

    def move(self, t, h):
        owner = jnp.clip(self.place.chip - (LINE - t), 0, LAST)
        device = self.place.chip_device(jnp.clip(self.place.chip - 1, 0, LAST))
        source, target = self.half(self.own(owner), h), self.half(self.lands.at[t - 1], h)
        return remote(source, target, self.left_sem, 2 * (t - 1) + h, device)

    def meet(self):
        for j in range(LINE):
            self.trades[j].wait_recv()
            add_into(self.own(j), self.own(j), self.others.at[j])

        @pl.when(self.past == 0)
        def _():
            for t in range(1, LINE):
                for h in range(2):
                    self.move(t, h).start()

    def take(self, t, h):
        self.move(t, h).wait_recv()
        mine = self.half(self.own(jnp.clip(self.place.chip - (LAST - t), 0, LAST)), h)
        add_into(mine, mine, self.half(self.lands.at[t - 1], h))

    def step(self, t):
        @pl.when((self.past >= 1) & (self.past <= min(t - 1, LINE - 2)))
        def _():
            for h in range(2):
                self.take(t - 1, h)
                self.move(t, h).start()

    def finish(self, out, cosine, sine):
        @pl.when(self.past >= 1)
        def _():
            for h in range(2):
                self.take(LAST, h)

        mine = self.own(self.place.chip)
        for i in range(2 * KEY_WIDTH // LANES):
            columns = slice(i * LANES, (i + 1) * LANES)
            tile = mine[:, columns]
            if i < KEY_WIDTH // LANES:
                tile = rotate(tile.astype(f32), cosine[...], -sine[...]).astype(bf16)
            out[:, columns] = tile

    def drain(self):
        for copy in self.trades:
            copy.wait_send()
        for t in range(1, LINE):

            @pl.when((self.past <= t - 1) & (self.past <= LINE - 2))
            def _():
                for h in range(2):
                    self.move(t, h).wait_send()


PARTS = 4


def backward_kernel(
    query_src,
    starts,
    cosine,
    sine,
    middle_src,
    cotangent_src,
    gain,
    pairs,
    turned_src,
    grads_src,
    active_src,
    gate_src,
    up_src,
    results_src,
    row_grads_src,
    output_src,
    query_low_out,
    pair_low,
    middle_low_out,
    middle_grad_out,
    gain_grad,
    block_output,
    gate_total,
    up_total,
    gate_rest,
    up_rest,
    down_rest,
    pair_grad,
    query,
    middle,
    cotangent,
    query_low,
    middle_low,
    middle_grad,
    rows,
    turned,
    grads,
    pool,
    send_gate,
    send_up,
    send_down,
    own_gate,
    own_up,
    own_down,
    other_gate,
    other_up,
    other_down,
    near_gate,
    near_up,
    far_gate,
    far_up,
    row_grad_own,
    row_grad_in,
    result_own,
    result_in,
    attn_grad,
    key_value,
    bias,
    pair_other,
    land_left,
    load_sem,
    weight_sem,
    trade_sem,
    rest_sem,
    row_sem,
    result_sem,
    key_sem,
    core_sem,
    left_sem,
    near_sem,
    far_sem,
    back_sem,
    pass_sem,
    store_sem,
    emit_sem,
):
    r = types.SimpleNamespace(**locals())
    place = Place()
    core, chip, shard = place.core, place.chip, place.shard
    rows = r.cosine.shape[0]
    tokens = MB * SHARDS * rows
    side = MODEL_WIDTH // 2
    local = pltpu.make_async_copy

    wide = SHARDS * rows
    loads = []

    def load(source, target):
        loads.append(local(source, target, r.load_sem.at[len(loads)]))
        loads[-1].start()
        return loads[-1]

    flat = lambda ref, m: [(ref.at[m, k], m * wide + k * rows) for k in range(SHARDS)]
    grad_loads, piece_loads = [], []
    turned_load = load(r.turned_src, r.turned)
    for i, ref in ((1, r.gate_src), (2, r.up_src), (0, r.active_src)):
        for m in range(MB):
            at = i * tokens + m * wide
            piece_loads.append(load(ref.at[m], r.pool.at[at : at + wide]))
    for m in range(MB):
        for source, at in flat(r.grads_src, m):
            grad_loads.append(load(source, r.grads.at[at : at + rows]))
    own_loads = [load(r.row_grads_src.at[m, shard], r.row_grad_own.at[m]) for m in range(MB)]
    own_loads.append(load(r.results_src.at[0, shard], r.result_own))

    vector_loads = [
        load(source, target)
        for source, target in ((r.middle_src, r.middle), (r.cotangent_src, r.cotangent), (r.query_src, r.query))
    ]
    greet_line(place)

    row_copies, result_copies = [], []
    for m in range(MB):
        for k in range(1, SHARDS):
            i = m * (SHARDS - 1) + k - 1
            at = place.peer_index(k)
            row_copies.append(
                remote(r.row_grads_src.at[m, at], r.row_grad_in.at[m, k - 1], r.row_sem, i, place.peer(k))
            )
            if m == 0:
                result_copies.append(
                    remote(r.results_src.at[m, at], r.result_in.at[k - 1], r.result_sem, i, place.peer(k))
                )
    for copy in row_copies:
        copy.start()

    for m in range(MB):
        r.bias[m] = visible_bias(r.starts, m, place.context, r.bias.shape[1:], 1)

    turned_load.wait()
    sends = (r.send_gate, r.send_up, r.send_down)
    owns = (r.own_gate, r.own_up, r.own_down)
    others = (r.other_gate, r.other_up, r.other_down)
    trades = [
        [remote(sends[i], others[i].at[b], r.trade_sem, b * 3 + i, place.partner) for i in range(3)]
        for b in range(2)
    ]

    def weight_block(b, expert, outs):
        column = pl.ds(pl.multiple_of(expert * F + b * F_BLOCK, F_BLOCK), F_BLOCK)
        for i in range(2):
            outs[i][...] = dot(r.turned[...], r.pool[(i + 1) * tokens : (i + 2) * tokens, column]).astype(bf16)

    def down_block(b, expert, out):
        column = pl.ds(pl.multiple_of(expert * F + b * F_BLOCK, F_BLOCK), F_BLOCK)
        out[...] = dot(r.pool[0:tokens, column], r.grads[...], TN).astype(bf16)

    def meet(b, i):
        trades[b][i].wait_recv()
        add_into(owns[i].at[b], owns[i].at[b], others[i].at[b])

    pieces = []
    for own, near, far, out in (
        (r.own_gate.at[0], r.near_gate, r.far_gate, r.gate_total),
        (r.own_up.at[0], r.near_up, r.far_up, r.up_total),
    ):
        pieces += line_pieces(place, own, near, far, out, PARTS)
    line = Line(place, pieces, (r.near_sem, r.far_sem, r.back_sem, r.pass_sem, r.store_sem))

    for copy in piece_loads[: 2 * MB]:
        copy.wait()

    def else_serve(b):
        if b == 1:
            line.serve([0])

    for b in range(2):
        if b == 1:
            for i in range(2):
                trades[0][i].wait_send()
        weight_block(b, 1 - core, sends)
        for i in range(2):
            trades[b][i].start()
        weight_block(b, core, [own.at[b] for own in owns[:2]])
        if b == 0:
            for i in range(2):
                meet(0, i)
                line.ready(*range(i * PARTS, (i + 1) * PARTS))
            for copy in piece_loads[2 * MB :] + grad_loads:
                copy.wait()
        else:
            trades[0][2].wait_send()
        else_serve(b)
        down_block(b, 1 - core, sends[2])
        trades[b][2].start()
        down_block(b, core, owns[2].at[b])
        if b == 0:
            meet(0, 2)

    weight_loads = []
    for i in range(2):
        source = r.output_src.at[:, i * side : (i + 1) * side]
        target = r.pool.at[i * MODEL_WIDTH : (i + 1) * MODEL_WIDTH, 0:side]
        weight_loads.append(local(source, target, r.weight_sem.at[i]))
        weight_loads[-1].start()
    for copy in result_copies:
        copy.start()
    for i in range(3):
        meet(1, i)
    rests = [
        local(r.own_gate.at[1], r.gate_rest, r.rest_sem.at[0]),
        local(r.own_up.at[1], r.up_rest, r.rest_sem.at[1]),
        local(r.own_down, r.down_rest, r.rest_sem.at[2]),
    ]
    for copy in rests:
        copy.start()

    r.gain_grad[...] = jnp.zeros_like(r.gain_grad)

    def prepare(m):
        own = slice(m * rows, (m + 1) * rows)
        own_loads[m].wait()
        moe_in_grad = r.row_grad_own[m].astype(f32)
        for k in range(1, SHARDS):
            row_copies[m * (SHARDS - 1) + k - 1].wait_recv()
            moe_in_grad = moe_in_grad + r.row_grad_in[m, k - 1].astype(f32)
        middle = r.middle[own]
        scale = lax.rsqrt(jnp.mean(middle * middle, axis=-1, keepdims=True) + eps)
        unit = middle * scale
        r.gain_grad[m : m + 1] = jnp.sum(moe_in_grad * unit, axis=0, keepdims=True)
        weighted = moe_in_grad * r.gain[1:2]
        inner = jnp.mean(weighted * unit, axis=-1, keepdims=True)
        middle_grad = r.cotangent[own].astype(f32) + (weighted - unit * inner) * scale
        r.middle_grad[own] = middle_grad
        r.middle_low[own] = middle_grad.astype(bf16)
        if m == 0:
            for copy in weight_loads:
                copy.wait()
        total = dot(r.middle_low[own, 0:side], r.pool[0:MODEL_WIDTH, 0:side], NT)
        total = total + dot(r.middle_low[own, side:], r.pool[MODEL_WIDTH : 2 * MODEL_WIDTH, 0:side], NT)
        r.attn_grad[m] = total.astype(bf16)

    def key_load(step, slot, i):
        m, p = step // PAIRS, step % PAIRS
        lane = pl.multiple_of(p * LANES, LANES) + i * KEY_WIDTH
        return local(r.pairs.at[m, :, pl.ds(lane, LANES)], r.key_value.at[slot, i], r.key_sem.at[slot, i])

    pair_grads = (r.rows, r.grads.at[:, 0 : 2 * KEY_WIDTH])

    def chunk(of_chip, of_core):
        return pair_grads[0].at[pl.ds(pl.multiple_of((2 * of_chip + of_core) * rows, rows), rows)]

    pair_sum = PairSum(
        place,
        lambda j: chunk(j, core),
        lambda j: chunk(j, 1 - core),
        r.pair_other,
        r.land_left,
        r.core_sem,
        r.left_sem,
    )

    def pair_step(step, carry):
        m, p = step // PAIRS, step % PAIRS
        slot = step % 2
        for i in range(2):
            key_load(step, slot, i).wait()

        @pl.when(step + 1 < MB * PAIRS)
        def _():
            for i in range(2):
                key_load(step + 1, 1 - slot, i).start()

        at = pl.multiple_of(m * rows, rows)
        column = pl.multiple_of(p * PAIR_QUERY, PAIR_QUERY)
        lane = pl.multiple_of(p * LANES, LANES)
        columns = [pl.ds(column + i * LANES, LANES) for i in range(GROUP)]
        scale = 1.0 / HEAD_SIZE
        tiles = [r.query[pl.ds(at, rows), c].astype(f32) * scale for c in columns]
        grads = [r.attn_grad[m, :, c].astype(f32) for c in columns]
        bias = jnp.concatenate([r.bias[m]] * GROUP, axis=1)
        query_grads, key_grad, value_grad = attention_pair_gradient(
            tiles, grads, r.key_value[slot, 0], r.key_value[slot, 1], bias
        )
        for c, tile in zip(columns, query_grads):
            tile = rotate(tile * scale, r.cosine[...], -r.sine[...])
            r.query_low[pl.ds(at, rows), c] = tile.astype(bf16)
        key_low, value_low = key_grad.astype(bf16), value_grad.astype(bf16)
        for micro in range(MB):

            @pl.when(m == micro)
            def _():
                pair_grads[micro][:, pl.ds(lane, LANES)] = key_low
                pair_grads[micro][:, pl.ds(lane + KEY_WIDTH, LANES)] = value_low

        for at_step, actions in SERVICE:

            @pl.when(step == at_step)
            def _():
                for action in actions:
                    action()

        return carry

    serve = line.serve
    SERVICE = (
        (1, (lambda: serve([3], [1]),)),
        (2, (lambda: serve([4], [2], [0]),)),
        (3, (pair_sum.trade, lambda: prepare(1), lambda: serve([5], [3], [1]), pair_sum.meet)),
        (4, (lambda: serve([6], [4], [2]),)),
        (5, (lambda: serve([7], [5], [3]),)),
        (6, (lambda: serve([], [6], [4]), lambda: pair_sum.step(2))),
        (7, (lambda: serve([], [7], [5]),)),
    )
    for i in range(2):
        key_load(0, 0, i).start()
    for copy in vector_loads:
        copy.wait()
    serve([1])
    prepare(0)
    serve([2], [0])
    lax.fori_loop(0, MB * PAIRS, pair_step, 0)
    second = local(pair_grads[1], r.pair_grad, r.rest_sem.at[3])
    second.start()
    emits = [
        local(source, target, r.emit_sem.at[i])
        for i, (source, target) in enumerate(
            (
                (r.query_low, r.query_low_out),
                (r.middle_low, r.middle_low_out),
                (r.middle_grad, r.middle_grad_out),
            )
        )
    ]
    for copy in emits:
        copy.start()
    pair_sum.step(3)
    own_loads[MB].wait()
    total = r.middle[0:rows] + r.result_own[...].astype(f32)
    for k in range(1, SHARDS):
        result_copies[k - 1].wait_recv()
        total = total + r.result_in[k - 1].astype(f32)
    r.block_output[...] = total.astype(bf16)
    for copy in trades[1]:
        copy.wait_send()
    for copy in rests:
        copy.wait()
    for copy in row_copies:
        copy.wait_send()
    for copy in result_copies:
        copy.wait_send()
    line.drain(range(4))
    serve([], [], [6, 7])
    pair_sum.finish(r.pair_low, r.cosine, r.sine)
    for copy in [second] + emits:
        copy.wait()

    pair_sum.drain()
    line.drain(range(4, 2 * PARTS))


def backward(query, starts, cosine, sine, middle, cotangent, gain, pairs, turned_rows, grad_blocks, pieces, results, row_grads, output_weight):
    rows = cosine.shape[0]
    length = pairs.shape[1]
    held_rows = 2 * MODEL_WIDTH
    tokens = MB * SHARDS * rows
    dma = pltpu.SemaphoreType.DMA
    anywhere = pl.BlockSpec(memory_space=pl.ANY)
    vmem = pl.BlockSpec(memory_space=pltpu.VMEM)
    shape = jax.ShapeDtypeStruct
    tall, flat = (MODEL_WIDTH, F_BLOCK), (F_BLOCK, MODEL_WIDTH)
    two = lambda s: (2,) + s
    low = lambda s: pltpu.VMEM(s, bf16)
    number = 2 * PARTS
    return pl.pallas_call(
        backward_kernel,
        in_specs=[anywhere, pl.BlockSpec(memory_space=pltpu.SMEM), vmem, vmem, anywhere, anywhere, vmem]
        + [anywhere] * 9,
        out_specs=[anywhere, vmem, anywhere, anywhere, vmem, vmem] + [anywhere] * 6,
        out_shape=[
            shape(query.shape, bf16),
            shape((rows, 2 * KEY_WIDTH), bf16),
            shape((MB * rows, MODEL_WIDTH), bf16),
            shape((MB * rows, MODEL_WIDTH), f32),
            shape((8, MODEL_WIDTH), f32),
            shape((rows, MODEL_WIDTH), bf16),
            shape((held_rows, F_BLOCK), bf16),
            shape((held_rows, F_BLOCK), bf16),
            shape(tall, bf16),
            shape(tall, bf16),
            shape(two(flat), bf16),
            shape((length, 2 * KEY_WIDTH), bf16),
        ],
        scratch_shapes=[
            low((MB * rows, MODEL_WIDTH)),
            pltpu.VMEM((MB * rows, MODEL_WIDTH), f32),
            low((MB * rows, MODEL_WIDTH)),
            low((MB * rows, MODEL_WIDTH)),
            low((MB * rows, MODEL_WIDTH)),
            pltpu.VMEM((MB * rows, MODEL_WIDTH), f32),
            low((length, 2 * KEY_WIDTH)),
            low((MODEL_WIDTH, tokens)),
            low((tokens, MODEL_WIDTH)),
            low((3 * tokens, 2 * F)),
            low(tall),
            low(tall),
            low(flat),
            low(two(tall)),
            low(two(tall)),
            low(two(flat)),
            low(two(tall)),
            low(two(tall)),
            low(two(flat)),
            low(tall),
            low(tall),
            low(tall),
            low(tall),
            low((MB, rows, MODEL_WIDTH)),
            low((MB, SHARDS - 1, rows, MODEL_WIDTH)),
            low((rows, MODEL_WIDTH)),
            low((SHARDS - 1, rows, MODEL_WIDTH)),
            low((MB, rows, MODEL_WIDTH)),
            low((2, 2, length, LANES)),
            pltpu.VMEM((MB, length, rows), f32),
            low((LINE, rows, 2 * KEY_WIDTH)),
            low((LINE - 1, rows, 2 * KEY_WIDTH)),
            dma((4 * MB * SHARDS,)),
            dma((2,)),
            dma((2, 6)),
            dma((4,)),
            dma((2, MB * (SHARDS - 1))),
            dma((2, SHARDS - 1)),
            dma((2, 2)),
            dma((2, LINE)),
            dma((2, 2 * (LINE - 1))),
        ]
        + line_sems(number)
        + [dma((3,))],
        compiler_params=pltpu.CompilerParams(
            collective_id=3, has_side_effects=True, vmem_limit_bytes=VMEM_LIMIT
        ),
        name="backward",
    )(query, starts, cosine, sine, middle, cotangent, gain, pairs, turned_rows, grad_blocks, *pieces, results, row_grads, output_weight)


DENSE = ("output", "query", "pair", "gain")
DENSE_PARTS = 4
FINE = 4
GATHER_AFTER = {4: ("output",), 9: ("query",), 13: ("pair", "gain")}
OUTPUT_AFTER = 19
DRAIN_LAG = 8


def dense_kernel(
    turned_normed_src,
    turned_attn_src,
    query_low_src,
    pair_low_first,
    middle_low_src,
    gain,
    gain_grad,
    cosine,
    sine,
    middle_grad_src,
    tokens_src,
    middle_src,
    query_src,
    pair_src,
    pair_grad,
    results_src,
    gate_rest,
    up_rest,
    down_rest,
    input_grad_out,
    block_output,
    results_in,
    output_total,
    query_total,
    pair_total,
    gain_total,
    gate_total,
    up_total,
    down_total,
    turned_normed,
    turned_attn,
    query_low,
    middle_low,
    input_grad,
    middle_grad,
    tokens,
    middle,
    pair_low,
    pair_own,
    pair_other,
    land_left,
    query_weight,
    pair_weight,
    gains,
    send_output,
    send_query,
    own_output,
    own_query,
    own_pair,
    own_gain,
    other_output,
    other_query,
    other_pair,
    other_gain,
    across_output,
    across_query,
    across_pair,
    across_gain,
    sum_output,
    sum_query,
    sum_pair,
    sum_gain,
    near_output,
    near_query,
    near_pair,
    near_gain,
    far_output,
    far_query,
    far_pair,
    far_gain,
    own_gate,
    own_up,
    own_down,
    near_gate,
    near_up,
    near_down,
    far_gate,
    far_up,
    far_down,
    load_sem,
    core_sem,
    left_sem,
    result_sem,
    trade_sem,
    across_sem,
    near_sem,
    far_sem,
    back_sem,
    pass_sem,
    store_sem,
    emit_sem,
):
    r = types.SimpleNamespace(**locals())
    at = lambda kind, name: getattr(r, kind + "_" + name)
    place = Place()
    core, shard = place.core, place.shard
    rows = r.middle.shape[0]
    held = MODEL_WIDTH // SHARDS
    half = held // 2
    loads = [
        pltpu.make_async_copy(source, target, r.load_sem.at[i])
        for i, (source, target) in enumerate(
            (
                (r.gate_rest, r.own_gate),
                (r.up_rest, r.own_up),
                (r.down_rest, r.own_down),
                (r.query_src, r.query_weight),
                (r.pair_src, r.pair_weight),
                (r.pair_grad.at[:, core], r.pair_own),
                (r.middle_grad_src, r.middle_grad),
                (r.tokens_src, r.tokens),
                (r.middle_src.at[rows : 2 * rows], r.middle),
                (r.turned_attn_src, r.turned_attn),
                (r.middle_low_src, r.middle_low),
                (r.turned_normed_src, r.turned_normed),
                (r.query_low_src, r.query_low),
            )
        )
    ]
    for load in loads:
        load.start()
    greet_line(place)
    pair_sum = PairSum(
        place,
        lambda j: r.pair_own.at[j],
        lambda j: r.pair_grad.at[j, 1 - core],
        r.pair_other,
        r.land_left,
        r.core_sem,
        r.left_sem,
    )
    pair_sum.trade()

    pieces = []
    for name, parts in (("gate", FINE), ("up", FINE), ("down", 2 * FINE)):
        pieces += line_pieces(place, at("own", name), at("near", name), at("far", name), getattr(r, name + "_total"), parts)
    expert_pieces = len(pieces)
    for name in DENSE:
        parts = 1 if name == "gain" else DENSE_PARTS
        pieces += line_pieces(
            place, at("sum", name), at("near", name), at("far", name), getattr(r, name + "_total"), parts
        )
    line = Line(place, pieces, (r.near_sem, r.far_sem, r.back_sem, r.pass_sem, r.store_sem))
    loads[0].wait()
    line.ready(0)
    loads[5].wait()
    pair_sum.meet()
    for i in (1, 2):
        loads[i].wait()
    line.ready(*range(1, expert_pieces))

    def block(b, of_core):
        return pl.ds(pl.multiple_of(b * held + of_core * half, half), half)

    trades = {}

    def dense(name, turned, right, sent):
        index = DENSE.index(name)
        trades[name] = []
        for b in range(SHARDS):
            sent[b] = dot(turned[block(b, 1 - core)], right[...]).astype(bf16)
            copy = remote(sent.at[b], at("other", name).at[b], r.trade_sem, index * SHARDS + b, place.partner)
            copy.start()
            trades[name].append(copy)
        for b in range(SHARDS):
            at("own", name)[b] = dot(turned[block(b, core)], right[...]).astype(bf16)

    crossings = {}

    def meet(name):
        own, other, across = at("own", name), at("other", name), at("across", name)
        for b in range(SHARDS):
            trades[name][b].wait_recv()
            add_into(own.at[b], own.at[b], other.at[b])
        crossings[name] = []
        for k in range(1, SHARDS):
            index = DENSE.index(name) * (SHARDS - 1) + k - 1
            copy = remote(own.at[place.peer_index(k)], across.at[k - 1], r.across_sem, index, place.peer(k))
            copy.start()
            crossings[name].append(copy)

    def gather(name):
        for copy in crossings[name]:
            copy.wait_recv()
        across = at("across", name)
        add_into(at("sum", name), at("own", name).at[shard], *[across.at[k] for k in range(SHARDS - 1)])

    for load in loads[9:]:
        load.wait()
    dense("output", r.turned_attn, r.middle_low, r.send_output)
    dense("query", r.turned_normed, r.query_low, r.send_query)
    meet("output")
    line.serve([0])
    pair_sum.step(2)
    meet("query")
    pair_sum.step(3)
    for copy in trades["output"]:
        copy.wait_send()
    r.pair_low[0:rows] = r.pair_low_first[...]
    pair_sum.finish(r.pair_low.at[rows : 2 * rows], r.cosine, r.sine)
    dense("pair", r.turned_normed, r.pair_low, r.send_output.at[:, :, 0 : 2 * KEY_WIDTH])
    line.serve([1], [0])
    for load in loads[3:5] + loads[6:9]:
        load.wait()

    gain_one_grad = jnp.zeros((1, MODEL_WIDTH), f32)
    for m in range(MB):
        own = slice(m * rows, (m + 1) * rows)
        values = r.tokens[own].astype(f32)
        scale = lax.rsqrt(jnp.mean(values * values, axis=-1, keepdims=True) + eps)
        unit = values * scale
        normed_grad = dot(r.query_low[own], r.query_weight[...], NT) + dot(r.pair_low[own], r.pair_weight[...], NT)
        gain_one_grad = gain_one_grad + jnp.sum(normed_grad * unit, axis=0, keepdims=True)
        weighted = normed_grad * r.gain[0:1]
        inner = jnp.mean(weighted * unit, axis=-1, keepdims=True)
        r.input_grad[own] = r.middle_grad[own] + (weighted - unit * inner) * scale
        if m == 0:
            meet("pair")
            line.serve([2], [1])
    line.serve([3], [2])
    grad_emit = pltpu.make_async_copy(r.input_grad, r.input_grad_out, r.emit_sem.at[0])
    grad_emit.start()
    gain_two_grad = jnp.sum(r.gain_grad[...], axis=0, keepdims=True)
    stacked = jnp.concatenate(
        [gain_one_grad, gain_two_grad, jnp.zeros((LANES - 2, MODEL_WIDTH), f32)], axis=0
    )
    r.gains[...] = stacked.T.astype(bf16)
    trades["gain"] = []
    for b in range(SHARDS):
        source = r.gains.at[block(b, 1 - core)]
        index = DENSE.index("gain") * SHARDS + b
        trades["gain"].append(remote(source, r.other_gain.at[b], r.trade_sem, index, place.partner))
        trades["gain"][b].start()
        r.own_gain[b] = r.gains[block(b, core)]
    meet("gain")

    result_copies = []
    for k in range(1, SHARDS):
        source = r.results_src.at[1, place.peer_index(k)]
        result_copies.append(remote(source, r.results_in.at[k - 1], r.result_sem, k - 1, place.peer(k)))
        result_copies[-1].start()
    for copy in trades["pair"]:
        copy.wait_send()
    result_parts = [r.send_output.at[k, 0:rows] for k in range(SHARDS)]
    result_loads = [
        pltpu.make_async_copy(source, target, r.load_sem.at[13 + k])
        for k, (source, target) in enumerate(
            zip([r.results_src.at[1, shard]] + [r.results_in.at[k] for k in range(SHARDS - 1)], result_parts)
        )
    ]
    result_loads[0].start()

    def output_rows():
        for copy, load in zip(result_copies, result_loads[1:]):
            copy.wait_recv()
            load.start()
        total = r.middle[...]
        for load, part in zip(result_loads, result_parts):
            load.wait()
            total = total + part[...].astype(f32)
        r.block_output[...] = total.astype(bf16)

    number = len(pieces)
    first = expert_pieces
    spans = {}
    for name in DENSE:
        parts = 1 if name == "gain" else DENSE_PARTS
        spans[name] = range(first, first + parts)
        first += parts
    lag = 4
    for i in range(number + lag):
        line.serve(
            [i] if 4 <= i < number else [],
            [i - 1] if 4 <= i <= number else [],
            [i - lag] if i >= lag else [],
        )
        for name in GATHER_AFTER.get(i, ()):
            gather(name)
            line.ready(*spans[name])
        if DRAIN_LAG <= i < number:
            line.drain([i - DRAIN_LAG])
        if i == OUTPUT_AFTER:
            output_rows()
            for name in DENSE:
                for copy in crossings[name]:
                    copy.wait_send()
                if name in ("query", "gain"):
                    for copy in trades[name]:
                        copy.wait_send()
            for copy in result_copies:
                copy.wait_send()
            pair_sum.drain()

    grad_emit.wait()
    line.drain(range(number - DRAIN_LAG, number))


def dense_weights(vectors, streamed, query_weight, pair_weight, pair_grad, results, rests):
    dma = pltpu.SemaphoreType.DMA
    anywhere = pl.BlockSpec(memory_space=pl.ANY)
    vmem = pl.BlockSpec(memory_space=pltpu.VMEM)
    shape = jax.ShapeDtypeStruct
    rows = pair_grad.shape[2]
    low = lambda *s: pltpu.VMEM(s, bf16)
    held = MODEL_WIDTH // SHARDS
    half = held // 2
    widths = (MODEL_WIDTH, MODEL_WIDTH, 2 * KEY_WIDTH, LANES)
    tall = (MODEL_WIDTH, F_BLOCK)
    number = 4 * FINE + 3 * DENSE_PARTS + 1
    return pl.pallas_call(
        dense_kernel,
        in_specs=[anywhere] * 3 + [vmem, anywhere] + [vmem] * 4 + [anywhere] * (7 + len(streamed)),
        out_specs=[anywhere, vmem] + [anywhere] * 8,
        out_shape=[
            shape((MB * rows, MODEL_WIDTH), f32),
            shape((rows, MODEL_WIDTH), bf16),
            shape((SHARDS - 1, rows, MODEL_WIDTH), bf16),
        ]
        + [shape((held, w), bf16) for w in widths]
        + [
            shape((2 * MODEL_WIDTH, F_BLOCK), bf16),
            shape((2 * MODEL_WIDTH, F_BLOCK), bf16),
            shape((2 * F, MODEL_WIDTH), bf16),
        ],
        scratch_shapes=[
            low(MODEL_WIDTH, MB * rows),
            low(MODEL_WIDTH, MB * rows),
            low(MB * rows, MODEL_WIDTH),
            low(MB * rows, MODEL_WIDTH),
            pltpu.VMEM((MB * rows, MODEL_WIDTH), f32),
            pltpu.VMEM((MB * rows, MODEL_WIDTH), f32),
            low(MB * rows, MODEL_WIDTH),
            pltpu.VMEM((rows, MODEL_WIDTH), f32),
            low(MB * rows, 2 * KEY_WIDTH),
            low(LINE, rows, 2 * KEY_WIDTH),
            low(LINE, rows, 2 * KEY_WIDTH),
            low(LINE - 1, rows, 2 * KEY_WIDTH),
            low(*query_weight.shape),
            low(*pair_weight.shape),
            low(MODEL_WIDTH, LANES),
            low(SHARDS, half, MODEL_WIDTH),
            low(SHARDS, half, MODEL_WIDTH),
        ]
        + [low(SHARDS, half, w) for w in widths] * 2
        + [low(SHARDS - 1, half, w) for w in widths]
        + [low(half, w) for w in widths] * 3
        + [low(*tall), low(*tall), low(F, MODEL_WIDTH)] * 3
        + [dma((13 + SHARDS,)), dma((2, LINE)), dma((2, 2 * (LINE - 1))), dma((2, SHARDS - 1)), dma((2, 4 * SHARDS)), dma((2, 4 * (SHARDS - 1)))]
        + line_sems(number)
        + [dma((1,))],
        compiler_params=pltpu.CompilerParams(
            collective_id=4, has_side_effects=True, vmem_limit_bytes=VMEM_LIMIT
        ),
        name="dense_weights",
    )(*vectors, *streamed, query_weight, pair_weight, pair_grad, results, *rests)


def widen_kernel(*refs):
    r = refs
    step = pl.program_id(0)
    parts, (shrink, dense, rows_in, gains, grad) = r[:4], (r[4], r[5:8], r[8:10], r[10], r[11])
    expand_out, shrink_out, dense_out, rows_out, gain_outs, grad_out = r[12], r[13], r[14:17], r[17], r[18:20], r[20]
    for i, ref in enumerate(parts):
        expand_out[:, i * F_BLOCK : (i + 1) * F_BLOCK] = ref[...].astype(f32)
    shrink_out[...] = shrink[...].astype(f32)
    grad_out[...] = grad[...]

    for source, target in zip(dense, dense_out):
        target[...] = source[...].astype(f32)

    for i in range(MB):

        @pl.when(step // (WIDEN_STEPS // MB) == i)
        def _():
            rows_out[...] = rows_in[i][...]

    @pl.when(step == 0)
    def _():
        turned = gains[...].astype(f32).T
        for i in range(2):
            gain_outs[i][...] = turned[i]


WIDEN_STEPS = 4


def widen(expand_parts, shrink, dense, rows, gains, grad):
    n = WIDEN_STEPS
    every = lambda a: pl.BlockSpec((a.shape[0] // n, a.shape[1]), lambda i: (i, 0))
    one = lambda a: pl.BlockSpec(a.shape, lambda i: (0, 0))
    size = MB * rows[0].shape[0] // n
    half = lambda m: pl.BlockSpec(
        (size, MODEL_WIDTH), lambda i: (jnp.clip(i - m * (n // MB), 0, n // MB - 1), 0)
    )
    shape = jax.ShapeDtypeStruct
    expand = shape((expand_parts[0].shape[0], 2 * F), f32)
    joined = shape((MB * rows[0].shape[0], MODEL_WIDTH), bf16)
    gain = shape((gains.shape[0],), f32)
    flat = pl.BlockSpec(gain.shape, lambda i: (0,))
    dense_out = [shape(a.shape, f32) for a in dense]
    return pl.pallas_call(
        widen_kernel,
        grid=(n,),
        in_specs=[every(a) for a in expand_parts]
        + [every(shrink)]
        + [every(a) for a in dense]
        + [half(m) for m in range(MB)]
        + [one(gains), every(grad)],
        out_specs=[every(expand), every(shrink)]
        + [every(a) for a in dense]
        + [every(joined), flat, flat, every(grad)],
        out_shape=[expand, shape(shrink.shape, f32), *dense_out, joined, gain, gain, shape(grad.shape, f32)],
        compiler_params=pltpu.CompilerParams(vmem_limit_bytes=VMEM_LIMIT),
        name="widen",
    )(*expand_parts, shrink, *dense, *rows, gains, grad)


def shards(
    tokens,
    doc_starts,
    routes,
    gates,
    attn_gain,
    w_q,
    key_value_weight,
    w_o,
    moe_gain,
    expert_in,
    expert_out,
    cotangent,
):
    links = Links()
    rows = tokens.shape[2]
    length = rows * links.contexts
    held = expert_in.shape[0]
    chained = links.chips == LINE and links.shards == SHARDS and held == 2
    width = w_q.shape[0]
    flat_tokens = tokens.reshape(MB * rows, MODEL_WIDTH)
    if chained:
        flat_cotangent = cotangent.reshape(MB * rows, MODEL_WIDTH)
        starts = doc_starts[:, 0]
        (
            turned_normed,
            query,
            turned_attn,
            middle,
            gains,
            cosine,
            sine,
            pair_weight,
            query_weight,
            output_weight,
            pairs,
            turned_rows,
            grad_blocks,
            result_blocks,
            row_grad_blocks,
            active,
            gate,
            up,
        ) = forward(
            flat_tokens,
            routes.transpose(0, 1, 3, 2),
            gates.transpose(0, 1, 3, 2),
            jnp.stack([attn_gain, moe_gain]),
            flat_cotangent,
            starts,
            rotation_constants(length),
            (key_value_weight, w_q, w_o),
            expert_in,
            expert_out,
        )
        result_blocks = result_blocks.reshape(grad_blocks.shape)
        row_grad_blocks = row_grad_blocks.reshape(grad_blocks.shape)
        (
            query_low,
            pair_low,
            middle_low,
            middle_grad,
            gain_two_grad,
            output_first,
            gate_first,
            up_first,
            gate_rest,
            up_rest,
            down_rest,
            pair_grad,
        ) = backward(
            query,
            starts,
            cosine,
            sine,
            middle,
            flat_cotangent,
            gains,
            pairs,
            turned_rows,
            grad_blocks,
            (active, gate, up),
            result_blocks,
            row_grad_blocks,
            output_weight,
        )
        (
            input_grad,
            output_second,
            _,
            output_total,
            query_total,
            pair_total,
            gain_total,
            gate_second,
            up_second,
            shrink_total,
        ) = dense_weights(
            (
                turned_normed,
                turned_attn,
                query_low,
                pair_low,
                middle_low,
                gains,
                gain_two_grad,
                cosine,
                sine,
            ),
            (middle_grad, flat_tokens, middle),
            query_weight,
            pair_weight,
            pair_grad.reshape(LINE, 2, rows, 2 * KEY_WIDTH),
            result_blocks,
            (gate_rest, up_rest, down_rest.reshape(F, MODEL_WIDTH)),
        )
        (
            expand_total,
            shrink_total,
            output_total,
            query_total,
            pair_total,
            block_output,
            gain_one_total,
            gain_two_total,
            input_grad,
        ) = widen(
            (gate_first, gate_second, up_first, up_second),
            shrink_total,
            (output_total, query_total, pair_total),
            (output_first, output_second),
            gain_total,
            input_grad,
        )
        return (
            block_output.reshape(MB, 1, rows, MODEL_WIDTH),
            input_grad.reshape(MB, 1, rows, MODEL_WIDTH),
            gain_one_total,
            query_total,
            pair_total,
            output_total,
            gain_two_total,
            expand_total.reshape(held, MODEL_WIDTH, 2 * F),
            shrink_total.reshape(held, F, MODEL_WIDTH),
        )

    positions = links.context * rows + jnp.arange(rows, dtype=jnp.int32)
    cosine, sine = rotation_tables(positions)
    key_places = jnp.arange(length, dtype=jnp.int32)
    flat_values = flat_tokens.astype(f32)
    scale_one = lax.rsqrt(jnp.mean(flat_values * flat_values, axis=-1, keepdims=True) + eps)
    unit_one = flat_values * scale_one
    expert_ids = jnp.arange(E, dtype=jnp.int32)
    chosen = (routes.reshape(MB, rows, TOP)[..., None] == expert_ids).astype(f32)
    combine = jnp.sum(gates.reshape(MB, rows, TOP)[..., None] * chosen, axis=2)
    gather = lambda w: lax.all_gather(w, "fsdp", axis=0, tiled=True)
    pair_weight, query_weight, output_weight = gather(key_value_weight), gather(w_q), gather(w_o)
    gain_one, gain_two = gather(attn_gain).astype(f32), gather(moe_gain).astype(f32)
    normed = (unit_one * gain_one).astype(bf16)
    both = lambda table: jnp.concatenate([table] * MB)
    own_pairs = rotate_columns(dot(normed, pair_weight), both(cosine), both(sine), KEY_WIDTH)
    query = rotate_columns(dot(normed, query_weight), both(cosine), both(sine), MODEL_WIDTH)
    own_pairs = own_pairs.reshape(MB, rows, 2 * KEY_WIDTH)
    pairs = lax.all_gather(own_pairs, "ctx", axis=1, tiled=True)

    combine = jnp.concatenate([combine] + [links.across(combine, k) for k in range(1, links.shards)], axis=1)
    combine = lax.dynamic_slice_in_dim(combine, links.shard * held, held, 2)
    combine = combine.transpose(0, 2, 1)[..., None]

    biases, biases_turned = [], []
    for m in range(MB):
        starts = doc_starts[m, 0]
        begin = jnp.max(jnp.where(starts[None, :] <= positions[:, None], starts[None, :], 0), axis=1)
        seen = (key_places[None, :] <= positions[:, None]) & (key_places[None, :] >= begin[:, None])
        biases.append(jnp.where(seen, 0.0, -1e30).astype(f32))
        places, begins = jnp.tile(positions, GROUP), jnp.tile(begin, GROUP)
        seen = (key_places[:, None] <= places[None, :]) & (key_places[:, None] >= begins[None, :])
        biases_turned.append(jnp.where(seen, 0.0, -1e30).astype(f32))

    middles, attns, results, row_grads = [], [], [], []
    rows_kept, grads_kept, pieces_kept = [], [], []
    for m in range(MB):
        own = slice(m * rows, (m + 1) * rows)
        attn = attention_forward(m, query, pairs, biases[m])
        middle = flat_tokens[own].astype(f32) + dot(attn, output_weight)
        scale_two = lax.rsqrt(jnp.mean(middle * middle, axis=-1, keepdims=True) + eps)
        moe_in = (middle * scale_two * gain_two).astype(bf16)
        out_grad = cotangent[m, 0]
        row_parts = [moe_in] + [links.across(moe_in, k) for k in range(1, links.shards)]
        grad_parts = [out_grad] + [links.across(out_grad, k) for k in range(1, links.shards)]
        result, row_grad, pieces = experts(row_parts, grad_parts, combine[m], expert_in, expert_out)
        for parts, sums in ((result, results), (row_grad, row_grads)):
            total = parts[0].astype(f32)
            for k in range(1, links.shards):
                total = total + links.across(parts[k], k).astype(f32)
            sums.append(total)
        middles.append(middle)
        attns.append(attn)
        rows_kept += row_parts
        grads_kept += grad_parts
        pieces_kept.append(pieces)
    merge = lambda items: jnp.concatenate(items, axis=0)
    expert_grads = expert_weights(
        merge(rows_kept), merge(grads_kept), *[merge([p[i] for p in pieces_kept]) for i in range(3)], held
    )
    expert_grads = [g.reshape(-1, g.shape[-1]) for g in expert_grads]
    outputs = [(middles[m] + results[m]).astype(bf16) for m in range(MB)]

    input_grads, query_lows, pair_lows, middle_lows = [], [], [], []
    gain_one_grad, gain_two_grad = 0.0, 0.0
    for m in range(MB):
        own = slice(m * rows, (m + 1) * rows)
        scale_two = lax.rsqrt(jnp.mean(middles[m] * middles[m], axis=-1, keepdims=True) + eps)
        unit_two = middles[m] * scale_two
        moe_in_grad = row_grads[m]
        gain_two_grad = gain_two_grad + jnp.sum(moe_in_grad * unit_two, axis=0)
        weighted = moe_in_grad * gain_two
        inner = jnp.mean(weighted * unit_two, axis=-1, keepdims=True)
        middle_grad = cotangent[m, 0].astype(f32) + (weighted - unit_two * inner) * scale_two
        middle_low = middle_grad.astype(bf16)
        attn_grad = dot(middle_low, output_weight, NT).astype(bf16)
        query_low, pair_grad = attention_backward(
            m, query, cosine, sine, pairs, biases_turned[m], attn_grad
        )
        parts = [lax.psum_scatter(pair_grad, "ctx", scatter_dimension=0, tiled=True)]
        pair_low = pair_gradient(parts, cosine, sine)
        normed_grad = dot(query_low, query_weight, NT) + dot(pair_low, pair_weight, NT)
        gain_one_grad = gain_one_grad + jnp.sum(normed_grad * unit_one[own], axis=0)
        weighted = normed_grad * gain_one
        inner = jnp.mean(weighted * unit_one[own], axis=-1, keepdims=True)
        residual_grad = (weighted - unit_one[own] * inner) * scale_one[own]
        input_grads.append(middle_grad + residual_grad)
        query_lows.append(query_low)
        pair_lows.append(pair_low)
        middle_lows.append(middle_low)

    join = lambda items: jnp.concatenate(items, axis=0)

    output_grad = dot(join(attns), join(middle_lows), TN).astype(bf16)
    query_grad = dot(normed, join(query_lows), TN).astype(bf16)
    pair_weight_grad = dot(normed, join(pair_lows), TN).astype(bf16)
    gain_grads = jnp.stack([gain_one_grad, gain_two_grad], axis=1)
    gain_grads = jnp.pad(gain_grads, ((0, 0), (0, LANES - 2))).astype(bf16)
    dense_grads = [output_grad, query_grad, jnp.concatenate([pair_weight_grad, gain_grads], axis=1)]
    totals = [lax.psum(g, "ctx") for g in expert_grads]
    for g in dense_grads:
        part = lax.psum_scatter(g, "fsdp", scatter_dimension=0, tiled=True)
        totals.append(lax.psum(part, "ctx"))
    gate_total, up_total, down_total, output_total, query_total, pair_total = [t.astype(f32) for t in totals]
    expand_total = jnp.concatenate([gate_total, up_total], axis=1)

    return (
        jnp.stack(outputs)[:, None],
        jnp.stack(input_grads)[:, None],
        pair_total[:, 2 * KEY_WIDTH],
        query_total,
        pair_total[:, : 2 * KEY_WIDTH],
        output_total,
        pair_total[:, 2 * KEY_WIDTH + 1],
        expand_total.reshape(held, MODEL_WIDTH, 2 * F),
        down_total.reshape(held, F, MODEL_WIDTH),
    )


def solution(mesh):
    return jax.shard_map(
        shards,
        mesh=mesh,
        in_specs=(
            P(None, "fsdp", "ctx", None),
            P(None, "fsdp", None),
            P(None, "fsdp", "ctx", None),
            P(None, "fsdp", "ctx", None),
            P("fsdp"),
            P("fsdp", None),
            P("fsdp", None),
            P("fsdp", None),
            P("fsdp"),
            P("fsdp", None, None),
            P("fsdp", None, None),
            P(None, "fsdp", "ctx", None),
        ),
        out_specs=(
            P(None, "fsdp", "ctx", None),
            P(None, "fsdp", "ctx", None),
            P("fsdp"),
            P("fsdp", None),
            P("fsdp", None),
            P("fsdp", None),
            P("fsdp"),
            P("fsdp", None, None),
            P("fsdp", None, None),
        ),
        check_vma=False,
    )
```

```python
import functools
import types

import jax
import jax.numpy as jnp
import numpy as np
from jax import lax
from jax.experimental import pallas as pl
from jax.experimental.pallas import tpu as pltpu
from jax.sharding import PartitionSpec as P

MODEL_WIDTH = 1536
QUERY_HEADS = 24
KEY_VALUE_HEADS = 8
HEAD_SIZE = 64
GROUP = QUERY_HEADS // KEY_VALUE_HEADS
KEY_WIDTH = KEY_VALUE_HEADS * HEAD_SIZE
F = 512
E = 8
TOP = 4
MB = 2
LANES = 128
PAIRS = KEY_WIDTH // LANES
PAIR_QUERY = 2 * GROUP * HEAD_SIZE
F_BLOCK = 256
VMEM_LIMIT = 60 * 1024 * 1024

eps = 1e-05
theta = 10000.0

NT = (((1,), (1,)), ((), ()))
TN = (((0,), (0,)), ((), ()))
bf16 = jnp.bfloat16
f32 = jnp.float32


def dot(left, right, dims=(((1,), (0,)), ((), ()))):
    return lax.dot_general(left, right, dims, preferred_element_type=f32)


def rotation_tables(positions):
    frequency = theta ** (-jnp.arange(0, HEAD_SIZE, 2, dtype=f32) / HEAD_SIZE)
    angles = positions.astype(f32)[:, None] * frequency[None, :]
    cosine, sine = jnp.cos(angles), jnp.sin(angles)
    repeat = LANES // HEAD_SIZE
    cosine = jnp.concatenate([cosine, cosine] * repeat, axis=1)
    sine = jnp.concatenate([-sine, sine] * repeat, axis=1)
    return cosine, sine


def rotation_constants(length):
    frequency = theta ** (-np.arange(0, HEAD_SIZE, 2, dtype=np.float64) / HEAD_SIZE)
    angles = np.arange(length, dtype=np.float64)[:, None] * frequency[None, :]
    cosine, sine = np.cos(angles), np.sin(angles)
    repeat = LANES // HEAD_SIZE
    cosine = np.concatenate([cosine, cosine] * repeat, axis=1)
    sine = np.concatenate([-sine, sine] * repeat, axis=1)
    return jnp.asarray(np.stack([cosine, sine]).astype(np.float32))


def visible_bias(starts, m, context, shape, query_axis):
    rows = shape[query_axis]
    narrow = (rows, 1) if query_axis == 0 else (1, rows)
    query = context * rows + lax.broadcasted_iota(jnp.int32, narrow, query_axis)
    begin = jnp.zeros(narrow, jnp.int32)
    for i in range(starts.shape[1]):
        begin = jnp.maximum(begin, jnp.where(query >= starts[m, i], starts[m, i], 0))
    key = lax.broadcasted_iota(jnp.int32, shape, 1 - query_axis)
    return jnp.where((key <= query) & (key >= begin), 0.0, -1e30).astype(f32)


def lane_index(shape):
    return lax.broadcasted_iota(jnp.int32, shape, 1)


def rotate(tile, cosine, sine):
    half = HEAD_SIZE // 2
    ahead = pltpu.roll(tile, LANES - half, 1)
    behind = pltpu.roll(tile, half, 1)
    first = lane_index(tile.shape) % HEAD_SIZE < half
    return tile * cosine + jnp.where(first, ahead, behind) * sine


def rotate_columns_kernel(rotated, values_ref, cosine_ref, sine_ref, out_ref):
    cosine, sine = cosine_ref[...], sine_ref[...]
    for i in range(values_ref.shape[1] // LANES):
        cols = slice(i * LANES, (i + 1) * LANES)
        tile = values_ref[:, cols]
        if i < rotated // LANES:
            tile = rotate(tile, cosine, sine)
        out_ref[:, cols] = tile.astype(bf16)


def rotate_columns(values, cosine, sine, rotated):
    return pl.pallas_call(
        functools.partial(rotate_columns_kernel, rotated),
        out_shape=jax.ShapeDtypeStruct(values.shape, bf16),
        compiler_params=pltpu.CompilerParams(vmem_limit_bytes=VMEM_LIMIT),
        name="rotate_columns",
    )(values, cosine, sine)


def pair_gradient_kernel(count, cosine_ref, sine_ref, *refs):
    out_ref = refs[-1]
    cosine, sine = cosine_ref[...], sine_ref[...]
    for i in range(2 * KEY_WIDTH // LANES):
        cols = slice(i * LANES, (i + 1) * LANES)
        total = refs[0][:, cols].astype(f32)
        for ref in refs[1:count]:
            total = total + ref[:, cols].astype(f32)
        if i < KEY_WIDTH // LANES:
            total = rotate(total, cosine, -sine)
        out_ref[:, cols] = total.astype(bf16)


def pair_gradient(parts, cosine, sine):
    return pl.pallas_call(
        functools.partial(pair_gradient_kernel, len(parts)),
        out_shape=jax.ShapeDtypeStruct(parts[0].shape, bf16),
        compiler_params=pltpu.CompilerParams(vmem_limit_bytes=VMEM_LIMIT),
        name="pair_gradient",
    )(cosine, sine, *parts)


def grouped(tiles, half):
    mine = lane_index(tiles[0].shape) // HEAD_SIZE == half
    rows = []
    for j in range(GROUP * half, GROUP * half + GROUP):
        tile = tiles[j // 2]
        if j % 2 != half:
            tile = pltpu.roll(tile, HEAD_SIZE, 1)
        rows.append(jnp.where(mine, tile, 0.0))
    return jnp.concatenate(rows, axis=0).astype(bf16)


def ungrouped(per_half, rows):
    heads = []
    for j in range(2 * GROUP):
        half, place = j // GROUP, j % GROUP
        tile = per_half[half][place * rows : (place + 1) * rows]
        if j % 2 != half:
            tile = pltpu.roll(tile, HEAD_SIZE, 1)
        heads.append(tile)
    low = lane_index(heads[0].shape) < HEAD_SIZE
    return [jnp.where(low, heads[2 * i], heads[2 * i + 1]) for i in range(GROUP)]


def query_tiles(query_ref):
    scale = 1.0 / HEAD_SIZE
    return [query_ref[:, i * LANES : (i + 1) * LANES].astype(f32) * scale for i in range(GROUP)]


def attention_pair(tiles, key, value, bias):
    rows = bias.shape[0]
    results = []
    for half in range(2):
        scores = dot(grouped(tiles, half), key, NT)
        scores = jnp.concatenate(
            [scores[g * rows : (g + 1) * rows] + bias for g in range(GROUP)], axis=0
        )
        peak = jnp.max(scores, axis=1, keepdims=True)
        weights = jnp.exp(scores - peak)
        total = jnp.sum(weights, axis=1, keepdims=True)
        results.append(dot(weights.astype(bf16), value) / total)
    return ungrouped(results, rows)


def attention_forward_kernel(query_ref, key_ref, value_ref, bias_ref, out_ref):
    tiles = attention_pair(query_tiles(query_ref), key_ref[...], value_ref[...], bias_ref[...])
    for i, tile in enumerate(tiles):
        out_ref[:, i * LANES : (i + 1) * LANES] = tile.astype(bf16)


def attention_forward(m, query, pairs, bias):
    rows, length = bias.shape
    return pl.pallas_call(
        attention_forward_kernel,
        grid=(PAIRS,),
        in_specs=[
            pl.BlockSpec((rows, PAIR_QUERY), lambda p: (m, p)),
            pl.BlockSpec((None, length, LANES), lambda p: (m, 0, p)),
            pl.BlockSpec((None, length, LANES), lambda p: (m, 0, p + PAIRS)),
            pl.BlockSpec((rows, length), lambda p: (0, 0)),
        ],
        out_specs=pl.BlockSpec((rows, PAIR_QUERY), lambda p: (0, p)),
        out_shape=jax.ShapeDtypeStruct((rows, MODEL_WIDTH), bf16),
        compiler_params=pltpu.CompilerParams(vmem_limit_bytes=VMEM_LIMIT),
        cost_estimate=pl.CostEstimate(
            flops=16 * rows * length * MODEL_WIDTH,
            bytes_accessed=4 * length * MODEL_WIDTH,
            transcendentals=rows * length * QUERY_HEADS,
        ),
        name="attention_forward",
    )(query, pairs, pairs, bias)


def attention_pair_gradient(tiles, grads, key, value, bias):
    rows = tiles[0].shape[0]
    key_grad, value_grad = None, None
    query_grads = []
    for half in range(2):
        query = grouped(tiles, half)
        grad = grouped(grads, half)
        scores = dot(key, query, NT) + bias
        weights = jnp.exp(scores - jnp.max(scores, axis=0, keepdims=True))
        prob = weights * (1.0 / jnp.sum(weights, axis=0, keepdims=True))
        prob_grad = dot(value, grad, NT)
        delta = jnp.sum(prob * prob_grad, axis=0, keepdims=True)
        score_grad = (prob * (prob_grad - delta)).astype(bf16)
        value_part = dot(prob.astype(bf16), grad)
        key_part = dot(score_grad, query)
        value_grad = value_part if half == 0 else value_grad + value_part
        key_grad = key_part if half == 0 else key_grad + key_part
        query_grads.append(dot(score_grad, key, TN))
    return ungrouped(query_grads, rows), key_grad, value_grad


def attention_backward_kernel(
    query_ref, cosine_ref, sine_ref, key_ref, value_ref, bias_ref, grad_ref, query_out, pair_out
):
    cosine, sine = cosine_ref[...], sine_ref[...]
    grads = [grad_ref[:, i * LANES : (i + 1) * LANES].astype(f32) for i in range(GROUP)]
    query_grads, key_grad, value_grad = attention_pair_gradient(
        query_tiles(query_ref), grads, key_ref[...], value_ref[...], bias_ref[...]
    )
    for i, tile in enumerate(query_grads):
        tile = rotate(tile * (1.0 / HEAD_SIZE), cosine, -sine)
        query_out[:, i * LANES : (i + 1) * LANES] = tile.astype(bf16)
    first = pl.multiple_of(pl.program_id(0) * LANES, LANES)
    pair_out[:, pl.ds(first, LANES)] = key_grad.astype(bf16)
    pair_out[:, pl.ds(first + KEY_WIDTH, LANES)] = value_grad.astype(bf16)


def attention_backward(m, query, cosine, sine, pairs, bias, grad):
    rows = cosine.shape[0]
    length = pairs.shape[1]
    whole = lambda shape: pl.BlockSpec(shape, lambda p: (0, 0))
    return pl.pallas_call(
        attention_backward_kernel,
        grid=(PAIRS,),
        in_specs=[
            pl.BlockSpec((rows, PAIR_QUERY), lambda p: (m, p)),
            whole((rows, LANES)),
            whole((rows, LANES)),
            pl.BlockSpec((None, length, LANES), lambda p: (m, 0, p)),
            pl.BlockSpec((None, length, LANES), lambda p: (m, 0, p + PAIRS)),
            whole(bias.shape),
            pl.BlockSpec((rows, PAIR_QUERY), lambda p: (0, p)),
        ],
        out_specs=[
            pl.BlockSpec((rows, PAIR_QUERY), lambda p: (0, p)),
            whole((length, 2 * KEY_WIDTH)),
        ],
        out_shape=[
            jax.ShapeDtypeStruct((rows, MODEL_WIDTH), bf16),
            jax.ShapeDtypeStruct((length, 2 * KEY_WIDTH), bf16),
        ],
        compiler_params=pltpu.CompilerParams(vmem_limit_bytes=VMEM_LIMIT),
        cost_estimate=pl.CostEstimate(
            flops=40 * rows * length * MODEL_WIDTH,
            bytes_accessed=8 * length * MODEL_WIDTH,
            transcendentals=rows * length * QUERY_HEADS,
        ),
        name="attention_backward",
    )(query, cosine, sine, pairs, pairs, bias, grad)


def expert_block(inputs, out_grad, combine, gate_weight, up_weight, down_weight):
    gate = dot(inputs, gate_weight)
    up = dot(inputs, up_weight)
    sigmoid = jax.nn.sigmoid(gate)
    silu = gate * sigmoid
    active = (silu * up * combine).astype(bf16)
    active_grad = dot(out_grad, down_weight, NT) * combine
    gate_grad = (active_grad * up * sigmoid * (1.0 + gate * (1.0 - sigmoid))).astype(bf16)
    up_grad = (active_grad * silu).astype(bf16)
    result = dot(active, down_weight)
    row_grad = dot(gate_grad, gate_weight, NT) + dot(up_grad, up_weight, NT)
    return active, gate_grad, up_grad, result, row_grad


def experts_kernel(parts, rows, steps, combine_ref, gate_ref, up_ref, down_ref, *refs):
    rows_in, grads_in = refs[:parts], refs[parts : 2 * parts]
    refs = refs[2 * parts :]
    results, row_grads = refs[:parts], refs[parts : 2 * parts]
    active_out, gate_out, up_out, rows_all, grads_all, result_sum, grad_sum = refs[2 * parts :]
    step = pl.program_id(0) * pl.num_programs(1) + pl.program_id(1)

    @pl.when(step == 0)
    def _():
        for k in range(parts):
            place = slice(k * rows, (k + 1) * rows)
            rows_all[place] = rows_in[k][...]
            grads_all[place] = grads_in[k][...]
        result_sum[...] = jnp.zeros_like(result_sum)
        grad_sum[...] = jnp.zeros_like(grad_sum)

    inputs, out_grad, combine = rows_all[...], grads_all[...], combine_ref[0]
    active, gate_grad, up_grad, result, row_grad = expert_block(
        inputs, out_grad, combine, gate_ref[0], up_ref[0], down_ref[0]
    )
    active_out[...] = active
    gate_out[...] = gate_grad
    up_out[...] = up_grad
    result_sum[...] += result
    grad_sum[...] += row_grad

    @pl.when(step == steps - 1)
    def _():
        for k in range(parts):
            place = slice(k * rows, (k + 1) * rows)
            results[k][...] = result_sum[place].astype(bf16)
            row_grads[k][...] = grad_sum[place].astype(bf16)


def experts(row_parts, grad_parts, combine, expert_in, expert_out):
    parts = len(row_parts)
    rows = row_parts[0].shape[0]
    held = expert_in.shape[0]
    tokens = parts * rows
    blocks = F // F_BLOCK
    whole = pl.BlockSpec((rows, MODEL_WIDTH), lambda e, b: (0, 0))
    piece = pl.BlockSpec((tokens, F_BLOCK), lambda e, b: (0, e * blocks + b))
    row_shape = jax.ShapeDtypeStruct((rows, MODEL_WIDTH), bf16)
    piece_shape = jax.ShapeDtypeStruct((tokens, held * F), bf16)
    out = pl.pallas_call(
        functools.partial(experts_kernel, parts, rows, held * blocks),
        grid=(held, blocks),
        in_specs=[
            pl.BlockSpec((1, tokens, 1), lambda e, b: (e, 0, 0)),
            pl.BlockSpec((1, MODEL_WIDTH, F_BLOCK), lambda e, b: (e, 0, b)),
            pl.BlockSpec((1, MODEL_WIDTH, F_BLOCK), lambda e, b: (e, 0, b + blocks)),
            pl.BlockSpec((1, F_BLOCK, MODEL_WIDTH), lambda e, b: (e, b, 0)),
        ]
        + [whole] * (2 * parts),
        out_specs=[whole] * (2 * parts) + [piece] * 3,
        out_shape=[row_shape] * (2 * parts) + [piece_shape] * 3,
        scratch_shapes=[
            pltpu.VMEM((tokens, MODEL_WIDTH), bf16),
            pltpu.VMEM((tokens, MODEL_WIDTH), bf16),
            pltpu.VMEM((tokens, MODEL_WIDTH), f32),
            pltpu.VMEM((tokens, MODEL_WIDTH), f32),
        ],
        compiler_params=pltpu.CompilerParams(vmem_limit_bytes=VMEM_LIMIT),
        cost_estimate=pl.CostEstimate(
            flops=12 * tokens * held * MODEL_WIDTH * F,
            bytes_accessed=6 * held * MODEL_WIDTH * F + 20 * tokens * MODEL_WIDTH,
            transcendentals=tokens * held * F,
        ),
        name="experts",
    )(combine, expert_in, expert_in, expert_out, *row_parts, *grad_parts)
    return out[:parts], out[parts : 2 * parts], out[2 * parts :]


def expert_weights_kernel(rows_ref, grads_ref, active_ref, gate_ref, up_ref, gate_out, up_out, down_out, turned):
    step = pl.program_id(0) * pl.num_programs(1) + pl.program_id(1)

    @pl.when(step == 0)
    def _():
        turned[...] = rows_ref[...].T

    gate_out[0] = dot(turned[...], gate_ref[...]).astype(bf16)
    up_out[0] = dot(turned[...], up_ref[...]).astype(bf16)
    down_out[0] = dot(active_ref[...], grads_ref[...], TN).astype(bf16)


def expert_weights(rows, grads, active, gate, up, held):
    tokens = rows.shape[0]
    blocks = F // F_BLOCK
    whole = pl.BlockSpec((tokens, MODEL_WIDTH), lambda e, b: (0, 0))
    piece = pl.BlockSpec((tokens, F_BLOCK), lambda e, b: (0, e * blocks + b))
    wide = pl.BlockSpec((1, MODEL_WIDTH, F_BLOCK), lambda e, b: (e, 0, b))
    return pl.pallas_call(
        expert_weights_kernel,
        grid=(held, blocks),
        in_specs=[whole] * 2 + [piece] * 3,
        out_specs=[wide, wide, pl.BlockSpec((1, F_BLOCK, MODEL_WIDTH), lambda e, b: (e, b, 0))],
        out_shape=[
            jax.ShapeDtypeStruct((held, MODEL_WIDTH, F), bf16),
            jax.ShapeDtypeStruct((held, MODEL_WIDTH, F), bf16),
            jax.ShapeDtypeStruct((held, F, MODEL_WIDTH), bf16),
        ],
        scratch_shapes=[pltpu.VMEM((MODEL_WIDTH, tokens), bf16)],
        compiler_params=pltpu.CompilerParams(vmem_limit_bytes=VMEM_LIMIT),
        cost_estimate=pl.CostEstimate(
            flops=6 * tokens * held * MODEL_WIDTH * F,
            bytes_accessed=6 * held * MODEL_WIDTH * F + 8 * tokens * MODEL_WIDTH,
            transcendentals=0,
        ),
        name="expert_weights",
    )(rows, grads, active, gate, up)


class Links:
    def __init__(self):
        self.shards = lax.axis_size("fsdp")
        self.contexts = lax.axis_size("ctx")
        self.chips = self.contexts // 2
        self.shard = lax.axis_index("fsdp")
        self.context = lax.axis_index("ctx")
        self.chip = self.context // 2
        self.core = self.context % 2

    def across(self, array, k):
        return lax.ppermute(array, "fsdp", [(i, i ^ k) for i in range(self.shards)])

    def other_core(self, array):
        return lax.ppermute(array, "ctx", [(i, i ^ 1) for i in range(self.contexts)])

    def shift(self, array, s):
        n = self.contexts
        return lax.ppermute(array, "ctx", [(i, (i + 2 * s) % n) for i in range(n)])


MESH = pl.DeviceIdType.MESH
LINE = 4


class Place:
    def __init__(self):
        self.shard, self.context = lax.axis_index("fsdp"), lax.axis_index("ctx")
        self.core, self.chip = self.context % 2, self.context // 2
        self.partner = {"ctx": 2 * self.chip + 1 - self.core}

    def peer_index(self, k):
        x, y = (self.shard % 2 + k % 2) % 2, (self.shard // 2 + k // 2) % 2
        return 2 * y + x

    def peer(self, k):
        return {"fsdp": self.peer_index(k)}

    def chip_device(self, chip):
        return {"ctx": 2 * chip + self.core}


def remote(source, target, sems, index, device):
    return pltpu.make_async_remote_copy(
        src_ref=source,
        dst_ref=target,
        send_sem=sems.at[0, index],
        recv_sem=sems.at[1, index],
        device_id=device,
        device_id_type=MESH,
    )


def greet(device):
    pl.semaphore_signal(pltpu.get_barrier_semaphore(), inc=1, device_id=device, device_id_type=MESH)


SHARDS = 4
GAIN_ROWS = 16


class Square:
    def __init__(self, place, blocks, direct_sem, relay_sem, base=0):
        half = blocks.shape[1] // 2
        own = blocks.at[place.shard]
        self.directs = [remote(own, own, direct_sem, base + k - 1, place.peer(k)) for k in (1, 2)]
        self.relays = []
        for k in (1, 2):
            spot = blocks.at[place.peer_index(k), (k - 1) * half : k * half]
            self.relays.append(remote(spot, spot, relay_sem, base + k - 1, place.peer(3 - k)))

    def start(self):
        for copy in self.directs:
            copy.start()

    def pass_on(self):
        for direct, relay in zip(self.directs, self.relays):
            direct.wait_recv()
            relay.start()

    def finish(self):
        for copy in self.relays:
            copy.wait_recv()

    def drain(self):
        for copy in self.directs + self.relays:
            copy.wait_send()


LAST = LINE - 1
WIDE = 4


def forward_kernel(
    tokens,
    routes,
    gates,
    gain_pair,
    cotangent,
    starts,
    tables,
    pair_src,
    query_src,
    output_src,
    expand_src,
    shrink_src,
    turned_normed_out,
    query_rows_out,
    turned_attn_out,
    middle_out,
    gain_rows_out,
    cosine,
    sine,
    pair_out,
    query_out,
    output_out,
    pairs,
    turned_out,
    grads_out,
    results_out,
    row_grads_out,
    active_out,
    gate_out,
    up_out,
    turned_normed,
    query,
    turned_attn,
    middle,
    gains,
    turned_rows,
    pair_weight,
    query_weight,
    output_weight,
    expand,
    shrink,
    own_pairs,
    normed,
    combine_in,
    combine_own,
    attn,
    bias,
    combine,
    rows_all,
    grads_all,
    result_sum,
    grad_sum,
    key_value,
    load_sem,
    table_sem,
    store_sem,
    expert_sem,
    gain_sem,
    combine_sem,
    direct_sem,
    relay_sem,
    pass_sem,
    right_sem,
    left_sem,
    core_sem,
    own_sem,
    square_direct_sem,
    square_relay_sem,
    key_sem,
    emit_sem,
    last_sem,
):
    r = types.SimpleNamespace(**locals())
    place = Place()
    core, chip, shard = place.core, place.chip, place.shard
    local = pltpu.make_async_copy
    rows = r.cosine.shape[0]
    wide = SHARDS * rows
    held = r.pair_src.shape[0]
    half, quarter = held // 2, held // 4
    greet_line(place)
    length = r.bias.shape[2]

    def rows_of(owner, piece, size):
        return pl.ds(pl.multiple_of(owner * held + core * half, half) + piece, size)

    sources = (r.pair_src, r.query_src, r.output_src)
    weights = (r.pair_weight, r.query_weight, r.output_weight)
    weight_outs = (r.pair_out, r.query_out, r.output_out)
    loads, directs, relays, passes, stores = [], [], [], [], []
    for w in range(3):
        weight = weights[w]
        own_rows = pl.ds(pl.multiple_of(shard * held, held), held)
        loads.append(local(sources[w], weight.at[own_rows], r.load_sem.at[w]))
        stores.append(local(weight, weight_outs[w], r.store_sem.at[w]))
        mine = sources[w].at[pl.ds(pl.multiple_of(core * half, half), half)]
        spot = weight.at[rows_of(shard, 0, half)]
        directs.append([remote(mine, spot, r.direct_sem, 2 * w + k - 1, place.peer(k)) for k in (1, 2)])
        relay, onward = [], []
        for k in (1, 2):
            spot = weight.at[rows_of(place.peer_index(k), (k - 1) * quarter, quarter)]
            relay.append(remote(spot, spot, r.relay_sem, 2 * w + k - 1, place.peer(3 - k)))
            spot = weight.at[rows_of(place.peer_index(k), 0, half)]
            onward.append(remote(spot, spot, r.pass_sem, 4 * w + k - 1, place.partner))
        for k in (1, 2):
            spot = weight.at[rows_of(place.peer_index(3), (k - 1) * quarter, quarter)]
            onward.append(remote(spot, spot, r.pass_sem, 4 * w + k + 1, place.partner))
        relays.append(relay)
        passes.append(onward)

    def send_weight(w):
        for copy in directs[w]:
            copy.start()

    def relay_weight(w):
        for k in (1, 2):
            directs[w][k - 1].wait_recv()
            relays[w][k - 1].start()
        for k in (1, 2):
            passes[w][k - 1].start()

    def pass_weight(w):
        for k in (1, 2):
            relays[w][k - 1].wait_recv()
            passes[w][k + 1].start()

    def settle_weight(w):
        loads[w].wait()
        for copy in passes[w]:
            copy.wait_recv()
        stores[w].start()

    def sent_weight(w):
        for copy in directs[w] + relays[w] + passes[w]:
            copy.wait_send()
        stores[w].wait()

    send_weight(0)

    gain_rows = r.gains.at[pl.ds(pl.multiple_of(shard * GAIN_ROWS, GAIN_ROWS), GAIN_ROWS)]
    gain_rows[...] = jnp.concatenate([r.gain_pair[...], jnp.zeros((GAIN_ROWS - 2, held), bf16)], axis=0)
    expert_row = lax.broadcasted_iota(jnp.int32, (E, rows), 0)
    for m in range(MB):
        combine = jnp.zeros((E, rows), f32)
        for k in range(TOP):
            combine += jnp.where(expert_row == r.routes[m, 0, k : k + 1], r.gates[m, 0, k : k + 1], 0.0)
        r.combine_own[:, m * rows : (m + 1) * rows] = combine
    r.combine_in[shard] = r.combine_own[...]
    small_copies = []
    for k in range(1, SHARDS):
        small_copies.append(remote(gain_rows, gain_rows, r.gain_sem, k - 1, place.peer(k)))
        small_copies.append(remote(r.combine_own, r.combine_in.at[shard], r.combine_sem, k - 1, place.peer(k)))

    for copy in small_copies:
        copy.start()
    at = pl.ds(pl.multiple_of(place.context * rows, rows), rows)
    table_loads = [
        local(r.tables.at[i, at], table, r.table_sem.at[i]) for i, table in enumerate((r.cosine, r.sine))
    ]
    for load in table_loads + loads:
        load.start()
    expert_loads = [
        local(r.expand_src, r.expand, r.expert_sem.at[0]),
        local(r.shrink_src, r.shrink, r.expert_sem.at[1]),
    ]
    for load in expert_loads:
        load.start()
    for m in range(MB):
        r.grads_all[m, shard] = r.cotangent[m * rows : (m + 1) * rows]
    grad_squares = [Square(place, r.grads_all.at[m], r.square_direct_sem, r.square_relay_sem, 2 * m) for m in range(MB)]
    row_squares = [
        Square(place, r.rows_all.at[m], r.square_direct_sem, r.square_relay_sem, 2 * (MB + m)) for m in range(MB)
    ]

    def spread_gains():
        r.gain_rows_out[...] = jnp.zeros_like(r.gain_rows_out)
        for b in range(SHARDS):
            pair = r.gains[b * GAIN_ROWS : b * GAIN_ROWS + 2]
            r.gain_rows_out[0:2, b * held : (b + 1) * held] = pair.astype(f32)

    def gain_times(values, row, write):
        for b in range(SHARDS):
            columns = slice(b * held, (b + 1) * held)
            write(columns, (values[:, columns] * r.gain_rows_out[row : row + 1, columns]).astype(bf16))

    values = r.tokens[...].astype(f32)
    unit = values * lax.rsqrt(jnp.mean(values * values, axis=-1, keepdims=True) + eps)
    for copy in small_copies:
        copy.wait_recv()

    def write_normed(columns, value):
        r.normed[:, columns] = value

    spread_gains()
    gain_times(unit, 0, write_normed)
    r.turned_normed[...] = r.normed[...].T
    for b in range(SHARDS):
        spread = jnp.concatenate([r.combine_in[b], jnp.zeros((LANES - E, MB * rows), f32)], axis=0)
        r.combine[b] = spread.T
    for m in range(MB):
        r.bias[m] = visible_bias(r.starts, m, place.context, (rows, length), 0)
    for load in table_loads:
        load.wait()

    relay_weight(0)
    send_weight(1)
    pass_weight(0)
    settle_weight(0)
    cosine, sine = r.cosine[...], r.sine[...]

    def project(weight, column, rotated):
        result = dot(r.normed[...], weight[:, pl.ds(column, WIDE * LANES)])
        tiles = []
        for m in range(MB):
            for i in range(WIDE):
                tile = result[m * rows : (m + 1) * rows, i * LANES : (i + 1) * LANES]
                tiles.append((m, i, rotate(tile, cosine, sine) if rotated else tile))
        return tiles

    blocks = KEY_WIDTH // (WIDE * LANES)
    for b in range(2 * blocks):
        column = b * WIDE * LANES
        for m, i, tile in project(r.pair_weight, column, b < blocks):
            r.own_pairs[m, :, pl.ds(column + i * LANES, LANES)] = tile.astype(bf16)

    def chunk(m, owner):
        owner = jnp.clip(owner, 0, LAST)
        return r.pairs.at[m, pl.ds(pl.multiple_of((2 * owner + core) * rows, rows), rows)]

    def move(m, t, direction):
        target = chunk(m, chip - direction * (t - 1))
        source = r.own_pairs.at[m] if t == 1 else target
        sems = r.right_sem if direction > 0 else r.left_sem
        device = place.chip_device(jnp.clip(chip + direction, 0, LAST))
        return remote(source, target, sems, m * LAST + t - 1, device)

    def sends(t, direction):
        owner = chip - direction * (t - 1)
        if direction > 0:
            return (chip < LAST) & (owner >= 0)
        return (chip > 0) & (owner <= LAST)

    def gets(t, direction):
        owner = chip - direction * t
        return owner >= 0 if direction > 0 else owner <= LAST

    def came(m, t, direction):
        spot = chunk(m, chip - direction * t)
        sems = r.right_sem if direction > 0 else r.left_sem
        return remote(spot, spot, sems, m * LAST + t - 1, place.partner)

    def pass_chunk(m, t, direction):
        spot = chunk(m, chip - direction * t)
        index = (m * LINE + t) * 2 + (1 if direction > 0 else 0)
        return remote(spot, spot, r.core_sem, index, place.partner)

    def take_step(m, t):
        for direction in (1, -1):

            @pl.when(gets(t, direction))
            def _():
                came(m, t, direction).wait_recv()
                if t < LAST:

                    @pl.when(sends(t + 1, direction))
                    def _():
                        move(m, t + 1, direction).start()

                pass_chunk(m, t, direction).start()

    own_copies = []
    for m in range(MB):
        for direction in (1, -1):

            @pl.when(sends(1, direction))
            def _():
                move(m, 1, direction).start()

        own_copies.append(
            (
                local(r.own_pairs.at[m], chunk(m, chip), r.own_sem.at[m]),
                remote(r.own_pairs.at[m], chunk(m, chip), r.core_sem, m * LINE * 2, place.partner),
            )
        )
        for copy in own_copies[m]:
            copy.start()

    def settle_pairs(m):
        own_copies[m][0].wait()
        own_copies[m][1].wait()
        for t in range(1, LINE):
            for direction in (1, -1):

                @pl.when(gets(t, direction))
                def _():
                    pass_chunk(m, t, direction).wait()

    def query_block(b, carry):
        column = pl.multiple_of(b * WIDE * LANES, WIDE * LANES)
        for m, i, tile in project(r.query_weight, column, True):
            r.query[m * rows : (m + 1) * rows, pl.ds(column + i * LANES, LANES)] = tile.astype(bf16)
        return carry

    def key_load(m, p, slot, i):
        lane = pl.multiple_of(p * LANES, LANES) + i * KEY_WIDTH
        return local(r.pairs.at[m, :, pl.ds(lane, LANES)], r.key_value.at[slot, i], r.key_sem.at[slot, i])

    def attend(m):
        own = slice(m * rows, (m + 1) * rows)
        for i in range(2):
            key_load(m, 0, 0, i).start()

        def pair(p, carry):
            slot = p % 2
            for i in range(2):
                key_load(m, p, slot, i).wait()

            @pl.when(p + 1 < PAIRS)
            def _():
                for i in range(2):
                    key_load(m, p + 1, 1 - slot, i).start()

            column = pl.multiple_of(p * PAIR_QUERY, PAIR_QUERY)
            columns = [pl.ds(column + i * LANES, LANES) for i in range(GROUP)]
            tiles = [r.query[own, c].astype(f32) * (1.0 / HEAD_SIZE) for c in columns]
            results = attention_pair(tiles, r.key_value[slot, 0], r.key_value[slot, 1], r.bias[m])
            for c, tile in zip(columns, results):
                r.attn[own, c] = tile.astype(bf16)
            return carry

        lax.fori_loop(0, PAIRS, pair, 0)
        r.turned_attn[:, own] = r.attn[own].T

    def finish_attention(m):
        own = slice(m * rows, (m + 1) * rows)
        middle = r.tokens[own].astype(f32) + dot(r.attn[own], r.output_weight[...])
        r.middle[own] = middle
        unit = middle * lax.rsqrt(jnp.mean(middle * middle, axis=-1, keepdims=True) + eps)

        def write(columns, value):
            r.rows_all[m, shard, :, columns] = value

        gain_times(unit, 1, write)

    active, gate, up = [r.pair_weight.at[i * wide : (i + 1) * wide] for i in range(3)]
    results, row_grads = [r.query_weight.at[i * wide : (i + 1) * wide] for i in range(2)]

    turned = r.turned_rows

    def turn(m):
        turned[...] = r.rows_all[m].reshape(wide, MODEL_WIDTH).T

    def emits(m):
        pairs = (
            (turned, r.turned_out.at[:, m * wide : (m + 1) * wide]),
            (r.grads_all.at[m], r.grads_out.at[m]),
            (results, r.results_out.at[m]),
            (row_grads, r.row_grads_out.at[m]),
        )
        for e in range(2):
            columns = slice(e * F, (e + 1) * F)
            pairs += tuple(
                (source.at[:, columns], target.at[m, :, columns])
                for source, target in ((active, r.active_out), (gate, r.gate_out), (up, r.up_out))
            )
        return [local(a, b, r.emit_sem.at[m * len(pairs) + i]) for i, (a, b) in enumerate(pairs)]

    def expert_steps(m, between):
        steps = [(e, b) for e in range(r.expand.shape[0]) for b in range(F // F_BLOCK)]
        for i, (e, b) in enumerate(steps):
            weight = r.combine[:, m * rows : (m + 1) * rows, :].reshape(wide, LANES)
            expert = shard * r.expand.shape[0] + e
            chosen = jnp.where(lane_index(weight.shape) == expert, weight, 0.0)
            columns = slice(b * F_BLOCK, (b + 1) * F_BLOCK)
            up_columns = slice(F + b * F_BLOCK, F + (b + 1) * F_BLOCK)
            a, g, u, result, row_grad = expert_block(
                r.rows_all[m].reshape(wide, MODEL_WIDTH),
                r.grads_all[m].reshape(wide, MODEL_WIDTH),
                jnp.sum(chosen, axis=1, keepdims=True),
                r.expand[e, :, columns],
                r.expand[e, :, up_columns],
                r.shrink[e, columns, :],
            )
            spot = slice(e * F + b * F_BLOCK, e * F + (b + 1) * F_BLOCK)
            active[:, spot], gate[:, spot], up[:, spot] = a, g, u
            if i == 0:
                r.result_sum[...] = result
                r.grad_sum[...] = row_grad
            elif i < len(steps) - 1:
                r.result_sum[...] += result
                r.grad_sum[...] += row_grad
            else:
                results[...] = (r.result_sum[...] + result).astype(bf16)
                row_grads[...] = (r.grad_sum[...] + row_grad).astype(bf16)
            if i in between:
                between[i]()

    relay_weight(1)
    send_weight(2)
    take_step(0, 1)
    take_step(1, 1)
    pass_weight(1)
    take_step(0, 2)
    settle_weight(1)
    lax.fori_loop(0, MODEL_WIDTH // (WIDE * LANES), query_block, 0)
    relay_weight(2)
    grad_squares[0].start()
    take_step(1, 2)
    take_step(0, 3)
    settle_pairs(0)
    attend(0)
    pass_weight(2)
    grad_squares[0].pass_on()
    take_step(1, 3)
    settle_weight(2)
    finish_attention(0)
    row_squares[0].start()
    settle_pairs(1)
    attend(1)
    row_squares[0].pass_on()
    finish_attention(1)
    row_squares[1].start()
    grad_squares[1].start()
    early = [
        local(source, target, r.last_sem.at[i])
        for i, (source, target) in enumerate(
            (
                (r.turned_normed, r.turned_normed_out),
                (r.query, r.query_rows_out),
                (r.turned_attn, r.turned_attn_out),
                (r.middle, r.middle_out),
            )
        )
    ]
    for emit in early:
        emit.start()
    for load in expert_loads:
        load.wait()
    sent_weight(0)
    sent_weight(1)
    grad_squares[0].finish()
    row_squares[0].finish()
    expert_steps(0, {1: row_squares[1].pass_on})
    turn(0)
    for emit in emits(0):
        emit.start()
    for emit in early:
        emit.wait()

    for copy in small_copies:
        copy.wait_send()
    sent_weight(2)
    for m in range(MB):
        for t in range(1, LINE):
            for direction in (1, -1):

                @pl.when(sends(t, direction))
                def _():
                    move(m, t, direction).wait_send()

    for square in grad_squares[:1] + row_squares[:1]:
        square.drain()
    grad_squares[1].pass_on()
    row_squares[1].finish()
    for emit in emits(0):
        emit.wait()
    turn(1)
    grad_squares[1].finish()
    last = emits(1)

    def emit_first():
        for emit in last[:2] + last[4:7]:
            emit.start()

    expert_steps(1, {1: emit_first})
    for emit in last[2:4] + last[7:]:
        emit.start()
    for square in grad_squares[1:] + row_squares[1:]:
        square.drain()
    for emit in last:
        emit.wait()


def forward(tokens, routes, gates, gain_pair, cotangent, starts, tables, weights, expert_in, expert_out):
    rows = tokens.shape[0] // MB
    length = tables.shape[1]
    wide = SHARDS * rows
    held = weights[0].shape[0]
    dma = pltpu.SemaphoreType.DMA
    anywhere = pl.BlockSpec(memory_space=pl.ANY)
    vmem = pl.BlockSpec(memory_space=pltpu.VMEM)
    shape = jax.ShapeDtypeStruct
    low = lambda *s: pltpu.VMEM(s, bf16)
    full = [(SHARDS * held, w.shape[1]) for w in weights]
    blocks = (MB, SHARDS, rows, MODEL_WIDTH)
    return pl.pallas_call(
        forward_kernel,
        in_specs=[vmem] * 5 + [pl.BlockSpec(memory_space=pltpu.SMEM)] + [anywhere] * 6,
        out_specs=[anywhere] * 4 + [vmem] * 3 + [anywhere] * 11,
        out_shape=[
            shape(tokens.shape[::-1], bf16),
            shape(tokens.shape, bf16),
            shape(tokens.shape[::-1], bf16),
            shape(tokens.shape, f32),
            shape((8, MODEL_WIDTH), f32),
            shape((rows, LANES), f32),
            shape((rows, LANES), f32),
        ]
        + [shape(f, bf16) for f in full]
        + [
            shape((MB, length, 2 * KEY_WIDTH), bf16),
            shape((MODEL_WIDTH, MB * wide), bf16),
            shape(blocks, bf16),
            shape((MB, wide, MODEL_WIDTH), bf16),
            shape((MB, wide, MODEL_WIDTH), bf16),
        ]
        + [shape((MB, wide, 2 * F), bf16)] * 3,
        scratch_shapes=[
            low(*tokens.shape[::-1]),
            low(*tokens.shape),
            low(*tokens.shape[::-1]),
            pltpu.VMEM(tokens.shape, f32),
            low(SHARDS * GAIN_ROWS, held),
            low(MODEL_WIDTH, wide),
        ]
        + [low(*f) for f in full]
        + [
            low(*expert_in.shape),
            low(*expert_out.shape),
            low(MB, rows, 2 * KEY_WIDTH),
            low(*tokens.shape),
            pltpu.VMEM((SHARDS, E, MB * rows), f32),
            pltpu.VMEM((E, MB * rows), f32),
            low(*tokens.shape),
            pltpu.VMEM((MB, rows, length), f32),
            pltpu.VMEM((SHARDS, MB * rows, LANES), f32),
            low(*blocks),
            low(*blocks),
            pltpu.VMEM((wide, MODEL_WIDTH), f32),
            pltpu.VMEM((wide, MODEL_WIDTH), f32),
            low(2, 2, length, LANES),
            dma((3,)),
            dma((2,)),
            dma((3,)),
            dma((2,)),
            dma((2, SHARDS - 1)),
            dma((2, SHARDS - 1)),
            dma((2, 6)),
            dma((2, 6)),
            dma((2, 12)),
            dma((2, MB * LAST)),
            dma((2, MB * LAST)),
            dma((2, 2 * MB * LINE)),
            dma((MB,)),
            dma((2, 4 * MB)),
            dma((2, 4 * MB)),
            dma((2, 2)),
            dma((10 * MB,)),
            dma((4,)),
        ],
        compiler_params=pltpu.CompilerParams(
            collective_id=1, has_side_effects=True, vmem_limit_bytes=VMEM_LIMIT
        ),
        name="forward",
    )(tokens, routes, gates, gain_pair, cotangent, starts, tables, *weights, expert_in, expert_out)


ADD_ROWS = 64


def add_into(out, *parts):
    rows = out.shape[0]
    size = max(d for d in range(16, ADD_ROWS + 1, 16) if rows % d == 0)

    def body(i, carry):
        spot = pl.ds(pl.multiple_of(i * size, size), size)
        total = parts[0][spot].astype(f32)
        for part in parts[1:]:
            total = total + part[spot].astype(f32)
        out[spot] = total.astype(out.dtype)
        return carry

    lax.fori_loop(0, rows // size, body, 0)


def greet_line(place):
    has_left, has_right = place.chip > 0, place.chip < LINE - 1
    greet(place.partner)
    for k in range(1, SHARDS):
        greet(place.peer(k))

    @pl.when(has_left)
    def _():
        greet(place.chip_device(place.chip - 1))

    @pl.when(has_right)
    def _():
        greet(place.chip_device(place.chip + 1))

    neighbours = jnp.where(has_left, 1, 0) + jnp.where(has_right, 1, 0)
    pl.semaphore_wait(pltpu.get_barrier_semaphore(), SHARDS + neighbours)


class Line:
    def __init__(self, place, pieces, sems):
        near_sem, far_sem, back_sem, pass_sem, store_sem = sems
        chip = place.chip
        self.inner = (chip == 1) | (chip == 2)
        outer = place.chip_device(3 * (chip // 2))
        inner = place.chip_device(1 + chip // 2)
        facing = place.chip_device(3 - chip)
        self.pieces = pieces
        numbered = list(enumerate(pieces))
        self.inward = [remote(p[0], p[1], near_sem, i, inner) for i, p in numbered]
        self.facing = [remote(p[0], p[2], far_sem, i, facing) for i, p in numbered]
        self.outward = [remote(p[1], p[3], back_sem, i, outer) for i, p in numbered]
        self.pass_inner = [remote(p[1], p[3], pass_sem, i, place.partner) for i, p in numbered]
        self.pass_outer = [remote(p[3], p[3], pass_sem, i, place.partner) for i, p in numbered]
        self.stores = [pltpu.make_async_copy(p[1], p[3], store_sem.at[i]) for i, p in numbered]

    def ready(self, *items):
        @pl.when(jnp.logical_not(self.inner))
        def _():
            for i in items:
                self.inward[i].start()

    def serve(self, halfway=(), finish=(), forward=()):
        @pl.when(self.inner)
        def _():
            for i in halfway:
                self.inward[i].wait_recv()
                own, near = self.pieces[i][:2]
                add_into(own, own, near)
                self.facing[i].start()
            for i in finish:
                self.facing[i].wait_recv()
                own, near, far = self.pieces[i][:3]
                add_into(near, own, far)
                self.outward[i].start()
                self.pass_inner[i].start()
                self.stores[i].start()

        @pl.when(jnp.logical_not(self.inner))
        def _():
            for i in forward:
                self.outward[i].wait_recv()
                self.pass_outer[i].start()

    def drain(self, items=None):
        items = range(len(self.pieces)) if items is None else items

        @pl.when(self.inner)
        def _():
            for i in items:
                self.facing[i].wait_send()
                self.outward[i].wait_send()
                self.pass_inner[i].wait_send()
                self.stores[i].wait()

        @pl.when(jnp.logical_not(self.inner))
        def _():
            for i in items:
                self.inward[i].wait_send()
                self.pass_outer[i].wait_send()

        for i in items:
            self.pass_outer[i].wait_recv()


def line_sems(number):
    dma = pltpu.SemaphoreType.DMA
    return [dma((2, number))] * 4 + [dma((number,))]


def split_rows(ref, parts):
    size = ref.shape[0] // parts
    return [ref.at[j * size : (j + 1) * size] for j in range(parts)]


def out_halves(place, ref, parts):
    half = ref.shape[0] // 2
    size = half // parts
    first = pl.multiple_of(place.core * half, half)
    return [ref.at[pl.ds(first + j * size, size)] for j in range(parts)]


def line_pieces(place, own, near, far, out, parts):
    return list(
        zip(split_rows(own, parts), split_rows(near, parts), split_rows(far, parts), out_halves(place, out, parts))
    )


class PairSum:
    def __init__(self, place, own, sources, others, lands, core_sem, left_sem):
        self.place, self.own, self.others, self.lands, self.left_sem = place, own, others, lands, left_sem
        self.trades = [remote(sources(j), others.at[j], core_sem, j, place.partner) for j in range(LINE)]
        self.past = LAST - place.chip

    def trade(self):
        for copy in self.trades:
            copy.start()

    def half(self, ref, h):
        size = ref.shape[0] // 2
        return ref.at[h * size : (h + 1) * size]

    def move(self, t, h):
        owner = jnp.clip(self.place.chip - (LINE - t), 0, LAST)
        device = self.place.chip_device(jnp.clip(self.place.chip - 1, 0, LAST))
        source, target = self.half(self.own(owner), h), self.half(self.lands.at[t - 1], h)
        return remote(source, target, self.left_sem, 2 * (t - 1) + h, device)

    def meet(self):
        for j in range(LINE):
            self.trades[j].wait_recv()
            add_into(self.own(j), self.own(j), self.others.at[j])

        @pl.when(self.past == 0)
        def _():
            for t in range(1, LINE):
                for h in range(2):
                    self.move(t, h).start()

    def take(self, t, h):
        self.move(t, h).wait_recv()
        mine = self.half(self.own(jnp.clip(self.place.chip - (LAST - t), 0, LAST)), h)
        add_into(mine, mine, self.half(self.lands.at[t - 1], h))

    def step(self, t):
        @pl.when((self.past >= 1) & (self.past <= min(t - 1, LINE - 2)))
        def _():
            for h in range(2):
                self.take(t - 1, h)
                self.move(t, h).start()

    def finish(self, out, cosine, sine):
        @pl.when(self.past >= 1)
        def _():
            for h in range(2):
                self.take(LAST, h)

        mine = self.own(self.place.chip)
        for i in range(2 * KEY_WIDTH // LANES):
            columns = slice(i * LANES, (i + 1) * LANES)
            tile = mine[:, columns]
            if i < KEY_WIDTH // LANES:
                tile = rotate(tile.astype(f32), cosine[...], -sine[...]).astype(bf16)
            out[:, columns] = tile

    def drain(self):
        for copy in self.trades:
            copy.wait_send()
        for t in range(1, LINE):

            @pl.when((self.past <= t - 1) & (self.past <= LINE - 2))
            def _():
                for h in range(2):
                    self.move(t, h).wait_send()


PARTS = 4


def backward_kernel(
    query_src,
    starts,
    cosine,
    sine,
    middle_src,
    cotangent_src,
    gain,
    pairs,
    turned_src,
    grads_src,
    active_src,
    gate_src,
    up_src,
    results_src,
    row_grads_src,
    output_src,
    query_low_out,
    pair_low,
    middle_low_out,
    middle_grad_out,
    gain_grad,
    block_output,
    gate_total,
    up_total,
    gate_rest,
    up_rest,
    down_rest,
    pair_grad,
    query,
    middle,
    cotangent,
    query_low,
    middle_low,
    middle_grad,
    rows,
    turned,
    grads,
    pool,
    send_gate,
    send_up,
    send_down,
    own_gate,
    own_up,
    own_down,
    other_gate,
    other_up,
    other_down,
    near_gate,
    near_up,
    far_gate,
    far_up,
    row_grad_own,
    row_grad_in,
    result_own,
    result_in,
    attn_grad,
    key_value,
    bias,
    pair_other,
    land_left,
    load_sem,
    weight_sem,
    trade_sem,
    rest_sem,
    row_sem,
    result_sem,
    key_sem,
    core_sem,
    left_sem,
    near_sem,
    far_sem,
    back_sem,
    pass_sem,
    store_sem,
    emit_sem,
):
    r = types.SimpleNamespace(**locals())
    place = Place()
    core, chip, shard = place.core, place.chip, place.shard
    rows = r.cosine.shape[0]
    tokens = MB * SHARDS * rows
    side = MODEL_WIDTH // 2
    local = pltpu.make_async_copy

    wide = SHARDS * rows
    loads = []

    def load(source, target):
        loads.append(local(source, target, r.load_sem.at[len(loads)]))
        loads[-1].start()
        return loads[-1]

    flat = lambda ref, m: [(ref.at[m, k], m * wide + k * rows) for k in range(SHARDS)]
    grad_loads, piece_loads = [], []
    turned_load = load(r.turned_src, r.turned)
    for i, ref in ((1, r.gate_src), (2, r.up_src), (0, r.active_src)):
        for m in range(MB):
            at = i * tokens + m * wide
            piece_loads.append(load(ref.at[m], r.pool.at[at : at + wide]))
    for m in range(MB):
        for source, at in flat(r.grads_src, m):
            grad_loads.append(load(source, r.grads.at[at : at + rows]))
    own_loads = [load(r.row_grads_src.at[m, shard], r.row_grad_own.at[m]) for m in range(MB)]
    own_loads.append(load(r.results_src.at[0, shard], r.result_own))

    vector_loads = [
        load(source, target)
        for source, target in ((r.middle_src, r.middle), (r.cotangent_src, r.cotangent), (r.query_src, r.query))
    ]
    greet_line(place)

    row_copies, result_copies = [], []
    for m in range(MB):
        for k in range(1, SHARDS):
            i = m * (SHARDS - 1) + k - 1
            at = place.peer_index(k)
            row_copies.append(
                remote(r.row_grads_src.at[m, at], r.row_grad_in.at[m, k - 1], r.row_sem, i, place.peer(k))
            )
            if m == 0:
                result_copies.append(
                    remote(r.results_src.at[m, at], r.result_in.at[k - 1], r.result_sem, i, place.peer(k))
                )
    for copy in row_copies:
        copy.start()

    for m in range(MB):
        r.bias[m] = visible_bias(r.starts, m, place.context, r.bias.shape[1:], 1)

    turned_load.wait()
    sends = (r.send_gate, r.send_up, r.send_down)
    owns = (r.own_gate, r.own_up, r.own_down)
    others = (r.other_gate, r.other_up, r.other_down)
    upper = MODEL_WIDTH // 2
    parts = [(0, 0), (0, upper), (1, None)]

    def some(ref, start):
        return ref if start is None else ref.at[start : start + upper]

    trades = {}
    for b, start in parts:
        for i in range(2):
            index = len(trades)
            trades[b, start, i] = remote(
                some(sends[i], start), some(others[i].at[b], start), r.trade_sem, index, place.partner
            )
    for b in range(2):
        trades[b, None, 2] = remote(sends[2], others[2].at[b], r.trade_sem, len(trades), place.partner)

    def weight_block(b, start, expert, outs):
        column = pl.ds(pl.multiple_of(expert * F + b * F_BLOCK, F_BLOCK), F_BLOCK)
        for i in range(2):
            part = r.pool[(i + 1) * tokens : (i + 2) * tokens, column]
            some(outs[i], start)[...] = dot(some(r.turned, start)[...], part).astype(bf16)

    def down_block(b, expert, out):
        column = pl.ds(pl.multiple_of(expert * F + b * F_BLOCK, F_BLOCK), F_BLOCK)
        out[...] = dot(r.pool[0:tokens, column], r.grads[...], TN).astype(bf16)

    def meet(b, start, i):
        trades[b, start, i].wait_recv()
        mine = some(owns[i].at[b], start)
        add_into(mine, mine, some(others[i].at[b], start))

    gate_pieces = line_pieces(place, r.own_gate.at[0], r.near_gate, r.far_gate, r.gate_total, PARTS)
    up_pieces = line_pieces(place, r.own_up.at[0], r.near_up, r.far_up, r.up_total, PARTS)
    middle_part = PARTS // 2
    pieces = gate_pieces[:middle_part] + up_pieces[:middle_part] + gate_pieces[middle_part:] + up_pieces[middle_part:]
    line = Line(place, pieces, (r.near_sem, r.far_sem, r.back_sem, r.pass_sem, r.store_sem))

    for copy in piece_loads[: 2 * MB]:
        copy.wait()
    for n, (b, start) in enumerate(parts):
        if b == 1:
            for first in (0, upper):
                for i in range(2):
                    trades[0, first, i].wait_send()
        weight_block(b, start, 1 - core, sends)
        for i in range(2):
            trades[b, start, i].start()
        weight_block(b, start, core, [own.at[b] for own in owns[:2]])
        if b == 0:
            for i in range(2):
                meet(b, start, i)
                line.ready(*range((2 * n + i) * middle_part, (2 * n + i + 1) * middle_part))
        if start == 0:
            continue
        if b == 0:
            for copy in piece_loads[2 * MB :] + grad_loads:
                copy.wait()
        else:
            trades[0, None, 2].wait_send()
            line.serve([0])
        down_block(b, 1 - core, sends[2])
        trades[b, None, 2].start()
        down_block(b, core, owns[2].at[b])
        if b == 0:
            meet(0, None, 2)

    weight_loads = []
    for i in range(2):
        source = r.output_src.at[:, i * side : (i + 1) * side]
        target = r.pool.at[i * MODEL_WIDTH : (i + 1) * MODEL_WIDTH, 0:side]
        weight_loads.append(local(source, target, r.weight_sem.at[i]))
        weight_loads[-1].start()
    for copy in result_copies:
        copy.start()
    for i in range(3):
        meet(1, None, i)
    rests = [
        local(r.own_gate.at[1], r.gate_rest, r.rest_sem.at[0]),
        local(r.own_up.at[1], r.up_rest, r.rest_sem.at[1]),
        local(r.own_down, r.down_rest, r.rest_sem.at[2]),
    ]
    for copy in rests:
        copy.start()

    r.gain_grad[...] = jnp.zeros_like(r.gain_grad)

    def prepare(m):
        own = slice(m * rows, (m + 1) * rows)
        own_loads[m].wait()
        moe_in_grad = r.row_grad_own[m].astype(f32)
        for k in range(1, SHARDS):
            row_copies[m * (SHARDS - 1) + k - 1].wait_recv()
            moe_in_grad = moe_in_grad + r.row_grad_in[m, k - 1].astype(f32)
        middle = r.middle[own]
        scale = lax.rsqrt(jnp.mean(middle * middle, axis=-1, keepdims=True) + eps)
        unit = middle * scale
        r.gain_grad[m : m + 1] = jnp.sum(moe_in_grad * unit, axis=0, keepdims=True)
        weighted = moe_in_grad * r.gain[1:2]
        inner = jnp.mean(weighted * unit, axis=-1, keepdims=True)
        middle_grad = r.cotangent[own].astype(f32) + (weighted - unit * inner) * scale
        r.middle_grad[own] = middle_grad
        r.middle_low[own] = middle_grad.astype(bf16)
        if m == 0:
            for copy in weight_loads:
                copy.wait()
        total = dot(r.middle_low[own, 0:side], r.pool[0:MODEL_WIDTH, 0:side], NT)
        total = total + dot(r.middle_low[own, side:], r.pool[MODEL_WIDTH : 2 * MODEL_WIDTH, 0:side], NT)
        r.attn_grad[m] = total.astype(bf16)

    def key_load(step, slot, i):
        m, p = step // PAIRS, step % PAIRS
        lane = pl.multiple_of(p * LANES, LANES) + i * KEY_WIDTH
        return local(r.pairs.at[m, :, pl.ds(lane, LANES)], r.key_value.at[slot, i], r.key_sem.at[slot, i])

    pair_grads = (r.rows, r.grads.at[:, 0 : 2 * KEY_WIDTH])

    def chunk(of_chip, of_core):
        return pair_grads[0].at[pl.ds(pl.multiple_of((2 * of_chip + of_core) * rows, rows), rows)]

    pair_sum = PairSum(
        place,
        lambda j: chunk(j, core),
        lambda j: chunk(j, 1 - core),
        r.pair_other,
        r.land_left,
        r.core_sem,
        r.left_sem,
    )

    def pair_step(step, carry):
        m, p = step // PAIRS, step % PAIRS
        slot = step % 2
        for i in range(2):
            key_load(step, slot, i).wait()

        @pl.when(step + 1 < MB * PAIRS)
        def _():
            for i in range(2):
                key_load(step + 1, 1 - slot, i).start()

        at = pl.multiple_of(m * rows, rows)
        column = pl.multiple_of(p * PAIR_QUERY, PAIR_QUERY)
        lane = pl.multiple_of(p * LANES, LANES)
        columns = [pl.ds(column + i * LANES, LANES) for i in range(GROUP)]
        scale = 1.0 / HEAD_SIZE
        tiles = [r.query[pl.ds(at, rows), c].astype(f32) * scale for c in columns]
        grads = [r.attn_grad[m, :, c].astype(f32) for c in columns]
        bias = jnp.concatenate([r.bias[m]] * GROUP, axis=1)
        query_grads, key_grad, value_grad = attention_pair_gradient(
            tiles, grads, r.key_value[slot, 0], r.key_value[slot, 1], bias
        )
        for c, tile in zip(columns, query_grads):
            tile = rotate(tile * scale, r.cosine[...], -r.sine[...])
            r.query_low[pl.ds(at, rows), c] = tile.astype(bf16)
        key_low, value_low = key_grad.astype(bf16), value_grad.astype(bf16)
        for micro in range(MB):

            @pl.when(m == micro)
            def _():
                pair_grads[micro][:, pl.ds(lane, LANES)] = key_low
                pair_grads[micro][:, pl.ds(lane + KEY_WIDTH, LANES)] = value_low

        for at_step, actions in SERVICE:

            @pl.when(step == at_step)
            def _():
                for action in actions:
                    action()

        return carry

    serve = line.serve
    SERVICE = (
        (0, (lambda: serve([3], [1]),)),
        (1, (lambda: serve([4], [2]),)),
        (2, (lambda: serve([5], [3], [0]),)),
        (3, (pair_sum.trade, lambda: prepare(1), lambda: serve([6], [4], [1]), pair_sum.meet)),
        (4, (lambda: serve([7], [5], [2]),)),
        (5, (lambda: serve([], [6], [3]),)),
        (6, (lambda: pair_sum.step(2), lambda: serve([], [7], [4]))),
        (7, (lambda: serve([], [], [5]),)),
    )
    for i in range(2):
        key_load(0, 0, i).start()
    for copy in vector_loads:
        copy.wait()
    serve([1])
    prepare(0)
    serve([2], [0])
    lax.fori_loop(0, MB * PAIRS, pair_step, 0)
    second = local(pair_grads[1], r.pair_grad, r.rest_sem.at[3])
    second.start()
    emits = [
        local(source, target, r.emit_sem.at[i])
        for i, (source, target) in enumerate(
            (
                (r.query_low, r.query_low_out),
                (r.middle_low, r.middle_low_out),
                (r.middle_grad, r.middle_grad_out),
            )
        )
    ]
    for copy in emits:
        copy.start()
    pair_sum.step(3)
    own_loads[MB].wait()
    total = r.middle[0:rows] + r.result_own[...].astype(f32)
    for k in range(1, SHARDS):
        result_copies[k - 1].wait_recv()
        total = total + r.result_in[k - 1].astype(f32)
    r.block_output[...] = total.astype(bf16)
    for i in range(3):
        trades[1, None, i].wait_send()
    for copy in rests:
        copy.wait()
    for copy in row_copies:
        copy.wait_send()
    for copy in result_copies:
        copy.wait_send()
    line.drain(range(4))
    serve([], [], [6, 7])
    pair_sum.finish(r.pair_low, r.cosine, r.sine)
    for copy in [second] + emits:
        copy.wait()

    pair_sum.drain()
    line.drain(range(4, 2 * PARTS))


def backward(query, starts, cosine, sine, middle, cotangent, gain, pairs, turned_rows, grad_blocks, pieces, results, row_grads, output_weight):
    rows = cosine.shape[0]
    length = pairs.shape[1]
    held_rows = 2 * MODEL_WIDTH
    tokens = MB * SHARDS * rows
    dma = pltpu.SemaphoreType.DMA
    anywhere = pl.BlockSpec(memory_space=pl.ANY)
    vmem = pl.BlockSpec(memory_space=pltpu.VMEM)
    shape = jax.ShapeDtypeStruct
    tall, flat = (MODEL_WIDTH, F_BLOCK), (F_BLOCK, MODEL_WIDTH)
    two = lambda s: (2,) + s
    low = lambda s: pltpu.VMEM(s, bf16)
    number = 2 * PARTS
    return pl.pallas_call(
        backward_kernel,
        in_specs=[anywhere, pl.BlockSpec(memory_space=pltpu.SMEM), vmem, vmem, anywhere, anywhere, vmem]
        + [anywhere] * 9,
        out_specs=[anywhere, vmem, anywhere, anywhere, vmem, vmem] + [anywhere] * 6,
        out_shape=[
            shape(query.shape, bf16),
            shape((rows, 2 * KEY_WIDTH), bf16),
            shape((MB * rows, MODEL_WIDTH), bf16),
            shape((MB * rows, MODEL_WIDTH), f32),
            shape((8, MODEL_WIDTH), f32),
            shape((rows, MODEL_WIDTH), bf16),
            shape((held_rows, F_BLOCK), bf16),
            shape((held_rows, F_BLOCK), bf16),
            shape(tall, bf16),
            shape(tall, bf16),
            shape(two(flat), bf16),
            shape((length, 2 * KEY_WIDTH), bf16),
        ],
        scratch_shapes=[
            low((MB * rows, MODEL_WIDTH)),
            pltpu.VMEM((MB * rows, MODEL_WIDTH), f32),
            low((MB * rows, MODEL_WIDTH)),
            low((MB * rows, MODEL_WIDTH)),
            low((MB * rows, MODEL_WIDTH)),
            pltpu.VMEM((MB * rows, MODEL_WIDTH), f32),
            low((length, 2 * KEY_WIDTH)),
            low((MODEL_WIDTH, tokens)),
            low((tokens, MODEL_WIDTH)),
            low((3 * tokens, 2 * F)),
            low(tall),
            low(tall),
            low(flat),
            low(two(tall)),
            low(two(tall)),
            low(two(flat)),
            low(two(tall)),
            low(two(tall)),
            low(two(flat)),
            low(tall),
            low(tall),
            low(tall),
            low(tall),
            low((MB, rows, MODEL_WIDTH)),
            low((MB, SHARDS - 1, rows, MODEL_WIDTH)),
            low((rows, MODEL_WIDTH)),
            low((SHARDS - 1, rows, MODEL_WIDTH)),
            low((MB, rows, MODEL_WIDTH)),
            low((2, 2, length, LANES)),
            pltpu.VMEM((MB, length, rows), f32),
            low((LINE, rows, 2 * KEY_WIDTH)),
            low((LINE - 1, rows, 2 * KEY_WIDTH)),
            dma((4 * MB * SHARDS,)),
            dma((2,)),
            dma((2, 8)),
            dma((4,)),
            dma((2, MB * (SHARDS - 1))),
            dma((2, SHARDS - 1)),
            dma((2, 2)),
            dma((2, LINE)),
            dma((2, 2 * (LINE - 1))),
        ]
        + line_sems(number)
        + [dma((3,))],
        compiler_params=pltpu.CompilerParams(
            collective_id=3, has_side_effects=True, vmem_limit_bytes=VMEM_LIMIT
        ),
        name="backward",
    )(query, starts, cosine, sine, middle, cotangent, gain, pairs, turned_rows, grad_blocks, *pieces, results, row_grads, output_weight)


DENSE = ("output", "query", "pair", "gain")
DENSE_PARTS = 4
FINE = 4
GATHER_AFTER = {4: ("output",), 9: ("query",), 13: ("pair", "gain")}
OUTPUT_AFTER = 19
DRAIN_LAG = 8


def dense_kernel(
    turned_normed_src,
    turned_attn_src,
    query_low_src,
    pair_low_first,
    middle_low_src,
    gain,
    gain_grad,
    cosine,
    sine,
    middle_grad_src,
    tokens_src,
    middle_src,
    query_src,
    pair_src,
    pair_grad,
    results_src,
    gate_rest,
    up_rest,
    down_rest,
    input_grad_out,
    block_output,
    results_in,
    output_total,
    query_total,
    pair_total,
    gain_total,
    gate_total,
    up_total,
    down_total,
    turned_normed,
    turned_attn,
    query_low,
    middle_low,
    input_grad,
    middle_grad,
    tokens,
    middle,
    pair_low,
    pair_own,
    pair_other,
    land_left,
    query_weight,
    pair_weight,
    gains,
    send_output,
    send_query,
    own_output,
    own_query,
    own_pair,
    own_gain,
    other_output,
    other_query,
    other_pair,
    other_gain,
    across_output,
    across_query,
    across_pair,
    across_gain,
    sum_output,
    sum_query,
    sum_pair,
    sum_gain,
    near_output,
    near_query,
    near_pair,
    near_gain,
    far_output,
    far_query,
    far_pair,
    far_gain,
    own_gate,
    own_up,
    own_down,
    near_gate,
    near_up,
    near_down,
    far_gate,
    far_up,
    far_down,
    load_sem,
    core_sem,
    left_sem,
    result_sem,
    trade_sem,
    across_sem,
    near_sem,
    far_sem,
    back_sem,
    pass_sem,
    store_sem,
    emit_sem,
):
    r = types.SimpleNamespace(**locals())
    at = lambda kind, name: getattr(r, kind + "_" + name)
    place = Place()
    core, shard = place.core, place.shard
    rows = r.middle.shape[0]
    held = MODEL_WIDTH // SHARDS
    half = held // 2
    loads = [
        pltpu.make_async_copy(source, target, r.load_sem.at[i])
        for i, (source, target) in enumerate(
            (
                (r.gate_rest, r.own_gate),
                (r.up_rest, r.own_up),
                (r.down_rest, r.own_down),
                (r.query_src, r.query_weight),
                (r.pair_src, r.pair_weight),
                (r.pair_grad.at[:, core], r.pair_own),
                (r.middle_grad_src, r.middle_grad),
                (r.tokens_src, r.tokens),
                (r.middle_src.at[rows : 2 * rows], r.middle),
                (r.turned_attn_src, r.turned_attn),
                (r.middle_low_src, r.middle_low),
                (r.turned_normed_src, r.turned_normed),
                (r.query_low_src, r.query_low),
            )
        )
    ]
    for load in loads:
        load.start()
    greet_line(place)
    pair_sum = PairSum(
        place,
        lambda j: r.pair_own.at[j],
        lambda j: r.pair_grad.at[j, 1 - core],
        r.pair_other,
        r.land_left,
        r.core_sem,
        r.left_sem,
    )
    pair_sum.trade()

    pieces = []
    for name, parts in (("gate", FINE), ("up", FINE), ("down", 2 * FINE)):
        pieces += line_pieces(place, at("own", name), at("near", name), at("far", name), getattr(r, name + "_total"), parts)
    expert_pieces = len(pieces)
    for name in DENSE:
        parts = 1 if name == "gain" else DENSE_PARTS
        pieces += line_pieces(
            place, at("sum", name), at("near", name), at("far", name), getattr(r, name + "_total"), parts
        )
    line = Line(place, pieces, (r.near_sem, r.far_sem, r.back_sem, r.pass_sem, r.store_sem))
    loads[0].wait()
    line.ready(0)
    loads[5].wait()
    pair_sum.meet()
    for i in (1, 2):
        loads[i].wait()
    line.ready(*range(1, expert_pieces))

    def block(b, of_core):
        return pl.ds(pl.multiple_of(b * held + of_core * half, half), half)

    trades = {}

    def dense(name, turned, right, sent):
        index = DENSE.index(name)
        trades[name] = []
        for b in range(SHARDS):
            sent[b] = dot(turned[block(b, 1 - core)], right[...]).astype(bf16)
            copy = remote(sent.at[b], at("other", name).at[b], r.trade_sem, index * SHARDS + b, place.partner)
            copy.start()
            trades[name].append(copy)
        for b in range(SHARDS):
            at("own", name)[b] = dot(turned[block(b, core)], right[...]).astype(bf16)

    crossings = {}

    def meet(name):
        own, other, across = at("own", name), at("other", name), at("across", name)
        for b in range(SHARDS):
            trades[name][b].wait_recv()
            add_into(own.at[b], own.at[b], other.at[b])
        crossings[name] = []
        for k in range(1, SHARDS):
            index = DENSE.index(name) * (SHARDS - 1) + k - 1
            copy = remote(own.at[place.peer_index(k)], across.at[k - 1], r.across_sem, index, place.peer(k))
            copy.start()
            crossings[name].append(copy)

    def gather(name):
        for copy in crossings[name]:
            copy.wait_recv()
        across = at("across", name)
        add_into(at("sum", name), at("own", name).at[shard], *[across.at[k] for k in range(SHARDS - 1)])

    for load in loads[9:]:
        load.wait()
    dense("output", r.turned_attn, r.middle_low, r.send_output)
    dense("query", r.turned_normed, r.query_low, r.send_query)
    meet("output")
    line.serve([0])
    pair_sum.step(2)
    meet("query")
    pair_sum.step(3)
    for copy in trades["output"]:
        copy.wait_send()
    r.pair_low[0:rows] = r.pair_low_first[...]
    pair_sum.finish(r.pair_low.at[rows : 2 * rows], r.cosine, r.sine)
    dense("pair", r.turned_normed, r.pair_low, r.send_output.at[:, :, 0 : 2 * KEY_WIDTH])
    line.serve([1], [0])
    for load in loads[3:5] + loads[6:9]:
        load.wait()

    gain_one_grad = jnp.zeros((1, MODEL_WIDTH), f32)
    for m in range(MB):
        own = slice(m * rows, (m + 1) * rows)
        values = r.tokens[own].astype(f32)
        scale = lax.rsqrt(jnp.mean(values * values, axis=-1, keepdims=True) + eps)
        unit = values * scale
        normed_grad = dot(r.query_low[own], r.query_weight[...], NT) + dot(r.pair_low[own], r.pair_weight[...], NT)
        gain_one_grad = gain_one_grad + jnp.sum(normed_grad * unit, axis=0, keepdims=True)
        weighted = normed_grad * r.gain[0:1]
        inner = jnp.mean(weighted * unit, axis=-1, keepdims=True)
        r.input_grad[own] = r.middle_grad[own] + (weighted - unit * inner) * scale
        if m == 0:
            meet("pair")
            line.serve([2], [1])
    line.serve([3], [2])
    grad_emit = pltpu.make_async_copy(r.input_grad, r.input_grad_out, r.emit_sem.at[0])
    grad_emit.start()
    gain_two_grad = jnp.sum(r.gain_grad[...], axis=0, keepdims=True)
    stacked = jnp.concatenate(
        [gain_one_grad, gain_two_grad, jnp.zeros((LANES - 2, MODEL_WIDTH), f32)], axis=0
    )
    r.gains[...] = stacked.T.astype(bf16)
    trades["gain"] = []
    for b in range(SHARDS):
        source = r.gains.at[block(b, 1 - core)]
        index = DENSE.index("gain") * SHARDS + b
        trades["gain"].append(remote(source, r.other_gain.at[b], r.trade_sem, index, place.partner))
        trades["gain"][b].start()
        r.own_gain[b] = r.gains[block(b, core)]
    meet("gain")

    result_copies = []
    for k in range(1, SHARDS):
        source = r.results_src.at[1, place.peer_index(k)]
        result_copies.append(remote(source, r.results_in.at[k - 1], r.result_sem, k - 1, place.peer(k)))
        result_copies[-1].start()
    for copy in trades["pair"]:
        copy.wait_send()
    result_parts = [r.send_output.at[k, 0:rows] for k in range(SHARDS)]
    result_loads = [
        pltpu.make_async_copy(source, target, r.load_sem.at[13 + k])
        for k, (source, target) in enumerate(
            zip([r.results_src.at[1, shard]] + [r.results_in.at[k] for k in range(SHARDS - 1)], result_parts)
        )
    ]
    result_loads[0].start()

    def output_rows():
        for copy, load in zip(result_copies, result_loads[1:]):
            copy.wait_recv()
            load.start()
        total = r.middle[...]
        for load, part in zip(result_loads, result_parts):
            load.wait()
            total = total + part[...].astype(f32)
        r.block_output[...] = total.astype(bf16)

    number = len(pieces)
    first = expert_pieces
    spans = {}
    for name in DENSE:
        parts = 1 if name == "gain" else DENSE_PARTS
        spans[name] = range(first, first + parts)
        first += parts
    lag = 4
    for i in range(number + lag):
        line.serve(
            [i] if 4 <= i < number else [],
            [i - 1] if 4 <= i <= number else [],
            [i - lag] if i >= lag else [],
        )
        for name in GATHER_AFTER.get(i, ()):
            gather(name)
            line.ready(*spans[name])
        if DRAIN_LAG <= i < number:
            line.drain([i - DRAIN_LAG])
        if i == OUTPUT_AFTER:
            output_rows()
            for name in DENSE:
                for copy in crossings[name]:
                    copy.wait_send()
                if name in ("query", "gain"):
                    for copy in trades[name]:
                        copy.wait_send()
            for copy in result_copies:
                copy.wait_send()
            pair_sum.drain()

    grad_emit.wait()
    line.drain(range(number - DRAIN_LAG, number))


def dense_weights(vectors, streamed, query_weight, pair_weight, pair_grad, results, rests):
    dma = pltpu.SemaphoreType.DMA
    anywhere = pl.BlockSpec(memory_space=pl.ANY)
    vmem = pl.BlockSpec(memory_space=pltpu.VMEM)
    shape = jax.ShapeDtypeStruct
    rows = pair_grad.shape[2]
    low = lambda *s: pltpu.VMEM(s, bf16)
    held = MODEL_WIDTH // SHARDS
    half = held // 2
    widths = (MODEL_WIDTH, MODEL_WIDTH, 2 * KEY_WIDTH, LANES)
    tall = (MODEL_WIDTH, F_BLOCK)
    number = 4 * FINE + 3 * DENSE_PARTS + 1
    return pl.pallas_call(
        dense_kernel,
        in_specs=[anywhere] * 3 + [vmem, anywhere] + [vmem] * 4 + [anywhere] * (7 + len(streamed)),
        out_specs=[anywhere, vmem] + [anywhere] * 8,
        out_shape=[
            shape((MB * rows, MODEL_WIDTH), f32),
            shape((rows, MODEL_WIDTH), bf16),
            shape((SHARDS - 1, rows, MODEL_WIDTH), bf16),
        ]
        + [shape((held, w), bf16) for w in widths]
        + [
            shape((2 * MODEL_WIDTH, F_BLOCK), bf16),
            shape((2 * MODEL_WIDTH, F_BLOCK), bf16),
            shape((2 * F, MODEL_WIDTH), bf16),
        ],
        scratch_shapes=[
            low(MODEL_WIDTH, MB * rows),
            low(MODEL_WIDTH, MB * rows),
            low(MB * rows, MODEL_WIDTH),
            low(MB * rows, MODEL_WIDTH),
            pltpu.VMEM((MB * rows, MODEL_WIDTH), f32),
            pltpu.VMEM((MB * rows, MODEL_WIDTH), f32),
            low(MB * rows, MODEL_WIDTH),
            pltpu.VMEM((rows, MODEL_WIDTH), f32),
            low(MB * rows, 2 * KEY_WIDTH),
            low(LINE, rows, 2 * KEY_WIDTH),
            low(LINE, rows, 2 * KEY_WIDTH),
            low(LINE - 1, rows, 2 * KEY_WIDTH),
            low(*query_weight.shape),
            low(*pair_weight.shape),
            low(MODEL_WIDTH, LANES),
            low(SHARDS, half, MODEL_WIDTH),
            low(SHARDS, half, MODEL_WIDTH),
        ]
        + [low(SHARDS, half, w) for w in widths] * 2
        + [low(SHARDS - 1, half, w) for w in widths]
        + [low(half, w) for w in widths] * 3
        + [low(*tall), low(*tall), low(F, MODEL_WIDTH)] * 3
        + [dma((13 + SHARDS,)), dma((2, LINE)), dma((2, 2 * (LINE - 1))), dma((2, SHARDS - 1)), dma((2, 4 * SHARDS)), dma((2, 4 * (SHARDS - 1)))]
        + line_sems(number)
        + [dma((1,))],
        compiler_params=pltpu.CompilerParams(
            collective_id=4, has_side_effects=True, vmem_limit_bytes=VMEM_LIMIT
        ),
        name="dense_weights",
    )(*vectors, *streamed, query_weight, pair_weight, pair_grad, results, *rests)


def widen_kernel(*refs):
    r = refs
    step = pl.program_id(0)
    parts, (shrink, dense, rows_in, gains, grad) = r[:4], (r[4], r[5:8], r[8:10], r[10], r[11])
    expand_out, shrink_out, dense_out, rows_out, gain_outs, grad_out = r[12], r[13], r[14:17], r[17], r[18:20], r[20]
    for i, ref in enumerate(parts):
        expand_out[:, i * F_BLOCK : (i + 1) * F_BLOCK] = ref[...].astype(f32)
    shrink_out[...] = shrink[...].astype(f32)
    grad_out[...] = grad[...]

    for source, target in zip(dense, dense_out):
        target[...] = source[...].astype(f32)

    for i in range(MB):

        @pl.when(step // (WIDEN_STEPS // MB) == i)
        def _():
            rows_out[...] = rows_in[i][...]

    @pl.when(step == 0)
    def _():
        turned = gains[...].astype(f32).T
        for i in range(2):
            gain_outs[i][...] = turned[i]


WIDEN_STEPS = 4


def widen(expand_parts, shrink, dense, rows, gains, grad):
    n = WIDEN_STEPS
    every = lambda a: pl.BlockSpec((a.shape[0] // n, a.shape[1]), lambda i: (i, 0))
    one = lambda a: pl.BlockSpec(a.shape, lambda i: (0, 0))
    size = MB * rows[0].shape[0] // n
    half = lambda m: pl.BlockSpec(
        (size, MODEL_WIDTH), lambda i: (jnp.clip(i - m * (n // MB), 0, n // MB - 1), 0)
    )
    shape = jax.ShapeDtypeStruct
    expand = shape((expand_parts[0].shape[0], 2 * F), f32)
    joined = shape((MB * rows[0].shape[0], MODEL_WIDTH), bf16)
    gain = shape((gains.shape[0],), f32)
    flat = pl.BlockSpec(gain.shape, lambda i: (0,))
    dense_out = [shape(a.shape, f32) for a in dense]
    return pl.pallas_call(
        widen_kernel,
        grid=(n,),
        in_specs=[every(a) for a in expand_parts]
        + [every(shrink)]
        + [every(a) for a in dense]
        + [half(m) for m in range(MB)]
        + [one(gains), every(grad)],
        out_specs=[every(expand), every(shrink)]
        + [every(a) for a in dense]
        + [every(joined), flat, flat, every(grad)],
        out_shape=[expand, shape(shrink.shape, f32), *dense_out, joined, gain, gain, shape(grad.shape, f32)],
        compiler_params=pltpu.CompilerParams(vmem_limit_bytes=VMEM_LIMIT),
        name="widen",
    )(*expand_parts, shrink, *dense, *rows, gains, grad)


def shards(
    tokens,
    doc_starts,
    routes,
    gates,
    attn_gain,
    w_q,
    key_value_weight,
    w_o,
    moe_gain,
    expert_in,
    expert_out,
    cotangent,
):
    links = Links()
    rows = tokens.shape[2]
    length = rows * links.contexts
    held = expert_in.shape[0]
    chained = links.chips == LINE and links.shards == SHARDS and held == 2
    width = w_q.shape[0]
    flat_tokens = tokens.reshape(MB * rows, MODEL_WIDTH)
    if chained:
        flat_cotangent = cotangent.reshape(MB * rows, MODEL_WIDTH)
        starts = doc_starts[:, 0]
        (
            turned_normed,
            query,
            turned_attn,
            middle,
            gains,
            cosine,
            sine,
            pair_weight,
            query_weight,
            output_weight,
            pairs,
            turned_rows,
            grad_blocks,
            result_blocks,
            row_grad_blocks,
            active,
            gate,
            up,
        ) = forward(
            flat_tokens,
            routes.transpose(0, 1, 3, 2),
            gates.transpose(0, 1, 3, 2),
            jnp.concatenate([attn_gain, moe_gain]).reshape(2, width),
            flat_cotangent,
            starts,
            rotation_constants(length),
            (key_value_weight, w_q, w_o),
            expert_in,
            expert_out,
        )
        result_blocks = result_blocks.reshape(grad_blocks.shape)
        row_grad_blocks = row_grad_blocks.reshape(grad_blocks.shape)
        (
            query_low,
            pair_low,
            middle_low,
            middle_grad,
            gain_two_grad,
            output_first,
            gate_first,
            up_first,
            gate_rest,
            up_rest,
            down_rest,
            pair_grad,
        ) = backward(
            query,
            starts,
            cosine,
            sine,
            middle,
            flat_cotangent,
            gains,
            pairs,
            turned_rows,
            grad_blocks,
            (active, gate, up),
            result_blocks,
            row_grad_blocks,
            output_weight,
        )
        (
            input_grad,
            output_second,
            _,
            output_total,
            query_total,
            pair_total,
            gain_total,
            gate_second,
            up_second,
            shrink_total,
        ) = dense_weights(
            (
                turned_normed,
                turned_attn,
                query_low,
                pair_low,
                middle_low,
                gains,
                gain_two_grad,
                cosine,
                sine,
            ),
            (middle_grad, flat_tokens, middle),
            query_weight,
            pair_weight,
            pair_grad.reshape(LINE, 2, rows, 2 * KEY_WIDTH),
            result_blocks,
            (gate_rest, up_rest, down_rest.reshape(F, MODEL_WIDTH)),
        )
        (
            expand_total,
            shrink_total,
            output_total,
            query_total,
            pair_total,
            block_output,
            gain_one_total,
            gain_two_total,
            input_grad,
        ) = widen(
            (gate_first, gate_second, up_first, up_second),
            shrink_total,
            (output_total, query_total, pair_total),
            (output_first, output_second),
            gain_total,
            input_grad,
        )
        return (
            block_output.reshape(MB, 1, rows, MODEL_WIDTH),
            input_grad.reshape(MB, 1, rows, MODEL_WIDTH),
            gain_one_total,
            query_total,
            pair_total,
            output_total,
            gain_two_total,
            expand_total.reshape(held, MODEL_WIDTH, 2 * F),
            shrink_total.reshape(held, F, MODEL_WIDTH),
        )

    positions = links.context * rows + jnp.arange(rows, dtype=jnp.int32)
    cosine, sine = rotation_tables(positions)
    key_places = jnp.arange(length, dtype=jnp.int32)
    flat_values = flat_tokens.astype(f32)
    scale_one = lax.rsqrt(jnp.mean(flat_values * flat_values, axis=-1, keepdims=True) + eps)
    unit_one = flat_values * scale_one
    expert_ids = jnp.arange(E, dtype=jnp.int32)
    chosen = (routes.reshape(MB, rows, TOP)[..., None] == expert_ids).astype(f32)
    combine = jnp.sum(gates.reshape(MB, rows, TOP)[..., None] * chosen, axis=2)
    gather = lambda w: lax.all_gather(w, "fsdp", axis=0, tiled=True)
    pair_weight, query_weight, output_weight = gather(key_value_weight), gather(w_q), gather(w_o)
    gain_one, gain_two = gather(attn_gain).astype(f32), gather(moe_gain).astype(f32)
    normed = (unit_one * gain_one).astype(bf16)
    both = lambda table: jnp.concatenate([table] * MB)
    own_pairs = rotate_columns(dot(normed, pair_weight), both(cosine), both(sine), KEY_WIDTH)
    query = rotate_columns(dot(normed, query_weight), both(cosine), both(sine), MODEL_WIDTH)
    own_pairs = own_pairs.reshape(MB, rows, 2 * KEY_WIDTH)
    pairs = lax.all_gather(own_pairs, "ctx", axis=1, tiled=True)

    combine = jnp.concatenate([combine] + [links.across(combine, k) for k in range(1, links.shards)], axis=1)
    combine = lax.dynamic_slice_in_dim(combine, links.shard * held, held, 2)
    combine = combine.transpose(0, 2, 1)[..., None]

    biases, biases_turned = [], []
    for m in range(MB):
        starts = doc_starts[m, 0]
        begin = jnp.max(jnp.where(starts[None, :] <= positions[:, None], starts[None, :], 0), axis=1)
        seen = (key_places[None, :] <= positions[:, None]) & (key_places[None, :] >= begin[:, None])
        biases.append(jnp.where(seen, 0.0, -1e30).astype(f32))
        places, begins = jnp.tile(positions, GROUP), jnp.tile(begin, GROUP)
        seen = (key_places[:, None] <= places[None, :]) & (key_places[:, None] >= begins[None, :])
        biases_turned.append(jnp.where(seen, 0.0, -1e30).astype(f32))

    middles, attns, results, row_grads = [], [], [], []
    rows_kept, grads_kept, pieces_kept = [], [], []
    for m in range(MB):
        own = slice(m * rows, (m + 1) * rows)
        attn = attention_forward(m, query, pairs, biases[m])
        middle = flat_tokens[own].astype(f32) + dot(attn, output_weight)
        scale_two = lax.rsqrt(jnp.mean(middle * middle, axis=-1, keepdims=True) + eps)
        moe_in = (middle * scale_two * gain_two).astype(bf16)
        out_grad = cotangent[m, 0]
        row_parts = [moe_in] + [links.across(moe_in, k) for k in range(1, links.shards)]
        grad_parts = [out_grad] + [links.across(out_grad, k) for k in range(1, links.shards)]
        result, row_grad, pieces = experts(row_parts, grad_parts, combine[m], expert_in, expert_out)
        for parts, sums in ((result, results), (row_grad, row_grads)):
            total = parts[0].astype(f32)
            for k in range(1, links.shards):
                total = total + links.across(parts[k], k).astype(f32)
            sums.append(total)
        middles.append(middle)
        attns.append(attn)
        rows_kept += row_parts
        grads_kept += grad_parts
        pieces_kept.append(pieces)
    merge = lambda items: jnp.concatenate(items, axis=0)
    expert_grads = expert_weights(
        merge(rows_kept), merge(grads_kept), *[merge([p[i] for p in pieces_kept]) for i in range(3)], held
    )
    expert_grads = [g.reshape(-1, g.shape[-1]) for g in expert_grads]
    outputs = [(middles[m] + results[m]).astype(bf16) for m in range(MB)]

    input_grads, query_lows, pair_lows, middle_lows = [], [], [], []
    gain_one_grad, gain_two_grad = 0.0, 0.0
    for m in range(MB):
        own = slice(m * rows, (m + 1) * rows)
        scale_two = lax.rsqrt(jnp.mean(middles[m] * middles[m], axis=-1, keepdims=True) + eps)
        unit_two = middles[m] * scale_two
        moe_in_grad = row_grads[m]
        gain_two_grad = gain_two_grad + jnp.sum(moe_in_grad * unit_two, axis=0)
        weighted = moe_in_grad * gain_two
        inner = jnp.mean(weighted * unit_two, axis=-1, keepdims=True)
        middle_grad = cotangent[m, 0].astype(f32) + (weighted - unit_two * inner) * scale_two
        middle_low = middle_grad.astype(bf16)
        attn_grad = dot(middle_low, output_weight, NT).astype(bf16)
        query_low, pair_grad = attention_backward(
            m, query, cosine, sine, pairs, biases_turned[m], attn_grad
        )
        parts = [lax.psum_scatter(pair_grad, "ctx", scatter_dimension=0, tiled=True)]
        pair_low = pair_gradient(parts, cosine, sine)
        normed_grad = dot(query_low, query_weight, NT) + dot(pair_low, pair_weight, NT)
        gain_one_grad = gain_one_grad + jnp.sum(normed_grad * unit_one[own], axis=0)
        weighted = normed_grad * gain_one
        inner = jnp.mean(weighted * unit_one[own], axis=-1, keepdims=True)
        residual_grad = (weighted - unit_one[own] * inner) * scale_one[own]
        input_grads.append(middle_grad + residual_grad)
        query_lows.append(query_low)
        pair_lows.append(pair_low)
        middle_lows.append(middle_low)

    join = lambda items: jnp.concatenate(items, axis=0)

    output_grad = dot(join(attns), join(middle_lows), TN).astype(bf16)
    query_grad = dot(normed, join(query_lows), TN).astype(bf16)
    pair_weight_grad = dot(normed, join(pair_lows), TN).astype(bf16)
    gain_grads = jnp.stack([gain_one_grad, gain_two_grad], axis=1)
    gain_grads = jnp.pad(gain_grads, ((0, 0), (0, LANES - 2))).astype(bf16)
    dense_grads = [output_grad, query_grad, jnp.concatenate([pair_weight_grad, gain_grads], axis=1)]
    totals = [lax.psum(g, "ctx") for g in expert_grads]
    for g in dense_grads:
        part = lax.psum_scatter(g, "fsdp", scatter_dimension=0, tiled=True)
        totals.append(lax.psum(part, "ctx"))
    gate_total, up_total, down_total, output_total, query_total, pair_total = [t.astype(f32) for t in totals]
    expand_total = jnp.concatenate([gate_total, up_total], axis=1)

    return (
        jnp.stack(outputs)[:, None],
        jnp.stack(input_grads)[:, None],
        pair_total[:, 2 * KEY_WIDTH],
        query_total,
        pair_total[:, : 2 * KEY_WIDTH],
        output_total,
        pair_total[:, 2 * KEY_WIDTH + 1],
        expand_total.reshape(held, MODEL_WIDTH, 2 * F),
        down_total.reshape(held, F, MODEL_WIDTH),
    )


def solution(mesh):
    return jax.shard_map(
        shards,
        mesh=mesh,
        in_specs=(
            P(None, "fsdp", "ctx", None),
            P(None, "fsdp", None),
            P(None, "fsdp", "ctx", None),
            P(None, "fsdp", "ctx", None),
            P("fsdp"),
            P("fsdp", None),
            P("fsdp", None),
            P("fsdp", None),
            P("fsdp"),
            P("fsdp", None, None),
            P("fsdp", None, None),
            P(None, "fsdp", "ctx", None),
        ),
        out_specs=(
            P(None, "fsdp", "ctx", None),
            P(None, "fsdp", "ctx", None),
            P("fsdp"),
            P("fsdp", None),
            P("fsdp", None),
            P("fsdp", None),
            P("fsdp"),
            P("fsdp", None, None),
            P("fsdp", None, None),
        ),
        check_vma=False,
    )
```

```python
import functools
import types

import jax
import jax.numpy as jnp
import numpy as np
from jax import lax
from jax.experimental import pallas as pl
from jax.experimental.pallas import tpu as pltpu
from jax.sharding import PartitionSpec as P

MODEL_WIDTH = 1536
QUERY_HEADS = 24
KEY_VALUE_HEADS = 8
HEAD_SIZE = 64
GROUP = QUERY_HEADS // KEY_VALUE_HEADS
KEY_WIDTH = KEY_VALUE_HEADS * HEAD_SIZE
F = 512
E = 8
TOP = 4
MB = 2
LANES = 128
PAIRS = KEY_WIDTH // LANES
PAIR_QUERY = 2 * GROUP * HEAD_SIZE
F_BLOCK = 256
VMEM_LIMIT = 60 * 1024 * 1024

eps = 1e-05
theta = 10000.0

NT = (((1,), (1,)), ((), ()))
TN = (((0,), (0,)), ((), ()))
bf16 = jnp.bfloat16
f32 = jnp.float32


def dot(left, right, dims=(((1,), (0,)), ((), ()))):
    return lax.dot_general(left, right, dims, preferred_element_type=f32)


def rotation_tables(positions):
    frequency = theta ** (-jnp.arange(0, HEAD_SIZE, 2, dtype=f32) / HEAD_SIZE)
    angles = positions.astype(f32)[:, None] * frequency[None, :]
    cosine, sine = jnp.cos(angles), jnp.sin(angles)
    repeat = LANES // HEAD_SIZE
    cosine = jnp.concatenate([cosine, cosine] * repeat, axis=1)
    sine = jnp.concatenate([-sine, sine] * repeat, axis=1)
    return cosine, sine


def rotation_constants(length):
    frequency = theta ** (-np.arange(0, HEAD_SIZE, 2, dtype=np.float64) / HEAD_SIZE)
    angles = np.arange(length, dtype=np.float64)[:, None] * frequency[None, :]
    cosine, sine = np.cos(angles), np.sin(angles)
    repeat = LANES // HEAD_SIZE
    cosine = np.concatenate([cosine, cosine] * repeat, axis=1)
    sine = np.concatenate([-sine, sine] * repeat, axis=1)
    return jnp.asarray(np.stack([cosine, sine]).astype(np.float32))


def visible_bias(starts, m, context, shape, query_axis):
    rows = shape[query_axis]
    narrow = (rows, 1) if query_axis == 0 else (1, rows)
    query = context * rows + lax.broadcasted_iota(jnp.int32, narrow, query_axis)
    begin = jnp.zeros(narrow, jnp.int32)
    for i in range(starts.shape[1]):
        begin = jnp.maximum(begin, jnp.where(query >= starts[m, i], starts[m, i], 0))
    key = lax.broadcasted_iota(jnp.int32, shape, 1 - query_axis)
    return jnp.where((key <= query) & (key >= begin), 0.0, -1e30).astype(f32)


def lane_index(shape):
    return lax.broadcasted_iota(jnp.int32, shape, 1)


def rotate(tile, cosine, sine):
    half = HEAD_SIZE // 2
    ahead = pltpu.roll(tile, LANES - half, 1)
    behind = pltpu.roll(tile, half, 1)
    first = lane_index(tile.shape) % HEAD_SIZE < half
    return tile * cosine + jnp.where(first, ahead, behind) * sine


def rotate_columns_kernel(rotated, values_ref, cosine_ref, sine_ref, out_ref):
    cosine, sine = cosine_ref[...], sine_ref[...]
    for i in range(values_ref.shape[1] // LANES):
        cols = slice(i * LANES, (i + 1) * LANES)
        tile = values_ref[:, cols]
        if i < rotated // LANES:
            tile = rotate(tile, cosine, sine)
        out_ref[:, cols] = tile.astype(bf16)


def rotate_columns(values, cosine, sine, rotated):
    return pl.pallas_call(
        functools.partial(rotate_columns_kernel, rotated),
        out_shape=jax.ShapeDtypeStruct(values.shape, bf16),
        compiler_params=pltpu.CompilerParams(vmem_limit_bytes=VMEM_LIMIT),
        name="rotate_columns",
    )(values, cosine, sine)


def pair_gradient_kernel(count, cosine_ref, sine_ref, *refs):
    out_ref = refs[-1]
    cosine, sine = cosine_ref[...], sine_ref[...]
    for i in range(2 * KEY_WIDTH // LANES):
        cols = slice(i * LANES, (i + 1) * LANES)
        total = refs[0][:, cols].astype(f32)
        for ref in refs[1:count]:
            total = total + ref[:, cols].astype(f32)
        if i < KEY_WIDTH // LANES:
            total = rotate(total, cosine, -sine)
        out_ref[:, cols] = total.astype(bf16)


def pair_gradient(parts, cosine, sine):
    return pl.pallas_call(
        functools.partial(pair_gradient_kernel, len(parts)),
        out_shape=jax.ShapeDtypeStruct(parts[0].shape, bf16),
        compiler_params=pltpu.CompilerParams(vmem_limit_bytes=VMEM_LIMIT),
        name="pair_gradient",
    )(cosine, sine, *parts)


def grouped(tiles, half):
    mine = lane_index(tiles[0].shape) // HEAD_SIZE == half
    rows = []
    for j in range(GROUP * half, GROUP * half + GROUP):
        tile = tiles[j // 2]
        if j % 2 != half:
            tile = pltpu.roll(tile, HEAD_SIZE, 1)
        rows.append(jnp.where(mine, tile, 0.0))
    return jnp.concatenate(rows, axis=0).astype(bf16)


def ungrouped(per_half, rows):
    heads = []
    for j in range(2 * GROUP):
        half, place = j // GROUP, j % GROUP
        tile = per_half[half][place * rows : (place + 1) * rows]
        if j % 2 != half:
            tile = pltpu.roll(tile, HEAD_SIZE, 1)
        heads.append(tile)
    low = lane_index(heads[0].shape) < HEAD_SIZE
    return [jnp.where(low, heads[2 * i], heads[2 * i + 1]) for i in range(GROUP)]


def query_tiles(query_ref):
    scale = 1.0 / HEAD_SIZE
    return [query_ref[:, i * LANES : (i + 1) * LANES].astype(f32) * scale for i in range(GROUP)]


def attention_pair(tiles, key, value, bias):
    rows = bias.shape[0]
    results = []
    for half in range(2):
        scores = dot(grouped(tiles, half), key, NT)
        scores = jnp.concatenate(
            [scores[g * rows : (g + 1) * rows] + bias for g in range(GROUP)], axis=0
        )
        peak = jnp.max(scores, axis=1, keepdims=True)
        weights = jnp.exp(scores - peak)
        total = jnp.sum(weights, axis=1, keepdims=True)
        results.append(dot(weights.astype(bf16), value) / total)
    return ungrouped(results, rows)


def attention_forward_kernel(query_ref, key_ref, value_ref, bias_ref, out_ref):
    tiles = attention_pair(query_tiles(query_ref), key_ref[...], value_ref[...], bias_ref[...])
    for i, tile in enumerate(tiles):
        out_ref[:, i * LANES : (i + 1) * LANES] = tile.astype(bf16)


def attention_forward(m, query, pairs, bias):
    rows, length = bias.shape
    return pl.pallas_call(
        attention_forward_kernel,
        grid=(PAIRS,),
        in_specs=[
            pl.BlockSpec((rows, PAIR_QUERY), lambda p: (m, p)),
            pl.BlockSpec((None, length, LANES), lambda p: (m, 0, p)),
            pl.BlockSpec((None, length, LANES), lambda p: (m, 0, p + PAIRS)),
            pl.BlockSpec((rows, length), lambda p: (0, 0)),
        ],
        out_specs=pl.BlockSpec((rows, PAIR_QUERY), lambda p: (0, p)),
        out_shape=jax.ShapeDtypeStruct((rows, MODEL_WIDTH), bf16),
        compiler_params=pltpu.CompilerParams(vmem_limit_bytes=VMEM_LIMIT),
        cost_estimate=pl.CostEstimate(
            flops=16 * rows * length * MODEL_WIDTH,
            bytes_accessed=4 * length * MODEL_WIDTH,
            transcendentals=rows * length * QUERY_HEADS,
        ),
        name="attention_forward",
    )(query, pairs, pairs, bias)


def attention_pair_gradient(tiles, grads, key, value, bias):
    rows = tiles[0].shape[0]
    key_grad, value_grad = None, None
    query_grads = []
    for half in range(2):
        query = grouped(tiles, half)
        grad = grouped(grads, half)
        scores = dot(key, query, NT) + bias
        weights = jnp.exp(scores - jnp.max(scores, axis=0, keepdims=True))
        prob = weights * (1.0 / jnp.sum(weights, axis=0, keepdims=True))
        prob_grad = dot(value, grad, NT)
        delta = jnp.sum(prob * prob_grad, axis=0, keepdims=True)
        score_grad = (prob * (prob_grad - delta)).astype(bf16)
        value_part = dot(prob.astype(bf16), grad)
        key_part = dot(score_grad, query)
        value_grad = value_part if half == 0 else value_grad + value_part
        key_grad = key_part if half == 0 else key_grad + key_part
        query_grads.append(dot(score_grad, key, TN))
    return ungrouped(query_grads, rows), key_grad, value_grad


def attention_backward_kernel(
    query_ref, cosine_ref, sine_ref, key_ref, value_ref, bias_ref, grad_ref, query_out, pair_out
):
    cosine, sine = cosine_ref[...], sine_ref[...]
    grads = [grad_ref[:, i * LANES : (i + 1) * LANES].astype(f32) for i in range(GROUP)]
    query_grads, key_grad, value_grad = attention_pair_gradient(
        query_tiles(query_ref), grads, key_ref[...], value_ref[...], bias_ref[...]
    )
    for i, tile in enumerate(query_grads):
        tile = rotate(tile * (1.0 / HEAD_SIZE), cosine, -sine)
        query_out[:, i * LANES : (i + 1) * LANES] = tile.astype(bf16)
    first = pl.multiple_of(pl.program_id(0) * LANES, LANES)
    pair_out[:, pl.ds(first, LANES)] = key_grad.astype(bf16)
    pair_out[:, pl.ds(first + KEY_WIDTH, LANES)] = value_grad.astype(bf16)


def attention_backward(m, query, cosine, sine, pairs, bias, grad):
    rows = cosine.shape[0]
    length = pairs.shape[1]
    whole = lambda shape: pl.BlockSpec(shape, lambda p: (0, 0))
    return pl.pallas_call(
        attention_backward_kernel,
        grid=(PAIRS,),
        in_specs=[
            pl.BlockSpec((rows, PAIR_QUERY), lambda p: (m, p)),
            whole((rows, LANES)),
            whole((rows, LANES)),
            pl.BlockSpec((None, length, LANES), lambda p: (m, 0, p)),
            pl.BlockSpec((None, length, LANES), lambda p: (m, 0, p + PAIRS)),
            whole(bias.shape),
            pl.BlockSpec((rows, PAIR_QUERY), lambda p: (0, p)),
        ],
        out_specs=[
            pl.BlockSpec((rows, PAIR_QUERY), lambda p: (0, p)),
            whole((length, 2 * KEY_WIDTH)),
        ],
        out_shape=[
            jax.ShapeDtypeStruct((rows, MODEL_WIDTH), bf16),
            jax.ShapeDtypeStruct((length, 2 * KEY_WIDTH), bf16),
        ],
        compiler_params=pltpu.CompilerParams(vmem_limit_bytes=VMEM_LIMIT),
        cost_estimate=pl.CostEstimate(
            flops=40 * rows * length * MODEL_WIDTH,
            bytes_accessed=8 * length * MODEL_WIDTH,
            transcendentals=rows * length * QUERY_HEADS,
        ),
        name="attention_backward",
    )(query, cosine, sine, pairs, pairs, bias, grad)


def expert_block(inputs, out_grad, combine, gate_weight, up_weight, down_weight):
    gate = dot(inputs, gate_weight)
    up = dot(inputs, up_weight)
    sigmoid = jax.nn.sigmoid(gate)
    silu = gate * sigmoid
    active = (silu * up * combine).astype(bf16)
    active_grad = dot(out_grad, down_weight, NT) * combine
    gate_grad = (active_grad * up * sigmoid * (1.0 + gate * (1.0 - sigmoid))).astype(bf16)
    up_grad = (active_grad * silu).astype(bf16)
    result = dot(active, down_weight)
    row_grad = dot(gate_grad, gate_weight, NT) + dot(up_grad, up_weight, NT)
    return active, gate_grad, up_grad, result, row_grad


def experts_kernel(parts, rows, steps, combine_ref, gate_ref, up_ref, down_ref, *refs):
    rows_in, grads_in = refs[:parts], refs[parts : 2 * parts]
    refs = refs[2 * parts :]
    results, row_grads = refs[:parts], refs[parts : 2 * parts]
    active_out, gate_out, up_out, rows_all, grads_all, result_sum, grad_sum = refs[2 * parts :]
    step = pl.program_id(0) * pl.num_programs(1) + pl.program_id(1)

    @pl.when(step == 0)
    def _():
        for k in range(parts):
            place = slice(k * rows, (k + 1) * rows)
            rows_all[place] = rows_in[k][...]
            grads_all[place] = grads_in[k][...]
        result_sum[...] = jnp.zeros_like(result_sum)
        grad_sum[...] = jnp.zeros_like(grad_sum)

    inputs, out_grad, combine = rows_all[...], grads_all[...], combine_ref[0]
    active, gate_grad, up_grad, result, row_grad = expert_block(
        inputs, out_grad, combine, gate_ref[0], up_ref[0], down_ref[0]
    )
    active_out[...] = active
    gate_out[...] = gate_grad
    up_out[...] = up_grad
    result_sum[...] += result
    grad_sum[...] += row_grad

    @pl.when(step == steps - 1)
    def _():
        for k in range(parts):
            place = slice(k * rows, (k + 1) * rows)
            results[k][...] = result_sum[place].astype(bf16)
            row_grads[k][...] = grad_sum[place].astype(bf16)


def experts(row_parts, grad_parts, combine, expert_in, expert_out):
    parts = len(row_parts)
    rows = row_parts[0].shape[0]
    held = expert_in.shape[0]
    tokens = parts * rows
    blocks = F // F_BLOCK
    whole = pl.BlockSpec((rows, MODEL_WIDTH), lambda e, b: (0, 0))
    piece = pl.BlockSpec((tokens, F_BLOCK), lambda e, b: (0, e * blocks + b))
    row_shape = jax.ShapeDtypeStruct((rows, MODEL_WIDTH), bf16)
    piece_shape = jax.ShapeDtypeStruct((tokens, held * F), bf16)
    out = pl.pallas_call(
        functools.partial(experts_kernel, parts, rows, held * blocks),
        grid=(held, blocks),
        in_specs=[
            pl.BlockSpec((1, tokens, 1), lambda e, b: (e, 0, 0)),
            pl.BlockSpec((1, MODEL_WIDTH, F_BLOCK), lambda e, b: (e, 0, b)),
            pl.BlockSpec((1, MODEL_WIDTH, F_BLOCK), lambda e, b: (e, 0, b + blocks)),
            pl.BlockSpec((1, F_BLOCK, MODEL_WIDTH), lambda e, b: (e, b, 0)),
        ]
        + [whole] * (2 * parts),
        out_specs=[whole] * (2 * parts) + [piece] * 3,
        out_shape=[row_shape] * (2 * parts) + [piece_shape] * 3,
        scratch_shapes=[
            pltpu.VMEM((tokens, MODEL_WIDTH), bf16),
            pltpu.VMEM((tokens, MODEL_WIDTH), bf16),
            pltpu.VMEM((tokens, MODEL_WIDTH), f32),
            pltpu.VMEM((tokens, MODEL_WIDTH), f32),
        ],
        compiler_params=pltpu.CompilerParams(vmem_limit_bytes=VMEM_LIMIT),
        cost_estimate=pl.CostEstimate(
            flops=12 * tokens * held * MODEL_WIDTH * F,
            bytes_accessed=6 * held * MODEL_WIDTH * F + 20 * tokens * MODEL_WIDTH,
            transcendentals=tokens * held * F,
        ),
        name="experts",
    )(combine, expert_in, expert_in, expert_out, *row_parts, *grad_parts)
    return out[:parts], out[parts : 2 * parts], out[2 * parts :]


def expert_weights_kernel(rows_ref, grads_ref, active_ref, gate_ref, up_ref, gate_out, up_out, down_out, turned):
    step = pl.program_id(0) * pl.num_programs(1) + pl.program_id(1)

    @pl.when(step == 0)
    def _():
        turned[...] = rows_ref[...].T

    gate_out[0] = dot(turned[...], gate_ref[...]).astype(bf16)
    up_out[0] = dot(turned[...], up_ref[...]).astype(bf16)
    down_out[0] = dot(active_ref[...], grads_ref[...], TN).astype(bf16)


def expert_weights(rows, grads, active, gate, up, held):
    tokens = rows.shape[0]
    blocks = F // F_BLOCK
    whole = pl.BlockSpec((tokens, MODEL_WIDTH), lambda e, b: (0, 0))
    piece = pl.BlockSpec((tokens, F_BLOCK), lambda e, b: (0, e * blocks + b))
    wide = pl.BlockSpec((1, MODEL_WIDTH, F_BLOCK), lambda e, b: (e, 0, b))
    return pl.pallas_call(
        expert_weights_kernel,
        grid=(held, blocks),
        in_specs=[whole] * 2 + [piece] * 3,
        out_specs=[wide, wide, pl.BlockSpec((1, F_BLOCK, MODEL_WIDTH), lambda e, b: (e, b, 0))],
        out_shape=[
            jax.ShapeDtypeStruct((held, MODEL_WIDTH, F), bf16),
            jax.ShapeDtypeStruct((held, MODEL_WIDTH, F), bf16),
            jax.ShapeDtypeStruct((held, F, MODEL_WIDTH), bf16),
        ],
        scratch_shapes=[pltpu.VMEM((MODEL_WIDTH, tokens), bf16)],
        compiler_params=pltpu.CompilerParams(vmem_limit_bytes=VMEM_LIMIT),
        cost_estimate=pl.CostEstimate(
            flops=6 * tokens * held * MODEL_WIDTH * F,
            bytes_accessed=6 * held * MODEL_WIDTH * F + 8 * tokens * MODEL_WIDTH,
            transcendentals=0,
        ),
        name="expert_weights",
    )(rows, grads, active, gate, up)


class Links:
    def __init__(self):
        self.shards = lax.axis_size("fsdp")
        self.contexts = lax.axis_size("ctx")
        self.chips = self.contexts // 2
        self.shard = lax.axis_index("fsdp")
        self.context = lax.axis_index("ctx")
        self.chip = self.context // 2
        self.core = self.context % 2

    def across(self, array, k):
        return lax.ppermute(array, "fsdp", [(i, i ^ k) for i in range(self.shards)])

    def other_core(self, array):
        return lax.ppermute(array, "ctx", [(i, i ^ 1) for i in range(self.contexts)])

    def shift(self, array, s):
        n = self.contexts
        return lax.ppermute(array, "ctx", [(i, (i + 2 * s) % n) for i in range(n)])


MESH = pl.DeviceIdType.MESH
LINE = 4


class Place:
    def __init__(self):
        self.shard, self.context = lax.axis_index("fsdp"), lax.axis_index("ctx")
        self.core, self.chip = self.context % 2, self.context // 2
        self.partner = {"ctx": 2 * self.chip + 1 - self.core}

    def peer_index(self, k):
        x, y = (self.shard % 2 + k % 2) % 2, (self.shard // 2 + k // 2) % 2
        return 2 * y + x

    def peer(self, k):
        return {"fsdp": self.peer_index(k)}

    def chip_device(self, chip):
        return {"ctx": 2 * chip + self.core}


def remote(source, target, sems, index, device):
    return pltpu.make_async_remote_copy(
        src_ref=source,
        dst_ref=target,
        send_sem=sems.at[0, index],
        recv_sem=sems.at[1, index],
        device_id=device,
        device_id_type=MESH,
    )


def greet(device):
    pl.semaphore_signal(pltpu.get_barrier_semaphore(), inc=1, device_id=device, device_id_type=MESH)


SHARDS = 4
GAIN_ROWS = 16


class Square:
    def __init__(self, place, blocks, direct_sem, relay_sem, base=0):
        half = blocks.shape[1] // 2
        own = blocks.at[place.shard]
        self.directs = [remote(own, own, direct_sem, base + k - 1, place.peer(k)) for k in (1, 2)]
        self.relays = []
        for k in (1, 2):
            spot = blocks.at[place.peer_index(k), (k - 1) * half : k * half]
            self.relays.append(remote(spot, spot, relay_sem, base + k - 1, place.peer(3 - k)))

    def start(self):
        for copy in self.directs:
            copy.start()

    def pass_on(self):
        for direct, relay in zip(self.directs, self.relays):
            direct.wait_recv()
            relay.start()

    def finish(self):
        for copy in self.relays:
            copy.wait_recv()

    def drain(self):
        for copy in self.directs + self.relays:
            copy.wait_send()


LAST = LINE - 1
WIDE = 4


def forward_kernel(
    tokens_src,
    routes,
    gates,
    gain_pair,
    cotangent,
    starts,
    tables,
    pair_src,
    query_src,
    output_src,
    expand_src,
    shrink_src,
    turned_normed_out,
    query_rows_out,
    turned_attn_out,
    middle_out,
    gain_rows_out,
    cosine,
    sine,
    pair_out,
    query_out,
    output_out,
    pairs,
    turned_out,
    grads_out,
    results_out,
    row_grads_out,
    active_out,
    gate_out,
    up_out,
    turned_normed,
    query,
    turned_attn,
    middle,
    tokens,
    gains,
    turned_rows,
    pair_weight,
    query_weight,
    output_weight,
    expand,
    shrink,
    own_pairs,
    normed,
    combine_in,
    combine_own,
    attn,
    bias,
    combine,
    rows_all,
    grads_all,
    result_sum,
    grad_sum,
    key_value,
    load_sem,
    table_sem,
    store_sem,
    expert_sem,
    gain_sem,
    combine_sem,
    direct_sem,
    relay_sem,
    pass_sem,
    right_sem,
    left_sem,
    core_sem,
    own_sem,
    square_direct_sem,
    square_relay_sem,
    key_sem,
    emit_sem,
    last_sem,
    input_sem,
):
    r = types.SimpleNamespace(**locals())
    place = Place()
    core, chip, shard = place.core, place.chip, place.shard
    local = pltpu.make_async_copy
    rows = r.cosine.shape[0]
    wide = SHARDS * rows
    held = r.pair_src.shape[0]
    half, quarter = held // 2, held // 4
    greet_line(place)
    length = r.bias.shape[2]

    def rows_of(owner, piece, size):
        return pl.ds(pl.multiple_of(owner * held + core * half, half) + piece, size)

    sources = (r.pair_src, r.query_src, r.output_src)
    weights = (r.pair_weight, r.query_weight, r.output_weight)
    weight_outs = (r.pair_out, r.query_out, r.output_out)
    loads, directs, relays, passes, stores = [], [], [], [], []
    for w in range(3):
        weight = weights[w]
        own_rows = pl.ds(pl.multiple_of(shard * held, held), held)
        loads.append(local(sources[w], weight.at[own_rows], r.load_sem.at[w]))
        stores.append(local(weight, weight_outs[w], r.store_sem.at[w]))
        mine = sources[w].at[pl.ds(pl.multiple_of(core * half, half), half)]
        spot = weight.at[rows_of(shard, 0, half)]
        directs.append([remote(mine, spot, r.direct_sem, 2 * w + k - 1, place.peer(k)) for k in (1, 2)])
        relay, onward = [], []
        for k in (1, 2):
            spot = weight.at[rows_of(place.peer_index(k), (k - 1) * quarter, quarter)]
            relay.append(remote(spot, spot, r.relay_sem, 2 * w + k - 1, place.peer(3 - k)))
            spot = weight.at[rows_of(place.peer_index(k), 0, half)]
            onward.append(remote(spot, spot, r.pass_sem, 4 * w + k - 1, place.partner))
        for k in (1, 2):
            spot = weight.at[rows_of(place.peer_index(3), (k - 1) * quarter, quarter)]
            onward.append(remote(spot, spot, r.pass_sem, 4 * w + k + 1, place.partner))
        relays.append(relay)
        passes.append(onward)

    def send_weight(w):
        for copy in directs[w]:
            copy.start()

    def relay_weight(w):
        for k in (1, 2):
            directs[w][k - 1].wait_recv()
            relays[w][k - 1].start()
        for k in (1, 2):
            passes[w][k - 1].start()

    def pass_weight(w):
        for k in (1, 2):
            relays[w][k - 1].wait_recv()
            passes[w][k + 1].start()

    def settle_weight(w):
        loads[w].wait()
        for copy in passes[w]:
            copy.wait_recv()
        stores[w].start()

    def sent_weight(w):
        for copy in directs[w] + relays[w] + passes[w]:
            copy.wait_send()
        stores[w].wait()

    send_weight(0)

    gain_rows = r.gains.at[pl.ds(pl.multiple_of(shard * GAIN_ROWS, GAIN_ROWS), GAIN_ROWS)]
    gain_rows[...] = jnp.concatenate([r.gain_pair[...], jnp.zeros((GAIN_ROWS - 2, held), bf16)], axis=0)
    expert_row = lax.broadcasted_iota(jnp.int32, (E, rows), 0)
    for m in range(MB):
        combine = jnp.zeros((E, rows), f32)
        for k in range(TOP):
            combine += jnp.where(expert_row == r.routes[m, 0, k : k + 1], r.gates[m, 0, k : k + 1], 0.0)
        r.combine_own[:, m * rows : (m + 1) * rows] = combine
    r.combine_in[shard] = r.combine_own[...]
    small_copies = []
    for k in range(1, SHARDS):
        small_copies.append(remote(gain_rows, gain_rows, r.gain_sem, k - 1, place.peer(k)))
        small_copies.append(remote(r.combine_own, r.combine_in.at[shard], r.combine_sem, k - 1, place.peer(k)))

    for copy in small_copies:
        copy.start()
    at = pl.ds(pl.multiple_of(place.context * rows, rows), rows)
    table_loads = [
        local(r.tables.at[i, at], table, r.table_sem.at[i]) for i, table in enumerate((r.cosine, r.sine))
    ]
    token_load = local(r.tokens_src, r.tokens, r.input_sem.at[MB])
    grad_loads = [
        local(r.cotangent.at[m * rows : (m + 1) * rows], r.grads_all.at[m, shard], r.input_sem.at[m])
        for m in range(MB)
    ]
    for load in [token_load] + table_loads + loads + grad_loads:
        load.start()
    expert_loads = [
        local(r.expand_src, r.expand, r.expert_sem.at[0]),
        local(r.shrink_src, r.shrink, r.expert_sem.at[1]),
    ]
    for load in expert_loads:
        load.start()
    grad_squares = [Square(place, r.grads_all.at[m], r.square_direct_sem, r.square_relay_sem, 2 * m) for m in range(MB)]
    row_squares = [
        Square(place, r.rows_all.at[m], r.square_direct_sem, r.square_relay_sem, 2 * (MB + m)) for m in range(MB)
    ]

    def spread_gains():
        r.gain_rows_out[...] = jnp.zeros_like(r.gain_rows_out)
        for b in range(SHARDS):
            pair = r.gains[b * GAIN_ROWS : b * GAIN_ROWS + 2]
            r.gain_rows_out[0:2, b * held : (b + 1) * held] = pair.astype(f32)

    def gain_times(values, row, write):
        for b in range(SHARDS):
            columns = slice(b * held, (b + 1) * held)
            write(columns, (values[:, columns] * r.gain_rows_out[row : row + 1, columns]).astype(bf16))

    token_load.wait()
    values = r.tokens[...].astype(f32)
    unit = values * lax.rsqrt(jnp.mean(values * values, axis=-1, keepdims=True) + eps)
    for copy in small_copies:
        copy.wait_recv()

    def write_normed(columns, value):
        r.normed[:, columns] = value

    spread_gains()
    gain_times(unit, 0, write_normed)
    r.turned_normed[...] = r.normed[...].T
    for b in range(SHARDS):
        spread = jnp.concatenate([r.combine_in[b], jnp.zeros((LANES - E, MB * rows), f32)], axis=0)
        r.combine[b] = spread.T
    for m in range(MB):
        r.bias[m] = visible_bias(r.starts, m, place.context, (rows, length), 0)
    for load in table_loads + grad_loads:
        load.wait()

    relay_weight(0)
    send_weight(1)
    pass_weight(0)
    settle_weight(0)
    cosine, sine = r.cosine[...], r.sine[...]

    def project(weight, column, rotated):
        result = dot(r.normed[...], weight[:, pl.ds(column, WIDE * LANES)])
        tiles = []
        for m in range(MB):
            for i in range(WIDE):
                tile = result[m * rows : (m + 1) * rows, i * LANES : (i + 1) * LANES]
                tiles.append((m, i, rotate(tile, cosine, sine) if rotated else tile))
        return tiles

    blocks = KEY_WIDTH // (WIDE * LANES)
    for b in range(2 * blocks):
        column = b * WIDE * LANES
        for m, i, tile in project(r.pair_weight, column, b < blocks):
            r.own_pairs[m, :, pl.ds(column + i * LANES, LANES)] = tile.astype(bf16)

    def chunk(m, owner):
        owner = jnp.clip(owner, 0, LAST)
        return r.pairs.at[m, pl.ds(pl.multiple_of((2 * owner + core) * rows, rows), rows)]

    def move(m, t, direction):
        target = chunk(m, chip - direction * (t - 1))
        source = r.own_pairs.at[m] if t == 1 else target
        sems = r.right_sem if direction > 0 else r.left_sem
        device = place.chip_device(jnp.clip(chip + direction, 0, LAST))
        return remote(source, target, sems, m * LAST + t - 1, device)

    def sends(t, direction):
        owner = chip - direction * (t - 1)
        if direction > 0:
            return (chip < LAST) & (owner >= 0)
        return (chip > 0) & (owner <= LAST)

    def gets(t, direction):
        owner = chip - direction * t
        return owner >= 0 if direction > 0 else owner <= LAST

    def came(m, t, direction):
        spot = chunk(m, chip - direction * t)
        sems = r.right_sem if direction > 0 else r.left_sem
        return remote(spot, spot, sems, m * LAST + t - 1, place.partner)

    def pass_chunk(m, t, direction):
        spot = chunk(m, chip - direction * t)
        index = (m * LINE + t) * 2 + (1 if direction > 0 else 0)
        return remote(spot, spot, r.core_sem, index, place.partner)

    def take_step(m, t):
        for direction in (1, -1):

            @pl.when(gets(t, direction))
            def _():
                came(m, t, direction).wait_recv()
                if t < LAST:

                    @pl.when(sends(t + 1, direction))
                    def _():
                        move(m, t + 1, direction).start()

                pass_chunk(m, t, direction).start()

    own_copies = []
    for m in range(MB):
        for direction in (1, -1):

            @pl.when(sends(1, direction))
            def _():
                move(m, 1, direction).start()

        own_copies.append(
            (
                local(r.own_pairs.at[m], chunk(m, chip), r.own_sem.at[m]),
                remote(r.own_pairs.at[m], chunk(m, chip), r.core_sem, m * LINE * 2, place.partner),
            )
        )
        for copy in own_copies[m]:
            copy.start()

    def settle_pairs(m):
        own_copies[m][0].wait()
        own_copies[m][1].wait()
        for t in range(1, LINE):
            for direction in (1, -1):

                @pl.when(gets(t, direction))
                def _():
                    pass_chunk(m, t, direction).wait()

    def query_block(b, carry):
        column = pl.multiple_of(b * WIDE * LANES, WIDE * LANES)
        for m, i, tile in project(r.query_weight, column, True):
            r.query[m * rows : (m + 1) * rows, pl.ds(column + i * LANES, LANES)] = tile.astype(bf16)
        return carry

    def key_load(m, p, slot, i):
        lane = pl.multiple_of(p * LANES, LANES) + i * KEY_WIDTH
        return local(r.pairs.at[m, :, pl.ds(lane, LANES)], r.key_value.at[slot, i], r.key_sem.at[slot, i])

    def attend(m):
        own = slice(m * rows, (m + 1) * rows)
        for i in range(2):
            key_load(m, 0, 0, i).start()

        def pair(p, carry):
            slot = p % 2
            for i in range(2):
                key_load(m, p, slot, i).wait()

            @pl.when(p + 1 < PAIRS)
            def _():
                for i in range(2):
                    key_load(m, p + 1, 1 - slot, i).start()

            column = pl.multiple_of(p * PAIR_QUERY, PAIR_QUERY)
            columns = [pl.ds(column + i * LANES, LANES) for i in range(GROUP)]
            tiles = [r.query[own, c].astype(f32) * (1.0 / HEAD_SIZE) for c in columns]
            results = attention_pair(tiles, r.key_value[slot, 0], r.key_value[slot, 1], r.bias[m])
            for c, tile in zip(columns, results):
                r.attn[own, c] = tile.astype(bf16)
            return carry

        lax.fori_loop(0, PAIRS, pair, 0)
        r.turned_attn[:, own] = r.attn[own].T

    def finish_attention(m):
        own = slice(m * rows, (m + 1) * rows)
        middle = r.tokens[own].astype(f32) + dot(r.attn[own], r.output_weight[...])
        r.middle[own] = middle
        unit = middle * lax.rsqrt(jnp.mean(middle * middle, axis=-1, keepdims=True) + eps)

        def write(columns, value):
            r.rows_all[m, shard, :, columns] = value

        gain_times(unit, 1, write)

    active, gate, up = [r.pair_weight.at[i * wide : (i + 1) * wide] for i in range(3)]
    results, row_grads = [r.query_weight.at[i * wide : (i + 1) * wide] for i in range(2)]

    turned = r.turned_rows

    def turn(m):
        turned[...] = r.rows_all[m].reshape(wide, MODEL_WIDTH).T

    def emits(m):
        pairs = (
            (turned, r.turned_out.at[:, m * wide : (m + 1) * wide]),
            (r.grads_all.at[m], r.grads_out.at[m]),
            (results, r.results_out.at[m]),
            (row_grads, r.row_grads_out.at[m]),
        )
        for e in range(2):
            columns = slice(e * F, (e + 1) * F)
            pairs += tuple(
                (source.at[:, columns], target.at[m, :, columns])
                for source, target in ((active, r.active_out), (gate, r.gate_out), (up, r.up_out))
            )
        return [local(a, b, r.emit_sem.at[m * len(pairs) + i]) for i, (a, b) in enumerate(pairs)]

    def expert_steps(m, between):
        steps = [(e, b) for e in range(r.expand.shape[0]) for b in range(F // F_BLOCK)]
        for i, (e, b) in enumerate(steps):
            weight = r.combine[:, m * rows : (m + 1) * rows, :].reshape(wide, LANES)
            expert = shard * r.expand.shape[0] + e
            chosen = jnp.where(lane_index(weight.shape) == expert, weight, 0.0)
            columns = slice(b * F_BLOCK, (b + 1) * F_BLOCK)
            up_columns = slice(F + b * F_BLOCK, F + (b + 1) * F_BLOCK)
            a, g, u, result, row_grad = expert_block(
                r.rows_all[m].reshape(wide, MODEL_WIDTH),
                r.grads_all[m].reshape(wide, MODEL_WIDTH),
                jnp.sum(chosen, axis=1, keepdims=True),
                r.expand[e, :, columns],
                r.expand[e, :, up_columns],
                r.shrink[e, columns, :],
            )
            spot = slice(e * F + b * F_BLOCK, e * F + (b + 1) * F_BLOCK)
            active[:, spot], gate[:, spot], up[:, spot] = a, g, u
            if i == 0:
                r.result_sum[...] = result
                r.grad_sum[...] = row_grad
            elif i < len(steps) - 1:
                r.result_sum[...] += result
                r.grad_sum[...] += row_grad
            else:
                results[...] = (r.result_sum[...] + result).astype(bf16)
                row_grads[...] = (r.grad_sum[...] + row_grad).astype(bf16)
            if i in between:
                between[i]()

    relay_weight(1)
    send_weight(2)
    take_step(0, 1)
    take_step(1, 1)
    pass_weight(1)
    take_step(0, 2)
    settle_weight(1)
    lax.fori_loop(0, MODEL_WIDTH // (WIDE * LANES), query_block, 0)
    relay_weight(2)
    grad_squares[0].start()
    take_step(1, 2)
    take_step(0, 3)
    settle_pairs(0)
    attend(0)
    pass_weight(2)
    grad_squares[0].pass_on()
    take_step(1, 3)
    settle_weight(2)
    finish_attention(0)
    row_squares[0].start()
    settle_pairs(1)
    attend(1)
    row_squares[0].pass_on()
    finish_attention(1)
    row_squares[1].start()
    grad_squares[1].start()
    early = [
        local(source, target, r.last_sem.at[i])
        for i, (source, target) in enumerate(
            (
                (r.turned_normed, r.turned_normed_out),
                (r.query, r.query_rows_out),
                (r.turned_attn, r.turned_attn_out),
                (r.middle, r.middle_out),
            )
        )
    ]
    for emit in early:
        emit.start()
    for load in expert_loads:
        load.wait()
    sent_weight(0)
    sent_weight(1)
    grad_squares[0].finish()
    row_squares[0].finish()
    expert_steps(0, {1: row_squares[1].pass_on})
    turn(0)
    for emit in emits(0):
        emit.start()
    for emit in early:
        emit.wait()

    for copy in small_copies:
        copy.wait_send()
    sent_weight(2)
    for m in range(MB):
        for t in range(1, LINE):
            for direction in (1, -1):

                @pl.when(sends(t, direction))
                def _():
                    move(m, t, direction).wait_send()

    for square in grad_squares[:1] + row_squares[:1]:
        square.drain()
    grad_squares[1].pass_on()
    row_squares[1].finish()
    for emit in emits(0):
        emit.wait()
    turn(1)
    grad_squares[1].finish()
    last = emits(1)

    def emit_first():
        for emit in last[:2] + last[4:7]:
            emit.start()

    expert_steps(1, {1: emit_first})
    for emit in last[2:4] + last[7:]:
        emit.start()
    for square in grad_squares[1:] + row_squares[1:]:
        square.drain()
    for emit in last:
        emit.wait()


def forward(tokens, routes, gates, gain_pair, cotangent, starts, tables, weights, expert_in, expert_out):
    rows = tokens.shape[0] // MB
    length = tables.shape[1]
    wide = SHARDS * rows
    held = weights[0].shape[0]
    dma = pltpu.SemaphoreType.DMA
    anywhere = pl.BlockSpec(memory_space=pl.ANY)
    vmem = pl.BlockSpec(memory_space=pltpu.VMEM)
    shape = jax.ShapeDtypeStruct
    low = lambda *s: pltpu.VMEM(s, bf16)
    full = [(SHARDS * held, w.shape[1]) for w in weights]
    blocks = (MB, SHARDS, rows, MODEL_WIDTH)
    return pl.pallas_call(
        forward_kernel,
        in_specs=[anywhere] + [vmem] * 3 + [anywhere, pl.BlockSpec(memory_space=pltpu.SMEM)] + [anywhere] * 6,
        out_specs=[anywhere] * 4 + [vmem] * 3 + [anywhere] * 11,
        out_shape=[
            shape(tokens.shape[::-1], bf16),
            shape(tokens.shape, bf16),
            shape(tokens.shape[::-1], bf16),
            shape(tokens.shape, f32),
            shape((8, MODEL_WIDTH), f32),
            shape((rows, LANES), f32),
            shape((rows, LANES), f32),
        ]
        + [shape(f, bf16) for f in full]
        + [
            shape((MB, length, 2 * KEY_WIDTH), bf16),
            shape((MODEL_WIDTH, MB * wide), bf16),
            shape(blocks, bf16),
            shape((MB, wide, MODEL_WIDTH), bf16),
            shape((MB, wide, MODEL_WIDTH), bf16),
        ]
        + [shape((MB, wide, 2 * F), bf16)] * 3,
        scratch_shapes=[
            low(*tokens.shape[::-1]),
            low(*tokens.shape),
            low(*tokens.shape[::-1]),
            pltpu.VMEM(tokens.shape, f32),
            low(*tokens.shape),
            low(SHARDS * GAIN_ROWS, held),
            low(MODEL_WIDTH, wide),
        ]
        + [low(*f) for f in full]
        + [
            low(*expert_in.shape),
            low(*expert_out.shape),
            low(MB, rows, 2 * KEY_WIDTH),
            low(*tokens.shape),
            pltpu.VMEM((SHARDS, E, MB * rows), f32),
            pltpu.VMEM((E, MB * rows), f32),
            low(*tokens.shape),
            pltpu.VMEM((MB, rows, length), f32),
            pltpu.VMEM((SHARDS, MB * rows, LANES), f32),
            low(*blocks),
            low(*blocks),
            pltpu.VMEM((wide, MODEL_WIDTH), f32),
            pltpu.VMEM((wide, MODEL_WIDTH), f32),
            low(2, 2, length, LANES),
            dma((3,)),
            dma((2,)),
            dma((3,)),
            dma((2,)),
            dma((2, SHARDS - 1)),
            dma((2, SHARDS - 1)),
            dma((2, 6)),
            dma((2, 6)),
            dma((2, 12)),
            dma((2, MB * LAST)),
            dma((2, MB * LAST)),
            dma((2, 2 * MB * LINE)),
            dma((MB,)),
            dma((2, 4 * MB)),
            dma((2, 4 * MB)),
            dma((2, 2)),
            dma((10 * MB,)),
            dma((4,)),
            dma((MB + 1,)),
        ],
        compiler_params=pltpu.CompilerParams(
            collective_id=1, has_side_effects=True, vmem_limit_bytes=VMEM_LIMIT
        ),
        name="forward",
    )(tokens, routes, gates, gain_pair, cotangent, starts, tables, *weights, expert_in, expert_out)


ADD_ROWS = 64


def add_into(out, *parts):
    rows = out.shape[0]
    size = max(d for d in range(16, ADD_ROWS + 1, 16) if rows % d == 0)

    def body(i, carry):
        spot = pl.ds(pl.multiple_of(i * size, size), size)
        total = parts[0][spot].astype(f32)
        for part in parts[1:]:
            total = total + part[spot].astype(f32)
        out[spot] = total.astype(out.dtype)
        return carry

    lax.fori_loop(0, rows // size, body, 0)


def greet_line(place):
    has_left, has_right = place.chip > 0, place.chip < LINE - 1
    greet(place.partner)
    for k in range(1, SHARDS):
        greet(place.peer(k))

    @pl.when(has_left)
    def _():
        greet(place.chip_device(place.chip - 1))

    @pl.when(has_right)
    def _():
        greet(place.chip_device(place.chip + 1))

    neighbours = jnp.where(has_left, 1, 0) + jnp.where(has_right, 1, 0)
    pl.semaphore_wait(pltpu.get_barrier_semaphore(), SHARDS + neighbours)


class Line:
    def __init__(self, place, pieces, sems):
        near_sem, far_sem, back_sem, pass_sem, store_sem = sems
        chip = place.chip
        self.inner = (chip == 1) | (chip == 2)
        outer = place.chip_device(3 * (chip // 2))
        inner = place.chip_device(1 + chip // 2)
        facing = place.chip_device(3 - chip)
        self.pieces = pieces
        numbered = list(enumerate(pieces))
        self.inward = [remote(p[0], p[1], near_sem, i, inner) for i, p in numbered]
        self.facing = [remote(p[0], p[2], far_sem, i, facing) for i, p in numbered]
        self.outward = [remote(p[1], p[3], back_sem, i, outer) for i, p in numbered]
        self.pass_inner = [remote(p[1], p[3], pass_sem, i, place.partner) for i, p in numbered]
        self.pass_outer = [remote(p[3], p[3], pass_sem, i, place.partner) for i, p in numbered]
        self.stores = [pltpu.make_async_copy(p[1], p[3], store_sem.at[i]) for i, p in numbered]

    def ready(self, *items):
        @pl.when(jnp.logical_not(self.inner))
        def _():
            for i in items:
                self.inward[i].start()

    def serve(self, halfway=(), finish=(), forward=()):
        @pl.when(self.inner)
        def _():
            for i in halfway:
                self.inward[i].wait_recv()
                own, near = self.pieces[i][:2]
                add_into(own, own, near)
                self.facing[i].start()
            for i in finish:
                self.facing[i].wait_recv()
                own, near, far = self.pieces[i][:3]
                add_into(near, own, far)
                self.outward[i].start()
                self.pass_inner[i].start()
                self.stores[i].start()

        @pl.when(jnp.logical_not(self.inner))
        def _():
            for i in forward:
                self.outward[i].wait_recv()
                self.pass_outer[i].start()

    def drain(self, items=None):
        items = range(len(self.pieces)) if items is None else items

        @pl.when(self.inner)
        def _():
            for i in items:
                self.facing[i].wait_send()
                self.outward[i].wait_send()
                self.pass_inner[i].wait_send()
                self.stores[i].wait()

        @pl.when(jnp.logical_not(self.inner))
        def _():
            for i in items:
                self.inward[i].wait_send()
                self.pass_outer[i].wait_send()

        for i in items:
            self.pass_outer[i].wait_recv()


def line_sems(number):
    dma = pltpu.SemaphoreType.DMA
    return [dma((2, number))] * 4 + [dma((number,))]


def split_rows(ref, parts):
    size = ref.shape[0] // parts
    return [ref.at[j * size : (j + 1) * size] for j in range(parts)]


def out_halves(place, ref, parts):
    half = ref.shape[0] // 2
    size = half // parts
    first = pl.multiple_of(place.core * half, half)
    return [ref.at[pl.ds(first + j * size, size)] for j in range(parts)]


def line_pieces(place, own, near, far, out, parts):
    return list(
        zip(split_rows(own, parts), split_rows(near, parts), split_rows(far, parts), out_halves(place, out, parts))
    )


class PairSum:
    def __init__(self, place, own, sources, others, lands, core_sem, left_sem):
        self.place, self.own, self.others, self.lands, self.left_sem = place, own, others, lands, left_sem
        self.trades = [remote(sources(j), others.at[j], core_sem, j, place.partner) for j in range(LINE)]
        self.past = LAST - place.chip

    def trade(self):
        for copy in self.trades:
            copy.start()

    def half(self, ref, h):
        size = ref.shape[0] // 2
        return ref.at[h * size : (h + 1) * size]

    def move(self, t, h):
        owner = jnp.clip(self.place.chip - (LINE - t), 0, LAST)
        device = self.place.chip_device(jnp.clip(self.place.chip - 1, 0, LAST))
        source, target = self.half(self.own(owner), h), self.half(self.lands.at[t - 1], h)
        return remote(source, target, self.left_sem, 2 * (t - 1) + h, device)

    def meet(self):
        for j in range(LINE):
            self.trades[j].wait_recv()
            add_into(self.own(j), self.own(j), self.others.at[j])

        @pl.when(self.past == 0)
        def _():
            for t in range(1, LINE):
                for h in range(2):
                    self.move(t, h).start()

    def take(self, t, h):
        self.move(t, h).wait_recv()
        mine = self.half(self.own(jnp.clip(self.place.chip - (LAST - t), 0, LAST)), h)
        add_into(mine, mine, self.half(self.lands.at[t - 1], h))

    def step(self, t):
        @pl.when((self.past >= 1) & (self.past <= min(t - 1, LINE - 2)))
        def _():
            for h in range(2):
                self.take(t - 1, h)
                self.move(t, h).start()

    def finish(self, out, cosine, sine):
        @pl.when(self.past >= 1)
        def _():
            for h in range(2):
                self.take(LAST, h)

        mine = self.own(self.place.chip)
        for i in range(2 * KEY_WIDTH // LANES):
            columns = slice(i * LANES, (i + 1) * LANES)
            tile = mine[:, columns]
            if i < KEY_WIDTH // LANES:
                tile = rotate(tile.astype(f32), cosine[...], -sine[...]).astype(bf16)
            out[:, columns] = tile

    def drain(self):
        for copy in self.trades:
            copy.wait_send()
        for t in range(1, LINE):

            @pl.when((self.past <= t - 1) & (self.past <= LINE - 2))
            def _():
                for h in range(2):
                    self.move(t, h).wait_send()


PARTS = 4


def backward_kernel(
    query_src,
    starts,
    cosine,
    sine,
    middle_src,
    cotangent_src,
    gain,
    pairs,
    turned_src,
    grads_src,
    active_src,
    gate_src,
    up_src,
    results_src,
    row_grads_src,
    output_src,
    query_low_out,
    pair_low,
    middle_low_out,
    middle_grad_out,
    gain_grad,
    block_output,
    gate_total,
    up_total,
    gate_rest,
    up_rest,
    down_rest,
    pair_grad,
    query,
    middle,
    cotangent,
    query_low,
    middle_low,
    middle_grad,
    rows,
    turned,
    grads,
    pool,
    send_gate,
    send_up,
    send_down,
    own_gate,
    own_up,
    own_down,
    other_gate,
    other_up,
    other_down,
    near_gate,
    near_up,
    far_gate,
    far_up,
    row_grad_own,
    row_grad_in,
    result_own,
    result_in,
    attn_grad,
    key_value,
    bias,
    pair_other,
    land_left,
    load_sem,
    weight_sem,
    trade_sem,
    rest_sem,
    row_sem,
    result_sem,
    key_sem,
    core_sem,
    left_sem,
    near_sem,
    far_sem,
    back_sem,
    pass_sem,
    store_sem,
    emit_sem,
):
    r = types.SimpleNamespace(**locals())
    place = Place()
    core, chip, shard = place.core, place.chip, place.shard
    rows = r.cosine.shape[0]
    tokens = MB * SHARDS * rows
    side = MODEL_WIDTH // 2
    local = pltpu.make_async_copy

    wide = SHARDS * rows
    loads = []

    def load(source, target):
        loads.append(local(source, target, r.load_sem.at[len(loads)]))
        loads[-1].start()
        return loads[-1]

    flat = lambda ref, m: [(ref.at[m, k], m * wide + k * rows) for k in range(SHARDS)]
    grad_loads, piece_loads = [], []
    turned_load = load(r.turned_src, r.turned)
    for i, ref in ((1, r.gate_src), (2, r.up_src), (0, r.active_src)):
        for m in range(MB):
            at = i * tokens + m * wide
            piece_loads.append(load(ref.at[m], r.pool.at[at : at + wide]))
    for m in range(MB):
        for source, at in flat(r.grads_src, m):
            grad_loads.append(load(source, r.grads.at[at : at + rows]))
    own_loads = [load(r.row_grads_src.at[m, shard], r.row_grad_own.at[m]) for m in range(MB)]
    own_loads.append(load(r.results_src.at[0, shard], r.result_own))

    vector_loads = [
        load(source, target)
        for source, target in ((r.middle_src, r.middle), (r.cotangent_src, r.cotangent), (r.query_src, r.query))
    ]
    greet_line(place)

    row_copies, result_copies = [], []
    for m in range(MB):
        for k in range(1, SHARDS):
            i = m * (SHARDS - 1) + k - 1
            at = place.peer_index(k)
            row_copies.append(
                remote(r.row_grads_src.at[m, at], r.row_grad_in.at[m, k - 1], r.row_sem, i, place.peer(k))
            )
            if m == 0:
                result_copies.append(
                    remote(r.results_src.at[m, at], r.result_in.at[k - 1], r.result_sem, i, place.peer(k))
                )
    for copy in row_copies:
        copy.start()

    for m in range(MB):
        r.bias[m] = visible_bias(r.starts, m, place.context, r.bias.shape[1:], 1)

    turned_load.wait()
    sends = (r.send_gate, r.send_up, r.send_down)
    owns = (r.own_gate, r.own_up, r.own_down)
    others = (r.other_gate, r.other_up, r.other_down)
    upper = MODEL_WIDTH // 2
    parts = [(0, 0), (0, upper), (1, None)]

    def some(ref, start):
        return ref if start is None else ref.at[start : start + upper]

    trades = {}
    for b, start in parts:
        for i in range(2):
            index = len(trades)
            trades[b, start, i] = remote(
                some(sends[i], start), some(others[i].at[b], start), r.trade_sem, index, place.partner
            )
    for b in range(2):
        trades[b, None, 2] = remote(sends[2], others[2].at[b], r.trade_sem, len(trades), place.partner)

    def weight_block(b, start, expert, outs):
        column = pl.ds(pl.multiple_of(expert * F + b * F_BLOCK, F_BLOCK), F_BLOCK)
        for i in range(2):
            part = r.pool[(i + 1) * tokens : (i + 2) * tokens, column]
            some(outs[i], start)[...] = dot(some(r.turned, start)[...], part).astype(bf16)

    def down_block(b, expert, out):
        column = pl.ds(pl.multiple_of(expert * F + b * F_BLOCK, F_BLOCK), F_BLOCK)
        out[...] = dot(r.pool[0:tokens, column], r.grads[...], TN).astype(bf16)

    def meet(b, start, i):
        trades[b, start, i].wait_recv()
        mine = some(owns[i].at[b], start)
        add_into(mine, mine, some(others[i].at[b], start))

    gate_pieces = line_pieces(place, r.own_gate.at[0], r.near_gate, r.far_gate, r.gate_total, PARTS)
    up_pieces = line_pieces(place, r.own_up.at[0], r.near_up, r.far_up, r.up_total, PARTS)
    middle_part = PARTS // 2
    pieces = gate_pieces[:middle_part] + up_pieces[:middle_part] + gate_pieces[middle_part:] + up_pieces[middle_part:]
    line = Line(place, pieces, (r.near_sem, r.far_sem, r.back_sem, r.pass_sem, r.store_sem))

    for copy in piece_loads[: 2 * MB]:
        copy.wait()
    for n, (b, start) in enumerate(parts):
        if b == 1:
            for first in (0, upper):
                for i in range(2):
                    trades[0, first, i].wait_send()
        weight_block(b, start, 1 - core, sends)
        for i in range(2):
            trades[b, start, i].start()
        weight_block(b, start, core, [own.at[b] for own in owns[:2]])
        if b == 0:
            for i in range(2):
                meet(b, start, i)
                line.ready(*range((2 * n + i) * middle_part, (2 * n + i + 1) * middle_part))
        if start == 0:
            continue
        if b == 0:
            for copy in piece_loads[2 * MB :] + grad_loads:
                copy.wait()
        else:
            trades[0, None, 2].wait_send()
            line.serve([0])
        down_block(b, 1 - core, sends[2])
        trades[b, None, 2].start()
        down_block(b, core, owns[2].at[b])
        if b == 0:
            meet(0, None, 2)

    weight_loads = []
    for i in range(2):
        source = r.output_src.at[:, i * side : (i + 1) * side]
        target = r.pool.at[i * MODEL_WIDTH : (i + 1) * MODEL_WIDTH, 0:side]
        weight_loads.append(local(source, target, r.weight_sem.at[i]))
        weight_loads[-1].start()
    for copy in result_copies:
        copy.start()
    for i in range(3):
        meet(1, None, i)
    rests = [
        local(r.own_gate.at[1], r.gate_rest, r.rest_sem.at[0]),
        local(r.own_up.at[1], r.up_rest, r.rest_sem.at[1]),
        local(r.own_down, r.down_rest, r.rest_sem.at[2]),
    ]
    for copy in rests:
        copy.start()

    r.gain_grad[...] = jnp.zeros_like(r.gain_grad)

    def prepare(m):
        own = slice(m * rows, (m + 1) * rows)
        own_loads[m].wait()
        moe_in_grad = r.row_grad_own[m].astype(f32)
        for k in range(1, SHARDS):
            row_copies[m * (SHARDS - 1) + k - 1].wait_recv()
            moe_in_grad = moe_in_grad + r.row_grad_in[m, k - 1].astype(f32)
        middle = r.middle[own]
        scale = lax.rsqrt(jnp.mean(middle * middle, axis=-1, keepdims=True) + eps)
        unit = middle * scale
        r.gain_grad[m : m + 1] = jnp.sum(moe_in_grad * unit, axis=0, keepdims=True)
        weighted = moe_in_grad * r.gain[1:2]
        inner = jnp.mean(weighted * unit, axis=-1, keepdims=True)
        middle_grad = r.cotangent[own].astype(f32) + (weighted - unit * inner) * scale
        r.middle_grad[own] = middle_grad
        r.middle_low[own] = middle_grad.astype(bf16)
        if m == 0:
            for copy in weight_loads:
                copy.wait()
        total = dot(r.middle_low[own, 0:side], r.pool[0:MODEL_WIDTH, 0:side], NT)
        total = total + dot(r.middle_low[own, side:], r.pool[MODEL_WIDTH : 2 * MODEL_WIDTH, 0:side], NT)
        r.attn_grad[m] = total.astype(bf16)

    def key_load(step, slot, i):
        m, p = step // PAIRS, step % PAIRS
        lane = pl.multiple_of(p * LANES, LANES) + i * KEY_WIDTH
        return local(r.pairs.at[m, :, pl.ds(lane, LANES)], r.key_value.at[slot, i], r.key_sem.at[slot, i])

    pair_grads = (r.rows, r.grads.at[:, 0 : 2 * KEY_WIDTH])

    def chunk(of_chip, of_core):
        return pair_grads[0].at[pl.ds(pl.multiple_of((2 * of_chip + of_core) * rows, rows), rows)]

    pair_sum = PairSum(
        place,
        lambda j: chunk(j, core),
        lambda j: chunk(j, 1 - core),
        r.pair_other,
        r.land_left,
        r.core_sem,
        r.left_sem,
    )

    def pair_step(step, carry):
        m, p = step // PAIRS, step % PAIRS
        slot = step % 2
        for i in range(2):
            key_load(step, slot, i).wait()

        @pl.when(step + 1 < MB * PAIRS)
        def _():
            for i in range(2):
                key_load(step + 1, 1 - slot, i).start()

        at = pl.multiple_of(m * rows, rows)
        column = pl.multiple_of(p * PAIR_QUERY, PAIR_QUERY)
        lane = pl.multiple_of(p * LANES, LANES)
        columns = [pl.ds(column + i * LANES, LANES) for i in range(GROUP)]
        scale = 1.0 / HEAD_SIZE
        tiles = [r.query[pl.ds(at, rows), c].astype(f32) * scale for c in columns]
        grads = [r.attn_grad[m, :, c].astype(f32) for c in columns]
        bias = jnp.concatenate([r.bias[m]] * GROUP, axis=1)
        query_grads, key_grad, value_grad = attention_pair_gradient(
            tiles, grads, r.key_value[slot, 0], r.key_value[slot, 1], bias
        )
        for c, tile in zip(columns, query_grads):
            tile = rotate(tile * scale, r.cosine[...], -r.sine[...])
            r.query_low[pl.ds(at, rows), c] = tile.astype(bf16)
        key_low, value_low = key_grad.astype(bf16), value_grad.astype(bf16)
        for micro in range(MB):

            @pl.when(m == micro)
            def _():
                pair_grads[micro][:, pl.ds(lane, LANES)] = key_low
                pair_grads[micro][:, pl.ds(lane + KEY_WIDTH, LANES)] = value_low

        for at_step, actions in SERVICE:

            @pl.when(step == at_step)
            def _():
                for action in actions:
                    action()

        return carry

    serve = line.serve
    SERVICE = (
        (0, (lambda: serve([3], [1]),)),
        (1, (lambda: serve([4], [2]),)),
        (2, (lambda: serve([5], [3], [0]),)),
        (3, (pair_sum.trade, lambda: prepare(1), lambda: serve([6], [4], [1]), pair_sum.meet)),
        (4, (lambda: serve([7], [5], [2]),)),
        (5, (lambda: serve([], [6], [3]),)),
        (6, (lambda: pair_sum.step(2), lambda: serve([], [7], [4]))),
        (7, (lambda: serve([], [], [5]),)),
    )
    for i in range(2):
        key_load(0, 0, i).start()
    for copy in vector_loads:
        copy.wait()
    serve([1])
    prepare(0)
    serve([2], [0])
    lax.fori_loop(0, MB * PAIRS, pair_step, 0)
    second = local(pair_grads[1], r.pair_grad, r.rest_sem.at[3])
    second.start()
    emits = [
        local(source, target, r.emit_sem.at[i])
        for i, (source, target) in enumerate(
            (
                (r.query_low, r.query_low_out),
                (r.middle_low, r.middle_low_out),
                (r.middle_grad, r.middle_grad_out),
            )
        )
    ]
    for copy in emits:
        copy.start()
    pair_sum.step(3)
    own_loads[MB].wait()
    total = r.middle[0:rows] + r.result_own[...].astype(f32)
    for k in range(1, SHARDS):
        result_copies[k - 1].wait_recv()
        total = total + r.result_in[k - 1].astype(f32)
    r.block_output[...] = total.astype(bf16)
    for i in range(3):
        trades[1, None, i].wait_send()
    for copy in rests:
        copy.wait()
    for copy in row_copies:
        copy.wait_send()
    for copy in result_copies:
        copy.wait_send()
    line.drain(range(4))
    serve([], [], [6, 7])
    pair_sum.finish(r.pair_low, r.cosine, r.sine)
    for copy in [second] + emits:
        copy.wait()

    pair_sum.drain()
    line.drain(range(4, 2 * PARTS))


def backward(query, starts, cosine, sine, middle, cotangent, gain, pairs, turned_rows, grad_blocks, pieces, results, row_grads, output_weight):
    rows = cosine.shape[0]
    length = pairs.shape[1]
    held_rows = 2 * MODEL_WIDTH
    tokens = MB * SHARDS * rows
    dma = pltpu.SemaphoreType.DMA
    anywhere = pl.BlockSpec(memory_space=pl.ANY)
    vmem = pl.BlockSpec(memory_space=pltpu.VMEM)
    shape = jax.ShapeDtypeStruct
    tall, flat = (MODEL_WIDTH, F_BLOCK), (F_BLOCK, MODEL_WIDTH)
    two = lambda s: (2,) + s
    low = lambda s: pltpu.VMEM(s, bf16)
    number = 2 * PARTS
    return pl.pallas_call(
        backward_kernel,
        in_specs=[anywhere, pl.BlockSpec(memory_space=pltpu.SMEM), vmem, vmem, anywhere, anywhere, vmem]
        + [anywhere] * 9,
        out_specs=[anywhere, vmem, anywhere, anywhere, vmem, vmem] + [anywhere] * 6,
        out_shape=[
            shape(query.shape, bf16),
            shape((rows, 2 * KEY_WIDTH), bf16),
            shape((MB * rows, MODEL_WIDTH), bf16),
            shape((MB * rows, MODEL_WIDTH), f32),
            shape((8, MODEL_WIDTH), f32),
            shape((rows, MODEL_WIDTH), bf16),
            shape((held_rows, F_BLOCK), bf16),
            shape((held_rows, F_BLOCK), bf16),
            shape(tall, bf16),
            shape(tall, bf16),
            shape(two(flat), bf16),
            shape((length, 2 * KEY_WIDTH), bf16),
        ],
        scratch_shapes=[
            low((MB * rows, MODEL_WIDTH)),
            pltpu.VMEM((MB * rows, MODEL_WIDTH), f32),
            low((MB * rows, MODEL_WIDTH)),
            low((MB * rows, MODEL_WIDTH)),
            low((MB * rows, MODEL_WIDTH)),
            pltpu.VMEM((MB * rows, MODEL_WIDTH), f32),
            low((length, 2 * KEY_WIDTH)),
            low((MODEL_WIDTH, tokens)),
            low((tokens, MODEL_WIDTH)),
            low((3 * tokens, 2 * F)),
            low(tall),
            low(tall),
            low(flat),
            low(two(tall)),
            low(two(tall)),
            low(two(flat)),
            low(two(tall)),
            low(two(tall)),
            low(two(flat)),
            low(tall),
            low(tall),
            low(tall),
            low(tall),
            low((MB, rows, MODEL_WIDTH)),
            low((MB, SHARDS - 1, rows, MODEL_WIDTH)),
            low((rows, MODEL_WIDTH)),
            low((SHARDS - 1, rows, MODEL_WIDTH)),
            low((MB, rows, MODEL_WIDTH)),
            low((2, 2, length, LANES)),
            pltpu.VMEM((MB, length, rows), f32),
            low((LINE, rows, 2 * KEY_WIDTH)),
            low((LINE - 1, rows, 2 * KEY_WIDTH)),
            dma((4 * MB * SHARDS,)),
            dma((2,)),
            dma((2, 8)),
            dma((4,)),
            dma((2, MB * (SHARDS - 1))),
            dma((2, SHARDS - 1)),
            dma((2, 2)),
            dma((2, LINE)),
            dma((2, 2 * (LINE - 1))),
        ]
        + line_sems(number)
        + [dma((3,))],
        compiler_params=pltpu.CompilerParams(
            collective_id=3, has_side_effects=True, vmem_limit_bytes=VMEM_LIMIT
        ),
        name="backward",
    )(query, starts, cosine, sine, middle, cotangent, gain, pairs, turned_rows, grad_blocks, *pieces, results, row_grads, output_weight)


DENSE = ("output", "query", "pair", "gain")
LINE_ORDER = ("output", "query", "gain", "pair")
DENSE_PARTS = 4
FINE = 4
GATHER_AFTER = {4: ("output",), 9: ("query",), 13: ("gain", "pair")}
OUTPUT_AFTER = 19
DRAIN_LAG = 8


def dense_kernel(
    turned_normed_src,
    turned_attn_src,
    query_low_src,
    pair_low_first,
    middle_low_src,
    gain,
    gain_grad,
    cosine,
    sine,
    middle_grad_src,
    tokens_src,
    middle_src,
    query_src,
    pair_src,
    pair_grad,
    results_src,
    gate_rest,
    up_rest,
    down_rest,
    input_grad_out,
    block_output,
    results_in,
    output_total,
    query_total,
    pair_total,
    gain_total,
    gate_total,
    up_total,
    down_total,
    turned_normed,
    turned_attn,
    query_low,
    middle_low,
    input_grad,
    middle_grad,
    tokens,
    middle,
    pair_low,
    pair_own,
    pair_other,
    land_left,
    query_weight,
    pair_weight,
    gains,
    send_output,
    send_query,
    own_output,
    own_query,
    own_pair,
    own_gain,
    other_output,
    other_query,
    other_pair,
    other_gain,
    across_output,
    across_query,
    across_pair,
    across_gain,
    sum_output,
    sum_query,
    sum_pair,
    sum_gain,
    near_output,
    near_query,
    near_pair,
    near_gain,
    far_output,
    far_query,
    far_pair,
    far_gain,
    own_gate,
    own_up,
    own_down,
    near_gate,
    near_up,
    near_down,
    far_gate,
    far_up,
    far_down,
    load_sem,
    core_sem,
    left_sem,
    result_sem,
    trade_sem,
    across_sem,
    near_sem,
    far_sem,
    back_sem,
    pass_sem,
    store_sem,
    emit_sem,
):
    r = types.SimpleNamespace(**locals())
    at = lambda kind, name: getattr(r, kind + "_" + name)
    place = Place()
    core, shard = place.core, place.shard
    rows = r.middle.shape[0]
    held = MODEL_WIDTH // SHARDS
    half = held // 2
    loads = [
        pltpu.make_async_copy(source, target, r.load_sem.at[i])
        for i, (source, target) in enumerate(
            (
                (r.gate_rest, r.own_gate),
                (r.up_rest, r.own_up),
                (r.down_rest, r.own_down),
                (r.query_src, r.query_weight),
                (r.pair_src, r.pair_weight),
                (r.pair_grad.at[:, core], r.pair_own),
                (r.middle_grad_src, r.middle_grad),
                (r.tokens_src, r.tokens),
                (r.middle_src.at[rows : 2 * rows], r.middle),
                (r.turned_attn_src, r.turned_attn),
                (r.middle_low_src, r.middle_low),
                (r.turned_normed_src, r.turned_normed),
                (r.query_low_src, r.query_low),
            )
        )
    ]
    for load in loads:
        load.start()
    greet_line(place)
    pair_sum = PairSum(
        place,
        lambda j: r.pair_own.at[j],
        lambda j: r.pair_grad.at[j, 1 - core],
        r.pair_other,
        r.land_left,
        r.core_sem,
        r.left_sem,
    )
    pair_sum.trade()

    pieces = []
    for name, parts in (("gate", FINE), ("up", FINE), ("down", 2 * FINE)):
        pieces += line_pieces(place, at("own", name), at("near", name), at("far", name), getattr(r, name + "_total"), parts)
    expert_pieces = len(pieces)
    for name in LINE_ORDER:
        parts = 1 if name == "gain" else DENSE_PARTS
        pieces += line_pieces(
            place, at("sum", name), at("near", name), at("far", name), getattr(r, name + "_total"), parts
        )
    line = Line(place, pieces, (r.near_sem, r.far_sem, r.back_sem, r.pass_sem, r.store_sem))
    loads[0].wait()
    line.ready(0)
    loads[5].wait()
    pair_sum.meet()
    for i in (1, 2):
        loads[i].wait()
    line.ready(*range(1, expert_pieces))

    def block(b, of_core):
        return pl.ds(pl.multiple_of(b * held + of_core * half, half), half)

    trades = {}

    def dense(name, turned, right, sent):
        index = DENSE.index(name)
        trades[name] = []
        for b in range(SHARDS):
            sent[b] = dot(turned[block(b, 1 - core)], right[...]).astype(bf16)
            copy = remote(sent.at[b], at("other", name).at[b], r.trade_sem, index * SHARDS + b, place.partner)
            copy.start()
            trades[name].append(copy)
        for b in range(SHARDS):
            at("own", name)[b] = dot(turned[block(b, core)], right[...]).astype(bf16)

    crossings = {}

    def meet(name):
        own, other, across = at("own", name), at("other", name), at("across", name)
        for b in range(SHARDS):
            trades[name][b].wait_recv()
            add_into(own.at[b], own.at[b], other.at[b])
        crossings[name] = []
        for k in range(1, SHARDS):
            index = DENSE.index(name) * (SHARDS - 1) + k - 1
            copy = remote(own.at[place.peer_index(k)], across.at[k - 1], r.across_sem, index, place.peer(k))
            copy.start()
            crossings[name].append(copy)

    def gather(name):
        for copy in crossings[name]:
            copy.wait_recv()
        across = at("across", name)
        add_into(at("sum", name), at("own", name).at[shard], *[across.at[k] for k in range(SHARDS - 1)])

    for load in loads[9:]:
        load.wait()
    dense("output", r.turned_attn, r.middle_low, r.send_output)
    dense("query", r.turned_normed, r.query_low, r.send_query)
    meet("output")
    line.serve([0])
    pair_sum.step(2)
    meet("query")
    pair_sum.step(3)
    for copy in trades["output"]:
        copy.wait_send()
    r.pair_low[0:rows] = r.pair_low_first[...]
    pair_sum.finish(r.pair_low.at[rows : 2 * rows], r.cosine, r.sine)
    dense("pair", r.turned_normed, r.pair_low, r.send_output.at[:, :, 0 : 2 * KEY_WIDTH])
    line.serve([1], [0])
    for load in loads[3:5] + loads[6:9]:
        load.wait()

    gain_one_grad = jnp.zeros((1, MODEL_WIDTH), f32)
    for m in range(MB):
        own = slice(m * rows, (m + 1) * rows)
        values = r.tokens[own].astype(f32)
        scale = lax.rsqrt(jnp.mean(values * values, axis=-1, keepdims=True) + eps)
        unit = values * scale
        normed_grad = dot(r.query_low[own], r.query_weight[...], NT) + dot(r.pair_low[own], r.pair_weight[...], NT)
        gain_one_grad = gain_one_grad + jnp.sum(normed_grad * unit, axis=0, keepdims=True)
        weighted = normed_grad * r.gain[0:1]
        inner = jnp.mean(weighted * unit, axis=-1, keepdims=True)
        r.input_grad[own] = r.middle_grad[own] + (weighted - unit * inner) * scale
        if m == 0:
            meet("pair")
            line.serve([2], [1])
    line.serve([3], [2])
    grad_emit = pltpu.make_async_copy(r.input_grad, r.input_grad_out, r.emit_sem.at[0])
    grad_emit.start()
    gain_two_grad = jnp.sum(r.gain_grad[...], axis=0, keepdims=True)
    stacked = jnp.concatenate(
        [gain_one_grad, gain_two_grad, jnp.zeros((LANES - 2, MODEL_WIDTH), f32)], axis=0
    )
    r.gains[...] = stacked.T.astype(bf16)
    trades["gain"] = []
    for b in range(SHARDS):
        source = r.gains.at[block(b, 1 - core)]
        index = DENSE.index("gain") * SHARDS + b
        trades["gain"].append(remote(source, r.other_gain.at[b], r.trade_sem, index, place.partner))
        trades["gain"][b].start()
        r.own_gain[b] = r.gains[block(b, core)]
    meet("gain")

    result_copies = []
    for k in range(1, SHARDS):
        source = r.results_src.at[1, place.peer_index(k)]
        result_copies.append(remote(source, r.results_in.at[k - 1], r.result_sem, k - 1, place.peer(k)))
        result_copies[-1].start()
    for copy in trades["pair"]:
        copy.wait_send()
    result_parts = [r.send_output.at[k, 0:rows] for k in range(SHARDS)]
    result_loads = [
        pltpu.make_async_copy(source, target, r.load_sem.at[13 + k])
        for k, (source, target) in enumerate(
            zip([r.results_src.at[1, shard]] + [r.results_in.at[k] for k in range(SHARDS - 1)], result_parts)
        )
    ]
    result_loads[0].start()

    def output_rows():
        for copy, load in zip(result_copies, result_loads[1:]):
            copy.wait_recv()
            load.start()
        total = r.middle[...]
        for load, part in zip(result_loads, result_parts):
            load.wait()
            total = total + part[...].astype(f32)
        r.block_output[...] = total.astype(bf16)

    number = len(pieces)
    first = expert_pieces
    spans = {}
    for name in LINE_ORDER:
        parts = 1 if name == "gain" else DENSE_PARTS
        spans[name] = range(first, first + parts)
        first += parts
    lag = 4
    for i in range(number + lag):
        line.serve(
            [i] if 4 <= i < number else [],
            [i - 1] if 4 <= i <= number else [],
            [i - lag] if i >= lag else [],
        )
        for name in GATHER_AFTER.get(i, ()):
            gather(name)
            line.ready(*spans[name])
        if DRAIN_LAG <= i < number:
            line.drain([i - DRAIN_LAG])
        if i == OUTPUT_AFTER:
            output_rows()
            for name in DENSE:
                for copy in crossings[name]:
                    copy.wait_send()
                if name in ("query", "gain"):
                    for copy in trades[name]:
                        copy.wait_send()
            for copy in result_copies:
                copy.wait_send()
            pair_sum.drain()

    grad_emit.wait()
    line.drain(range(number - DRAIN_LAG, number))


def dense_weights(vectors, streamed, query_weight, pair_weight, pair_grad, results, rests):
    dma = pltpu.SemaphoreType.DMA
    anywhere = pl.BlockSpec(memory_space=pl.ANY)
    vmem = pl.BlockSpec(memory_space=pltpu.VMEM)
    shape = jax.ShapeDtypeStruct
    rows = pair_grad.shape[2]
    low = lambda *s: pltpu.VMEM(s, bf16)
    held = MODEL_WIDTH // SHARDS
    half = held // 2
    widths = (MODEL_WIDTH, MODEL_WIDTH, 2 * KEY_WIDTH, LANES)
    tall = (MODEL_WIDTH, F_BLOCK)
    number = 4 * FINE + 3 * DENSE_PARTS + 1
    return pl.pallas_call(
        dense_kernel,
        in_specs=[anywhere] * 3 + [vmem, anywhere] + [vmem] * 4 + [anywhere] * (7 + len(streamed)),
        out_specs=[anywhere, vmem] + [anywhere] * 8,
        out_shape=[
            shape((MB * rows, MODEL_WIDTH), f32),
            shape((rows, MODEL_WIDTH), bf16),
            shape((SHARDS - 1, rows, MODEL_WIDTH), bf16),
        ]
        + [shape((held, w), bf16) for w in widths]
        + [
            shape((2 * MODEL_WIDTH, F_BLOCK), bf16),
            shape((2 * MODEL_WIDTH, F_BLOCK), bf16),
            shape((2 * F, MODEL_WIDTH), bf16),
        ],
        scratch_shapes=[
            low(MODEL_WIDTH, MB * rows),
            low(MODEL_WIDTH, MB * rows),
            low(MB * rows, MODEL_WIDTH),
            low(MB * rows, MODEL_WIDTH),
            pltpu.VMEM((MB * rows, MODEL_WIDTH), f32),
            pltpu.VMEM((MB * rows, MODEL_WIDTH), f32),
            low(MB * rows, MODEL_WIDTH),
            pltpu.VMEM((rows, MODEL_WIDTH), f32),
            low(MB * rows, 2 * KEY_WIDTH),
            low(LINE, rows, 2 * KEY_WIDTH),
            low(LINE, rows, 2 * KEY_WIDTH),
            low(LINE - 1, rows, 2 * KEY_WIDTH),
            low(*query_weight.shape),
            low(*pair_weight.shape),
            low(MODEL_WIDTH, LANES),
            low(SHARDS, half, MODEL_WIDTH),
            low(SHARDS, half, MODEL_WIDTH),
        ]
        + [low(SHARDS, half, w) for w in widths] * 2
        + [low(SHARDS - 1, half, w) for w in widths]
        + [low(half, w) for w in widths] * 3
        + [low(*tall), low(*tall), low(F, MODEL_WIDTH)] * 3
        + [dma((13 + SHARDS,)), dma((2, LINE)), dma((2, 2 * (LINE - 1))), dma((2, SHARDS - 1)), dma((2, 4 * SHARDS)), dma((2, 4 * (SHARDS - 1)))]
        + line_sems(number)
        + [dma((1,))],
        compiler_params=pltpu.CompilerParams(
            collective_id=4, has_side_effects=True, vmem_limit_bytes=VMEM_LIMIT
        ),
        name="dense_weights",
    )(*vectors, *streamed, query_weight, pair_weight, pair_grad, results, *rests)


def widen_kernel(*refs):
    r = refs
    step = pl.program_id(0)
    parts, (shrink, dense, rows_in, gains, grad) = r[:4], (r[4], r[5:8], r[8:10], r[10], r[11])
    expand_out, shrink_out, dense_out, rows_out, gain_outs, grad_out = r[12], r[13], r[14:17], r[17], r[18:20], r[20]
    for i, ref in enumerate(parts):
        expand_out[:, i * F_BLOCK : (i + 1) * F_BLOCK] = ref[...].astype(f32)
    shrink_out[...] = shrink[...].astype(f32)
    grad_out[...] = grad[...]

    for source, target in zip(dense, dense_out):
        target[...] = source[...].astype(f32)

    for i in range(MB):

        @pl.when(step // (WIDEN_STEPS // MB) == i)
        def _():
            rows_out[...] = rows_in[i][...]

    @pl.when(step == 0)
    def _():
        turned = gains[...].astype(f32).T
        for i in range(2):
            gain_outs[i][...] = turned[i]


WIDEN_STEPS = 4


def widen(expand_parts, shrink, dense, rows, gains, grad):
    n = WIDEN_STEPS
    every = lambda a: pl.BlockSpec((a.shape[0] // n, a.shape[1]), lambda i: (i, 0))
    one = lambda a: pl.BlockSpec(a.shape, lambda i: (0, 0))
    size = MB * rows[0].shape[0] // n
    half = lambda m: pl.BlockSpec(
        (size, MODEL_WIDTH), lambda i: (jnp.clip(i - m * (n // MB), 0, n // MB - 1), 0)
    )
    shape = jax.ShapeDtypeStruct
    expand = shape((expand_parts[0].shape[0], 2 * F), f32)
    joined = shape((MB * rows[0].shape[0], MODEL_WIDTH), bf16)
    gain = shape((gains.shape[0],), f32)
    flat = pl.BlockSpec(gain.shape, lambda i: (0,))
    dense_out = [shape(a.shape, f32) for a in dense]
    return pl.pallas_call(
        widen_kernel,
        grid=(n,),
        in_specs=[every(a) for a in expand_parts]
        + [every(shrink)]
        + [every(a) for a in dense]
        + [half(m) for m in range(MB)]
        + [one(gains), every(grad)],
        out_specs=[every(expand), every(shrink)]
        + [every(a) for a in dense]
        + [every(joined), flat, flat, every(grad)],
        out_shape=[expand, shape(shrink.shape, f32), *dense_out, joined, gain, gain, shape(grad.shape, f32)],
        compiler_params=pltpu.CompilerParams(vmem_limit_bytes=VMEM_LIMIT),
        name="widen",
    )(*expand_parts, shrink, *dense, *rows, gains, grad)


def shards(
    tokens,
    doc_starts,
    routes,
    gates,
    attn_gain,
    w_q,
    key_value_weight,
    w_o,
    moe_gain,
    expert_in,
    expert_out,
    cotangent,
):
    links = Links()
    rows = tokens.shape[2]
    length = rows * links.contexts
    held = expert_in.shape[0]
    chained = links.chips == LINE and links.shards == SHARDS and held == 2
    width = w_q.shape[0]
    flat_tokens = tokens.reshape(MB * rows, MODEL_WIDTH)
    if chained:
        flat_cotangent = cotangent.reshape(MB * rows, MODEL_WIDTH)
        starts = doc_starts[:, 0]
        (
            turned_normed,
            query,
            turned_attn,
            middle,
            gains,
            cosine,
            sine,
            pair_weight,
            query_weight,
            output_weight,
            pairs,
            turned_rows,
            grad_blocks,
            result_blocks,
            row_grad_blocks,
            active,
            gate,
            up,
        ) = forward(
            flat_tokens,
            routes.transpose(0, 1, 3, 2),
            gates.transpose(0, 1, 3, 2),
            jnp.concatenate([attn_gain, moe_gain]).reshape(2, width),
            flat_cotangent,
            starts,
            rotation_constants(length),
            (key_value_weight, w_q, w_o),
            expert_in,
            expert_out,
        )
        result_blocks = result_blocks.reshape(grad_blocks.shape)
        row_grad_blocks = row_grad_blocks.reshape(grad_blocks.shape)
        (
            query_low,
            pair_low,
            middle_low,
            middle_grad,
            gain_two_grad,
            output_first,
            gate_first,
            up_first,
            gate_rest,
            up_rest,
            down_rest,
            pair_grad,
        ) = backward(
            query,
            starts,
            cosine,
            sine,
            middle,
            flat_cotangent,
            gains,
            pairs,
            turned_rows,
            grad_blocks,
            (active, gate, up),
            result_blocks,
            row_grad_blocks,
            output_weight,
        )
        (
            input_grad,
            output_second,
            _,
            output_total,
            query_total,
            pair_total,
            gain_total,
            gate_second,
            up_second,
            shrink_total,
        ) = dense_weights(
            (
                turned_normed,
                turned_attn,
                query_low,
                pair_low,
                middle_low,
                gains,
                gain_two_grad,
                cosine,
                sine,
            ),
            (middle_grad, flat_tokens, middle),
            query_weight,
            pair_weight,
            pair_grad.reshape(LINE, 2, rows, 2 * KEY_WIDTH),
            result_blocks,
            (gate_rest, up_rest, down_rest.reshape(F, MODEL_WIDTH)),
        )
        (
            expand_total,
            shrink_total,
            output_total,
            query_total,
            pair_total,
            block_output,
            gain_one_total,
            gain_two_total,
            input_grad,
        ) = widen(
            (gate_first, gate_second, up_first, up_second),
            shrink_total,
            (output_total, query_total, pair_total),
            (output_first, output_second),
            gain_total,
            input_grad,
        )
        return (
            block_output.reshape(MB, 1, rows, MODEL_WIDTH),
            input_grad.reshape(MB, 1, rows, MODEL_WIDTH),
            gain_one_total,
            query_total,
            pair_total,
            output_total,
            gain_two_total,
            expand_total.reshape(held, MODEL_WIDTH, 2 * F),
            shrink_total.reshape(held, F, MODEL_WIDTH),
        )

    positions = links.context * rows + jnp.arange(rows, dtype=jnp.int32)
    cosine, sine = rotation_tables(positions)
    key_places = jnp.arange(length, dtype=jnp.int32)
    flat_values = flat_tokens.astype(f32)
    scale_one = lax.rsqrt(jnp.mean(flat_values * flat_values, axis=-1, keepdims=True) + eps)
    unit_one = flat_values * scale_one
    expert_ids = jnp.arange(E, dtype=jnp.int32)
    chosen = (routes.reshape(MB, rows, TOP)[..., None] == expert_ids).astype(f32)
    combine = jnp.sum(gates.reshape(MB, rows, TOP)[..., None] * chosen, axis=2)
    gather = lambda w: lax.all_gather(w, "fsdp", axis=0, tiled=True)
    pair_weight, query_weight, output_weight = gather(key_value_weight), gather(w_q), gather(w_o)
    gain_one, gain_two = gather(attn_gain).astype(f32), gather(moe_gain).astype(f32)
    normed = (unit_one * gain_one).astype(bf16)
    both = lambda table: jnp.concatenate([table] * MB)
    own_pairs = rotate_columns(dot(normed, pair_weight), both(cosine), both(sine), KEY_WIDTH)
    query = rotate_columns(dot(normed, query_weight), both(cosine), both(sine), MODEL_WIDTH)
    own_pairs = own_pairs.reshape(MB, rows, 2 * KEY_WIDTH)
    pairs = lax.all_gather(own_pairs, "ctx", axis=1, tiled=True)

    combine = jnp.concatenate([combine] + [links.across(combine, k) for k in range(1, links.shards)], axis=1)
    combine = lax.dynamic_slice_in_dim(combine, links.shard * held, held, 2)
    combine = combine.transpose(0, 2, 1)[..., None]

    biases, biases_turned = [], []
    for m in range(MB):
        starts = doc_starts[m, 0]
        begin = jnp.max(jnp.where(starts[None, :] <= positions[:, None], starts[None, :], 0), axis=1)
        seen = (key_places[None, :] <= positions[:, None]) & (key_places[None, :] >= begin[:, None])
        biases.append(jnp.where(seen, 0.0, -1e30).astype(f32))
        places, begins = jnp.tile(positions, GROUP), jnp.tile(begin, GROUP)
        seen = (key_places[:, None] <= places[None, :]) & (key_places[:, None] >= begins[None, :])
        biases_turned.append(jnp.where(seen, 0.0, -1e30).astype(f32))

    middles, attns, results, row_grads = [], [], [], []
    rows_kept, grads_kept, pieces_kept = [], [], []
    for m in range(MB):
        own = slice(m * rows, (m + 1) * rows)
        attn = attention_forward(m, query, pairs, biases[m])
        middle = flat_tokens[own].astype(f32) + dot(attn, output_weight)
        scale_two = lax.rsqrt(jnp.mean(middle * middle, axis=-1, keepdims=True) + eps)
        moe_in = (middle * scale_two * gain_two).astype(bf16)
        out_grad = cotangent[m, 0]
        row_parts = [moe_in] + [links.across(moe_in, k) for k in range(1, links.shards)]
        grad_parts = [out_grad] + [links.across(out_grad, k) for k in range(1, links.shards)]
        result, row_grad, pieces = experts(row_parts, grad_parts, combine[m], expert_in, expert_out)
        for parts, sums in ((result, results), (row_grad, row_grads)):
            total = parts[0].astype(f32)
            for k in range(1, links.shards):
                total = total + links.across(parts[k], k).astype(f32)
            sums.append(total)
        middles.append(middle)
        attns.append(attn)
        rows_kept += row_parts
        grads_kept += grad_parts
        pieces_kept.append(pieces)
    merge = lambda items: jnp.concatenate(items, axis=0)
    expert_grads = expert_weights(
        merge(rows_kept), merge(grads_kept), *[merge([p[i] for p in pieces_kept]) for i in range(3)], held
    )
    expert_grads = [g.reshape(-1, g.shape[-1]) for g in expert_grads]
    outputs = [(middles[m] + results[m]).astype(bf16) for m in range(MB)]

    input_grads, query_lows, pair_lows, middle_lows = [], [], [], []
    gain_one_grad, gain_two_grad = 0.0, 0.0
    for m in range(MB):
        own = slice(m * rows, (m + 1) * rows)
        scale_two = lax.rsqrt(jnp.mean(middles[m] * middles[m], axis=-1, keepdims=True) + eps)
        unit_two = middles[m] * scale_two
        moe_in_grad = row_grads[m]
        gain_two_grad = gain_two_grad + jnp.sum(moe_in_grad * unit_two, axis=0)
        weighted = moe_in_grad * gain_two
        inner = jnp.mean(weighted * unit_two, axis=-1, keepdims=True)
        middle_grad = cotangent[m, 0].astype(f32) + (weighted - unit_two * inner) * scale_two
        middle_low = middle_grad.astype(bf16)
        attn_grad = dot(middle_low, output_weight, NT).astype(bf16)
        query_low, pair_grad = attention_backward(
            m, query, cosine, sine, pairs, biases_turned[m], attn_grad
        )
        parts = [lax.psum_scatter(pair_grad, "ctx", scatter_dimension=0, tiled=True)]
        pair_low = pair_gradient(parts, cosine, sine)
        normed_grad = dot(query_low, query_weight, NT) + dot(pair_low, pair_weight, NT)
        gain_one_grad = gain_one_grad + jnp.sum(normed_grad * unit_one[own], axis=0)
        weighted = normed_grad * gain_one
        inner = jnp.mean(weighted * unit_one[own], axis=-1, keepdims=True)
        residual_grad = (weighted - unit_one[own] * inner) * scale_one[own]
        input_grads.append(middle_grad + residual_grad)
        query_lows.append(query_low)
        pair_lows.append(pair_low)
        middle_lows.append(middle_low)

    join = lambda items: jnp.concatenate(items, axis=0)

    output_grad = dot(join(attns), join(middle_lows), TN).astype(bf16)
    query_grad = dot(normed, join(query_lows), TN).astype(bf16)
    pair_weight_grad = dot(normed, join(pair_lows), TN).astype(bf16)
    gain_grads = jnp.stack([gain_one_grad, gain_two_grad], axis=1)
    gain_grads = jnp.pad(gain_grads, ((0, 0), (0, LANES - 2))).astype(bf16)
    dense_grads = [output_grad, query_grad, jnp.concatenate([pair_weight_grad, gain_grads], axis=1)]
    totals = [lax.psum(g, "ctx") for g in expert_grads]
    for g in dense_grads:
        part = lax.psum_scatter(g, "fsdp", scatter_dimension=0, tiled=True)
        totals.append(lax.psum(part, "ctx"))
    gate_total, up_total, down_total, output_total, query_total, pair_total = [t.astype(f32) for t in totals]
    expand_total = jnp.concatenate([gate_total, up_total], axis=1)

    return (
        jnp.stack(outputs)[:, None],
        jnp.stack(input_grads)[:, None],
        pair_total[:, 2 * KEY_WIDTH],
        query_total,
        pair_total[:, : 2 * KEY_WIDTH],
        output_total,
        pair_total[:, 2 * KEY_WIDTH + 1],
        expand_total.reshape(held, MODEL_WIDTH, 2 * F),
        down_total.reshape(held, F, MODEL_WIDTH),
    )


def solution(mesh):
    return jax.shard_map(
        shards,
        mesh=mesh,
        in_specs=(
            P(None, "fsdp", "ctx", None),
            P(None, "fsdp", None),
            P(None, "fsdp", "ctx", None),
            P(None, "fsdp", "ctx", None),
            P("fsdp"),
            P("fsdp", None),
            P("fsdp", None),
            P("fsdp", None),
            P("fsdp"),
            P("fsdp", None, None),
            P("fsdp", None, None),
            P(None, "fsdp", "ctx", None),
        ),
        out_specs=(
            P(None, "fsdp", "ctx", None),
            P(None, "fsdp", "ctx", None),
            P("fsdp"),
            P("fsdp", None),
            P("fsdp", None),
            P("fsdp", None),
            P("fsdp"),
            P("fsdp", None, None),
            P("fsdp", None, None),
        ),
        check_vma=False,
    )
```
